32 devices in a mesh: cam: 4 (over y, x), tile: 8 (over z, core).
Axes of the slice: x: 2, y: 2, z: 4, core: 2. Of those that a mesh axis runs over, the one named last changes fastest.
Arguments:
- positions: float32 [3, 32768], P(None, ('cam', 'tile')), may hold values from -1 to 1
- log_scales: float32 [3, 32768], P(None, ('cam', 'tile')), may hold values from -4.5 to -2.5
- rotations: float32 [4, 32768], P(None, ('cam', 'tile')), may hold values from 0.3 to 1
- opacities: float32 [32768], P(('cam', 'tile')), may hold values from -6 to -3
- colors: float32 [48, 32768], P(None, ('cam', 'tile')), may hold values from -3 to 3
- cameras: float32 [2, 4, 6], replicated, may hold values from -0.05 to 0.05
- targets: float32 [2, 4, 8, 3, 256], P(None, 'cam', 'tile'), may hold values from 0 to 1
- tile_ids: int32 [2, 4, 8], P(None, 'cam', 'tile'), may hold values from 15488 to 17280, as said below
- tile_counts: int32 [2, 4, 8], P(None, 'cam', 'tile'), may hold values from 128 to 256, as said below
- tile_lists: int32 [2, 4, 8, 256], P(None, 'cam', 'tile'), may hold values from 0 to 1023, as said below
- fetch_ids: int32 [2, 4, 8, 4, 8, 32], P(None, 'cam', 'tile'), may hold values from 0 to 1023, as said below
Outputs:
- grad_positions: float32 [3, 32768], P(None, ('cam', 'tile'))
- grad_log_scales: float32 [3, 32768], P(None, ('cam', 'tile'))
- grad_rotations: float32 [4, 32768], P(None, ('cam', 'tile'))
- grad_opacities: float32 [32768], P(('cam', 'tile'))
- grad_colors: float32 [48, 32768], P(None, ('cam', 'tile'))
The draws below stay inside these ranges and needn't reach their ends.
Inputs may be any that keep to these rules, and one draw needn't show every extreme that they name: Within one row fetch_ids[p, c, t, a, b, :] the entries are distinct local columns of the owner at cam a, tile b, all within the block of 1024 // 8 columns that belongs to the device's row of tiles; not every slot is named by a list. `tile_lists`: entries are slots of the rendering device, distinct within a tile, in increasing order of the third coordinate of their Gaussians' positions. `tile_counts`: each device has a tile with 256 live entries in each pass. `tile_ids`: each device renders one image tile in a pass; in each pass and camera group the devices' rows are distinct and together form a window of 8 rows.
All inputs are finite; a program needn't handle non-finite values.
Results may differ from the reference program's by a relative error of at most 0.0003.
Values sent between devices are 32-bit elements; how exact they have to be, the bound alone decides.
No kernel may reach another device: no remote copies, remote signals or barrier semaphores. Data moves between devices by JAX's collectives and lax.ppermute only.
A program may use at most 192 MiB of HBM per device.

```python
import jax
import jax.numpy as jnp
from jax import lax

G_DEV = 1024
TILES_DEV = 1
PASSES = 2
LIST = 256
PIX = 256
COEFS = 48
CAP = 32
TILES = 8
NG = 32768
N_CAM = 4
N_TILE = 8


def region_ranks(key):
    count = N_CAM * N_TILE * (G_DEV // N_TILE)
    region_keys = jax.random.split(jax.random.fold_in(key, 13), N_TILE)

    def shuffle(region_key):
        return jax.random.permutation(region_key, count)
    return jax.vmap(shuffle)(region_keys).astype(jnp.int32)


def region_layout(key):
    ranks = region_ranks(key)
    seeds = jax.random.split(jax.random.fold_in(key, 11), 6)
    owners = N_CAM * N_TILE
    slots = owners * CAP
    lead = (PASSES, N_CAM, N_TILE)
    per_region = G_DEV // N_TILE
    count = owners * per_region

    def shuffle_rows(row_key):
        return jax.random.permutation(row_key, N_TILE)
    assigned = jax.vmap(shuffle_rows)(jax.random.split(seeds[0], PASSES * N_CAM)).reshape(lead).astype(jnp.int32)
    owner_index = jnp.arange(owners, dtype=jnp.int32)
    usage = jax.random.randint(seeds[1], lead + (owners,), max(1, CAP // 4), CAP + 1, dtype=jnp.int32)
    heavy = jax.random.randint(seeds[2], (PASSES, 1, 1, 1), 0, owners, dtype=jnp.int32)
    usage = jnp.where(owner_index == heavy, CAP, usage)
    extra = jax.random.randint(seeds[3], lead + (1,), 0, owners, dtype=jnp.int32)
    usage = jnp.where(owner_index == extra, CAP, usage)
    usage = usage.at[0, 0, 0, owners - 1].set(CAP)
    limit = 2 ** 31 // (per_region + 1)
    noise = jax.random.randint(seeds[4], lead + (owners, per_region), 0, limit, dtype=jnp.int32)
    scores = noise * per_region + jnp.arange(per_region, dtype=jnp.int32)
    scores = scores.at[0, 0, :, 0, 0].set(2147483647).at[0, 0, :, owners - 1, per_region - 1].set(2147483646)
    unused, within = lax.top_k(scores, CAP)
    within = within.astype(jnp.int32)
    fetched = assigned[..., None, None] * per_region + within
    fetched = fetched.reshape(PASSES, N_CAM, N_TILE, N_CAM, N_TILE, CAP).astype(jnp.int32)
    slot_index = jnp.arange(CAP, dtype=jnp.int32)
    valid = (slot_index < usage[..., None]).reshape(lead + (slots,))
    home = (within % TILES_DEV).reshape(lead + (slots,))
    slot_rank = ranks[assigned[..., None, None], owner_index[:, None] * per_region + within].reshape(lead + (slots,))
    tile_index = jnp.arange(TILES_DEV, dtype=jnp.int32)
    distance = jnp.abs(home[..., None, :] - tile_index[:, None])
    spread = 2 ** 31 // ((TILES_DEV + 1) * (slots + 1))
    jitter = jax.random.randint(seeds[5], lead + (TILES_DEV, slots), 0, spread, dtype=jnp.int32)
    flat_index = jnp.arange(slots, dtype=jnp.int32)
    closeness = ((TILES_DEV - distance) * spread + jitter) * slots + flat_index
    closeness = jnp.where(valid[..., None, :], closeness, -1 - flat_index)
    closeness = closeness.at[0, 0, 0, 0, 0].set(2147483647).at[0, 0, 0, 0, slots - 1].set(2147483646)
    unused, near = lax.top_k(closeness, LIST)
    near = near.astype(jnp.int32)
    near_rank = jnp.take_along_axis(jnp.broadcast_to(slot_rank[..., None, :], lead + (TILES_DEV, slots)), near, axis=-1)
    unused, front = lax.top_k(count - near_rank, LIST)
    chosen = jnp.take_along_axis(near, front.astype(jnp.int32), axis=-1)
    chosen = chosen.reshape(PASSES, N_CAM, N_TILE * TILES_DEV, LIST).astype(jnp.int32)
    first_row = 64 - N_TILE // 2
    first_col = 128 - TILES_DEV // 2
    numbers = (first_row + assigned)[..., None] * 256 + first_col + tile_index
    numbers = numbers.reshape(PASSES, N_CAM, N_TILE * TILES_DEV).astype(jnp.int32)
    return (fetched, chosen, numbers)


def draw_fetch_ids(key, part):
    return region_layout(key)[0]


def draw_tile_lists(key, part):
    return region_layout(key)[1]


def draw_tile_ids(key, part):
    return region_layout(key)[2]


def draw_tile_counts(key, part):
    seeds = jax.random.split(jax.random.fold_in(key, 5), 2)
    counts = jax.random.randint(seeds[0], (PASSES, N_CAM, N_TILE, TILES_DEV), LIST // 2, LIST + 1, dtype=jnp.int32)
    full = jax.random.randint(seeds[1], (PASSES, N_CAM, N_TILE, 1), 0, TILES_DEV, dtype=jnp.int32)
    counts = jnp.where(jnp.arange(TILES_DEV, dtype=jnp.int32) == full, LIST, counts)
    return counts.reshape(PASSES, N_CAM, N_TILE * TILES_DEV).astype(jnp.int32)


def draw_positions(key, part):
    ranks = region_ranks(key)
    owners = N_CAM * N_TILE
    per_region = G_DEV // N_TILE
    count = owners * per_region
    owner_index = jnp.arange(owners, dtype=jnp.int32)[:, None]
    column = jnp.arange(G_DEV, dtype=jnp.int32)[None, :]
    region = column // per_region
    within = column % per_region
    rank = ranks[region, owner_index * per_region + within]
    home_col = jnp.broadcast_to(128 - TILES_DEV // 2 + within % TILES_DEV, (owners, G_DEV)).astype(jnp.float32)
    home_row = jnp.broadcast_to(64 - N_TILE // 2 + region, (owners, G_DEV)).astype(jnp.float32)
    float_keys = jax.random.split(jax.random.fold_in(key, 23), 3)
    shape = (owners, G_DEV)
    shift_x = jax.random.uniform(float_keys[0], shape, jnp.float32, -8.0, 24.0)
    shift_y = jax.random.uniform(float_keys[1], shape, jnp.float32, -8.0, 24.0)
    depth_shift = jax.random.uniform(float_keys[2], shape, jnp.float32, 0.2, 0.8)
    screen_x = 16.0 * home_col + shift_x
    screen_y = 16.0 * home_row + shift_y
    depth = 5.0 + 2.0 * (rank.astype(jnp.float32) + depth_shift) / count
    placed = jnp.stack([(screen_x - 2048.0) * depth / 4096.0, (screen_y - 1024.0) * depth / 4096.0, depth - 6.0])
    return placed.reshape(3, owners * G_DEV).astype(jnp.float32)


def draw_cameras(key, part):
    reach = jnp.array([0.0001, 0.0001, 0.002, 0.01, 0.01, 0.05], dtype=jnp.float32)
    float_keys = jax.random.split(jax.random.fold_in(key, 31), 1)
    shape = (PASSES, N_CAM, 6)
    values = jax.random.uniform(float_keys[0], shape, jnp.float32, -1.0, 1.0)
    return (values * reach).astype(jnp.float32)


def steps_of(own_key, shape, shards, low, largest):
    level, own = 1.0, jax.random.fold_in(own_key, 6)
    for axis_at, parts in shards:
        steps = jnp.exp(jax.random.uniform(jax.random.fold_in(own, axis_at), (parts,), jnp.float32, low / len(shards), largest / len(shards)))
        level = level * jnp.repeat(steps, shape[axis_at] // parts).reshape([-1 if axis == axis_at else 1 for axis in range(len(shape))])
    return level


def centred(rng, shape, scale, most, cuts=(), held_as=jnp.bfloat16):
    values = jax.random.normal(rng, shape, jnp.float32) * scale
    if len(cuts) > 0:
        values = steps_of(rng, shape, cuts, -0.22, 0.18) * values
    return jnp.clip(values, min=-most, max=most).astype(held_as)


def setup_inputs(seed: int = 0) -> dict:
    arg_keys = jax.random.split(jax.random.key(seed), 12)
    positions = draw_positions(jax.random.fold_in(arg_keys[11], 71), 0)
    log_scales = jnp.clip(-4.5 + 2.0 * jax.random.uniform(arg_keys[1], (3, NG), jnp.float32) ** steps_of(arg_keys[1], (3, NG), ((1, 32),), -0.2, 0.2), -4.5, -2.5)
    rotations = jnp.clip(0.3 + 0.7 * jax.random.uniform(arg_keys[2], (4, NG), jnp.float32) ** steps_of(arg_keys[2], (4, NG), ((1, 32),), -0.2, 0.2), 0.3, 1.0)
    opacities = jnp.clip(-6.0 + 3.0 * jax.random.uniform(arg_keys[3], (NG,), jnp.float32) ** steps_of(arg_keys[3], (NG,), ((0, 32),), -0.2, 0.2), -6.0, -3.0)
    colors = centred(arg_keys[4], (COEFS, NG), 0.5, 3.0, ((1, 32),), jnp.float32)
    cameras = draw_cameras(jax.random.fold_in(arg_keys[11], 71), 0)
    targets = jnp.clip(1.0 * jax.random.uniform(arg_keys[6], (PASSES, N_CAM, TILES, 3, PIX), jnp.float32) ** steps_of(arg_keys[6], (PASSES, N_CAM, TILES, 3, PIX), ((1, 4), (2, 8)), -0.2, 0.2), 0.0, 1.0)
    tile_ids = draw_tile_ids(jax.random.fold_in(arg_keys[11], 71), 0)
    tile_counts = draw_tile_counts(jax.random.fold_in(arg_keys[11], 71), 0)
    tile_lists = draw_tile_lists(jax.random.fold_in(arg_keys[11], 71), 0)
    fetch_ids = draw_fetch_ids(jax.random.fold_in(arg_keys[11], 71), 0)
    return {"positions": positions, "log_scales": log_scales, "rotations": rotations, "opacities": opacities, "colors": colors, "cameras": cameras, "targets": targets, "tile_ids": tile_ids, "tile_counts": tile_counts, "tile_lists": tile_lists, "fetch_ids": fetch_ids}


FOCAL = 4096.0
SH_ZERO = 0.28209479177387814
SH_ONE = 0.4886025119029199
SH_TWO = [1.0925484305920792, -1.0925484305920792, 0.31539156525252005, -1.0925484305920792, 0.5462742152960396]
SH_THREE = [-0.5900435899266435, 2.890611442640554, -0.4570457994644658, 0.3731763325901154, -0.4570457994644658, 1.445305721320277, -0.5900435899266435]

def matmul3(left, right):
    return [[left[i][0] * right[0][j] + left[i][1] * right[1][j] + left[i][2] * right[2][j] for j in range(3)] for i in range(3)]

def project(raw, camera):
    cos_a, sin_a = (jnp.cos(camera[0]), jnp.sin(camera[0]))
    cos_b, sin_b = (jnp.cos(camera[1]), jnp.sin(camera[1]))
    cos_c, sin_c = (jnp.cos(camera[2]), jnp.sin(camera[2]))
    turn_x = [[1.0, 0.0, 0.0], [0.0, cos_a, -sin_a], [0.0, sin_a, cos_a]]
    turn_y = [[cos_b, 0.0, sin_b], [0.0, 1.0, 0.0], [-sin_b, 0.0, cos_b]]
    turn_z = [[cos_c, -sin_c, 0.0], [sin_c, cos_c, 0.0], [0.0, 0.0, 1.0]]
    rotate = matmul3(matmul3(turn_z, turn_y), turn_x)
    offset = [camera[3], camera[4], 6.0 + camera[5]]
    point = [raw[0], raw[1], raw[2]]
    viewed = [rotate[i][0] * point[0] + rotate[i][1] * point[1] + rotate[i][2] * point[2] + offset[i] for i in range(3)]
    anchor = [-(rotate[0][j] * offset[0] + rotate[1][j] * offset[1] + rotate[2][j] * offset[2]) for j in range(3)]
    toward = [point[j] - anchor[j] for j in range(3)]
    length = jnp.sqrt(toward[0] * toward[0] + toward[1] * toward[1] + toward[2] * toward[2])
    ux, uy, uz = (toward[0] / length, toward[1] / length, toward[2] / length)
    quat_norm = jnp.sqrt(raw[6] * raw[6] + raw[7] * raw[7] + raw[8] * raw[8] + raw[9] * raw[9])
    qw, qx, qy, qz = (raw[6] / quat_norm, raw[7] / quat_norm, raw[8] / quat_norm, raw[9] / quat_norm)
    spin = [[1.0 - 2.0 * (qy * qy + qz * qz), 2.0 * (qx * qy - qw * qz), 2.0 * (qx * qz + qw * qy)], [2.0 * (qx * qy + qw * qz), 1.0 - 2.0 * (qx * qx + qz * qz), 2.0 * (qy * qz - qw * qx)], [2.0 * (qx * qz - qw * qy), 2.0 * (qy * qz + qw * qx), 1.0 - 2.0 * (qx * qx + qy * qy)]]
    squares = [jnp.exp(2.0 * raw[3 + k]) for k in range(3)]
    cov_world = [[spin[i][0] * spin[j][0] * squares[0] + spin[i][1] * spin[j][1] * squares[1] + spin[i][2] * spin[j][2] * squares[2] for j in range(3)] for i in range(3)]
    half_way = matmul3(rotate, cov_world)
    view_cov = [[half_way[a][0] * rotate[b][0] + half_way[a][1] * rotate[b][1] + half_way[a][2] * rotate[b][2] for b in range(3)] for a in range(3)]
    inverse = 1.0 / viewed[2]
    j_main = FOCAL * inverse
    j_side_x = -FOCAL * viewed[0] * inverse * inverse
    j_side_y = -FOCAL * viewed[1] * inverse * inverse
    s_xx = j_main * j_main * view_cov[0][0] + 2.0 * j_main * j_side_x * view_cov[0][2] + j_side_x * j_side_x * view_cov[2][2] + 0.3
    s_xy = j_main * j_main * view_cov[0][1] + j_main * j_side_y * view_cov[0][2] + j_side_x * j_main * view_cov[1][2] + j_side_x * j_side_y * view_cov[2][2]
    s_yy = j_main * j_main * view_cov[1][1] + 2.0 * j_main * j_side_y * view_cov[1][2] + j_side_y * j_side_y * view_cov[2][2] + 0.3
    determinant = s_xx * s_yy - s_xy * s_xy
    conic_a = s_yy / determinant
    conic_b = -s_xy / determinant
    conic_c = s_xx / determinant
    screen_u = FOCAL * viewed[0] * inverse + 2048.0
    screen_v = FOCAL * viewed[1] * inverse + 1024.0
    opacity = jax.nn.sigmoid(raw[10])
    xx, yy, zz = (ux * ux, uy * uy, uz * uz)
    basis = [SH_ZERO + 0.0 * ux, -SH_ONE * uy, SH_ONE * uz, -SH_ONE * ux, SH_TWO[0] * ux * uy, SH_TWO[1] * uy * uz, SH_TWO[2] * (2.0 * zz - xx - yy), SH_TWO[3] * ux * uz, SH_TWO[4] * (xx - yy), SH_THREE[0] * uy * (3.0 * xx - yy), SH_THREE[1] * ux * uy * uz, SH_THREE[2] * uy * (4.0 * zz - xx - yy), SH_THREE[3] * uz * (2.0 * zz - 3.0 * xx - 3.0 * yy), SH_THREE[4] * ux * (4.0 * zz - xx - yy), SH_THREE[5] * uz * (xx - yy), SH_THREE[6] * ux * (xx - 3.0 * yy)]
    channels = []
    for channel in range(3):
        total = 0.5 + basis[0] * raw[11 + channel]
        for k in range(1, 16):
            total = total + basis[k] * raw[11 + 3 * k + channel]
        channels.append(total)
    return jnp.stack([screen_u, screen_v, conic_a, conic_b, conic_c, opacity, channels[0], channels[1], channels[2]])

def render_loss(records, chosen, places, live_counts, wanted):
    picked = records[:, chosen]
    pixel = jnp.arange(256, dtype=jnp.int32)
    pixel_x = (places % 256 * 16)[:, None] + (pixel % 16)[None, :]
    pixel_y = (places // 256 * 16)[:, None] + (pixel // 16)[None, :]
    pixel_x = pixel_x.astype(jnp.float32) + 0.5
    pixel_y = pixel_y.astype(jnp.float32) + 0.5
    delta_x = pixel_x[:, None, :] - picked[0][:, :, None]
    delta_y = pixel_y[:, None, :] - picked[1][:, :, None]
    quad = picked[2][:, :, None] * delta_x * delta_x + 2.0 * picked[3][:, :, None] * delta_x * delta_y + picked[4][:, :, None] * delta_y * delta_y
    entries = chosen.shape[1]
    live = (jnp.arange(entries, dtype=jnp.int32)[None, :] < live_counts[:, None]).astype(jnp.float32)
    alpha = picked[5][:, :, None] * jnp.exp(-0.5 * quad) * live[:, :, None]
    through = jnp.cumprod(1.0 - alpha, axis=1)
    before = jnp.concatenate([jnp.ones_like(through[:, :1]), through[:, :-1]], axis=1)
    weight = alpha * before
    shown = jnp.einsum('ctl,tlx->tcx', picked[6:9], weight, precision=lax.Precision.HIGHEST)
    return 0.5 * jnp.sum((shown - wanted) ** 2)

def reference(positions, log_scales, rotations, opacities, colors, cameras, targets, tile_ids, tile_counts, tile_lists, fetch_ids):
    params = jnp.concatenate([positions, log_scales, rotations, opacities[None, :], colors], axis=0)
    owners = N_CAM * N_TILE
    slots = owners * CAP
    requesters = PASSES * N_CAM * N_TILE
    offsets = (jnp.arange(owners, dtype=jnp.int32) * G_DEV).reshape(N_CAM, N_TILE, 1)
    global_ids = (fetch_ids + offsets).reshape(requesters, slots).astype(jnp.int32)
    chosen = tile_lists.reshape(requesters, TILES_DEV, tile_lists.shape[-1])
    places = tile_ids.reshape(requesters, TILES_DEV)
    live_counts = tile_counts.reshape(requesters, TILES_DEV)
    wanted = targets.reshape(requesters, TILES_DEV, 3, targets.shape[-1])
    views = jnp.broadcast_to(cameras[:, :, None, :], (PASSES, N_CAM, N_TILE, 6)).reshape(requesters, 6)

    def one_device(item):
        ids_here, list_here, place_here, count_here, goal_here, view_here = item
        raw = params[:, ids_here]

        def loss_of(values):
            return render_loss(project(values, view_here[:, None]), list_here, place_here, count_here, goal_here)
        return jax.grad(loss_of)(raw)
    slot_grads = lax.map(one_device, (global_ids, chosen, places, live_counts, wanted, views))
    flat_grads = jnp.moveaxis(slot_grads, 1, 0).reshape(params.shape[0], requesters * slots)
    total = jnp.zeros_like(params).at[:, global_ids.reshape(-1)].add(flat_grads)
    return (total[0:3], total[3:6], total[6:10], total[10], total[11:])
```

```python
import functools

import jax
import jax.numpy as jnp
from jax import lax
from jax.experimental import pallas as pl
from jax.experimental.pallas import tpu as pltpu
from jax.sharding import PartitionSpec as P

FOCAL = 4096.0
CENTER_X = 2048.0
CENTER_Y = 1024.0
SH_ZERO = 0.28209479177387814
SH_ONE = 0.4886025119029199
SH_TWO = [
    1.0925484305920792,
    -1.0925484305920792,
    0.31539156525252005,
    -1.0925484305920792,
    0.5462742152960396,
]
SH_THREE = [
    -0.5900435899266435,
    2.890611442640554,
    -0.4570457994644658,
    0.3731763325901154,
    -0.4570457994644658,
    1.445305721320277,
    -0.5900435899266435,
]
LANES = 128
HALF = LANES // 2
FIELDS = 9
SENT = 8
RAW = 59
TERMS = 15
F32 = jnp.float32
BF16 = jnp.bfloat16


def dot(left, right, contract):
    return lax.dot_general(left, right, ((contract[0], contract[1]), ((), ())), preferred_element_type=F32)


def split(x):
    high = x.astype(BF16)
    return high, (x - high.astype(F32)).astype(BF16)


def lane_pick(source, index):
    return jnp.take_along_axis(source, index, axis=1, mode="promise_in_bounds")


def row_pick(source, index):
    return jnp.take_along_axis(source, index, axis=0, mode="promise_in_bounds")


def spin_of(quat):
    norm = jnp.sqrt(quat[0] * quat[0] + quat[1] * quat[1] + quat[2] * quat[2] + quat[3] * quat[3])
    back = 1.0 / norm
    w, x, y, z = [q * back for q in quat]
    spin = [
        [1.0 - 2.0 * (y * y + z * z), 2.0 * (x * y - w * z), 2.0 * (x * z + w * y)],
        [2.0 * (x * y + w * z), 1.0 - 2.0 * (x * x + z * z), 2.0 * (y * z - w * x)],
        [2.0 * (x * z - w * y), 2.0 * (y * z + w * x), 1.0 - 2.0 * (x * x + y * y)],
    ]
    return spin, (w, x, y, z), back


def world_cov(spin, squares):
    scaled = [[spin[i][k] * squares[k] for k in range(3)] for i in range(3)]
    cov = [[None] * 3 for _ in range(3)]
    for i in range(3):
        for j in range(i, 3):
            cov[i][j] = scaled[i][0] * spin[j][0] + scaled[i][1] * spin[j][1] + scaled[i][2] * spin[j][2]
            cov[j][i] = cov[i][j]
    return cov


def dot3(a, b):
    return a[0] * b[0] + a[1] * b[1] + a[2] * b[2]


def screen_of(point, cov, rotate, offset):
    m = [dot3(rotate[i], point) + offset[i] for i in range(3)]
    inverse = 1.0 / m[2]
    main = FOCAL * inverse
    at_x, at_y = m[0] * inverse, m[1] * inverse
    side_x, side_y = -main * at_x, -main * at_y
    t_x = [main * rotate[0][i] + side_x * rotate[2][i] for i in range(3)]
    t_y = [main * rotate[1][i] + side_y * rotate[2][i] for i in range(3)]
    w_x = [dot3(cov[i], t_x) for i in range(3)]
    w_y = [dot3(cov[i], t_y) for i in range(3)]
    s_xx = dot3(t_x, w_x) + 0.3
    s_xy = dot3(t_y, w_x)
    s_yy = dot3(t_y, w_y) + 0.3
    back = 1.0 / (s_xx * s_yy - s_xy * s_xy)
    conic = (s_yy * back, -s_xy * back, s_xx * back)
    return m, inverse, main, at_x, at_y, t_x, t_y, w_x, w_y, conic


def direction_of(point, center):
    toward = [point[j] - center[j] for j in range(3)]
    back = lax.rsqrt(dot3(toward, toward))
    return [t * back for t in toward], back


def basis_of(x, y, z):
    xx, yy, zz = x * x, y * y, z * z
    xy, yz, xz = x * y, y * z, x * z
    less = xx - yy
    four = 4.0 * zz - xx - yy
    return [
        None,
        -SH_ONE * y,
        SH_ONE * z,
        -SH_ONE * x,
        SH_TWO[0] * xy,
        SH_TWO[1] * yz,
        SH_TWO[2] * (2.0 * zz - xx - yy),
        SH_TWO[3] * xz,
        SH_TWO[4] * less,
        SH_THREE[0] * y * (3.0 * xx - yy),
        SH_THREE[1] * xy * z,
        SH_THREE[2] * y * four,
        SH_THREE[3] * z * (2.0 * zz - 3.0 * xx - 3.0 * yy),
        SH_THREE[4] * x * four,
        SH_THREE[5] * z * less,
        SH_THREE[6] * x * (xx - 3.0 * yy),
    ]


def basis_pull(x, y, z, g):
    xx, yy, zz = x * x, y * y, z * z
    xy, yz, xz = x * y, y * z, x * z
    less = xx - yy
    four = 4.0 * zz - xx - yy
    g4, g5, g6, g7, g8 = [SH_TWO[i] * g[4 + i] for i in range(5)]
    h = [SH_THREE[i] * g[9 + i] for i in range(7)]
    g_x = (
        -SH_ONE * g[3] + g4 * y - 2.0 * g6 * x + g7 * z + 2.0 * g8 * x
        + 6.0 * h[0] * xy + h[1] * yz - 2.0 * h[2] * xy - 6.0 * h[3] * xz
        + h[4] * (four - 2.0 * xx) + 2.0 * h[5] * xz + 3.0 * h[6] * less
    )
    g_y = (
        -SH_ONE * g[1] + g4 * x + g5 * z - 2.0 * g6 * y - 2.0 * g8 * y
        + 3.0 * h[0] * less + h[1] * xz + h[2] * (four - 2.0 * yy) - 6.0 * h[3] * yz
        - 2.0 * h[4] * xy - 2.0 * h[5] * yz - 6.0 * h[6] * xy
    )
    g_z = (
        SH_ONE * g[2] + g5 * y + 4.0 * g6 * z + g7 * x
        + h[1] * xy + 8.0 * h[2] * yz + h[3] * (6.0 * zz - 3.0 * xx - 3.0 * yy)
        + 8.0 * h[4] * xz + h[5] * less
    )
    return [g_x, g_y, g_z]


def camera_rows(cam_ref, table, passes, cams):
    views = passes * cams
    for p in range(passes):
        cam = cam_ref[p]
        cos, sin = jnp.cos(cam), jnp.sin(cam)
        ca, cb, cg = [cos[:, k : k + 1] for k in range(3)]
        sa, sb, sg = [sin[:, k : k + 1] for k in range(3)]
        rotate = [
            [cg * cb, cg * sb * sa - sg * ca, cg * sb * ca + sg * sa],
            [sg * cb, sg * sb * sa + cg * ca, sg * sb * ca - cg * sa],
            [-sb, cb * sa, cb * ca],
        ]
        offset = [cam[:, 3:4], cam[:, 4:5], 6.0 + cam[:, 5:6]]
        center = [-(rotate[0][j] * offset[0] + rotate[1][j] * offset[1] + rotate[2][j] * offset[2]) for j in range(3)]
        for k, term in enumerate(rotate[0] + rotate[1] + rotate[2] + offset + center):
            table[k * views + p * cams : k * views + (p + 1) * cams, :] = jnp.broadcast_to(term, (cams, LANES))


def camera_of(table, view, views, shape):
    terms = [jnp.broadcast_to(table[k * views + view : k * views + view + 1, :], shape) for k in range(TERMS)]
    return [terms[0:3], terms[3:6], terms[6:9]], terms[9:12], terms[12:15]


def project_kernel(passes, cams, rows, pos, scales, rots, opac, cols, cam, rec, raw, table):
    views = passes * cams
    shape = (rows, LANES)
    camera_rows(cam, table, passes, cams)
    base = 0
    for ref in (pos, scales, rots):
        count = ref.shape[0]
        for i in range(rows):
            raw[pl.ds(base * rows + i, count, stride=rows), :] = ref[:, i * LANES : (i + 1) * LANES]
        base += count
    raw[base * rows : (base + 1) * rows, :] = opac[...]
    base += 1
    for i in range(rows):
        raw[pl.ds(base * rows + i, cols.shape[0], stride=rows), :] = cols[:, i * LANES : (i + 1) * LANES]

    def at(k):
        return raw[k * rows : (k + 1) * rows, :]

    point = [at(k) for k in range(3)]
    squares = [jnp.exp(2.0 * at(3 + k)) for k in range(3)]
    spin, _, _ = spin_of([at(6 + k) for k in range(4)])
    cov = world_cov(spin, squares)
    opacity = 1.0 / (1.0 + jnp.exp(-at(10)))
    for view in range(views):
        rotate, offset, center = camera_of(table, view, views, shape)
        _, _, _, at_x, at_y, _, _, _, _, conic = screen_of(point, cov, rotate, offset)
        direction, _ = direction_of(point, center)
        basis = basis_of(*direction)
        fields = [FOCAL * at_x + CENTER_X, FOCAL * at_y + CENTER_Y, conic[0], conic[1], conic[2], opacity]
        for channel in range(3):
            total = 0.5 + SH_ZERO * at(11 + channel)
            for k in range(1, 16):
                total = total + basis[k] * at(11 + 3 * k + channel)
            fields.append(total)
        for f, value in enumerate(fields):
            rec[(view * FIELDS + f) * rows : (view * FIELDS + f + 1) * rows, :] = value


def lane_pass(shape, cap):
    lane = lax.broadcasted_iota(jnp.int32, shape, 1) % HALF
    return lane // cap, lane % cap


def pick_kernel(passes, cams, tiles, rows, cap, aligned, ids, rec, out):
    group = 8
    shape = (group, LANES)
    lane = lax.broadcasted_iota(jnp.int32, shape, 1)
    lane_p, _ = lane_pass(shape, cap)

    def packets(first, c):
        asked = ids[pl.ds(first, group), :]
        low, high = asked % LANES, asked // LANES
        if aligned:
            blocks = [
                jnp.broadcast_to(high[:, p * cap : p * cap + 1], shape) for p in range(passes)
            ]

        def pick(f):
            found = jnp.zeros(shape, F32)
            for p in range(passes):
                start = ((p * cams + c) * FIELDS + f) * rows
                if aligned:
                    own = lane_pick(row_pick(rec[start : start + rows, :], blocks[p]), low)
                else:
                    own = jnp.zeros(shape, F32)
                    for b in range(rows):
                        line = jnp.broadcast_to(rec[start + b : start + b + 1, :], shape)
                        own = jnp.where(high == b, lane_pick(line, low), own)
                found = jnp.where(lane_p == p, own, found)
            return found

        for f in range(SENT):
            value = pick(f)
            if f == 0:
                value = jnp.where(lane < HALF, value, pick(FIELDS - 1))
            out[pl.ds(first * SENT + f, group, stride=SENT), :] = value

    for c in range(cams):
        if tiles == group:
            packets(c * tiles, c)
        else:

            def step(k, carry, c=c):
                packets(pl.multiple_of(c * tiles + k * group, group), c)
                return carry

            lax.fori_loop(0, tiles // group, step, 0)


def inverse_kernel(passes, cams, tiles, rows, cap, ids, inverse):
    shape = (LANES, LANES)
    column = lax.broadcasted_iota(jnp.int32, shape, 0)
    _, lane_j = lane_pass(shape, cap)
    place = (lane_j + 1).astype(F32)
    wide = (passes * rows, LANES)
    lane_p, _ = lane_pass(wide, cap)
    lane = lax.broadcasted_iota(jnp.int32, wide, 1)
    key = lax.broadcasted_iota(jnp.int32, wide, 0)
    lane_key = jnp.where(lane < passes * cap, lane_p * rows, -(1 << 20))

    def one(c, t, found):
        asked = ids[pl.ds(c * tiles + t, 1), :]
        low = jnp.broadcast_to(asked % LANES, shape)
        high = jnp.broadcast_to(asked // LANES, wide)
        match = jnp.where(low == column, place, 0.0).astype(BF16)
        owner = jnp.where(high + lane_key == key, 1.0, 0.0).astype(BF16)
        hit = dot(owner, match, ((1,), (1,)))
        return jnp.where(hit > 0.5, hit.astype(jnp.int32) + t * cap, found)

    for c in range(cams):
        found = jnp.zeros(wide, jnp.int32)
        if tiles <= 8:
            for t in range(tiles):
                found = one(c, t, found)
        else:
            found = lax.fori_loop(0, tiles, lambda t, f, c=c: one(c, t, f), found)
        for p in range(passes):
            start = (p * cams + c) * rows
            inverse[start : start + rows, :] = found[p * rows : (p + 1) * rows, :]


def render_kernel(passes, owners, cap, entries, pixels, got, lists, counts, places, wanted, out, alphas, logs, weights):
    halves = entries // LANES
    shape = (SENT, LANES)
    wide = 16
    lane = lax.broadcasted_iota(jnp.int32, shape, 1)
    sub = lax.broadcasted_iota(jnp.int32, shape, 0)

    slot_owner, slot_lane = [], []
    for p in range(passes):
        for h in range(halves):
            slot = jnp.broadcast_to(lists[p, 0, :, h * LANES : (h + 1) * LANES], shape)
            slot_owner.append(slot // cap)
            slot_lane.append(slot % cap + p * cap)
    total = passes * halves

    def gather(o, found):
        packet = got[pl.ds(pl.multiple_of(o * SENT, SENT), SENT), :]
        return tuple(
            jnp.where(slot_owner[i] == o, lane_pick(packet, slot_lane[i]), found[i]) for i in range(total)
        )

    def gather_last(g, found):
        lines = got[pl.ds(g * SENT * SENT, SENT, stride=SENT), :]
        return tuple(
            jnp.where(slot_owner[i] == g * SENT + sub, lane_pick(lines, slot_lane[i] + HALF), found[i])
            for i in range(total)
        )

    empty = tuple(jnp.zeros(shape, F32) for _ in range(total))
    if owners <= 32:
        fields, last = empty, empty
        for o in range(owners):
            fields = gather(o, fields)
        for g in range(owners // SENT):
            last = gather_last(g, last)
    else:
        fields = lax.fori_loop(0, owners, gather, empty)
        last = lax.fori_loop(0, owners // SENT, gather_last, empty)
    last = [jnp.sum(x, axis=0, keepdims=True) for x in last]

    pair = (LANES, LANES)
    lane_p, lane_j = lane_pass(pair, cap)
    turned_p, turned_j = lax.broadcasted_iota(jnp.int32, pair, 0) % HALF // cap, lax.broadcasted_iota(jnp.int32, pair, 0) % cap
    entry = (lax.broadcasted_iota(jnp.int32, pair, 1) + 1).astype(F32)
    owner_row = lax.broadcasted_iota(jnp.int32, (owners, LANES), 0)
    source = jnp.zeros((owners, LANES), jnp.int32)
    for p in range(passes):
        for h in range(halves):
            i = p * halves + h
            slot = lists[p, 0, :, h * LANES : (h + 1) * LANES]
            mine = jnp.where(jnp.broadcast_to(slot // cap, (owners, LANES)) == owner_row, 1.0, 0.0).astype(BF16)
            here = jnp.where(
                (jnp.broadcast_to(slot % cap, pair) == turned_j) & (turned_p == p), entry, 0.0
            ).astype(BF16)
            hit = dot(mine, here, ((1,), (1,)))
            source = jnp.where(hit > 0.5, hit.astype(jnp.int32) + h * LANES, source)

    before = jnp.where(
        lax.broadcasted_iota(jnp.int32, (entries, entries), 0) < lax.broadcasted_iota(jnp.int32, (entries, entries), 1),
        1.0,
        0.0,
    ).astype(BF16)
    after = jnp.where(
        lax.broadcasted_iota(jnp.int32, (entries, entries), 0) > lax.broadcasted_iota(jnp.int32, (entries, entries), 1),
        1.0,
        0.0,
    ).astype(BF16)
    entry_row = lax.broadcasted_iota(jnp.int32, (1, entries), 1)
    pixel = lax.broadcasted_iota(jnp.int32, (SENT, pixels), 1)
    local_x = (pixel % wide).astype(F32) - 7.5
    local_y = (pixel // wide).astype(F32) - 7.5
    kind = lax.broadcasted_iota(jnp.int32, (SENT, pixels), 0)
    moment = jnp.where(
        kind == 0,
        1.0,
        jnp.where(
            kind == 1,
            local_x,
            jnp.where(
                kind == 2,
                local_y,
                jnp.where(kind == 3, local_x * local_x, jnp.where(kind == 4, local_x * local_y, local_y * local_y)),
            ),
        ),
    ).astype(BF16)
    column_x = lax.broadcasted_iota(jnp.int32, (wide, entries), 0).astype(F32) - 7.5

    grads = []
    for p in range(passes):
        line = [
            jnp.concatenate([fields[p * halves + h][f : f + 1, :] for h in range(halves)], axis=1) for f in range(SENT)
        ]
        blue = jnp.concatenate([last[p * halves + h] for h in range(halves)], axis=1)
        place = places[p, 0, 0]
        u = line[0] - (place % 256 * 16 + 8).astype(F32)
        v = line[1] - (place // 256 * 16 + 8).astype(F32)
        c_a, c_b, c_c, base = line[2], line[3], line[4], line[5]
        color = jnp.concatenate([line[6], line[7], blue], axis=0)
        live = jnp.where(entry_row < counts[p, 0, 0], base, 0.0)

        d_x = column_x - u
        q_xx = (-0.5 * c_a) * d_x * d_x
        q_x = c_b * d_x
        for y in range(pixels // wide):
            d_y = (y - 7.5) - v
            power = q_xx - (q_x * d_y + 0.5 * c_c * d_y * d_y)
            alpha = live * jnp.exp(power)
            alphas[p, y * wide : (y + 1) * wide, :] = alpha
            logs[y * wide : (y + 1) * wide, :] = jnp.log(1.0 - alpha)
        high, low = split(logs[...])
        through = jnp.exp(dot(high, before, ((1,), (0,))) + dot(low, before, ((1,), (0,))))
        alpha = alphas[p]
        weight = alpha * through
        weights[p] = weight
        w_high, w_low = split(weight)
        c_high, c_low = split(color)
        shown = (
            dot(c_high, w_high, ((1,), (1,))) + dot(c_low, w_high, ((1,), (1,))) + dot(c_high, w_low, ((1,), (1,)))
        )
        residual = shown - wanted[p, 0, 0]
        r_high, r_low = split(residual)
        left = jnp.concatenate([r_high, r_high, r_low], axis=0)
        right = jnp.concatenate([c_high, c_low, c_high], axis=0)
        slope = dot(left, right, ((0,), (0,)))
        pulled = weight * slope
        high, low = split(pulled)
        rest = dot(high, after, ((1,), (0,))) + dot(low, after, ((1,), (0,)))
        power_grad = pulled - alpha / (1.0 - alpha) * rest
        high, low = split(power_grad)
        moments = dot(moment, high, ((1,), (0,))) + dot(moment, low, ((1,), (0,)))
        color_grad = (
            dot(r_high, w_high, ((1,), (0,))) + dot(r_low, w_high, ((1,), (0,))) + dot(r_high, w_low, ((1,), (0,)))
        )
        m_1, m_x, m_y, m_xx, m_xy, m_yy = [moments[k : k + 1, :] for k in range(6)]
        s_x = m_x - u * m_1
        s_y = m_y - v * m_1
        s_xx = m_xx - u * (m_x + s_x)
        s_yy = m_yy - v * (m_y + s_y)
        s_xy = m_xy - u * m_y - v * s_x
        grads.append(
            [
                c_a * s_x + c_b * s_y,
                c_b * s_x + c_c * s_y,
                -0.5 * s_xx,
                -s_xy,
                -0.5 * s_yy,
                m_1 / base,
                color_grad[0:1, :],
                color_grad[1:2, :],
                color_grad[2:3, :],
            ]
        )

    def packets(first, origin):
        origin = origin - 1
        which = jnp.where(origin < 0, -1, origin // LANES)
        index = jnp.maximum(origin, 0) % LANES
        own_p, _ = lane_pass(shape, cap)

        def pick(f):
            found = jnp.zeros(shape, F32)
            for p in range(passes):
                for h in range(halves):
                    line = jnp.broadcast_to(grads[p][f][:, h * LANES : (h + 1) * LANES], shape)
                    found = jnp.where((which == h) & (own_p == p), lane_pick(line, index), found)
            return found

        for f in range(SENT):
            value = pick(f)
            if f == 0:
                value = jnp.where(lane < HALF, value, pick(FIELDS - 1))
            out[pl.ds(first * SENT + f, SENT, stride=SENT), :] = value

    for g in range(owners // SENT):
        packets(g * SENT, source[g * SENT : (g + 1) * SENT, :])


def pull_kernel(passes, cams, tiles, rows, cap, aligned, got, inverse, raw, table, pos, scales, rots, opac, cols, total):
    views = passes * cams
    shape = (rows, LANES)

    def at(k):
        return raw[k * rows : (k + 1) * rows, :]

    point = [at(k) for k in range(3)]
    squares = [jnp.exp(2.0 * at(3 + k)) for k in range(3)]
    spin, quat, quat_back = spin_of([at(6 + k) for k in range(4)])
    cov = world_cov(spin, squares)

    g_point = [jnp.zeros(shape, F32) for _ in range(3)]
    g_cov = [[jnp.zeros(shape, F32) for _ in range(3)] for _ in range(3)]
    g_opacity = jnp.zeros(shape, F32)
    for view in range(views):
        p, c = view // cams, view % cams
        slot = inverse[view * rows : (view + 1) * rows, :] - 1
        valid = slot >= 0
        slot = jnp.maximum(slot, 0)
        slot_t, slot_lane = slot // cap, slot % cap + p * cap
        if aligned:
            row_t = jnp.broadcast_to(jnp.max(slot_t, axis=1, keepdims=True), shape)

        def fetch(f, row, shift):
            if aligned:
                lines = got[pl.ds(c * tiles * SENT + row, tiles, stride=SENT), :]
                return jnp.where(valid, lane_pick(row_pick(lines, row_t), slot_lane + shift), 0.0)

            def one(t, found):
                line = jnp.broadcast_to(got[pl.ds((c * tiles + t) * SENT + row, 1), :], shape)
                return jnp.where(valid & (slot_t == t), lane_pick(line, slot_lane + shift), found)

            return lax.fori_loop(0, tiles, one, jnp.zeros(shape, F32))

        g = [fetch(f, f, 0) for f in range(SENT)] + [fetch(FIELDS - 1, 0, HALF)]
        rotate, offset, center = camera_of(table, view, views, shape)
        m, inv, main, at_x, at_y, t_x, t_y, w_x, w_y, conic = screen_of(point, cov, rotate, offset)
        c_a, c_b, c_c = conic
        half = 0.5 * g[3]
        p00, p01 = g[2] * c_a + half * c_b, g[2] * c_b + half * c_c
        p10, p11 = half * c_a + g[4] * c_b, half * c_b + g[4] * c_c
        g_xx = -(c_a * p00 + c_b * p10)
        g_xy = -(c_a * p01 + c_b * p11)
        g_yy = -(c_b * p01 + c_c * p11)
        left = [g_xx * t_x[i] + g_xy * t_y[i] for i in range(3)]
        right = [g_yy * t_y[i] + g_xy * t_x[i] for i in range(3)]
        for i in range(3):
            for j in range(i, 3):
                g_cov[i][j] = g_cov[i][j] + (t_x[i] * left[j] + t_y[i] * right[j])
        g_tx = [2.0 * (g_xx * w_x[i] + g_xy * w_y[i]) for i in range(3)]
        g_ty = [2.0 * (g_yy * w_y[i] + g_xy * w_x[i]) for i in range(3)]
        g_main = dot3(rotate[0], g_tx) + dot3(rotate[1], g_ty)
        g_sx, g_sy = dot3(rotate[2], g_tx), dot3(rotate[2], g_ty)
        g_m0 = main * (g[0] - inv * g_sx)
        g_m1 = main * (g[1] - inv * g_sy)
        g_m2 = -main * (
            at_x * g[0] + at_y * g[1] + inv * g_main - 2.0 * inv * (at_x * g_sx + at_y * g_sy)
        )
        direction, length_back = direction_of(point, center)
        basis = basis_of(*direction)
        g_basis = [None]
        for k in range(1, 16):
            g_basis.append(
                at(11 + 3 * k) * g[6] + at(12 + 3 * k) * g[7] + at(13 + 3 * k) * g[8]
            )
        g_dir = basis_pull(*direction, g_basis)
        along = dot3(direction, g_dir)
        for j in range(3):
            g_point[j] = g_point[j] + (
                rotate[0][j] * g_m0 + rotate[1][j] * g_m1 + rotate[2][j] * g_m2
                + (g_dir[j] - direction[j] * along) * length_back
            )
        g_opacity = g_opacity + g[5]
        for k in range(16):
            for channel in range(3):
                term = SH_ZERO * g[6 + channel] if k == 0 else basis[k] * g[6 + channel]
                start = (11 + 3 * k + channel) * rows
                if view == 0:
                    total[start : start + rows, :] = term
                else:
                    total[start : start + rows, :] += term
    for i in range(3):
        for j in range(i):
            g_cov[i][j] = g_cov[j][i]

    g_scales = []
    g_spin = [[None] * 3 for _ in range(3)]
    for k in range(3):
        column = [spin[j][k] for j in range(3)]
        turned = [dot3(g_cov[i], column) for i in range(3)]
        g_scales.append(2.0 * squares[k] * dot3(column, turned))
        for i in range(3):
            g_spin[i][k] = 2.0 * squares[k] * turned[i]
    w, x, y, z = quat
    d = g_spin
    g_quat = [
        2.0 * (z * (d[1][0] - d[0][1]) + y * (d[0][2] - d[2][0]) + x * (d[2][1] - d[1][2])),
        2.0 * (y * (d[0][1] + d[1][0]) + z * (d[0][2] + d[2][0]) + w * (d[2][1] - d[1][2]) - 2.0 * x * (d[1][1] + d[2][2])),
        2.0 * (x * (d[0][1] + d[1][0]) + z * (d[1][2] + d[2][1]) + w * (d[0][2] - d[2][0]) - 2.0 * y * (d[0][0] + d[2][2])),
        2.0 * (x * (d[0][2] + d[2][0]) + y * (d[1][2] + d[2][1]) + w * (d[1][0] - d[0][1]) - 2.0 * z * (d[0][0] + d[1][1])),
    ]
    along = w * g_quat[0] + x * g_quat[1] + y * g_quat[2] + z * g_quat[3]
    g_rots = [(g_quat[k] - quat[k] * along) * quat_back for k in range(4)]
    opacity = 1.0 / (1.0 + jnp.exp(-at(10)))
    opac[...] = g_opacity * opacity * (1.0 - opacity)
    for k, value in enumerate(g_point + g_scales + g_rots):
        total[k * rows : (k + 1) * rows, :] = value
    base = 0
    for ref in (pos, scales, rots, cols):
        count = ref.shape[0]
        if ref is cols:
            base = 11
        for i in range(rows):
            ref[:, i * LANES : (i + 1) * LANES] = total[pl.ds(base * rows + i, count, stride=rows), :]
        base += count


def vmem(count):
    return [pl.BlockSpec(memory_space=pltpu.VMEM)] * count


def call(kernel, outs, operands, in_specs=None, scratch=(), flops=1_000_000):
    return pl.pallas_call(
        kernel,
        out_shape=outs,
        in_specs=in_specs or vmem(len(operands)),
        out_specs=jax.tree.map(lambda _: pl.BlockSpec(memory_space=pltpu.VMEM), outs),
        scratch_shapes=list(scratch),
        compiler_params=pltpu.CompilerParams(vmem_limit_bytes=32 << 20),
        cost_estimate=pl.CostEstimate(flops=flops, bytes_accessed=1 << 20, transcendentals=0),
    )(*operands)


def body(
    cams,
    tiles,
    positions,
    log_scales,
    rotations,
    opacities,
    colors,
    cameras,
    targets,
    tile_ids,
    tile_counts,
    tile_lists,
    fetch_ids,
):
    axes = ("cam", "tile")
    passes, cap = fetch_ids.shape[0], fetch_ids.shape[-1]
    entries, pixels = tile_lists.shape[-1], targets.shape[-1]
    columns = positions.shape[-1]
    rows = columns // LANES
    owners = cams * tiles
    views = passes * cams
    aligned = tiles == rows == 8

    def shaped(*shape):
        return jax.ShapeDtypeStruct(shape, F32)

    def exchange(x):
        return lax.all_to_all(x, axes, split_axis=0, concat_axis=0, tiled=True)

    wanted_ids = jnp.transpose(fetch_ids[:, 0, 0], (1, 2, 0, 3)).reshape(owners, passes * cap)
    wanted_ids = jnp.pad(wanted_ids, ((0, 0), (0, HALF - passes * cap)))
    arrived = exchange(jnp.concatenate([wanted_ids, wanted_ids], axis=1))

    records, raw, table = call(
        functools.partial(project_kernel, passes, cams, rows),
        [shaped(views * FIELDS * rows, LANES), shaped(RAW * rows, LANES), shaped(TERMS * views, LANES)],
        [positions, log_scales, rotations, opacities.reshape(rows, LANES), colors, cameras],
    )
    packets = call(
        functools.partial(pick_kernel, passes, cams, tiles, rows, cap, aligned),
        shaped(owners * SENT, LANES),
        [arrived, records],
    )
    fetched = exchange(packets)
    inverse = call(
        functools.partial(inverse_kernel, passes, cams, tiles, rows, cap),
        jax.ShapeDtypeStruct((views * rows, LANES), jnp.int32),
        [arrived],
    )
    smem = pl.BlockSpec(memory_space=pltpu.SMEM)
    whole = vmem(1)[0]
    slot_grads = call(
        functools.partial(render_kernel, passes, owners, cap, entries, pixels),
        shaped(owners * SENT, LANES),
        [fetched, tile_lists, tile_counts, tile_ids, targets],
        in_specs=[whole, whole, smem, smem, whole],
        scratch=[
            pltpu.VMEM((passes, pixels, entries), F32),
            pltpu.VMEM((pixels, entries), F32),
            pltpu.VMEM((passes, pixels, entries), F32),
        ],
    )
    coming = exchange(slot_grads)
    g_pos, g_scales, g_rots, g_opac, g_cols = call(
        functools.partial(pull_kernel, passes, cams, tiles, rows, cap, aligned),
        [shaped(3, columns), shaped(3, columns), shaped(4, columns), shaped(rows, LANES), shaped(48, columns)],
        [coming, inverse, raw, table],
        scratch=[pltpu.VMEM((RAW * rows, LANES), F32)],
    )
    return (g_pos, g_scales, g_rots, g_opac.reshape(columns), g_cols)


def solution(mesh):
    return jax.shard_map(
        functools.partial(body, mesh.shape["cam"], mesh.shape["tile"]),
        mesh=mesh,
        in_specs=(
            P(None, ("cam", "tile")),
            P(None, ("cam", "tile")),
            P(None, ("cam", "tile")),
            P(("cam", "tile")),
            P(None, ("cam", "tile")),
            P(),
            P(None, "cam", "tile", None, None),
            P(None, "cam", "tile"),
            P(None, "cam", "tile"),
            P(None, "cam", "tile", None),
            P(None, "cam", "tile", None, None, None),
        ),
        out_specs=(
            P(None, ("cam", "tile")),
            P(None, ("cam", "tile")),
            P(None, ("cam", "tile")),
            P(("cam", "tile")),
            P(None, ("cam", "tile")),
        ),
        check_vma=False,
    )
```

```python
import functools

import jax
import jax.numpy as jnp
from jax import lax
from jax.experimental import pallas as pl
from jax.experimental.pallas import tpu as pltpu
from jax.sharding import PartitionSpec as P

FOCAL = 4096.0
CENTER_X = 2048.0
CENTER_Y = 1024.0
SH_ZERO = 0.28209479177387814
SH_ONE = 0.4886025119029199
SH_TWO = [
    1.0925484305920792,
    -1.0925484305920792,
    0.31539156525252005,
    -1.0925484305920792,
    0.5462742152960396,
]
SH_THREE = [
    -0.5900435899266435,
    2.890611442640554,
    -0.4570457994644658,
    0.3731763325901154,
    -0.4570457994644658,
    1.445305721320277,
    -0.5900435899266435,
]
LANES = 128
HALF = LANES // 2
FIELDS = 9
SENT = 5
GROUP = 8
RAW = 59
TERMS = 15
F32 = jnp.float32
BF16 = jnp.bfloat16


def dot(left, right, contract):
    return lax.dot_general(left, right, ((contract[0], contract[1]), ((), ())), preferred_element_type=F32)


def split(x):
    high = x.astype(BF16)
    return high, (x - high.astype(F32)).astype(BF16)


def lane_pick(source, index):
    return jnp.take_along_axis(source, index, axis=1, mode="promise_in_bounds")


def row_pick(source, index):
    return jnp.take_along_axis(source, index, axis=0, mode="promise_in_bounds")


def spin_of(quat):
    norm = jnp.sqrt(quat[0] * quat[0] + quat[1] * quat[1] + quat[2] * quat[2] + quat[3] * quat[3])
    back = 1.0 / norm
    w, x, y, z = [q * back for q in quat]
    spin = [
        [1.0 - 2.0 * (y * y + z * z), 2.0 * (x * y - w * z), 2.0 * (x * z + w * y)],
        [2.0 * (x * y + w * z), 1.0 - 2.0 * (x * x + z * z), 2.0 * (y * z - w * x)],
        [2.0 * (x * z - w * y), 2.0 * (y * z + w * x), 1.0 - 2.0 * (x * x + y * y)],
    ]
    return spin, (w, x, y, z), back


def world_cov(spin, squares):
    scaled = [[spin[i][k] * squares[k] for k in range(3)] for i in range(3)]
    cov = [[None] * 3 for _ in range(3)]
    for i in range(3):
        for j in range(i, 3):
            cov[i][j] = scaled[i][0] * spin[j][0] + scaled[i][1] * spin[j][1] + scaled[i][2] * spin[j][2]
            cov[j][i] = cov[i][j]
    return cov


def dot3(a, b):
    return a[0] * b[0] + a[1] * b[1] + a[2] * b[2]


def screen_of(point, cov, rotate, offset):
    m = [dot3(rotate[i], point) + offset[i] for i in range(3)]
    inverse = 1.0 / m[2]
    main = FOCAL * inverse
    at_x, at_y = m[0] * inverse, m[1] * inverse
    side_x, side_y = -main * at_x, -main * at_y
    t_x = [main * rotate[0][i] + side_x * rotate[2][i] for i in range(3)]
    t_y = [main * rotate[1][i] + side_y * rotate[2][i] for i in range(3)]
    w_x = [dot3(cov[i], t_x) for i in range(3)]
    w_y = [dot3(cov[i], t_y) for i in range(3)]
    s_xx = dot3(t_x, w_x) + 0.3
    s_xy = dot3(t_y, w_x)
    s_yy = dot3(t_y, w_y) + 0.3
    back = 1.0 / (s_xx * s_yy - s_xy * s_xy)
    conic = (s_yy * back, -s_xy * back, s_xx * back)
    return m, inverse, main, at_x, at_y, t_x, t_y, w_x, w_y, conic


def direction_of(point, center):
    toward = [point[j] - center[j] for j in range(3)]
    back = lax.rsqrt(dot3(toward, toward))
    return [t * back for t in toward], back


def basis_of(x, y, z):
    xx, yy, zz = x * x, y * y, z * z
    xy, yz, xz = x * y, y * z, x * z
    less = xx - yy
    four = 4.0 * zz - xx - yy
    return [
        None,
        -SH_ONE * y,
        SH_ONE * z,
        -SH_ONE * x,
        SH_TWO[0] * xy,
        SH_TWO[1] * yz,
        SH_TWO[2] * (2.0 * zz - xx - yy),
        SH_TWO[3] * xz,
        SH_TWO[4] * less,
        SH_THREE[0] * y * (3.0 * xx - yy),
        SH_THREE[1] * xy * z,
        SH_THREE[2] * y * four,
        SH_THREE[3] * z * (2.0 * zz - 3.0 * xx - 3.0 * yy),
        SH_THREE[4] * x * four,
        SH_THREE[5] * z * less,
        SH_THREE[6] * x * (xx - 3.0 * yy),
    ]


def basis_pull(x, y, z, g):
    xx, yy, zz = x * x, y * y, z * z
    xy, yz, xz = x * y, y * z, x * z
    less = xx - yy
    four = 4.0 * zz - xx - yy
    g4, g5, g6, g7, g8 = [SH_TWO[i] * g[4 + i] for i in range(5)]
    h = [SH_THREE[i] * g[9 + i] for i in range(7)]
    g_x = (
        -SH_ONE * g[3] + g4 * y - 2.0 * g6 * x + g7 * z + 2.0 * g8 * x
        + 6.0 * h[0] * xy + h[1] * yz - 2.0 * h[2] * xy - 6.0 * h[3] * xz
        + h[4] * (four - 2.0 * xx) + 2.0 * h[5] * xz + 3.0 * h[6] * less
    )
    g_y = (
        -SH_ONE * g[1] + g4 * x + g5 * z - 2.0 * g6 * y - 2.0 * g8 * y
        + 3.0 * h[0] * less + h[1] * xz + h[2] * (four - 2.0 * yy) - 6.0 * h[3] * yz
        - 2.0 * h[4] * xy - 2.0 * h[5] * yz - 6.0 * h[6] * xy
    )
    g_z = (
        SH_ONE * g[2] + g5 * y + 4.0 * g6 * z + g7 * x
        + h[1] * xy + 8.0 * h[2] * yz + h[3] * (6.0 * zz - 3.0 * xx - 3.0 * yy)
        + 8.0 * h[4] * xz + h[5] * less
    )
    return [g_x, g_y, g_z]


def camera_rows(cam_ref, table, passes, cams):
    views = passes * cams
    for p in range(passes):
        cam = cam_ref[p]
        cos, sin = jnp.cos(cam), jnp.sin(cam)
        ca, cb, cg = [cos[:, k : k + 1] for k in range(3)]
        sa, sb, sg = [sin[:, k : k + 1] for k in range(3)]
        rotate = [
            [cg * cb, cg * sb * sa - sg * ca, cg * sb * ca + sg * sa],
            [sg * cb, sg * sb * sa + cg * ca, sg * sb * ca - cg * sa],
            [-sb, cb * sa, cb * ca],
        ]
        offset = [cam[:, 3:4], cam[:, 4:5], 6.0 + cam[:, 5:6]]
        center = [-(rotate[0][j] * offset[0] + rotate[1][j] * offset[1] + rotate[2][j] * offset[2]) for j in range(3)]
        for k, term in enumerate(rotate[0] + rotate[1] + rotate[2] + offset + center):
            table[k * views + p * cams : k * views + (p + 1) * cams, :] = jnp.broadcast_to(term, (cams, LANES))


def camera_of(table, view, views, shape):
    terms = [jnp.broadcast_to(table[k * views + view : k * views + view + 1, :], shape) for k in range(TERMS)]
    return [terms[0:3], terms[3:6], terms[6:9]], terms[9:12], terms[12:15]


def project_kernel(passes, cams, rows, pos, scales, rots, opac, cols, cam, rec, raw, table):
    views = passes * cams
    shape = (rows, LANES)
    camera_rows(cam, table, passes, cams)
    base = 0
    for ref in (pos, scales, rots):
        count = ref.shape[0]
        for i in range(rows):
            raw[pl.ds(base * rows + i, count, stride=rows), :] = ref[:, i * LANES : (i + 1) * LANES]
        base += count
    raw[base * rows : (base + 1) * rows, :] = opac[...]
    base += 1
    for i in range(rows):
        raw[pl.ds(base * rows + i, cols.shape[0], stride=rows), :] = cols[:, i * LANES : (i + 1) * LANES]

    def at(k):
        return raw[k * rows : (k + 1) * rows, :]

    point = [at(k) for k in range(3)]
    squares = [jnp.exp(2.0 * at(3 + k)) for k in range(3)]
    spin, _, _ = spin_of([at(6 + k) for k in range(4)])
    cov = world_cov(spin, squares)
    opacity = 1.0 / (1.0 + jnp.exp(-at(10)))
    for view in range(views):
        rotate, offset, center = camera_of(table, view, views, shape)
        _, _, _, at_x, at_y, _, _, _, _, conic = screen_of(point, cov, rotate, offset)
        direction, _ = direction_of(point, center)
        basis = basis_of(*direction)
        fields = [FOCAL * at_x + CENTER_X, FOCAL * at_y + CENTER_Y, conic[0], conic[1], conic[2], opacity]
        for channel in range(3):
            total = 0.5 + SH_ZERO * at(11 + channel)
            for k in range(1, 16):
                total = total + basis[k] * at(11 + 3 * k + channel)
            fields.append(total)
        for f, value in enumerate(fields):
            rec[(view * FIELDS + f) * rows : (view * FIELDS + f + 1) * rows, :] = value


def lane_pass(shape, cap):
    lane = lax.broadcasted_iota(jnp.int32, shape, 1) % HALF
    return lane // cap, lane % cap


def ids_kernel(passes, cams, cap, ids, out):
    for c in range(cams):
        parts = [ids[p, 0, 0, c] for p in range(passes)]
        tiles = parts[0].shape[0]
        if passes * cap < HALF:
            parts.append(jnp.zeros((tiles, HALF - passes * cap), jnp.int32))
        out[c * tiles : (c + 1) * tiles, :] = jnp.concatenate(parts + parts, axis=1)


def pick_kernel(passes, cams, tiles, rows, cap, aligned, ids, rec, out, inverse):
    shape = (GROUP, LANES)
    lane = lax.broadcasted_iota(jnp.int32, shape, 1)
    lane_p, _ = lane_pass(shape, cap)

    def packets(first, c):
        asked = ids[pl.ds(first, GROUP), :]
        low, high = asked % LANES, asked // LANES
        if aligned:
            blocks = [jnp.broadcast_to(high[:, p * cap : p * cap + 1], shape) for p in range(passes)]

        def pick(f):
            found = jnp.zeros(shape, F32)
            for p in range(passes):
                start = ((p * cams + c) * FIELDS + f) * rows
                if aligned:
                    own = lane_pick(row_pick(rec[start : start + rows, :], blocks[p]), low)
                else:
                    own = jnp.zeros(shape, F32)
                    for b in range(rows):
                        line = jnp.broadcast_to(rec[start + b : start + b + 1, :], shape)
                        own = jnp.where(high == b, lane_pick(line, low), own)
                found = own if p == 0 else jnp.where(lane_p == p, own, found)
            return found

        for r in range(SENT):
            value = pick(2 * r)
            if 2 * r + 1 < FIELDS:
                value = jnp.where(lane < HALF, value, pick(2 * r + 1))
            out[pl.ds(first * SENT + r, GROUP, stride=SENT), :] = value

    for c in range(cams):
        if tiles == GROUP:
            packets(c * tiles, c)
        else:

            def step(k, carry, c=c):
                packets(pl.multiple_of(c * tiles + k * GROUP, GROUP), c)
                return carry

            lax.fori_loop(0, tiles // GROUP, step, 0)

    square = (LANES, LANES)
    column = lax.broadcasted_iota(jnp.int32, square, 0)
    _, lane_j = lane_pass(square, cap)
    place = (lane_j + 1 + lax.broadcasted_iota(jnp.int32, square, 1) // HALF * cap).astype(F32)
    wide = (passes * rows, LANES)
    wide_lane = lax.broadcasted_iota(jnp.int32, wide, 1)
    key = lax.broadcasted_iota(jnp.int32, wide, 0)
    lane_key = jnp.where(wide_lane % HALF < passes * cap, lane_pass(wide, cap)[0] * rows, -(1 << 20))
    line_lane = lax.broadcasted_iota(jnp.int32, (1, LANES), 1)

    def two(c, t, found):
        asked = jnp.where(line_lane < HALF, ids[pl.ds(c * tiles + t, 1), :], ids[pl.ds(c * tiles + t + 1, 1), :])
        low = jnp.broadcast_to(asked % LANES, square)
        high = jnp.broadcast_to(asked // LANES, wide)
        match = jnp.where(low == column, place, 0.0).astype(BF16)
        owner = jnp.where(high + lane_key == key, 1.0, 0.0).astype(BF16)
        hit = dot(owner, match, ((1,), (1,)))
        return jnp.where(hit > 0.5, hit.astype(jnp.int32) + t * cap, found)

    for c in range(cams):
        found = jnp.zeros(wide, jnp.int32)
        if tiles <= 8:
            for t in range(0, tiles, 2):
                found = two(c, t, found)
        else:
            found = lax.fori_loop(0, tiles // 2, lambda t, f, c=c: two(c, 2 * t, f), found)
        for p in range(passes):
            start = (p * cams + c) * rows
            inverse[start : start + rows, :] = found[p * rows : (p + 1) * rows, :]


def render_kernel(passes, owners, cap, entries, pixels, got, lists, counts, places, wanted, out, alphas, logs):
    halves = entries // LANES
    shape = (GROUP, LANES)
    wide = 16
    lane = lax.broadcasted_iota(jnp.int32, shape, 1)
    sub = lax.broadcasted_iota(jnp.int32, shape, 0)

    slot_owner, slot_lane = [], []
    for p in range(passes):
        for h in range(halves):
            slot = jnp.broadcast_to(lists[p, 0, :, h * LANES : (h + 1) * LANES], shape)
            slot_owner.append(slot // cap)
            slot_lane.append(slot % cap + p * cap)
    total = passes * halves

    def gather(g, found):
        mine = [slot_owner[i] == g * GROUP + sub for i in range(total)]
        new = []
        for f in range(FIELDS):
            lines = got[pl.ds(g * (GROUP * SENT) + f // 2, GROUP, stride=SENT), :]
            for i in range(total):
                new.append(jnp.where(mine[i], lane_pick(lines, slot_lane[i] + f % 2 * HALF), found[f * total + i]))
        return tuple(new)

    fields = tuple(jnp.zeros(shape, F32) for _ in range(FIELDS * total))
    if owners <= 32:
        for g in range(owners // GROUP):
            fields = gather(g, fields)
    else:
        fields = lax.fori_loop(0, owners // GROUP, gather, fields)
    fields = [jnp.sum(x, axis=0, keepdims=True) for x in fields]

    pair = (LANES, LANES)
    lane_p, lane_j = lane_pass(pair, cap)
    turned_p, turned_j = lax.broadcasted_iota(jnp.int32, pair, 0) % HALF // cap, lax.broadcasted_iota(jnp.int32, pair, 0) % cap
    entry = (lax.broadcasted_iota(jnp.int32, pair, 1) + 1).astype(F32)
    owner_row = lax.broadcasted_iota(jnp.int32, (owners, LANES), 0)
    source = jnp.zeros((owners, LANES), jnp.int32)
    for p in range(passes):
        for h in range(halves):
            i = p * halves + h
            slot = lists[p, 0, :, h * LANES : (h + 1) * LANES]
            mine = jnp.where(jnp.broadcast_to(slot // cap, (owners, LANES)) == owner_row, 1.0, 0.0).astype(BF16)
            here = jnp.where(
                (jnp.broadcast_to(slot % cap, pair) == turned_j) & (turned_p == p), entry, 0.0
            ).astype(BF16)
            hit = dot(mine, here, ((1,), (1,)))
            source = jnp.where(hit > 0.5, hit.astype(jnp.int32) + h * LANES, source)

    before = jnp.where(
        lax.broadcasted_iota(jnp.int32, (entries, entries), 0) < lax.broadcasted_iota(jnp.int32, (entries, entries), 1),
        1.0,
        0.0,
    ).astype(BF16)
    after = jnp.where(
        lax.broadcasted_iota(jnp.int32, (entries, entries), 0) > lax.broadcasted_iota(jnp.int32, (entries, entries), 1),
        1.0,
        0.0,
    ).astype(BF16)
    entry_row = lax.broadcasted_iota(jnp.int32, (1, entries), 1)
    pixel = lax.broadcasted_iota(jnp.int32, (GROUP, pixels), 1)
    local_x = (pixel % wide).astype(F32) - 7.5
    local_y = (pixel // wide).astype(F32) - 7.5
    kind = lax.broadcasted_iota(jnp.int32, (GROUP, pixels), 0)
    moment = jnp.where(
        kind == 0,
        1.0,
        jnp.where(
            kind == 1,
            local_x,
            jnp.where(
                kind == 2,
                local_y,
                jnp.where(kind == 3, local_x * local_x, jnp.where(kind == 4, local_x * local_y, local_y * local_y)),
            ),
        ),
    ).astype(BF16)
    column_x = lax.broadcasted_iota(jnp.int32, (wide, entries), 0).astype(F32) - 7.5

    grads = []
    for p in range(passes):
        line = [
            jnp.concatenate([fields[f * total + p * halves + h] for h in range(halves)], axis=1) for f in range(FIELDS)
        ]
        place = places[0, p]
        u = line[0] - (place % 256 * 16 + 8).astype(F32)
        v = line[1] - (place // 256 * 16 + 8).astype(F32)
        c_a, c_b, c_c, base = line[2], line[3], line[4], line[5]
        color = jnp.concatenate(line[6:9], axis=0)
        live = jnp.where(entry_row < counts[0, p], base, 0.0)

        d_x = column_x - u
        q_xx = (-0.5 * c_a) * d_x * d_x
        q_x = c_b * d_x
        for y in range(pixels // wide):
            d_y = (y - 7.5) - v
            power = q_xx - (q_x * d_y + 0.5 * c_c * d_y * d_y)
            alpha = live * jnp.exp(power)
            alphas[p, y * wide : (y + 1) * wide, :] = alpha
            logs[y * wide : (y + 1) * wide, :] = jnp.log(1.0 - alpha)
        high, low = split(logs[...])
        through = jnp.exp(dot(high, before, ((1,), (0,))) + dot(low, before, ((1,), (0,))))
        alpha = alphas[p]
        weight = alpha * through
        w_high, w_low = split(weight)
        c_high, c_low = split(color)
        shown = (
            dot(c_high, w_high, ((1,), (1,))) + dot(c_low, w_high, ((1,), (1,))) + dot(c_high, w_low, ((1,), (1,)))
        )
        residual = shown - jnp.concatenate([wanted[p, k] for k in range(3)], axis=0)
        r_high, r_low = split(residual)
        left = jnp.concatenate([r_high, r_high, r_low], axis=0)
        right = jnp.concatenate([c_high, c_low, c_high], axis=0)
        slope = dot(left, right, ((0,), (0,)))
        pulled = weight * slope
        high, low = split(pulled)
        rest = dot(high, after, ((1,), (0,))) + dot(low, after, ((1,), (0,)))
        power_grad = pulled - alpha / (1.0 - alpha) * rest
        high, low = split(power_grad)
        moments = dot(moment, high, ((1,), (0,))) + dot(moment, low, ((1,), (0,)))
        color_grad = (
            dot(r_high, w_high, ((1,), (0,))) + dot(r_low, w_high, ((1,), (0,))) + dot(r_high, w_low, ((1,), (0,)))
        )
        m_1, m_x, m_y, m_xx, m_xy, m_yy = [moments[k : k + 1, :] for k in range(6)]
        s_x = m_x - u * m_1
        s_y = m_y - v * m_1
        s_xx = m_xx - u * (m_x + s_x)
        s_yy = m_yy - v * (m_y + s_y)
        s_xy = m_xy - u * m_y - v * s_x
        grads.append(
            [
                c_a * s_x + c_b * s_y,
                c_b * s_x + c_c * s_y,
                -0.5 * s_xx,
                -s_xy,
                -0.5 * s_yy,
                m_1 / base,
                color_grad[0:1, :],
                color_grad[1:2, :],
                color_grad[2:3, :],
            ]
        )

    def packets(first, origin):
        origin = origin - 1
        which = jnp.where(origin < 0, -1, origin // LANES)
        index = jnp.maximum(origin, 0) % LANES
        own_p, _ = lane_pass(shape, cap)

        def pick(f):
            found = jnp.zeros(shape, F32)
            for p in range(passes):
                for h in range(halves):
                    line = jnp.broadcast_to(grads[p][f][:, h * LANES : (h + 1) * LANES], shape)
                    found = jnp.where((which == h) & (own_p == p), lane_pick(line, index), found)
            return found

        for r in range(SENT):
            value = pick(2 * r)
            if 2 * r + 1 < FIELDS:
                value = jnp.where(lane < HALF, value, pick(2 * r + 1))
            out[pl.ds(first * SENT + r, GROUP, stride=SENT), :] = value

    for g in range(owners // GROUP):
        packets(g * GROUP, source[g * GROUP : (g + 1) * GROUP, :])


def pull_kernel(passes, cams, tiles, rows, cap, aligned, got, inverse, raw, table, pos, scales, rots, opac, cols, total):
    views = passes * cams
    shape = (rows, LANES)

    def at(k):
        return raw[k * rows : (k + 1) * rows, :]

    point = [at(k) for k in range(3)]
    squares = [jnp.exp(2.0 * at(3 + k)) for k in range(3)]
    spin, quat, quat_back = spin_of([at(6 + k) for k in range(4)])
    cov = world_cov(spin, squares)

    g_point = [jnp.zeros(shape, F32) for _ in range(3)]
    g_cov = [[jnp.zeros(shape, F32) for _ in range(3)] for _ in range(3)]
    g_opacity = jnp.zeros(shape, F32)
    for view in range(views):
        p, c = view // cams, view % cams
        slot = inverse[view * rows : (view + 1) * rows, :] - 1
        valid = slot >= 0
        slot = jnp.maximum(slot, 0)
        slot_t, slot_lane = slot // cap, slot % cap + p * cap
        if aligned:
            row_t = jnp.broadcast_to(jnp.max(slot_t, axis=1, keepdims=True), shape)

        def fetch(f):
            row, shift = f // 2, f % 2 * HALF
            if aligned:
                lines = got[pl.ds(c * tiles * SENT + row, tiles, stride=SENT), :]
                return jnp.where(valid, lane_pick(row_pick(lines, row_t), slot_lane + shift), 0.0)

            def one(t, found):
                line = jnp.broadcast_to(got[pl.ds((c * tiles + t) * SENT + row, 1), :], shape)
                return jnp.where(valid & (slot_t == t), lane_pick(line, slot_lane + shift), found)

            return lax.fori_loop(0, tiles, one, jnp.zeros(shape, F32))

        g = [fetch(f) for f in range(FIELDS)]
        rotate, offset, center = camera_of(table, view, views, shape)
        m, inv, main, at_x, at_y, t_x, t_y, w_x, w_y, conic = screen_of(point, cov, rotate, offset)
        c_a, c_b, c_c = conic
        half = 0.5 * g[3]
        p00, p01 = g[2] * c_a + half * c_b, g[2] * c_b + half * c_c
        p10, p11 = half * c_a + g[4] * c_b, half * c_b + g[4] * c_c
        g_xx = -(c_a * p00 + c_b * p10)
        g_xy = -(c_a * p01 + c_b * p11)
        g_yy = -(c_b * p01 + c_c * p11)
        left = [g_xx * t_x[i] + g_xy * t_y[i] for i in range(3)]
        right = [g_yy * t_y[i] + g_xy * t_x[i] for i in range(3)]
        for i in range(3):
            for j in range(i, 3):
                g_cov[i][j] = g_cov[i][j] + (t_x[i] * left[j] + t_y[i] * right[j])
        g_tx = [2.0 * (g_xx * w_x[i] + g_xy * w_y[i]) for i in range(3)]
        g_ty = [2.0 * (g_yy * w_y[i] + g_xy * w_x[i]) for i in range(3)]
        g_main = dot3(rotate[0], g_tx) + dot3(rotate[1], g_ty)
        g_sx, g_sy = dot3(rotate[2], g_tx), dot3(rotate[2], g_ty)
        g_m0 = main * (g[0] - inv * g_sx)
        g_m1 = main * (g[1] - inv * g_sy)
        g_m2 = -main * (
            at_x * g[0] + at_y * g[1] + inv * g_main - 2.0 * inv * (at_x * g_sx + at_y * g_sy)
        )
        direction, length_back = direction_of(point, center)
        basis = basis_of(*direction)
        g_basis = [None]
        for k in range(1, 16):
            g_basis.append(
                at(11 + 3 * k) * g[6] + at(12 + 3 * k) * g[7] + at(13 + 3 * k) * g[8]
            )
        g_dir = basis_pull(*direction, g_basis)
        along = dot3(direction, g_dir)
        for j in range(3):
            g_point[j] = g_point[j] + (
                rotate[0][j] * g_m0 + rotate[1][j] * g_m1 + rotate[2][j] * g_m2
                + (g_dir[j] - direction[j] * along) * length_back
            )
        g_opacity = g_opacity + g[5]
        for k in range(16):
            for channel in range(3):
                term = SH_ZERO * g[6 + channel] if k == 0 else basis[k] * g[6 + channel]
                start = (11 + 3 * k + channel) * rows
                if view == 0:
                    total[start : start + rows, :] = term
                else:
                    total[start : start + rows, :] += term
    for i in range(3):
        for j in range(i):
            g_cov[i][j] = g_cov[j][i]

    g_scales = []
    g_spin = [[None] * 3 for _ in range(3)]
    for k in range(3):
        column = [spin[j][k] for j in range(3)]
        turned = [dot3(g_cov[i], column) for i in range(3)]
        g_scales.append(2.0 * squares[k] * dot3(column, turned))
        for i in range(3):
            g_spin[i][k] = 2.0 * squares[k] * turned[i]
    w, x, y, z = quat
    d = g_spin
    g_quat = [
        2.0 * (z * (d[1][0] - d[0][1]) + y * (d[0][2] - d[2][0]) + x * (d[2][1] - d[1][2])),
        2.0 * (y * (d[0][1] + d[1][0]) + z * (d[0][2] + d[2][0]) + w * (d[2][1] - d[1][2]) - 2.0 * x * (d[1][1] + d[2][2])),
        2.0 * (x * (d[0][1] + d[1][0]) + z * (d[1][2] + d[2][1]) + w * (d[0][2] - d[2][0]) - 2.0 * y * (d[0][0] + d[2][2])),
        2.0 * (x * (d[0][2] + d[2][0]) + y * (d[1][2] + d[2][1]) + w * (d[1][0] - d[0][1]) - 2.0 * z * (d[0][0] + d[1][1])),
    ]
    along = w * g_quat[0] + x * g_quat[1] + y * g_quat[2] + z * g_quat[3]
    g_rots = [(g_quat[k] - quat[k] * along) * quat_back for k in range(4)]
    opacity = 1.0 / (1.0 + jnp.exp(-at(10)))
    opac[...] = g_opacity * opacity * (1.0 - opacity)
    for k, value in enumerate(g_point + g_scales + g_rots):
        total[k * rows : (k + 1) * rows, :] = value
    base = 0
    for ref in (pos, scales, rots, cols):
        count = ref.shape[0]
        if ref is cols:
            base = 11
        for i in range(rows):
            ref[:, i * LANES : (i + 1) * LANES] = total[pl.ds(base * rows + i, count, stride=rows), :]
        base += count


def vmem(count):
    return [pl.BlockSpec(memory_space=pltpu.VMEM)] * count


def call(kernel, outs, operands, in_specs=None, scratch=(), flops=1_000_000):
    return pl.pallas_call(
        kernel,
        out_shape=outs,
        in_specs=in_specs or vmem(len(operands)),
        out_specs=jax.tree.map(lambda _: pl.BlockSpec(memory_space=pltpu.VMEM), outs),
        scratch_shapes=list(scratch),
        compiler_params=pltpu.CompilerParams(vmem_limit_bytes=32 << 20),
        cost_estimate=pl.CostEstimate(flops=flops, bytes_accessed=1 << 20, transcendentals=0),
    )(*operands)


def body(
    cams,
    tiles,
    positions,
    log_scales,
    rotations,
    opacities,
    colors,
    cameras,
    targets,
    tile_ids,
    tile_counts,
    tile_lists,
    fetch_ids,
):
    axes = ("cam", "tile")
    passes, cap = fetch_ids.shape[0], fetch_ids.shape[-1]
    entries, pixels = tile_lists.shape[-1], targets.shape[-1]
    columns = positions.shape[-1]
    rows = columns // LANES
    owners = cams * tiles
    views = passes * cams
    aligned = tiles == rows == 8

    def shaped(*shape):
        return jax.ShapeDtypeStruct(shape, F32)

    def exchange(x):
        lines = x.reshape(owners, 1, -1)
        return lax.all_to_all(lines, axes, split_axis=0, concat_axis=0, tiled=True).reshape(x.shape)

    wanted_ids = call(
        functools.partial(ids_kernel, passes, cams, cap),
        jax.ShapeDtypeStruct((owners, LANES), jnp.int32),
        [fetch_ids],
    )
    arrived = exchange(wanted_ids)
    records, raw, table = call(
        functools.partial(project_kernel, passes, cams, rows),
        [shaped(views * FIELDS * rows, LANES), shaped(RAW * rows, LANES), shaped(TERMS * views, LANES)],
        [positions, log_scales, rotations, opacities.reshape(rows, LANES), colors, cameras],
    )
    packets, inverse = call(
        functools.partial(pick_kernel, passes, cams, tiles, rows, cap, aligned),
        [shaped(owners * SENT, LANES), jax.ShapeDtypeStruct((views * rows, LANES), jnp.int32)],
        [arrived, records],
    )
    fetched = exchange(packets)
    smem = pl.BlockSpec(memory_space=pltpu.SMEM)
    whole = vmem(1)[0]
    slot_grads = call(
        functools.partial(render_kernel, passes, owners, cap, entries, pixels),
        shaped(owners * SENT, LANES),
        [
            fetched,
            tile_lists,
            tile_counts.reshape(1, passes),
            tile_ids.reshape(1, passes),
            targets.reshape(passes, 3, 1, pixels),
        ],
        in_specs=[whole, whole, smem, smem, whole],
        scratch=[
            pltpu.VMEM((passes, pixels, entries), F32),
            pltpu.VMEM((pixels, entries), F32),
        ],
    )
    coming = exchange(slot_grads)
    g_pos, g_scales, g_rots, g_opac, g_cols = call(
        functools.partial(pull_kernel, passes, cams, tiles, rows, cap, aligned),
        [shaped(3, columns), shaped(3, columns), shaped(4, columns), shaped(rows, LANES), shaped(48, columns)],
        [coming, inverse, raw, table],
        scratch=[pltpu.VMEM((RAW * rows, LANES), F32)],
    )
    return (g_pos, g_scales, g_rots, g_opac.reshape(columns), g_cols)


def solution(mesh):
    return jax.shard_map(
        functools.partial(body, mesh.shape["cam"], mesh.shape["tile"]),
        mesh=mesh,
        in_specs=(
            P(None, ("cam", "tile")),
            P(None, ("cam", "tile")),
            P(None, ("cam", "tile")),
            P(("cam", "tile")),
            P(None, ("cam", "tile")),
            P(),
            P(None, "cam", "tile", None, None),
            P(None, "cam", "tile"),
            P(None, "cam", "tile"),
            P(None, "cam", "tile", None),
            P(None, "cam", "tile", None, None, None),
        ),
        out_specs=(
            P(None, ("cam", "tile")),
            P(None, ("cam", "tile")),
            P(None, ("cam", "tile")),
            P(("cam", "tile")),
            P(None, ("cam", "tile")),
        ),
        check_vma=False,
    )
```

```python
import functools

import jax
import jax.numpy as jnp
from jax import lax
from jax.experimental import pallas as pl
from jax.experimental.pallas import tpu as pltpu
from jax.sharding import PartitionSpec as P

FOCAL = 4096.0
CENTER_X = 2048.0
CENTER_Y = 1024.0
SH_ZERO = 0.28209479177387814
SH_ONE = 0.4886025119029199
SH_TWO = [
    1.0925484305920792,
    -1.0925484305920792,
    0.31539156525252005,
    -1.0925484305920792,
    0.5462742152960396,
]
SH_THREE = [
    -0.5900435899266435,
    2.890611442640554,
    -0.4570457994644658,
    0.3731763325901154,
    -0.4570457994644658,
    1.445305721320277,
    -0.5900435899266435,
]
LANES = 128
HALF = LANES // 2
FIELDS = 9
SENT = 5
GROUP = 8
RAW = 59
KEPT = 38
SCENE = 6
TERMS = 15
F32 = jnp.float32
BF16 = jnp.bfloat16


def dot(left, right, contract):
    return lax.dot_general(left, right, ((contract[0], contract[1]), ((), ())), preferred_element_type=F32)


def split(x):
    high = x.astype(BF16)
    return high, (x - high.astype(F32)).astype(BF16)


def lane_pick(source, index):
    return jnp.take_along_axis(source, index, axis=1, mode="promise_in_bounds")


def row_pick(source, index):
    return jnp.take_along_axis(source, index, axis=0, mode="promise_in_bounds")


def spin_of(quat):
    norm = jnp.sqrt(quat[0] * quat[0] + quat[1] * quat[1] + quat[2] * quat[2] + quat[3] * quat[3])
    back = 1.0 / norm
    w, x, y, z = [q * back for q in quat]
    spin = [
        [1.0 - 2.0 * (y * y + z * z), 2.0 * (x * y - w * z), 2.0 * (x * z + w * y)],
        [2.0 * (x * y + w * z), 1.0 - 2.0 * (x * x + z * z), 2.0 * (y * z - w * x)],
        [2.0 * (x * z - w * y), 2.0 * (y * z + w * x), 1.0 - 2.0 * (x * x + y * y)],
    ]
    return spin, (w, x, y, z), back


def world_cov(spin, squares):
    scaled = [[spin[i][k] * squares[k] for k in range(3)] for i in range(3)]
    cov = [[None] * 3 for _ in range(3)]
    for i in range(3):
        for j in range(i, 3):
            cov[i][j] = scaled[i][0] * spin[j][0] + scaled[i][1] * spin[j][1] + scaled[i][2] * spin[j][2]
            cov[j][i] = cov[i][j]
    return cov


def dot3(a, b):
    return a[0] * b[0] + a[1] * b[1] + a[2] * b[2]


def screen_of(point, cov, rotate, offset):
    m = [dot3(rotate[i], point) + offset[i] for i in range(3)]
    inverse = 1.0 / m[2]
    main = FOCAL * inverse
    at_x, at_y = m[0] * inverse, m[1] * inverse
    side_x, side_y = -main * at_x, -main * at_y
    t_x = [main * rotate[0][i] + side_x * rotate[2][i] for i in range(3)]
    t_y = [main * rotate[1][i] + side_y * rotate[2][i] for i in range(3)]
    w_x = [dot3(cov[i], t_x) for i in range(3)]
    w_y = [dot3(cov[i], t_y) for i in range(3)]
    s_xx = dot3(t_x, w_x) + 0.3
    s_xy = dot3(t_y, w_x)
    s_yy = dot3(t_y, w_y) + 0.3
    back = 1.0 / (s_xx * s_yy - s_xy * s_xy)
    conic = (s_yy * back, -s_xy * back, s_xx * back)
    return m, inverse, main, at_x, at_y, t_x, t_y, w_x, w_y, conic


def direction_of(point, center):
    toward = [point[j] - center[j] for j in range(3)]
    back = lax.rsqrt(dot3(toward, toward))
    return [t * back for t in toward], back


def basis_of(x, y, z):
    xx, yy, zz = x * x, y * y, z * z
    xy, yz, xz = x * y, y * z, x * z
    less = xx - yy
    four = 4.0 * zz - xx - yy
    return [
        None,
        -SH_ONE * y,
        SH_ONE * z,
        -SH_ONE * x,
        SH_TWO[0] * xy,
        SH_TWO[1] * yz,
        SH_TWO[2] * (2.0 * zz - xx - yy),
        SH_TWO[3] * xz,
        SH_TWO[4] * less,
        SH_THREE[0] * y * (3.0 * xx - yy),
        SH_THREE[1] * xy * z,
        SH_THREE[2] * y * four,
        SH_THREE[3] * z * (2.0 * zz - 3.0 * xx - 3.0 * yy),
        SH_THREE[4] * x * four,
        SH_THREE[5] * z * less,
        SH_THREE[6] * x * (xx - 3.0 * yy),
    ]


def basis_pull(x, y, z, g):
    xx, yy, zz = x * x, y * y, z * z
    xy, yz, xz = x * y, y * z, x * z
    less = xx - yy
    four = 4.0 * zz - xx - yy
    g4, g5, g6, g7, g8 = [SH_TWO[i] * g[4 + i] for i in range(5)]
    h = [SH_THREE[i] * g[9 + i] for i in range(7)]
    g_x = (
        -SH_ONE * g[3] + g4 * y - 2.0 * g6 * x + g7 * z + 2.0 * g8 * x
        + 6.0 * h[0] * xy + h[1] * yz - 2.0 * h[2] * xy - 6.0 * h[3] * xz
        + h[4] * (four - 2.0 * xx) + 2.0 * h[5] * xz + 3.0 * h[6] * less
    )
    g_y = (
        -SH_ONE * g[1] + g4 * x + g5 * z - 2.0 * g6 * y - 2.0 * g8 * y
        + 3.0 * h[0] * less + h[1] * xz + h[2] * (four - 2.0 * yy) - 6.0 * h[3] * yz
        - 2.0 * h[4] * xy - 2.0 * h[5] * yz - 6.0 * h[6] * xy
    )
    g_z = (
        SH_ONE * g[2] + g5 * y + 4.0 * g6 * z + g7 * x
        + h[1] * xy + 8.0 * h[2] * yz + h[3] * (6.0 * zz - 3.0 * xx - 3.0 * yy)
        + 8.0 * h[4] * xz + h[5] * less
    )
    return [g_x, g_y, g_z]


def camera_rows(cam_ref, table, passes, cams):
    views = passes * cams
    for p in range(passes):
        cam = cam_ref[p]
        cos, sin = jnp.cos(cam), jnp.sin(cam)
        ca, cb, cg = [cos[:, k : k + 1] for k in range(3)]
        sa, sb, sg = [sin[:, k : k + 1] for k in range(3)]
        rotate = [
            [cg * cb, cg * sb * sa - sg * ca, cg * sb * ca + sg * sa],
            [sg * cb, sg * sb * sa + cg * ca, sg * sb * ca - cg * sa],
            [-sb, cb * sa, cb * ca],
        ]
        offset = [cam[:, 3:4], cam[:, 4:5], 6.0 + cam[:, 5:6]]
        center = [-(rotate[0][j] * offset[0] + rotate[1][j] * offset[1] + rotate[2][j] * offset[2]) for j in range(3)]
        for k, term in enumerate(rotate[0] + rotate[1] + rotate[2] + offset + center):
            table[k * views + p * cams : k * views + (p + 1) * cams, :] = jnp.broadcast_to(term, (cams, LANES))


def camera_of(table, view, views, shape):
    terms = [jnp.broadcast_to(table[k * views + view : k * views + view + 1, :], shape) for k in range(TERMS)]
    return [terms[0:3], terms[3:6], terms[6:9]], terms[9:12], terms[12:15]


def project_kernel(
    passes, cams, rows, owners, cap, far_pos, far_scales, far_rots, far_opac, far_cols, far_cam, far_lists, far_wanted,
    far_counts, far_places, rec, raw, table, kept, scene, source, chosen,
    pos, scales, rots, opac, cols, cam, lists, wanted, counts, places, done,
):
    views = passes * cams
    shape = (rows, LANES)
    fars = (far_cam, far_pos, far_scales, far_rots, far_opac, far_lists, far_wanted, far_counts, far_places, far_cols)
    nears = (cam, pos, scales, rots, opac, lists, wanted, counts, places, cols)
    copies = [pltpu.make_async_copy(a, b, done.at[k]) for k, (a, b) in enumerate(zip(fars, nears))]
    for copy in copies:
        copy.start()
    for copy in copies[:-1]:
        copy.wait()
    camera_rows(cam, table, passes, cams)
    base = 0
    for ref in (pos, scales, rots):
        count = ref.shape[0]
        for i in range(rows):
            raw[pl.ds(base * rows + i, count, stride=rows), :] = ref[:, i * LANES : (i + 1) * LANES]
        base += count
    raw[base * rows : (base + 1) * rows, :] = opac[...]

    def at(k):
        return raw[k * rows : (k + 1) * rows, :]

    def put(ref, k, value):
        ref[k * rows : (k + 1) * rows, :] = value

    point = [at(k) for k in range(3)]
    squares = [jnp.exp(2.0 * at(3 + k)) for k in range(3)]
    spin, _, _ = spin_of([at(6 + k) for k in range(4)])
    cov = world_cov(spin, squares)
    opacity = 1.0 / (1.0 + jnp.exp(-at(10)))
    for view in range(views):
        rotate, offset, center = camera_of(table, view, views, shape)
        _, inv, main, at_x, at_y, t_x, t_y, w_x, w_y, conic = screen_of(point, cov, rotate, offset)
        direction, back = direction_of(point, center)
        basis = basis_of(*direction)
        fields = [FOCAL * at_x + CENTER_X, FOCAL * at_y + CENTER_Y, conic[0], conic[1], conic[2], opacity]
        for f, value in enumerate(fields):
            put(rec, view * FIELDS + f, value)
        for k, value in enumerate([inv, main, at_x, at_y, *t_x, *t_y, *w_x, *w_y, *conic, *direction, back, *basis[1:]]):
            put(kept, view * KEPT + k, value)

    entries, pixels = lists.shape[-1], wanted.shape[-1]
    entry_row = lax.broadcasted_iota(jnp.int32, (1, entries), 1)
    for p in range(passes):
        for k in range(3):
            scene[p * SCENE + k : p * SCENE + k + 1, :] = wanted[p, k]
        count = jnp.broadcast_to(counts[:, p : p + 1], (1, entries))
        scene[p * SCENE + 3 : p * SCENE + 4, :] = jnp.where(entry_row < count, 1.0, 0.0)
        place = jnp.broadcast_to(places[:, p : p + 1], (1, entries))
        for k, value in enumerate((place % 256 * 16 + 8, place // 256 * 16 + 8)):
            scene[p * SCENE + 4 + k : p * SCENE + 5 + k, :] = value.astype(F32)
        chosen[p : p + 1, :] = lists[p, 0]
    pair = (LANES, LANES)
    turned = lax.broadcasted_iota(jnp.int32, pair, 0)
    turned_p, turned_j = turned % HALF // cap, turned % cap
    entry = (lax.broadcasted_iota(jnp.int32, pair, 1) + 1).astype(F32)
    owner_row = lax.broadcasted_iota(jnp.int32, (owners, LANES), 0)
    found = jnp.zeros((owners, LANES), jnp.int32)
    for p in range(passes):
        for h in range(entries // LANES):
            slot = lists[p, 0, :, h * LANES : (h + 1) * LANES]
            mine = jnp.where(jnp.broadcast_to(slot // cap, (owners, LANES)) == owner_row, 1.0, 0.0).astype(BF16)
            here = jnp.where(
                (jnp.broadcast_to(slot % cap, pair) == turned_j) & (turned_p == p), entry, 0.0
            ).astype(BF16)
            hit = dot(mine, here, ((1,), (1,)))
            found = jnp.where(hit > 0.5, hit.astype(jnp.int32) + h * LANES, found)
    source[...] = found

    copies[-1].wait()
    for i in range(rows):
        raw[pl.ds(11 * rows + i, cols.shape[0], stride=rows), :] = cols[:, i * LANES : (i + 1) * LANES]
    for channel in range(3):
        totals = [0.5 + SH_ZERO * at(11 + channel)] * views
        for k in range(1, 16):
            color = at(11 + 3 * k + channel)
            for view in range(views):
                start = (view * KEPT + KEPT - 16 + k) * rows
                totals[view] = totals[view] + kept[start : start + rows, :] * color
        for view in range(views):
            put(rec, view * FIELDS + 6 + channel, totals[view])


def lane_pass(shape, cap):
    lane = lax.broadcasted_iota(jnp.int32, shape, 1) % HALF
    return lane // cap, lane % cap


def ids_kernel(passes, cams, cap, ids, out, landed, lines, done):
    copy = pltpu.make_async_copy(ids, landed, done)
    copy.start()
    copy.wait()
    for c in range(cams):
        parts = [landed[p, 0, 0, c] for p in range(passes)]
        tiles = parts[0].shape[0]
        if passes * cap < HALF:
            parts.append(jnp.zeros((tiles, HALF - passes * cap), jnp.int32))
        lines[c * tiles : (c + 1) * tiles, :] = jnp.concatenate(parts + parts, axis=1)
    copy = pltpu.make_async_copy(lines, out, done)
    copy.start()
    copy.wait()


def pick_kernel(passes, cams, tiles, rows, cap, aligned, ids, rec, out, inverse):
    shape = (GROUP, LANES)
    lane = lax.broadcasted_iota(jnp.int32, shape, 1)
    lane_p, _ = lane_pass(shape, cap)

    def packets(first, c):
        asked = ids[pl.ds(first, GROUP), :]
        low, high = asked % LANES, asked // LANES
        if aligned:
            blocks = [jnp.broadcast_to(high[:, p * cap : p * cap + 1], shape) for p in range(passes)]

        def pick(f):
            found = jnp.zeros(shape, F32)
            for p in range(passes):
                start = ((p * cams + c) * FIELDS + f) * rows
                if aligned:
                    own = lane_pick(row_pick(rec[start : start + rows, :], blocks[p]), low)
                else:
                    own = jnp.zeros(shape, F32)
                    for b in range(rows):
                        line = jnp.broadcast_to(rec[start + b : start + b + 1, :], shape)
                        own = jnp.where(high == b, lane_pick(line, low), own)
                found = own if p == 0 else jnp.where(lane_p == p, own, found)
            return found

        for r in range(SENT):
            value = pick(2 * r)
            if 2 * r + 1 < FIELDS:
                value = jnp.where(lane < HALF, value, pick(2 * r + 1))
            out[pl.ds(first * SENT + r, GROUP, stride=SENT), :] = value

    for c in range(cams):
        if tiles == GROUP:
            packets(c * tiles, c)
        else:

            def step(k, carry, c=c):
                packets(pl.multiple_of(c * tiles + k * GROUP, GROUP), c)
                return carry

            lax.fori_loop(0, tiles // GROUP, step, 0)

    square = (LANES, LANES)
    column = lax.broadcasted_iota(jnp.int32, square, 0)
    _, lane_j = lane_pass(square, cap)
    place = (lane_j + 1 + lax.broadcasted_iota(jnp.int32, square, 1) // HALF * cap).astype(F32)
    wide = (passes * rows, LANES)
    wide_lane = lax.broadcasted_iota(jnp.int32, wide, 1)
    key = lax.broadcasted_iota(jnp.int32, wide, 0)
    lane_key = jnp.where(wide_lane % HALF < passes * cap, lane_pass(wide, cap)[0] * rows, -(1 << 20))
    line_lane = lax.broadcasted_iota(jnp.int32, (1, LANES), 1)

    def two(c, t, found):
        asked = jnp.where(line_lane < HALF, ids[pl.ds(c * tiles + t, 1), :], ids[pl.ds(c * tiles + t + 1, 1), :])
        low = jnp.broadcast_to(asked % LANES, square)
        high = jnp.broadcast_to(asked // LANES, wide)
        match = jnp.where(low == column, place, 0.0).astype(BF16)
        owner = jnp.where(high + lane_key == key, 1.0, 0.0).astype(BF16)
        hit = dot(owner, match, ((1,), (1,)))
        return jnp.where(hit > 0.5, hit.astype(jnp.int32) + t * cap, found)

    for c in range(cams):
        found = jnp.zeros(wide, jnp.int32)
        if tiles <= 8:
            for t in range(0, tiles, 2):
                found = two(c, t, found)
        else:
            found = lax.fori_loop(0, tiles // 2, lambda t, f, c=c: two(c, 2 * t, f), found)
        for p in range(passes):
            start = (p * cams + c) * rows
            inverse[start : start + rows, :] = found[p * rows : (p + 1) * rows, :]


def render_kernel(passes, owners, cap, entries, pixels, got, lists, scene, source, out, *scratch):
    alphas, ratios, sums, high, low = [scratch[k * passes : (k + 1) * passes] for k in range(5)]
    halves = entries // LANES
    shape = (GROUP, LANES)
    wide = 16
    lane = lax.broadcasted_iota(jnp.int32, shape, 1)
    sub = lax.broadcasted_iota(jnp.int32, shape, 0)

    slot_owner, slot_lane = [], []
    for p in range(passes):
        for h in range(halves):
            slot = jnp.broadcast_to(lists[p : p + 1, h * LANES : (h + 1) * LANES], shape)
            slot_owner.append(slot // cap)
            slot_lane.append(slot % cap + p * cap)
    total = passes * halves

    def gather(g, found):
        mine = [slot_owner[i] == g * GROUP + sub for i in range(total)]
        new = []
        for f in range(FIELDS):
            lines = got[pl.ds(g * (GROUP * SENT) + f // 2, GROUP, stride=SENT), :]
            for i in range(total):
                new.append(jnp.where(mine[i], lane_pick(lines, slot_lane[i] + f % 2 * HALF), found[f * total + i]))
        return tuple(new)

    fields = tuple(jnp.zeros(shape, F32) for _ in range(FIELDS * total))
    if owners <= 32:
        for g in range(owners // GROUP):
            fields = gather(g, fields)
    else:
        fields = lax.fori_loop(0, owners // GROUP, gather, fields)
    fields = [jnp.sum(x, axis=0, keepdims=True) for x in fields]

    square = (entries, entries)
    row_at, column_at = lax.broadcasted_iota(jnp.int32, square, 0), lax.broadcasted_iota(jnp.int32, square, 1)
    before = jnp.where(row_at < column_at, 1.0, 0.0).astype(BF16)
    after = jnp.where(row_at > column_at, 1.0, 0.0).astype(BF16)
    column_x = lax.broadcasted_iota(jnp.int32, (wide, entries), 0).astype(F32) - 7.5
    steps = [slice(y * wide, (y + 1) * wide) for y in range(pixels // wide)]

    lines, spans = [], []
    for p in range(passes):
        line = [
            jnp.concatenate([fields[f * total + p * halves + h] for h in range(halves)], axis=1) for f in range(FIELDS)
        ]
        line[0] = line[0] - scene[p * SCENE + 4 : p * SCENE + 5, :]
        line[1] = line[1] - scene[p * SCENE + 5 : p * SCENE + 6, :]
        lines.append(line)
        spans.append(column_x - line[0])

    def offset_y(p, y):
        return (y - 7.5) - lines[p][1]

    for p in range(passes):
        _, _, c_a, c_b, c_c, base = lines[p][:6]
        live = base * scene[p * SCENE + 3 : p * SCENE + 4, :]
        d_x = spans[p]
        q_xx = (-0.5 * c_a) * d_x * d_x
        q_x = -c_b * d_x
        for y, at in enumerate(steps):
            d_y = offset_y(p, y)
            alpha = live * jnp.exp(q_xx + (q_x * d_y - 0.5 * c_c * d_y * d_y))
            clear = jnp.log(1.0 - alpha)
            alphas[p][at, :] = alpha
            ratios[p][at, :] = alpha * jnp.exp(-clear)
            high[p][at, :], low[p][at, :] = split(clear)
    for p in range(passes):
        sums[p][...] = dot(high[p][...], before, ((1,), (0,))) + dot(low[p][...], before, ((1,), (0,)))
    for p in range(passes):
        for at in steps:
            weight = alphas[p][at, :] * jnp.exp(sums[p][at, :])
            alphas[p][at, :] = weight
            high[p][at, :], low[p][at, :] = split(weight)
    residuals, pair_rows = [], []
    for p in range(passes):
        c_high, c_low = split(jnp.concatenate(lines[p][6:9], axis=0))
        both = dot(jnp.concatenate([c_high, c_low], axis=0), high[p][...], ((1,), (1,)))
        shown = both[0:3, :] + both[3:6, :] + dot(c_high, low[p][...], ((1,), (1,)))
        residuals.append(split(shown - scene[p * SCENE : p * SCENE + 3, :]))
        pair_rows.append(jnp.concatenate([c_high, c_low, c_high], axis=0))
    color_grads = []
    for p in range(passes):
        r_high, r_low = residuals[p]
        sums[p][...] = dot(jnp.concatenate([r_high, r_high, r_low], axis=0), pair_rows[p], ((0,), (0,)))
        both = dot(jnp.concatenate([r_high, r_low], axis=0), high[p][...], ((1,), (0,)))
        color_grads.append(both[0:3, :] + both[3:6, :] + dot(r_high, low[p][...], ((1,), (0,))))
    for p in range(passes):
        for at in steps:
            pulled = alphas[p][at, :] * sums[p][at, :]
            alphas[p][at, :] = pulled
            high[p][at, :], low[p][at, :] = split(pulled)
    for p in range(passes):
        sums[p][...] = dot(high[p][...], after, ((1,), (0,))) + dot(low[p][...], after, ((1,), (0,)))
    grads = []
    for p in range(passes):
        m_1 = m_y = m_yy = jnp.zeros((wide, entries), F32)
        for y, at in enumerate(steps):
            grad = alphas[p][at, :] - ratios[p][at, :] * sums[p][at, :]
            d_y = offset_y(p, y)
            grad_y = grad * d_y
            m_1, m_y, m_yy = m_1 + grad, m_y + grad_y, m_yy + grad_y * d_y
        d_x = spans[p]
        m_x = m_1 * d_x
        s_1, s_x, s_y, s_xx, s_xy, s_yy = [
            jnp.sum(m, axis=0, keepdims=True) for m in (m_1, m_x, m_y, m_x * d_x, m_y * d_x, m_yy)
        ]
        _, _, c_a, c_b, c_c, base = lines[p][:6]
        grads.append(
            [
                c_a * s_x + c_b * s_y,
                c_b * s_x + c_c * s_y,
                -0.5 * s_xx,
                -s_xy,
                -0.5 * s_yy,
                s_1 / base,
                color_grads[p][0:1, :],
                color_grads[p][1:2, :],
                color_grads[p][2:3, :],
            ]
        )

    def packets(first, origin):
        origin = origin - 1
        which = jnp.where(origin < 0, -1, origin // LANES)
        index = jnp.maximum(origin, 0) % LANES
        own_p, _ = lane_pass(shape, cap)

        def pick(f):
            found = jnp.zeros(shape, F32)
            for p in range(passes):
                for h in range(halves):
                    line = jnp.broadcast_to(grads[p][f][:, h * LANES : (h + 1) * LANES], shape)
                    found = jnp.where((which == h) & (own_p == p), lane_pick(line, index), found)
            return found

        for r in range(SENT):
            value = pick(2 * r)
            if 2 * r + 1 < FIELDS:
                value = jnp.where(lane < HALF, value, pick(2 * r + 1))
            out[pl.ds(first * SENT + r, GROUP, stride=SENT), :] = value

    for g in range(owners // GROUP):
        packets(g * GROUP, source[g * GROUP : (g + 1) * GROUP, :])


def pull_kernel(
    passes, cams, tiles, rows, cap, aligned, got, inverse, raw, table, kept,
    pos, scales, rots, opac, cols, total, leaving, done,
):
    views = passes * cams
    shape = (rows, LANES)

    def at(k):
        return raw[k * rows : (k + 1) * rows, :]

    def fetcher(view):
        p, c = view // cams, view % cams
        slot = inverse[view * rows : (view + 1) * rows, :] - 1
        valid = slot >= 0
        slot = jnp.maximum(slot, 0)
        slot_t, slot_lane = slot // cap, slot % cap + p * cap
        if aligned:
            row_t = jnp.broadcast_to(jnp.max(slot_t, axis=1, keepdims=True), shape)

        def fetch(f):
            row, shift = f // 2, f % 2 * HALF
            if aligned:
                lines = got[pl.ds(c * tiles * SENT + row, tiles, stride=SENT), :]
                return jnp.where(valid, lane_pick(row_pick(lines, row_t), slot_lane + shift), 0.0)

            def one(t, found):
                line = jnp.broadcast_to(got[pl.ds((c * tiles + t) * SENT + row, 1), :], shape)
                return jnp.where(valid & (slot_t == t), lane_pick(line, slot_lane + shift), found)

            return lax.fori_loop(0, tiles, one, jnp.zeros(shape, F32))

        return fetch

    def held(view, k):
        start = (view * KEPT + k) * rows
        return kept[start : start + rows, :]

    fetchers = [fetcher(view) for view in range(views)]
    shades = [[fetchers[view](6 + channel) for view in range(views)] for channel in range(3)]
    for k in range(16):
        basis = [held(view, KEPT - 16 + k) for view in range(views)] if k else None
        for channel in range(3):
            terms = shades[channel] if k == 0 else [basis[view] * shades[channel][view] for view in range(views)]
            while len(terms) > 1:
                terms = [sum(terms[n : n + 2][1:], terms[n]) for n in range(0, len(terms), 2)]
            start = (11 + 3 * k + channel) * rows
            total[start : start + rows, :] = terms[0] if k else SH_ZERO * terms[0]
    for i in range(rows):
        leaving[:, i * LANES : (i + 1) * LANES] = total[pl.ds(11 * rows + i, cols.shape[0], stride=rows), :]
    copy = pltpu.make_async_copy(leaving, cols, done)
    copy.start()

    point = [at(k) for k in range(3)]
    squares = [jnp.exp(2.0 * at(3 + k)) for k in range(3)]
    spin, quat, quat_back = spin_of([at(6 + k) for k in range(4)])

    g_point = [jnp.zeros(shape, F32) for _ in range(3)]
    g_cov = [[jnp.zeros(shape, F32) for _ in range(3)] for _ in range(3)]
    g_opacity = jnp.zeros(shape, F32)
    for view in range(views):
        g = [fetchers[view](f) for f in range(6)] + [shades[channel][view] for channel in range(3)]
        rotate, _, _ = camera_of(table, view, views, shape)
        inv, main, at_x, at_y = [held(view, k) for k in range(4)]
        t_x, t_y, w_x, w_y, conic, direction = [[held(view, 4 + 3 * n + k) for k in range(3)] for n in range(6)]
        length_back = held(view, 22)
        c_a, c_b, c_c = conic
        half = 0.5 * g[3]
        p00, p01 = g[2] * c_a + half * c_b, g[2] * c_b + half * c_c
        p10, p11 = half * c_a + g[4] * c_b, half * c_b + g[4] * c_c
        g_xx = -(c_a * p00 + c_b * p10)
        g_xy = -(c_a * p01 + c_b * p11)
        g_yy = -(c_b * p01 + c_c * p11)
        left = [g_xx * t_x[i] + g_xy * t_y[i] for i in range(3)]
        right = [g_yy * t_y[i] + g_xy * t_x[i] for i in range(3)]
        for i in range(3):
            for j in range(i, 3):
                g_cov[i][j] = g_cov[i][j] + (t_x[i] * left[j] + t_y[i] * right[j])
        g_tx = [2.0 * (g_xx * w_x[i] + g_xy * w_y[i]) for i in range(3)]
        g_ty = [2.0 * (g_yy * w_y[i] + g_xy * w_x[i]) for i in range(3)]
        g_main = dot3(rotate[0], g_tx) + dot3(rotate[1], g_ty)
        g_sx, g_sy = dot3(rotate[2], g_tx), dot3(rotate[2], g_ty)
        g_m0 = main * (g[0] - inv * g_sx)
        g_m1 = main * (g[1] - inv * g_sy)
        g_m2 = -main * (at_x * g[0] + at_y * g[1] + inv * g_main - 2.0 * inv * (at_x * g_sx + at_y * g_sy))
        g_basis = [None]
        for k in range(1, 16):
            g_basis.append(at(11 + 3 * k) * g[6] + at(12 + 3 * k) * g[7] + at(13 + 3 * k) * g[8])
        g_dir = basis_pull(*direction, g_basis)
        along = dot3(direction, g_dir)
        for j in range(3):
            g_point[j] = g_point[j] + (
                rotate[0][j] * g_m0 + rotate[1][j] * g_m1 + rotate[2][j] * g_m2
                + (g_dir[j] - direction[j] * along) * length_back
            )
        g_opacity = g_opacity + g[5]
    for i in range(3):
        for j in range(i):
            g_cov[i][j] = g_cov[j][i]

    g_scales = []
    g_spin = [[None] * 3 for _ in range(3)]
    for k in range(3):
        column = [spin[j][k] for j in range(3)]
        turned = [dot3(g_cov[i], column) for i in range(3)]
        g_scales.append(2.0 * squares[k] * dot3(column, turned))
        for i in range(3):
            g_spin[i][k] = 2.0 * squares[k] * turned[i]
    w, x, y, z = quat
    d = g_spin
    g_quat = [
        2.0 * (z * (d[1][0] - d[0][1]) + y * (d[0][2] - d[2][0]) + x * (d[2][1] - d[1][2])),
        2.0 * (y * (d[0][1] + d[1][0]) + z * (d[0][2] + d[2][0]) + w * (d[2][1] - d[1][2]) - 2.0 * x * (d[1][1] + d[2][2])),
        2.0 * (x * (d[0][1] + d[1][0]) + z * (d[1][2] + d[2][1]) + w * (d[0][2] - d[2][0]) - 2.0 * y * (d[0][0] + d[2][2])),
        2.0 * (x * (d[0][2] + d[2][0]) + y * (d[1][2] + d[2][1]) + w * (d[1][0] - d[0][1]) - 2.0 * z * (d[0][0] + d[1][1])),
    ]
    along = w * g_quat[0] + x * g_quat[1] + y * g_quat[2] + z * g_quat[3]
    g_rots = [(g_quat[k] - quat[k] * along) * quat_back for k in range(4)]
    opacity = 1.0 / (1.0 + jnp.exp(-at(10)))
    opac[...] = g_opacity * opacity * (1.0 - opacity)
    for k, value in enumerate(g_point + g_scales + g_rots):
        total[k * rows : (k + 1) * rows, :] = value
    base = 0
    for ref in (pos, scales, rots):
        count = ref.shape[0]
        for i in range(rows):
            ref[:, i * LANES : (i + 1) * LANES] = total[pl.ds(base * rows + i, count, stride=rows), :]
        base += count
    copy.wait()


def vmem(count):
    return [pl.BlockSpec(memory_space=pltpu.VMEM)] * count


def call(kernel, outs, operands, in_specs=None, scratch=(), flops=1_000_000, out_specs=None):
    return pl.pallas_call(
        kernel,
        out_shape=outs,
        in_specs=in_specs or vmem(len(operands)),
        out_specs=out_specs or jax.tree.map(lambda _: pl.BlockSpec(memory_space=pltpu.VMEM), outs),
        scratch_shapes=list(scratch),
        compiler_params=pltpu.CompilerParams(vmem_limit_bytes=32 << 20),
        cost_estimate=pl.CostEstimate(flops=flops, bytes_accessed=1 << 20, transcendentals=0),
    )(*operands)


def body(
    cams,
    tiles,
    positions,
    log_scales,
    rotations,
    opacities,
    colors,
    cameras,
    targets,
    tile_ids,
    tile_counts,
    tile_lists,
    fetch_ids,
):
    axes = ("cam", "tile")
    passes, cap = fetch_ids.shape[0], fetch_ids.shape[-1]
    entries, pixels = tile_lists.shape[-1], targets.shape[-1]
    columns = positions.shape[-1]
    rows = columns // LANES
    owners = cams * tiles
    views = passes * cams
    aligned = tiles == rows == 8

    def shaped(*shape):
        return jax.ShapeDtypeStruct(shape, F32)

    def exchange(x):
        lines = x.reshape(owners, 1, -1)
        return lax.all_to_all(lines, axes, split_axis=0, concat_axis=0, tiled=True).reshape(x.shape)

    whole, smem, far = [pl.BlockSpec(memory_space=space) for space in (pltpu.VMEM, pltpu.SMEM, pltpu.HBM)]
    near = [
        positions,
        log_scales,
        rotations,
        opacities.reshape(rows, LANES),
        colors,
        cameras,
        tile_lists,
        targets.reshape(passes, 3, 1, pixels),
        tile_counts.reshape(1, passes),
        tile_ids.reshape(1, passes),
    ]
    wanted_ids = call(
        functools.partial(ids_kernel, passes, cams, cap),
        jax.ShapeDtypeStruct((owners, LANES), jnp.int32),
        [pltpu.with_memory_space_constraint(fetch_ids, pltpu.HBM)],
        in_specs=[far],
        out_specs=far,
        scratch=[
            pltpu.VMEM(fetch_ids.shape, jnp.int32),
            pltpu.VMEM((owners, LANES), jnp.int32),
            pltpu.SemaphoreType.DMA,
        ],
    )
    arrived = exchange(wanted_ids)
    records, raw, table, kept, scene, source, lists = call(
        functools.partial(project_kernel, passes, cams, rows, owners, cap),
        [
            shaped(views * FIELDS * rows, LANES),
            shaped(RAW * rows, LANES),
            shaped(TERMS * views, LANES),
            shaped(views * KEPT * rows, LANES),
            shaped(passes * SCENE, entries),
            jax.ShapeDtypeStruct((owners, LANES), jnp.int32),
            jax.ShapeDtypeStruct((passes, entries), jnp.int32),
        ],
        [pltpu.with_memory_space_constraint(x, pltpu.HBM) for x in near],
        in_specs=[far] * len(near),
        scratch=[pltpu.VMEM(x.shape, x.dtype) for x in near] + [pltpu.SemaphoreType.DMA((len(near),))],
    )
    packets, inverse = call(
        functools.partial(pick_kernel, passes, cams, tiles, rows, cap, aligned),
        [shaped(owners * SENT, LANES), jax.ShapeDtypeStruct((views * rows, LANES), jnp.int32)],
        [arrived, records],
    )
    fetched = exchange(packets)
    slot_grads = call(
        functools.partial(render_kernel, passes, owners, cap, entries, pixels),
        shaped(owners * SENT, LANES),
        [fetched, lists, scene, source],
        scratch=[pltpu.VMEM((pixels, entries), kind) for kind in (F32, F32, F32, BF16, BF16) for _ in range(passes)],
    )
    coming = exchange(slot_grads)
    g_pos, g_scales, g_rots, g_opac, g_cols = call(
        functools.partial(pull_kernel, passes, cams, tiles, rows, cap, aligned),
        [shaped(3, columns), shaped(3, columns), shaped(4, columns), shaped(rows, LANES), shaped(*colors.shape)],
        [coming, inverse, raw, table, kept],
        out_specs=[whole] * 4 + [far],
        scratch=[pltpu.VMEM((RAW * rows, LANES), F32), pltpu.VMEM(colors.shape, F32), pltpu.SemaphoreType.DMA],
    )
    return (g_pos, g_scales, g_rots, g_opac.reshape(columns), g_cols)


def solution(mesh):
    return jax.shard_map(
        functools.partial(body, mesh.shape["cam"], mesh.shape["tile"]),
        mesh=mesh,
        in_specs=(
            P(None, ("cam", "tile")),
            P(None, ("cam", "tile")),
            P(None, ("cam", "tile")),
            P(("cam", "tile")),
            P(None, ("cam", "tile")),
            P(),
            P(None, "cam", "tile", None, None),
            P(None, "cam", "tile"),
            P(None, "cam", "tile"),
            P(None, "cam", "tile", None),
            P(None, "cam", "tile", None, None, None),
        ),
        out_specs=(
            P(None, ("cam", "tile")),
            P(None, ("cam", "tile")),
            P(None, ("cam", "tile")),
            P(("cam", "tile")),
            P(None, ("cam", "tile")),
        ),
        check_vma=False,
    )
```

```python
import functools

import jax
import jax.numpy as jnp
from jax import lax
from jax.experimental import pallas as pl
from jax.experimental.pallas import tpu as pltpu
from jax.sharding import PartitionSpec as P

FOCAL = 4096.0
CENTER_X = 2048.0
CENTER_Y = 1024.0
SH_ZERO = 0.28209479177387814
SH_ONE = 0.4886025119029199
SH_TWO = [
    1.0925484305920792,
    -1.0925484305920792,
    0.31539156525252005,
    -1.0925484305920792,
    0.5462742152960396,
]
SH_THREE = [
    -0.5900435899266435,
    2.890611442640554,
    -0.4570457994644658,
    0.3731763325901154,
    -0.4570457994644658,
    1.445305721320277,
    -0.5900435899266435,
]
LANES = 128
HALF = LANES // 2
FIELDS = 9
SENT = 5
GROUP = 8
RAW = 59
KEPT = 38
SCENE = 6
TERMS = 15
F32 = jnp.float32
BF16 = jnp.bfloat16


def dot(left, right, contract):
    return lax.dot_general(left, right, ((contract[0], contract[1]), ((), ())), preferred_element_type=F32)


def split(x):
    high = x.astype(BF16)
    return high, (x - high.astype(F32)).astype(BF16)


def parted(x):
    return x & (LANES - 1), lax.shift_right_arithmetic(x, LANES.bit_length() - 1)


def lane_pick(source, index):
    return jnp.take_along_axis(source, index, axis=1, mode="promise_in_bounds")


def row_pick(source, index):
    return jnp.take_along_axis(source, index, axis=0, mode="promise_in_bounds")


def spin_of(quat):
    norm = jnp.sqrt(quat[0] * quat[0] + quat[1] * quat[1] + quat[2] * quat[2] + quat[3] * quat[3])
    back = 1.0 / norm
    w, x, y, z = [q * back for q in quat]
    spin = [
        [1.0 - 2.0 * (y * y + z * z), 2.0 * (x * y - w * z), 2.0 * (x * z + w * y)],
        [2.0 * (x * y + w * z), 1.0 - 2.0 * (x * x + z * z), 2.0 * (y * z - w * x)],
        [2.0 * (x * z - w * y), 2.0 * (y * z + w * x), 1.0 - 2.0 * (x * x + y * y)],
    ]
    return spin, (w, x, y, z), back


def world_cov(spin, squares):
    scaled = [[spin[i][k] * squares[k] for k in range(3)] for i in range(3)]
    cov = [[None] * 3 for _ in range(3)]
    for i in range(3):
        for j in range(i, 3):
            cov[i][j] = scaled[i][0] * spin[j][0] + scaled[i][1] * spin[j][1] + scaled[i][2] * spin[j][2]
            cov[j][i] = cov[i][j]
    return cov


def dot3(a, b):
    return a[0] * b[0] + a[1] * b[1] + a[2] * b[2]


def screen_of(point, cov, rotate, offset):
    m = [dot3(rotate[i], point) + offset[i] for i in range(3)]
    inverse = 1.0 / m[2]
    main = FOCAL * inverse
    at_x, at_y = m[0] * inverse, m[1] * inverse
    side_x, side_y = -main * at_x, -main * at_y
    t_x = [main * rotate[0][i] + side_x * rotate[2][i] for i in range(3)]
    t_y = [main * rotate[1][i] + side_y * rotate[2][i] for i in range(3)]
    w_x = [dot3(cov[i], t_x) for i in range(3)]
    w_y = [dot3(cov[i], t_y) for i in range(3)]
    s_xx = dot3(t_x, w_x) + 0.3
    s_xy = dot3(t_y, w_x)
    s_yy = dot3(t_y, w_y) + 0.3
    back = 1.0 / (s_xx * s_yy - s_xy * s_xy)
    conic = (s_yy * back, -s_xy * back, s_xx * back)
    return m, inverse, main, at_x, at_y, t_x, t_y, w_x, w_y, conic


def direction_of(point, center):
    toward = [point[j] - center[j] for j in range(3)]
    back = lax.rsqrt(dot3(toward, toward))
    return [t * back for t in toward], back


def basis_of(x, y, z):
    xx, yy, zz = x * x, y * y, z * z
    xy, yz, xz = x * y, y * z, x * z
    less = xx - yy
    four = 4.0 * zz - xx - yy
    return [
        None,
        -SH_ONE * y,
        SH_ONE * z,
        -SH_ONE * x,
        SH_TWO[0] * xy,
        SH_TWO[1] * yz,
        SH_TWO[2] * (2.0 * zz - xx - yy),
        SH_TWO[3] * xz,
        SH_TWO[4] * less,
        SH_THREE[0] * y * (3.0 * xx - yy),
        SH_THREE[1] * xy * z,
        SH_THREE[2] * y * four,
        SH_THREE[3] * z * (2.0 * zz - 3.0 * xx - 3.0 * yy),
        SH_THREE[4] * x * four,
        SH_THREE[5] * z * less,
        SH_THREE[6] * x * (xx - 3.0 * yy),
    ]


def basis_pull(x, y, z, g):
    xx, yy, zz = x * x, y * y, z * z
    xy, yz, xz = x * y, y * z, x * z
    less = xx - yy
    four = 4.0 * zz - xx - yy
    g4, g5, g6, g7, g8 = [SH_TWO[i] * g[4 + i] for i in range(5)]
    h = [SH_THREE[i] * g[9 + i] for i in range(7)]
    g_x = (
        -SH_ONE * g[3] + g4 * y - 2.0 * g6 * x + g7 * z + 2.0 * g8 * x
        + 6.0 * h[0] * xy + h[1] * yz - 2.0 * h[2] * xy - 6.0 * h[3] * xz
        + h[4] * (four - 2.0 * xx) + 2.0 * h[5] * xz + 3.0 * h[6] * less
    )
    g_y = (
        -SH_ONE * g[1] + g4 * x + g5 * z - 2.0 * g6 * y - 2.0 * g8 * y
        + 3.0 * h[0] * less + h[1] * xz + h[2] * (four - 2.0 * yy) - 6.0 * h[3] * yz
        - 2.0 * h[4] * xy - 2.0 * h[5] * yz - 6.0 * h[6] * xy
    )
    g_z = (
        SH_ONE * g[2] + g5 * y + 4.0 * g6 * z + g7 * x
        + h[1] * xy + 8.0 * h[2] * yz + h[3] * (6.0 * zz - 3.0 * xx - 3.0 * yy)
        + 8.0 * h[4] * xz + h[5] * less
    )
    return [g_x, g_y, g_z]


def camera_rows(cam_ref, table, passes, cams):
    views = passes * cams
    for p in range(passes):
        cam = cam_ref[p]
        cos, sin = jnp.cos(cam), jnp.sin(cam)
        ca, cb, cg = [cos[:, k : k + 1] for k in range(3)]
        sa, sb, sg = [sin[:, k : k + 1] for k in range(3)]
        rotate = [
            [cg * cb, cg * sb * sa - sg * ca, cg * sb * ca + sg * sa],
            [sg * cb, sg * sb * sa + cg * ca, sg * sb * ca - cg * sa],
            [-sb, cb * sa, cb * ca],
        ]
        offset = [cam[:, 3:4], cam[:, 4:5], 6.0 + cam[:, 5:6]]
        center = [-(rotate[0][j] * offset[0] + rotate[1][j] * offset[1] + rotate[2][j] * offset[2]) for j in range(3)]
        for k, term in enumerate(rotate[0] + rotate[1] + rotate[2] + offset + center):
            table[k * views + p * cams : k * views + (p + 1) * cams, :] = jnp.broadcast_to(term, (cams, LANES))


def camera_of(table, view, views, shape):
    terms = [jnp.broadcast_to(table[k * views + view : k * views + view + 1, :], shape) for k in range(TERMS)]
    return [terms[0:3], terms[3:6], terms[6:9]], terms[9:12], terms[12:15]


def project_kernel(
    passes, cams, rows, owners, cap, far_pos, far_scales, far_rots, far_opac, far_cols, far_cam, far_lists, far_wanted,
    far_counts, far_places, rec, raw, table, kept, scene, source, chosen,
    pos, scales, rots, opac, cols, cam, lists, wanted, counts, places, done,
):
    views = passes * cams
    shape = (rows, LANES)
    fars = (far_cam, far_pos, far_scales, far_rots, far_opac, far_lists, far_wanted, far_counts, far_places, far_cols)
    nears = (cam, pos, scales, rots, opac, lists, wanted, counts, places, cols)
    copies = [pltpu.make_async_copy(a, b, done.at[k]) for k, (a, b) in enumerate(zip(fars, nears))]
    for copy in copies:
        copy.start()
    for copy in copies[:-1]:
        copy.wait()
    camera_rows(cam, table, passes, cams)
    base = 0
    for ref in (pos, scales, rots):
        count = ref.shape[0]
        for i in range(rows):
            raw[pl.ds(base * rows + i, count, stride=rows), :] = ref[:, i * LANES : (i + 1) * LANES]
        base += count
    raw[base * rows : (base + 1) * rows, :] = opac[...]

    def at(k):
        return raw[k * rows : (k + 1) * rows, :]

    def put(ref, k, value):
        ref[k * rows : (k + 1) * rows, :] = value

    point = [at(k) for k in range(3)]
    squares = [jnp.exp(2.0 * at(3 + k)) for k in range(3)]
    spin, _, _ = spin_of([at(6 + k) for k in range(4)])
    cov = world_cov(spin, squares)
    opacity = 1.0 / (1.0 + jnp.exp(-at(10)))
    for view in range(views):
        rotate, offset, center = camera_of(table, view, views, shape)
        _, inv, main, at_x, at_y, t_x, t_y, w_x, w_y, conic = screen_of(point, cov, rotate, offset)
        direction, back = direction_of(point, center)
        basis = basis_of(*direction)
        fields = [FOCAL * at_x + CENTER_X, FOCAL * at_y + CENTER_Y, conic[0], conic[1], conic[2], opacity]
        for f, value in enumerate(fields):
            put(rec, view * FIELDS + f, value)
        for k, value in enumerate([inv, main, at_x, at_y, *t_x, *t_y, *w_x, *w_y, *conic, *direction, back, *basis[1:]]):
            put(kept, view * KEPT + k, value)

    entries, pixels = lists.shape[-1], wanted.shape[-1]
    entry_row = lax.broadcasted_iota(jnp.int32, (1, entries), 1)
    for p in range(passes):
        for k in range(3):
            scene[p * SCENE + k : p * SCENE + k + 1, :] = wanted[p, k]
        count = jnp.broadcast_to(counts[:, p : p + 1], (1, entries))
        scene[p * SCENE + 3 : p * SCENE + 4, :] = jnp.where(entry_row < count, 1.0, 0.0)
        place = jnp.broadcast_to(places[:, p : p + 1], (1, entries))
        for k, value in enumerate((place % 256 * 16 + 8, place // 256 * 16 + 8)):
            scene[p * SCENE + 4 + k : p * SCENE + 5 + k, :] = value.astype(F32)
        chosen[p : p + 1, :] = lists[p, 0] // cap
        chosen[passes + p : passes + p + 1, :] = lists[p, 0] % cap + p * cap
    pair = (LANES, LANES)
    turned = lax.broadcasted_iota(jnp.int32, pair, 0)
    turned_p, turned_j = turned % HALF // cap, turned % cap
    entry = (lax.broadcasted_iota(jnp.int32, pair, 1) + 1).astype(F32)
    owner_row = lax.broadcasted_iota(jnp.int32, (owners, LANES), 0)
    halves = entries // LANES
    found = jnp.full((owners, LANES), -LANES, jnp.int32)
    for p in range(passes):
        for h in range(halves):
            slot = lists[p, 0, :, h * LANES : (h + 1) * LANES]
            mine = jnp.where(jnp.broadcast_to(slot // cap, (owners, LANES)) == owner_row, 1.0, 0.0).astype(BF16)
            here = jnp.where(
                (jnp.broadcast_to(slot % cap, pair) == turned_j) & (turned_p == p), entry, 0.0
            ).astype(BF16)
            hit = dot(mine, here, ((1,), (1,)))
            found = jnp.where(hit > 0.5, hit.astype(jnp.int32) + ((p * halves + h) * LANES - 1), found)
    source[...] = found

    copies[-1].wait()
    for i in range(rows):
        raw[pl.ds(11 * rows + i, cols.shape[0], stride=rows), :] = cols[:, i * LANES : (i + 1) * LANES]
    for channel in range(3):
        totals = [0.5 + SH_ZERO * at(11 + channel)] * views
        for k in range(1, 16):
            color = at(11 + 3 * k + channel)
            for view in range(views):
                start = (view * KEPT + KEPT - 16 + k) * rows
                totals[view] = totals[view] + kept[start : start + rows, :] * color
        for view in range(views):
            put(rec, view * FIELDS + 6 + channel, totals[view])


def lane_pass(shape, cap):
    lane = lax.broadcasted_iota(jnp.int32, shape, 1) % HALF
    return lane // cap, lane % cap


def ids_kernel(passes, cams, cap, ids, out, landed, lines, done):
    copy = pltpu.make_async_copy(ids, landed, done)
    copy.start()
    copy.wait()
    for c in range(cams):
        parts = [landed[p, 0, 0, c] for p in range(passes)]
        tiles = parts[0].shape[0]
        if passes * cap < HALF:
            parts.append(jnp.zeros((tiles, HALF - passes * cap), jnp.int32))
        lines[c * tiles : (c + 1) * tiles, :] = jnp.concatenate(parts + parts, axis=1)
    copy = pltpu.make_async_copy(lines, out, done)
    copy.start()
    copy.wait()


def pick_kernel(passes, cams, tiles, rows, cap, aligned, ids, rec, out, inverse):
    shape = (GROUP, LANES)
    lane = lax.broadcasted_iota(jnp.int32, shape, 1)
    lane_p, _ = lane_pass(shape, cap)

    def packets(first, c):
        low, high = parted(ids[pl.ds(first, GROUP), :])
        if aligned:
            blocks = [jnp.broadcast_to(high[:, p * cap : p * cap + 1], shape) for p in range(passes)]

        def pick(f):
            found = jnp.zeros(shape, F32)
            for p in range(passes):
                start = ((p * cams + c) * FIELDS + f) * rows
                if aligned:
                    own = lane_pick(row_pick(rec[start : start + rows, :], blocks[p]), low)
                else:
                    own = jnp.zeros(shape, F32)
                    for b in range(rows):
                        line = jnp.broadcast_to(rec[start + b : start + b + 1, :], shape)
                        own = jnp.where(high == b, lane_pick(line, low), own)
                found = own if p == 0 else jnp.where(lane_p == p, own, found)
            return found

        for r in range(SENT):
            value = pick(2 * r)
            if 2 * r + 1 < FIELDS:
                value = jnp.where(lane < HALF, value, pick(2 * r + 1))
            out[pl.ds(first * SENT + r, GROUP, stride=SENT), :] = value

    for c in range(cams):
        if tiles == GROUP:
            packets(c * tiles, c)
        else:

            def step(k, carry, c=c):
                packets(pl.multiple_of(c * tiles + k * GROUP, GROUP), c)
                return carry

            lax.fori_loop(0, tiles // GROUP, step, 0)

    square = (LANES, LANES)
    column = lax.broadcasted_iota(jnp.int32, square, 0)
    turn = lax.broadcasted_iota(jnp.int32, square, 1)
    place = (turn % HALF + 1 + turn // HALF * LANES).astype(F32)
    wide = (passes * rows, LANES)
    wide_lane = lax.broadcasted_iota(jnp.int32, wide, 1)
    key = lax.broadcasted_iota(jnp.int32, wide, 0)
    lane_key = jnp.where(wide_lane % HALF < passes * cap, lane_pass(wide, cap)[0] * rows, -(1 << 20))
    line_lane = lax.broadcasted_iota(jnp.int32, (1, LANES), 1)

    def two(c, t, found):
        low, high = parted(
            jnp.where(line_lane < HALF, ids[pl.ds(c * tiles + t, 1), :], ids[pl.ds(c * tiles + t + 1, 1), :])
        )
        low = jnp.broadcast_to(low, square)
        high = jnp.broadcast_to(high, wide)
        match = jnp.where(low == column, place, 0.0).astype(BF16)
        owner = jnp.where(high + lane_key == key, 1.0, 0.0).astype(BF16)
        hit = dot(owner, match, ((1,), (1,)))
        return jnp.where(hit > 0.5, hit.astype(jnp.int32) + t * LANES, found)

    for c in range(cams):
        found = jnp.zeros(wide, jnp.int32)
        if tiles <= 8:
            for t in range(0, tiles, 2):
                found = two(c, t, found)
        else:
            found = lax.fori_loop(0, tiles // 2, lambda t, f, c=c: two(c, 2 * t, f), found)
        for p in range(passes):
            start = (p * cams + c) * rows
            inverse[start : start + rows, :] = found[p * rows : (p + 1) * rows, :]


def render_kernel(passes, owners, cap, entries, pixels, got, lists, scene, source, out, *scratch):
    alphas, ratios, sums, high, low = [scratch[k * passes : (k + 1) * passes] for k in range(5)]
    halves = entries // LANES
    shape = (GROUP, LANES)
    wide = 16
    lane = lax.broadcasted_iota(jnp.int32, shape, 1)
    sub = lax.broadcasted_iota(jnp.int32, shape, 0)

    slot_owner, slot_lane = [], []
    for p in range(passes):
        for h in range(halves):
            part = slice(h * LANES, (h + 1) * LANES)
            slot_owner.append(jnp.broadcast_to(lists[p : p + 1, part], shape))
            slot_lane.append(jnp.broadcast_to(lists[passes + p : passes + p + 1, part], shape))
    total = passes * halves

    def gather(g, found):
        mine = [slot_owner[i] == g * GROUP + sub for i in range(total)]
        new = []
        for f in range(FIELDS):
            lines = got[pl.ds(g * (GROUP * SENT) + f // 2, GROUP, stride=SENT), :]
            for i in range(total):
                new.append(jnp.where(mine[i], lane_pick(lines, slot_lane[i] + f % 2 * HALF), found[f * total + i]))
        return tuple(new)

    fields = tuple(jnp.zeros(shape, F32) for _ in range(FIELDS * total))
    if owners <= 32:
        for g in range(owners // GROUP):
            fields = gather(g, fields)
    else:
        fields = lax.fori_loop(0, owners // GROUP, gather, fields)
    fields = [jnp.sum(x, axis=0, keepdims=True) for x in fields]

    square = (entries, entries)
    row_at, column_at = lax.broadcasted_iota(jnp.int32, square, 0), lax.broadcasted_iota(jnp.int32, square, 1)
    before = jnp.where(row_at < column_at, 1.0, 0.0).astype(BF16)
    after = jnp.where(row_at > column_at, 1.0, 0.0).astype(BF16)
    column_x = lax.broadcasted_iota(jnp.int32, (wide, entries), 0).astype(F32) - 7.5
    steps = [slice(y * wide, (y + 1) * wide) for y in range(pixels // wide)]

    lines, spans = [], []
    for p in range(passes):
        line = [
            jnp.concatenate([fields[f * total + p * halves + h] for h in range(halves)], axis=1) for f in range(FIELDS)
        ]
        line[0] = line[0] - scene[p * SCENE + 4 : p * SCENE + 5, :]
        line[1] = line[1] - scene[p * SCENE + 5 : p * SCENE + 6, :]
        lines.append(line)
        spans.append(column_x - line[0])

    def offset_y(p, y):
        return (y - 7.5) - lines[p][1]

    for p in range(passes):
        _, _, c_a, c_b, c_c, base = lines[p][:6]
        live = base * scene[p * SCENE + 3 : p * SCENE + 4, :]
        d_x = spans[p]
        q_xx = (-0.5 * c_a) * d_x * d_x
        q_x = -c_b * d_x
        for y, at in enumerate(steps):
            d_y = offset_y(p, y)
            alpha = live * jnp.exp(q_xx + (q_x * d_y - 0.5 * c_c * d_y * d_y))
            clear = jnp.log(1.0 - alpha)
            alphas[p][at, :] = alpha
            ratios[p][at, :] = alpha * jnp.exp(-clear)
            high[p][at, :], low[p][at, :] = split(clear)
    for p in range(passes):
        sums[p][...] = dot(high[p][...], before, ((1,), (0,))) + dot(low[p][...], before, ((1,), (0,)))
    for p in range(passes):
        for at in steps:
            weight = alphas[p][at, :] * jnp.exp(sums[p][at, :])
            alphas[p][at, :] = weight
            high[p][at, :], low[p][at, :] = split(weight)
    residuals, pair_rows = [], []
    for p in range(passes):
        c_high, c_low = split(jnp.concatenate(lines[p][6:9], axis=0))
        both = dot(jnp.concatenate([c_high, c_low], axis=0), high[p][...], ((1,), (1,)))
        shown = both[0:3, :] + both[3:6, :] + dot(c_high, low[p][...], ((1,), (1,)))
        residuals.append(split(shown - scene[p * SCENE : p * SCENE + 3, :]))
        pair_rows.append(jnp.concatenate([c_high, c_low, c_high], axis=0))
    color_grads = []
    for p in range(passes):
        r_high, r_low = residuals[p]
        sums[p][...] = dot(jnp.concatenate([r_high, r_high, r_low], axis=0), pair_rows[p], ((0,), (0,)))
        both = dot(jnp.concatenate([r_high, r_low], axis=0), high[p][...], ((1,), (0,)))
        color_grads.append(both[0:3, :] + both[3:6, :] + dot(r_high, low[p][...], ((1,), (0,))))
    for p in range(passes):
        for at in steps:
            pulled = alphas[p][at, :] * sums[p][at, :]
            alphas[p][at, :] = pulled
            high[p][at, :], low[p][at, :] = split(pulled)
    for p in range(passes):
        sums[p][...] = dot(high[p][...], after, ((1,), (0,))) + dot(low[p][...], after, ((1,), (0,)))
    grads = []
    for p in range(passes):
        m_1 = m_y = m_yy = jnp.zeros((wide, entries), F32)
        for y, at in enumerate(steps):
            grad = alphas[p][at, :] - ratios[p][at, :] * sums[p][at, :]
            d_y = offset_y(p, y)
            grad_y = grad * d_y
            m_1, m_y, m_yy = m_1 + grad, m_y + grad_y, m_yy + grad_y * d_y
        d_x = spans[p]
        m_x = m_1 * d_x
        s_1, s_x, s_y, s_xx, s_xy, s_yy = [
            jnp.sum(m, axis=0, keepdims=True) for m in (m_1, m_x, m_y, m_x * d_x, m_y * d_x, m_yy)
        ]
        _, _, c_a, c_b, c_c, base = lines[p][:6]
        grads.append(
            [
                c_a * s_x + c_b * s_y,
                c_b * s_x + c_c * s_y,
                -0.5 * s_xx,
                -s_xy,
                -0.5 * s_yy,
                s_1 / base,
                color_grads[p][0:1, :],
                color_grads[p][1:2, :],
                color_grads[p][2:3, :],
            ]
        )

    def packets(first, origin):
        index, which = parted(origin)

        def pick(f):
            found = jnp.zeros(shape, F32)
            for p in range(passes):
                for h in range(halves):
                    line = jnp.broadcast_to(grads[p][f][:, h * LANES : (h + 1) * LANES], shape)
                    found = jnp.where(which == p * halves + h, lane_pick(line, index), found)
            return found

        for r in range(SENT):
            value = pick(2 * r)
            if 2 * r + 1 < FIELDS:
                value = jnp.where(lane < HALF, value, pick(2 * r + 1))
            out[pl.ds(first * SENT + r, GROUP, stride=SENT), :] = value

    for g in range(owners // GROUP):
        packets(g * GROUP, source[g * GROUP : (g + 1) * GROUP, :])


def pull_kernel(
    passes, cams, tiles, rows, cap, aligned, got, inverse, raw, table, kept,
    far_pos, far_scales, far_rots, far_opac, far_cols, total, pos, scales, rots, opac, cols, done,
):
    views = passes * cams
    shape = (rows, LANES)

    def at(k):
        return raw[k * rows : (k + 1) * rows, :]

    def fetcher(view):
        p, c = view // cams, view % cams
        slot = inverse[view * rows : (view + 1) * rows, :] - 1
        valid = slot >= 0
        slot_lane, slot_t = parted(jnp.maximum(slot, 0))
        if aligned:
            row_t = jnp.broadcast_to(jnp.max(slot_t, axis=1, keepdims=True), shape)
        turned = {}

        def fetch(f):
            row, shift = f // 2, f % 2 * HALF
            if aligned:
                if row not in turned:
                    turned[row] = row_pick(got[pl.ds(c * tiles * SENT + row, tiles, stride=SENT), :], row_t)
                return jnp.where(valid, lane_pick(turned[row], slot_lane + shift), 0.0)

            def one(t, found):
                line = jnp.broadcast_to(got[pl.ds((c * tiles + t) * SENT + row, 1), :], shape)
                return jnp.where(valid & (slot_t == t), lane_pick(line, slot_lane + shift), found)

            return lax.fori_loop(0, tiles, one, jnp.zeros(shape, F32))

        return fetch

    def held(view, k):
        start = (view * KEPT + k) * rows
        return kept[start : start + rows, :]

    fetchers = [fetcher(view) for view in range(views)]
    shades = [[fetchers[view](6 + channel) for view in range(views)] for channel in range(3)]
    copies = []

    def send(near, away):
        copies.append(pltpu.make_async_copy(near, away, done.at[len(copies)]))
        copies[-1].start()

    sent = 0
    for k in range(16):
        basis = [held(view, KEPT - 16 + k) for view in range(views)] if k else None
        for channel in range(3):
            terms = shades[channel] if k == 0 else [basis[view] * shades[channel][view] for view in range(views)]
            while len(terms) > 1:
                terms = [sum(terms[n : n + 2][1:], terms[n]) for n in range(0, len(terms), 2)]
            start = (11 + 3 * k + channel) * rows
            total[start : start + rows, :] = terms[0] if k else SH_ZERO * terms[0]
        ready = (3 * k + 3) // 16 * 16
        if ready > sent:
            for i in range(rows):
                cols[sent:ready, i * LANES : (i + 1) * LANES] = total[pl.ds((11 + sent) * rows + i, ready - sent, stride=rows), :]
            send(cols.at[pl.ds(sent, ready - sent), :], far_cols.at[pl.ds(sent, ready - sent), :])
            sent = ready

    point = [at(k) for k in range(3)]
    squares = [jnp.exp(2.0 * at(3 + k)) for k in range(3)]
    spin, quat, quat_back = spin_of([at(6 + k) for k in range(4)])

    g_point = [jnp.zeros(shape, F32) for _ in range(3)]
    g_cov = [[jnp.zeros(shape, F32) for _ in range(3)] for _ in range(3)]
    g_opacity = jnp.zeros(shape, F32)
    for view in range(views):
        g = [fetchers[view](f) for f in range(6)] + [shades[channel][view] for channel in range(3)]
        rotate, _, _ = camera_of(table, view, views, shape)
        inv, main, at_x, at_y = [held(view, k) for k in range(4)]
        t_x, t_y, w_x, w_y, conic, direction = [[held(view, 4 + 3 * n + k) for k in range(3)] for n in range(6)]
        length_back = held(view, 22)
        c_a, c_b, c_c = conic
        half = 0.5 * g[3]
        p00, p01 = g[2] * c_a + half * c_b, g[2] * c_b + half * c_c
        p10, p11 = half * c_a + g[4] * c_b, half * c_b + g[4] * c_c
        g_xx = -(c_a * p00 + c_b * p10)
        g_xy = -(c_a * p01 + c_b * p11)
        g_yy = -(c_b * p01 + c_c * p11)
        left = [g_xx * t_x[i] + g_xy * t_y[i] for i in range(3)]
        right = [g_yy * t_y[i] + g_xy * t_x[i] for i in range(3)]
        for i in range(3):
            for j in range(i, 3):
                g_cov[i][j] = g_cov[i][j] + (t_x[i] * left[j] + t_y[i] * right[j])
        g_tx = [2.0 * (g_xx * w_x[i] + g_xy * w_y[i]) for i in range(3)]
        g_ty = [2.0 * (g_yy * w_y[i] + g_xy * w_x[i]) for i in range(3)]
        g_main = dot3(rotate[0], g_tx) + dot3(rotate[1], g_ty)
        g_sx, g_sy = dot3(rotate[2], g_tx), dot3(rotate[2], g_ty)
        g_m0 = main * (g[0] - inv * g_sx)
        g_m1 = main * (g[1] - inv * g_sy)
        g_m2 = -main * (at_x * g[0] + at_y * g[1] + inv * g_main - 2.0 * inv * (at_x * g_sx + at_y * g_sy))
        g_basis = [None]
        for k in range(1, 16):
            g_basis.append(at(11 + 3 * k) * g[6] + at(12 + 3 * k) * g[7] + at(13 + 3 * k) * g[8])
        g_dir = basis_pull(*direction, g_basis)
        along = dot3(direction, g_dir)
        for j in range(3):
            g_point[j] = g_point[j] + (
                rotate[0][j] * g_m0 + rotate[1][j] * g_m1 + rotate[2][j] * g_m2
                + (g_dir[j] - direction[j] * along) * length_back
            )
        g_opacity = g_opacity + g[5]
    for i in range(3):
        for j in range(i):
            g_cov[i][j] = g_cov[j][i]

    g_scales = []
    g_spin = [[None] * 3 for _ in range(3)]
    for k in range(3):
        column = [spin[j][k] for j in range(3)]
        turned = [dot3(g_cov[i], column) for i in range(3)]
        g_scales.append(2.0 * squares[k] * dot3(column, turned))
        for i in range(3):
            g_spin[i][k] = 2.0 * squares[k] * turned[i]
    w, x, y, z = quat
    d = g_spin
    g_quat = [
        2.0 * (z * (d[1][0] - d[0][1]) + y * (d[0][2] - d[2][0]) + x * (d[2][1] - d[1][2])),
        2.0 * (y * (d[0][1] + d[1][0]) + z * (d[0][2] + d[2][0]) + w * (d[2][1] - d[1][2]) - 2.0 * x * (d[1][1] + d[2][2])),
        2.0 * (x * (d[0][1] + d[1][0]) + z * (d[1][2] + d[2][1]) + w * (d[0][2] - d[2][0]) - 2.0 * y * (d[0][0] + d[2][2])),
        2.0 * (x * (d[0][2] + d[2][0]) + y * (d[1][2] + d[2][1]) + w * (d[1][0] - d[0][1]) - 2.0 * z * (d[0][0] + d[1][1])),
    ]
    along = w * g_quat[0] + x * g_quat[1] + y * g_quat[2] + z * g_quat[3]
    g_rots = [(g_quat[k] - quat[k] * along) * quat_back for k in range(4)]
    opacity = 1.0 / (1.0 + jnp.exp(-at(10)))
    opac[...] = g_opacity * opacity * (1.0 - opacity)
    for k, value in enumerate(g_point + g_scales + g_rots):
        total[k * rows : (k + 1) * rows, :] = value
    base = 0
    for ref in (pos, scales, rots):
        count = ref.shape[0]
        for i in range(rows):
            ref[:, i * LANES : (i + 1) * LANES] = total[pl.ds(base * rows + i, count, stride=rows), :]
        base += count
    for near, away in ((pos, far_pos), (scales, far_scales), (rots, far_rots), (opac, far_opac)):
        send(near, away)
    for copy in copies:
        copy.wait()


def vmem(count):
    return [pl.BlockSpec(memory_space=pltpu.VMEM)] * count


def call(kernel, outs, operands, in_specs=None, scratch=(), flops=1_000_000, out_specs=None):
    return pl.pallas_call(
        kernel,
        out_shape=outs,
        in_specs=in_specs or vmem(len(operands)),
        out_specs=out_specs or jax.tree.map(lambda _: pl.BlockSpec(memory_space=pltpu.VMEM), outs),
        scratch_shapes=list(scratch),
        compiler_params=pltpu.CompilerParams(vmem_limit_bytes=32 << 20),
        cost_estimate=pl.CostEstimate(flops=flops, bytes_accessed=1 << 20, transcendentals=0),
    )(*operands)


def body(
    cams,
    tiles,
    positions,
    log_scales,
    rotations,
    opacities,
    colors,
    cameras,
    targets,
    tile_ids,
    tile_counts,
    tile_lists,
    fetch_ids,
):
    axes = ("cam", "tile")
    passes, cap = fetch_ids.shape[0], fetch_ids.shape[-1]
    entries, pixels = tile_lists.shape[-1], targets.shape[-1]
    columns = positions.shape[-1]
    rows = columns // LANES
    owners = cams * tiles
    views = passes * cams
    aligned = tiles == rows == 8

    def shaped(*shape):
        return jax.ShapeDtypeStruct(shape, F32)

    def exchange(x):
        lines = x.reshape(owners, 1, -1)
        return lax.all_to_all(lines, axes, split_axis=0, concat_axis=0, tiled=True).reshape(x.shape)

    whole, smem, far = [pl.BlockSpec(memory_space=space) for space in (pltpu.VMEM, pltpu.SMEM, pltpu.HBM)]
    near = [
        positions,
        log_scales,
        rotations,
        opacities.reshape(rows, LANES),
        colors,
        cameras,
        tile_lists,
        targets.reshape(passes, 3, 1, pixels),
        tile_counts.reshape(1, passes),
        tile_ids.reshape(1, passes),
    ]
    wanted_ids = call(
        functools.partial(ids_kernel, passes, cams, cap),
        jax.ShapeDtypeStruct((owners, LANES), jnp.int32),
        [pltpu.with_memory_space_constraint(fetch_ids, pltpu.HBM)],
        in_specs=[far],
        out_specs=far,
        scratch=[
            pltpu.VMEM(fetch_ids.shape, jnp.int32),
            pltpu.VMEM((owners, LANES), jnp.int32),
            pltpu.SemaphoreType.DMA,
        ],
    )
    arrived = exchange(wanted_ids)
    records, raw, table, kept, scene, source, lists = call(
        functools.partial(project_kernel, passes, cams, rows, owners, cap),
        [
            shaped(views * FIELDS * rows, LANES),
            shaped(RAW * rows, LANES),
            shaped(TERMS * views, LANES),
            shaped(views * KEPT * rows, LANES),
            shaped(passes * SCENE, entries),
            jax.ShapeDtypeStruct((owners, LANES), jnp.int32),
            jax.ShapeDtypeStruct((2 * passes, entries), jnp.int32),
        ],
        [pltpu.with_memory_space_constraint(x, pltpu.HBM) for x in near],
        in_specs=[far] * len(near),
        scratch=[pltpu.VMEM(x.shape, x.dtype) for x in near] + [pltpu.SemaphoreType.DMA((len(near),))],
    )
    packets, inverse = call(
        functools.partial(pick_kernel, passes, cams, tiles, rows, cap, aligned),
        [shaped(owners * SENT, LANES), jax.ShapeDtypeStruct((views * rows, LANES), jnp.int32)],
        [arrived, records],
    )
    fetched = exchange(packets)
    slot_grads = call(
        functools.partial(render_kernel, passes, owners, cap, entries, pixels),
        shaped(owners * SENT, LANES),
        [fetched, lists, scene, source],
        scratch=[pltpu.VMEM((pixels, entries), kind) for kind in (F32, F32, F32, BF16, BF16) for _ in range(passes)],
    )
    coming = exchange(slot_grads)
    g_pos, g_scales, g_rots, g_opac, g_cols = call(
        functools.partial(pull_kernel, passes, cams, tiles, rows, cap, aligned),
        [shaped(3, columns), shaped(3, columns), shaped(4, columns), shaped(rows, LANES), shaped(*colors.shape)],
        [coming, inverse, raw, table, kept],
        out_specs=[far] * 5,
        scratch=[pltpu.VMEM((RAW * rows, LANES), F32)]
        + [pltpu.VMEM(x.shape, F32) for x in near[:5]]
        + [pltpu.SemaphoreType.DMA((7,))],
    )
    return (g_pos, g_scales, g_rots, g_opac.reshape(columns), g_cols)


def solution(mesh):
    return jax.shard_map(
        functools.partial(body, mesh.shape["cam"], mesh.shape["tile"]),
        mesh=mesh,
        in_specs=(
            P(None, ("cam", "tile")),
            P(None, ("cam", "tile")),
            P(None, ("cam", "tile")),
            P(("cam", "tile")),
            P(None, ("cam", "tile")),
            P(),
            P(None, "cam", "tile", None, None),
            P(None, "cam", "tile"),
            P(None, "cam", "tile"),
            P(None, "cam", "tile", None),
            P(None, "cam", "tile", None, None, None),
        ),
        out_specs=(
            P(None, ("cam", "tile")),
            P(None, ("cam", "tile")),
            P(None, ("cam", "tile")),
            P(("cam", "tile")),
            P(None, ("cam", "tile")),
        ),
        check_vma=False,
    )
```

```python
import functools

import jax
import jax.numpy as jnp
from jax import lax
from jax.experimental import pallas as pl
from jax.experimental.pallas import tpu as pltpu
from jax.sharding import PartitionSpec as P

FOCAL = 4096.0
CENTER_X = 2048.0
CENTER_Y = 1024.0
SH_ZERO = 0.28209479177387814
SH_ONE = 0.4886025119029199
SH_TWO = [
    1.0925484305920792,
    -1.0925484305920792,
    0.31539156525252005,
    -1.0925484305920792,
    0.5462742152960396,
]
SH_THREE = [
    -0.5900435899266435,
    2.890611442640554,
    -0.4570457994644658,
    0.3731763325901154,
    -0.4570457994644658,
    1.445305721320277,
    -0.5900435899266435,
]
LANES = 128
HALF = LANES // 2
FIELDS = 9
SENT = 5
GROUP = 8
RAW = 59
KEPT = 42
SHADE = 18
SCENE = 6
TERMS = 15
F32 = jnp.float32
BF16 = jnp.bfloat16


def dot(left, right, contract):
    return lax.dot_general(left, right, ((contract[0], contract[1]), ((), ())), preferred_element_type=F32)


def split(x):
    high = x.astype(BF16)
    return high, (x - high.astype(F32)).astype(BF16)


def parted(x):
    return x & (LANES - 1), lax.shift_right_arithmetic(x, LANES.bit_length() - 1)


def lane_pick(source, index):
    return jnp.take_along_axis(source, index, axis=1, mode="promise_in_bounds")


def row_pick(source, index):
    return jnp.take_along_axis(source, index, axis=0, mode="promise_in_bounds")


def spin_of(quat):
    norm = jnp.sqrt(quat[0] * quat[0] + quat[1] * quat[1] + quat[2] * quat[2] + quat[3] * quat[3])
    back = 1.0 / norm
    w, x, y, z = [q * back for q in quat]
    spin = [
        [1.0 - 2.0 * (y * y + z * z), 2.0 * (x * y - w * z), 2.0 * (x * z + w * y)],
        [2.0 * (x * y + w * z), 1.0 - 2.0 * (x * x + z * z), 2.0 * (y * z - w * x)],
        [2.0 * (x * z - w * y), 2.0 * (y * z + w * x), 1.0 - 2.0 * (x * x + y * y)],
    ]
    return spin, (w, x, y, z), back


def world_cov(spin, squares):
    scaled = [[spin[i][k] * squares[k] for k in range(3)] for i in range(3)]
    cov = [[None] * 3 for _ in range(3)]
    for i in range(3):
        for j in range(i, 3):
            cov[i][j] = scaled[i][0] * spin[j][0] + scaled[i][1] * spin[j][1] + scaled[i][2] * spin[j][2]
            cov[j][i] = cov[i][j]
    return cov


def dot3(a, b):
    return a[0] * b[0] + a[1] * b[1] + a[2] * b[2]


def screen_of(point, cov, rotate, offset):
    m = [dot3(rotate[i], point) + offset[i] for i in range(3)]
    inverse = 1.0 / m[2]
    main = FOCAL * inverse
    at_x, at_y = m[0] * inverse, m[1] * inverse
    side_x, side_y = -main * at_x, -main * at_y
    t_x = [main * rotate[0][i] + side_x * rotate[2][i] for i in range(3)]
    t_y = [main * rotate[1][i] + side_y * rotate[2][i] for i in range(3)]
    w_x = [dot3(cov[i], t_x) for i in range(3)]
    w_y = [dot3(cov[i], t_y) for i in range(3)]
    s_xx = dot3(t_x, w_x) + 0.3
    s_xy = dot3(t_y, w_x)
    s_yy = dot3(t_y, w_y) + 0.3
    back = 1.0 / (s_xx * s_yy - s_xy * s_xy)
    conic = (s_yy * back, -s_xy * back, s_xx * back)
    return m, inverse, main, at_x, at_y, t_x, t_y, w_x, w_y, conic


def direction_of(point, center):
    toward = [point[j] - center[j] for j in range(3)]
    back = lax.rsqrt(dot3(toward, toward))
    return [t * back for t in toward], back


def basis_of(x, y, z):
    xx, yy, zz = x * x, y * y, z * z
    xy, yz, xz = x * y, y * z, x * z
    less = xx - yy
    four = 4.0 * zz - xx - yy
    return [
        None,
        -SH_ONE * y,
        SH_ONE * z,
        -SH_ONE * x,
        SH_TWO[0] * xy,
        SH_TWO[1] * yz,
        SH_TWO[2] * (2.0 * zz - xx - yy),
        SH_TWO[3] * xz,
        SH_TWO[4] * less,
        SH_THREE[0] * y * (3.0 * xx - yy),
        SH_THREE[1] * xy * z,
        SH_THREE[2] * y * four,
        SH_THREE[3] * z * (2.0 * zz - 3.0 * xx - 3.0 * yy),
        SH_THREE[4] * x * four,
        SH_THREE[5] * z * less,
        SH_THREE[6] * x * (xx - 3.0 * yy),
    ]


def basis_pull(x, y, z, g):
    xx, yy, zz = x * x, y * y, z * z
    xy, yz, xz = x * y, y * z, x * z
    less = xx - yy
    four = 4.0 * zz - xx - yy
    g4, g5, g6, g7, g8 = [SH_TWO[i] * g[4 + i] for i in range(5)]
    h = [SH_THREE[i] * g[9 + i] for i in range(7)]
    g_x = (
        -SH_ONE * g[3] + g4 * y - 2.0 * g6 * x + g7 * z + 2.0 * g8 * x
        + 6.0 * h[0] * xy + h[1] * yz - 2.0 * h[2] * xy - 6.0 * h[3] * xz
        + h[4] * (four - 2.0 * xx) + 2.0 * h[5] * xz + 3.0 * h[6] * less
    )
    g_y = (
        -SH_ONE * g[1] + g4 * x + g5 * z - 2.0 * g6 * y - 2.0 * g8 * y
        + 3.0 * h[0] * less + h[1] * xz + h[2] * (four - 2.0 * yy) - 6.0 * h[3] * yz
        - 2.0 * h[4] * xy - 2.0 * h[5] * yz - 6.0 * h[6] * xy
    )
    g_z = (
        SH_ONE * g[2] + g5 * y + 4.0 * g6 * z + g7 * x
        + h[1] * xy + 8.0 * h[2] * yz + h[3] * (6.0 * zz - 3.0 * xx - 3.0 * yy)
        + 8.0 * h[4] * xz + h[5] * less
    )
    return [g_x, g_y, g_z]


def camera_rows(cam_ref, table, passes, cams):
    views = passes * cams
    for p in range(passes):
        cam = cam_ref[p]
        cos, sin = jnp.cos(cam), jnp.sin(cam)
        ca, cb, cg = [cos[:, k : k + 1] for k in range(3)]
        sa, sb, sg = [sin[:, k : k + 1] for k in range(3)]
        rotate = [
            [cg * cb, cg * sb * sa - sg * ca, cg * sb * ca + sg * sa],
            [sg * cb, sg * sb * sa + cg * ca, sg * sb * ca - cg * sa],
            [-sb, cb * sa, cb * ca],
        ]
        offset = [cam[:, 3:4], cam[:, 4:5], 6.0 + cam[:, 5:6]]
        center = [-(rotate[0][j] * offset[0] + rotate[1][j] * offset[1] + rotate[2][j] * offset[2]) for j in range(3)]
        for k, term in enumerate(rotate[0] + rotate[1] + rotate[2] + offset + center):
            table[k * views + p * cams : k * views + (p + 1) * cams, :] = jnp.broadcast_to(term, (cams, LANES))


def camera_of(table, view, views, shape):
    terms = [jnp.broadcast_to(table[k * views + view : k * views + view + 1, :], shape) for k in range(TERMS)]
    return [terms[0:3], terms[3:6], terms[6:9]], terms[9:12], terms[12:15]


def project_kernel(
    passes, cams, rows, owners, cap, cols, far_pos, far_scales, far_rots, far_opac, far_cam, far_lists, far_wanted, far_counts, far_places,
    rec, raw, kept, scene, source, chosen, table, pos, scales, rots, opac, cam, lists, wanted, counts, places, done,
):
    views = passes * cams
    shape = (rows, LANES)
    fars = (far_cam, far_pos, far_scales, far_rots, far_opac, far_lists, far_wanted, far_counts, far_places)
    nears = (cam, pos, scales, rots, opac, lists, wanted, counts, places)
    copies = [pltpu.make_async_copy(away, near, done.at[k]) for k, (away, near) in enumerate(zip(fars, nears))]
    for copy in copies:
        copy.start()
    for i in range(rows):
        raw[pl.ds(11 * rows + i, cols.shape[0], stride=rows), :] = cols[:, i * LANES : (i + 1) * LANES]
    for copy in copies[:5]:
        copy.wait()
    camera_rows(cam, table, passes, cams)
    base = 0
    for ref in (pos, scales, rots):
        count = ref.shape[0]
        for i in range(rows):
            raw[pl.ds(base * rows + i, count, stride=rows), :] = ref[:, i * LANES : (i + 1) * LANES]
        base += count
    raw[base * rows : (base + 1) * rows, :] = opac[...]

    def at(k):
        return raw[k * rows : (k + 1) * rows, :]

    def put(ref, k, value):
        ref[k * rows : (k + 1) * rows, :] = value

    point = [at(k) for k in range(3)]
    squares = [jnp.exp(2.0 * at(3 + k)) for k in range(3)]
    spin, _, _ = spin_of([at(6 + k) for k in range(4)])
    cov = world_cov(spin, squares)
    opacity = 1.0 / (1.0 + jnp.exp(-at(10)))
    sight = []
    for view in range(views):
        rotate, offset, center = camera_of(table, view, views, shape)
        _, inv, main, at_x, at_y, t_x, t_y, w_x, w_y, conic = screen_of(point, cov, rotate, offset)
        direction, back = direction_of(point, center)
        basis = basis_of(*direction)
        fields = [FOCAL * at_x + CENTER_X, FOCAL * at_y + CENTER_Y, conic[0], conic[1], conic[2], opacity]
        for f, value in enumerate(fields):
            put(rec, view * FIELDS + f, value)
        r_x, r_y = [[dot3(rotate[i], w) for i in range(3)] for w in (w_x, w_y)]
        moves = []
        for g_main, g_sx, g_sy in (
            (2.0 * r_x[0], 2.0 * r_x[2], 0.0),
            (r_y[0] + r_x[1], r_y[2], r_x[2]),
            (2.0 * r_y[1], 0.0, 2.0 * r_y[2]),
        ):
            g_m = [g_sx, g_sy, g_main - 2.0 * (at_x * g_sx + at_y * g_sy)]
            size = -main * inv
            moves += [size * (rotate[0][j] * g_m[0] + rotate[1][j] * g_m[1] + rotate[2][j] * g_m[2]) for j in range(3)]
        sight.append((direction, back))
        for k, value in enumerate([*t_x, *t_y, *conic, *moves]):
            put(kept, view * KEPT + k, value)
        for k in range(1, 16):
            put(kept, view * KEPT + KEPT - 16 + k, basis[k])

    for copy in copies[5:]:
        copy.wait()
    entries, pixels = lists.shape[-1], wanted.shape[-1]
    entry_row = lax.broadcasted_iota(jnp.int32, (1, entries), 1)
    for p in range(passes):
        for k in range(3):
            scene[p * SCENE + k : p * SCENE + k + 1, :] = wanted[p, k]
        count = jnp.broadcast_to(counts[:, p : p + 1], (1, entries))
        scene[p * SCENE + 3 : p * SCENE + 4, :] = jnp.where(entry_row < count, 1.0, 0.0)
        place = jnp.broadcast_to(places[:, p : p + 1], (1, entries))
        for k, value in enumerate((place % 256 * 16 + 8, place // 256 * 16 + 8)):
            scene[p * SCENE + 4 + k : p * SCENE + 5 + k, :] = value.astype(F32)
        chosen[p : p + 1, :] = lists[p, 0] // cap
        chosen[passes + p : passes + p + 1, :] = lists[p, 0] % cap + p * cap
    pair = (LANES, LANES)
    turned = lax.broadcasted_iota(jnp.int32, pair, 0)
    turned_p, turned_j = turned % HALF // cap, turned % cap
    entry = (lax.broadcasted_iota(jnp.int32, pair, 1) + 1).astype(F32)
    owner_row = lax.broadcasted_iota(jnp.int32, (owners, LANES), 0)
    halves = entries // LANES
    found = jnp.full((owners, LANES), -LANES, jnp.int32)
    for p in range(passes):
        for h in range(halves):
            slot = lists[p, 0, :, h * LANES : (h + 1) * LANES]
            mine = jnp.where(jnp.broadcast_to(slot // cap, (owners, LANES)) == owner_row, 1.0, 0.0).astype(BF16)
            here = jnp.where(
                (jnp.broadcast_to(slot % cap, pair) == turned_j) & (turned_p == p), entry, 0.0
            ).astype(BF16)
            hit = dot(mine, here, ((1,), (1,)))
            found = jnp.where(hit > 0.5, hit.astype(jnp.int32) + ((p * halves + h) * LANES - 1), found)
    source[...] = found

    for channel in range(3):
        totals = [0.5 + SH_ZERO * at(11 + channel)] * views
        for k in range(1, 16):
            color = at(11 + 3 * k + channel)
            for view in range(views):
                start = (view * KEPT + KEPT - 16 + k) * rows
                totals[view] = totals[view] + kept[start : start + rows, :] * color
        for view in range(views):
            put(rec, view * FIELDS + 6 + channel, totals[view])
    for view in range(views):
        direction, back = sight[view]
        for channel in range(3):
            slope = basis_pull(*direction, [at(11 + 3 * k + channel) for k in range(16)])
            along = dot3(direction, slope)
            for j in range(3):
                put(kept, view * KEPT + SHADE + 3 * channel + j, (slope[j] - direction[j] * along) * back)


def lane_pass(shape, cap):
    lane = lax.broadcasted_iota(jnp.int32, shape, 1) % HALF
    return lane // cap, lane % cap


def ids_kernel(passes, cams, cap, ids, *refs):
    count = (len(refs) - 6) // 2
    sources, out, results = refs[:count], refs[count], refs[count + 1 : 2 * count + 1]
    landed, lines, ids_done, out_done, done = refs[2 * count + 1 :]
    first = pltpu.make_async_copy(ids, landed, ids_done)
    first.start()
    copies = [pltpu.make_async_copy(source, result, done.at[k]) for k, (source, result) in enumerate(zip(sources, results))]
    for copy in copies:
        copy.start()
    first.wait()
    for c in range(cams):
        parts = [landed[p, 0, 0, c] for p in range(passes)]
        tiles = parts[0].shape[0]
        if passes * cap < HALF:
            parts.append(jnp.zeros((tiles, HALF - passes * cap), jnp.int32))
        lines[c * tiles : (c + 1) * tiles, :] = jnp.concatenate(parts + parts, axis=1)
    last = pltpu.make_async_copy(lines, out, out_done)
    last.start()
    for copy in copies:
        copy.wait()
    last.wait()


def pick_kernel(passes, cams, tiles, rows, cap, aligned, ids, rec, out, inverse, turns):
    shape = (GROUP, LANES)
    lane = lax.broadcasted_iota(jnp.int32, shape, 1)
    sub = lax.broadcasted_iota(jnp.int32, shape, 0)
    lane_p, _ = lane_pass(shape, cap)
    if not aligned:
        turns[...] = jnp.zeros(turns.shape, jnp.int32)

    def packets(first, c):
        low, high = parted(ids[pl.ds(first, GROUP), :])
        if aligned:
            blocks = [jnp.broadcast_to(high[:, p * cap : p * cap + 1], shape) for p in range(passes)]
            for p in range(passes):
                turn = jnp.zeros(shape, jnp.int32)
                for t in range(1, tiles):
                    turn = jnp.where(jnp.broadcast_to(blocks[p][t : t + 1, :], shape) == sub, t, turn)
                turns[(p * cams + c) * rows : (p * cams + c + 1) * rows, :] = turn

        def pick(f):
            found = jnp.zeros(shape, F32)
            for p in range(passes):
                start = ((p * cams + c) * FIELDS + f) * rows
                if aligned:
                    own = lane_pick(row_pick(rec[start : start + rows, :], blocks[p]), low)
                else:
                    own = jnp.zeros(shape, F32)
                    for b in range(rows):
                        line = jnp.broadcast_to(rec[start + b : start + b + 1, :], shape)
                        own = jnp.where(high == b, lane_pick(line, low), own)
                found = own if p == 0 else jnp.where(lane_p == p, own, found)
            return found

        for r in range(SENT):
            value = pick(2 * r)
            if 2 * r + 1 < FIELDS:
                value = jnp.where(lane < HALF, value, pick(2 * r + 1))
            out[pl.ds(first * SENT + r, GROUP, stride=SENT), :] = value

    for c in range(cams):
        if tiles == GROUP:
            packets(c * tiles, c)
        else:

            def step(k, carry, c=c):
                packets(pl.multiple_of(c * tiles + k * GROUP, GROUP), c)
                return carry

            lax.fori_loop(0, tiles // GROUP, step, 0)

    square = (LANES, LANES)
    column = lax.broadcasted_iota(jnp.int32, square, 0)
    turn = lax.broadcasted_iota(jnp.int32, square, 1)
    place = (turn % HALF + 1 + turn // HALF * LANES).astype(F32)
    wide = (passes * rows, LANES)
    wide_lane = lax.broadcasted_iota(jnp.int32, wide, 1)
    key = lax.broadcasted_iota(jnp.int32, wide, 0)
    lane_key = jnp.where(wide_lane % HALF < passes * cap, lane_pass(wide, cap)[0] * rows, -(1 << 20))
    line_lane = lax.broadcasted_iota(jnp.int32, (1, LANES), 1)

    def two(c, t, found):
        low, high = parted(
            jnp.where(line_lane < HALF, ids[pl.ds(c * tiles + t, 1), :], ids[pl.ds(c * tiles + t + 1, 1), :])
        )
        low = jnp.broadcast_to(low, square)
        high = jnp.broadcast_to(high, wide)
        match = jnp.where(low == column, place, 0.0).astype(BF16)
        owner = jnp.where(high + lane_key == key, 1.0, 0.0).astype(BF16)
        hit = dot(owner, match, ((1,), (1,)))
        return jnp.where(hit > 0.5, hit.astype(jnp.int32) + t * LANES, found)

    for c in range(cams):
        found = jnp.zeros(wide, jnp.int32)
        if tiles <= 8:
            for t in range(0, tiles, 2):
                found = two(c, t, found)
        else:
            found = lax.fori_loop(0, tiles // 2, lambda t, f, c=c: two(c, 2 * t, f), found)
        for p in range(passes):
            start = (p * cams + c) * rows
            inverse[start : start + rows, :] = found[p * rows : (p + 1) * rows, :]


def render_kernel(passes, owners, cap, entries, pixels, got, lists, scene, source, out, *scratch):
    alphas, ratios, sums, high, low = [scratch[k * passes : (k + 1) * passes] for k in range(5)]
    halves = entries // LANES
    shape = (GROUP, LANES)
    wide = 16
    lane = lax.broadcasted_iota(jnp.int32, shape, 1)
    sub = lax.broadcasted_iota(jnp.int32, shape, 0)

    slot_owner, slot_lane = [], []
    for p in range(passes):
        for h in range(halves):
            part = slice(h * LANES, (h + 1) * LANES)
            slot_owner.append(jnp.broadcast_to(lists[p : p + 1, part], shape))
            slot_lane.append(jnp.broadcast_to(lists[passes + p : passes + p + 1, part], shape))
    total = passes * halves

    def gather(g, found):
        mine = [slot_owner[i] == g * GROUP + sub for i in range(total)]
        new = []
        for f in range(FIELDS):
            lines = got[pl.ds(g * (GROUP * SENT) + f // 2, GROUP, stride=SENT), :]
            for i in range(total):
                new.append(jnp.where(mine[i], lane_pick(lines, slot_lane[i] + f % 2 * HALF), found[f * total + i]))
        return tuple(new)

    fields = tuple(jnp.zeros(shape, F32) for _ in range(FIELDS * total))
    if owners <= 32:
        for g in range(owners // GROUP):
            fields = gather(g, fields)
    else:
        fields = lax.fori_loop(0, owners // GROUP, gather, fields)
    fields = [jnp.sum(x, axis=0, keepdims=True) for x in fields]

    row_at, column_at = [lax.broadcasted_iota(jnp.int32, (entries, entries), k) for k in range(2)]
    before = jnp.where(row_at < column_at, 1.0, 0.0).astype(BF16)
    after = jnp.where(row_at > column_at, 1.0, 0.0).astype(BF16)
    column_x = lax.broadcasted_iota(jnp.int32, (wide, entries), 0).astype(F32) - 7.5
    steps = [slice(y * wide, (y + 1) * wide) for y in range(pixels // wide)]

    lines, spans = [], []
    for p in range(passes):
        line = [
            jnp.concatenate([fields[f * total + p * halves + h] for h in range(halves)], axis=1) for f in range(FIELDS)
        ]
        line[0] = line[0] - scene[p * SCENE + 4 : p * SCENE + 5, :]
        line[1] = line[1] - scene[p * SCENE + 5 : p * SCENE + 6, :]
        lines.append(line)
        spans.append(column_x - line[0])

    def offset_y(p, y):
        return (y - 7.5) - lines[p][1]

    for p in range(passes):
        _, _, c_a, c_b, c_c, base = lines[p][:6]
        live = base * scene[p * SCENE + 3 : p * SCENE + 4, :]
        d_x = spans[p]
        q_xx = (-0.5 * c_a) * d_x * d_x
        q_x = -c_b * d_x
        for y, at in enumerate(steps):
            d_y = offset_y(p, y)
            alpha = live * jnp.exp(q_xx + (q_x * d_y - 0.5 * c_c * d_y * d_y))
            clear = jnp.log(1.0 - alpha)
            alphas[p][at, :] = alpha
            ratios[p][at, :] = alpha * jnp.exp(-clear)
            high[p][at, :], low[p][at, :] = split(clear)
    for p in range(passes):
        sums[p][...] = dot(high[p][...], before, ((1,), (0,))) + dot(low[p][...], before, ((1,), (0,)))
    for p in range(passes):
        for at in steps:
            weight = alphas[p][at, :] * jnp.exp(sums[p][at, :])
            alphas[p][at, :] = weight
            high[p][at, :], low[p][at, :] = split(weight)
    residuals, pair_rows = [], []
    for p in range(passes):
        c_high, c_low = split(jnp.concatenate(lines[p][6:9], axis=0))
        both = dot(jnp.concatenate([c_high, c_low], axis=0), high[p][...], ((1,), (1,)))
        shown = both[0:3, :] + both[3:6, :] + dot(c_high, low[p][...], ((1,), (1,)))
        residuals.append(split(shown - scene[p * SCENE : p * SCENE + 3, :]))
        pair_rows.append(jnp.concatenate([c_high, c_low, c_high], axis=0))
    color_grads = []
    for p in range(passes):
        r_high, r_low = residuals[p]
        sums[p][...] = dot(jnp.concatenate([r_high, r_high, r_low], axis=0), pair_rows[p], ((0,), (0,)))
        both = dot(jnp.concatenate([r_high, r_low], axis=0), high[p][...], ((1,), (0,)))
        color_grads.append(both[0:3, :] + both[3:6, :] + dot(r_high, low[p][...], ((1,), (0,))))
    for p in range(passes):
        for at in steps:
            pulled = alphas[p][at, :] * sums[p][at, :]
            alphas[p][at, :] = pulled
            high[p][at, :], low[p][at, :] = split(pulled)
    for p in range(passes):
        sums[p][...] = dot(high[p][...], after, ((1,), (0,))) + dot(low[p][...], after, ((1,), (0,)))
    grads = []
    for p in range(passes):
        m_1 = m_y = m_yy = jnp.zeros((wide, entries), F32)
        for y, at in enumerate(steps):
            grad = alphas[p][at, :] - ratios[p][at, :] * sums[p][at, :]
            d_y = offset_y(p, y)
            grad_y = grad * d_y
            m_1, m_y, m_yy = m_1 + grad, m_y + grad_y, m_yy + grad_y * d_y
        d_x = spans[p]
        m_x = m_1 * d_x
        s_1, s_x, s_y, s_xx, s_xy, s_yy = [
            jnp.sum(m, axis=0, keepdims=True) for m in (m_1, m_x, m_y, m_x * d_x, m_y * d_x, m_yy)
        ]
        _, _, c_a, c_b, c_c, base = lines[p][:6]
        grads.append(
            [
                c_a * s_x + c_b * s_y,
                c_b * s_x + c_c * s_y,
                -0.5 * s_xx,
                -s_xy,
                -0.5 * s_yy,
                s_1 / base,
                color_grads[p][0:1, :],
                color_grads[p][1:2, :],
                color_grads[p][2:3, :],
            ]
        )

    def packets(first, origin):
        index, which = parted(origin)

        def pick(f):
            found = jnp.zeros(shape, F32)
            for p in range(passes):
                for h in range(halves):
                    line = jnp.broadcast_to(grads[p][f][:, h * LANES : (h + 1) * LANES], shape)
                    found = jnp.where(which == p * halves + h, lane_pick(line, index), found)
            return found

        for r in range(SENT):
            value = pick(2 * r)
            if 2 * r + 1 < FIELDS:
                value = jnp.where(lane < HALF, value, pick(2 * r + 1))
            out[pl.ds(first * SENT + r, GROUP, stride=SENT), :] = value

    for g in range(owners // GROUP):
        packets(g * GROUP, source[g * GROUP : (g + 1) * GROUP, :])


def pull_kernel(
    passes, cams, tiles, rows, cap, aligned, got, inverse, turns, raw, kept,
    far_pos, far_scales, far_rots, far_opac, far_cols, total, pos, scales, rots, opac, cols, done,
):
    views = passes * cams
    shape = (rows, LANES)

    def at(k):
        return raw[k * rows : (k + 1) * rows, :]

    def fetcher(view):
        p, c = view // cams, view % cams
        slot = inverse[view * rows : (view + 1) * rows, :] - 1
        valid = slot >= 0
        slot_lane, slot_t = parted(jnp.maximum(slot, 0))
        row_t = turns[view * rows : (view + 1) * rows, :]
        turned = {}

        def fetch(f):
            row, shift = f // 2, f % 2 * HALF
            if aligned:
                if row not in turned:
                    turned[row] = row_pick(got[pl.ds(c * tiles * SENT + row, tiles, stride=SENT), :], row_t)
                return jnp.where(valid, lane_pick(turned[row], slot_lane + shift), 0.0)

            def one(t, found):
                line = jnp.broadcast_to(got[pl.ds((c * tiles + t) * SENT + row, 1), :], shape)
                return jnp.where(valid & (slot_t == t), lane_pick(line, slot_lane + shift), found)

            return lax.fori_loop(0, tiles, one, jnp.zeros(shape, F32))

        return fetch

    def held(view, k):
        start = (view * KEPT + k) * rows
        return kept[start : start + rows, :]

    fetchers = [fetcher(view) for view in range(views)]
    shades = [[fetchers[view](6 + channel) for view in range(views)] for channel in range(3)]
    copies = []

    def send(near, away):
        copies.append(pltpu.make_async_copy(near, away, done.at[len(copies)]))
        copies[-1].start()

    sent = 0
    for k in range(16):
        basis = [held(view, KEPT - 16 + k) for view in range(views)] if k else None
        for channel in range(3):
            terms = shades[channel] if k == 0 else [basis[view] * shades[channel][view] for view in range(views)]
            while len(terms) > 1:
                terms = [sum(terms[n : n + 2][1:], terms[n]) for n in range(0, len(terms), 2)]
            start = (11 + 3 * k + channel) * rows
            total[start : start + rows, :] = terms[0] if k else SH_ZERO * terms[0]
        ready = (3 * k + 3) // 16 * 16
        if ready > sent:
            for i in range(rows):
                cols[sent:ready, i * LANES : (i + 1) * LANES] = total[pl.ds((11 + sent) * rows + i, ready - sent, stride=rows), :]
            send(cols.at[pl.ds(sent, ready - sent), :], far_cols.at[pl.ds(sent, ready - sent), :])
            sent = ready

    squares = [jnp.exp(2.0 * at(3 + k)) for k in range(3)]
    spin, quat, quat_back = spin_of([at(6 + k) for k in range(4)])

    g_point = [jnp.zeros(shape, F32) for _ in range(3)]
    g_cov = [[jnp.zeros(shape, F32) for _ in range(3)] for _ in range(3)]
    g_opacity = jnp.zeros(shape, F32)
    for view in range(views):
        g = [fetchers[view](f) for f in range(6)] + [shades[channel][view] for channel in range(3)]
        t_x, t_y, conic, m_xx, m_xy, m_yy, s_r, s_g, s_b = [[held(view, 3 * n + k) for k in range(3)] for n in range(9)]
        c_a, c_b, c_c = conic
        half = 0.5 * g[3]
        p00, p01 = g[2] * c_a + half * c_b, g[2] * c_b + half * c_c
        p10, p11 = half * c_a + g[4] * c_b, half * c_b + g[4] * c_c
        g_xx = -(c_a * p00 + c_b * p10)
        g_xy = -(c_a * p01 + c_b * p11)
        g_yy = -(c_b * p01 + c_c * p11)
        left = [g_xx * t_x[i] + g_xy * t_y[i] for i in range(3)]
        right = [g_yy * t_y[i] + g_xy * t_x[i] for i in range(3)]
        for i in range(3):
            for j in range(i, 3):
                g_cov[i][j] = g_cov[i][j] + (t_x[i] * left[j] + t_y[i] * right[j])
        pulls = ((t_x, g[0]), (t_y, g[1]), (m_xx, g_xx), (m_xy, 2.0 * g_xy), (m_yy, g_yy), (s_r, g[6]), (s_g, g[7]), (s_b, g[8]))
        for j in range(3):
            for slope, value in pulls:
                g_point[j] = g_point[j] + slope[j] * value
        g_opacity = g_opacity + g[5]
    for i in range(3):
        for j in range(i):
            g_cov[i][j] = g_cov[j][i]

    g_scales = []
    g_spin = [[None] * 3 for _ in range(3)]
    for k in range(3):
        column = [spin[j][k] for j in range(3)]
        turned = [dot3(g_cov[i], column) for i in range(3)]
        g_scales.append(2.0 * squares[k] * dot3(column, turned))
        for i in range(3):
            g_spin[i][k] = 2.0 * squares[k] * turned[i]
    w, x, y, z = quat
    d = g_spin
    g_quat = [
        2.0 * (z * (d[1][0] - d[0][1]) + y * (d[0][2] - d[2][0]) + x * (d[2][1] - d[1][2])),
        2.0 * (y * (d[0][1] + d[1][0]) + z * (d[0][2] + d[2][0]) + w * (d[2][1] - d[1][2]) - 2.0 * x * (d[1][1] + d[2][2])),
        2.0 * (x * (d[0][1] + d[1][0]) + z * (d[1][2] + d[2][1]) + w * (d[0][2] - d[2][0]) - 2.0 * y * (d[0][0] + d[2][2])),
        2.0 * (x * (d[0][2] + d[2][0]) + y * (d[1][2] + d[2][1]) + w * (d[1][0] - d[0][1]) - 2.0 * z * (d[0][0] + d[1][1])),
    ]
    along = w * g_quat[0] + x * g_quat[1] + y * g_quat[2] + z * g_quat[3]
    g_rots = [(g_quat[k] - quat[k] * along) * quat_back for k in range(4)]
    opacity = 1.0 / (1.0 + jnp.exp(-at(10)))
    opac[...] = g_opacity * opacity * (1.0 - opacity)
    for k, value in enumerate(g_point + g_scales + g_rots):
        total[k * rows : (k + 1) * rows, :] = value
    base = 0
    for ref in (pos, scales, rots):
        count = ref.shape[0]
        for i in range(rows):
            ref[:, i * LANES : (i + 1) * LANES] = total[pl.ds(base * rows + i, count, stride=rows), :]
        base += count
    for near, away in ((pos, far_pos), (scales, far_scales), (rots, far_rots), (opac, far_opac)):
        send(near, away)
    for copy in copies:
        copy.wait()


def vmem(count):
    return [pl.BlockSpec(memory_space=pltpu.VMEM)] * count


def call(kernel, outs, operands, in_specs=None, scratch=(), flops=1_000_000, out_specs=None):
    return pl.pallas_call(
        kernel,
        out_shape=outs,
        in_specs=in_specs or vmem(len(operands)),
        out_specs=out_specs or jax.tree.map(lambda _: pl.BlockSpec(memory_space=pltpu.VMEM), outs),
        scratch_shapes=list(scratch),
        compiler_params=pltpu.CompilerParams(vmem_limit_bytes=32 << 20),
        cost_estimate=pl.CostEstimate(flops=flops, bytes_accessed=1 << 20, transcendentals=0),
    )(*operands)


def body(
    cams,
    tiles,
    positions,
    log_scales,
    rotations,
    opacities,
    colors,
    cameras,
    targets,
    tile_ids,
    tile_counts,
    tile_lists,
    fetch_ids,
):
    axes = ("cam", "tile")
    passes, cap = fetch_ids.shape[0], fetch_ids.shape[-1]
    entries, pixels = tile_lists.shape[-1], targets.shape[-1]
    columns = positions.shape[-1]
    rows = columns // LANES
    owners = cams * tiles
    views = passes * cams
    aligned = tiles == rows == 8

    def shaped(*shape):
        return jax.ShapeDtypeStruct(shape, F32)

    def exchange(x):
        lines = x.reshape(owners, 1, -1)
        return lax.all_to_all(lines, axes, split_axis=0, concat_axis=0, tiled=True).reshape(x.shape)

    whole, smem, far = [pl.BlockSpec(memory_space=space) for space in (pltpu.VMEM, pltpu.SMEM, pltpu.HBM)]
    near = [colors]
    wanted_ids, *near = call(
        functools.partial(ids_kernel, passes, cams, cap),
        [jax.ShapeDtypeStruct((owners, LANES), jnp.int32)]
        + [pltpu.VMEM(x.shape, x.dtype) for x in near],
        [pltpu.with_memory_space_constraint(x, pltpu.HBM) for x in (fetch_ids, *near)],
        in_specs=[far] * (1 + len(near)),
        out_specs=[far] + [whole] * len(near),
        scratch=[
            pltpu.VMEM(fetch_ids.shape, jnp.int32),
            pltpu.VMEM((owners, LANES), jnp.int32),
            pltpu.SemaphoreType.DMA,
            pltpu.SemaphoreType.DMA,
            pltpu.SemaphoreType.DMA((len(near),)),
        ],
    )
    arrived = exchange(wanted_ids)
    small = [
        positions,
        log_scales,
        rotations,
        opacities.reshape(rows, LANES),
        cameras,
        tile_lists,
        targets.reshape(passes, 3, 1, pixels),
        tile_counts.reshape(1, passes),
        tile_ids.reshape(1, passes),
    ]
    records, raw, kept, scene, source, lists = call(
        functools.partial(project_kernel, passes, cams, rows, owners, cap),
        [
            shaped(views * FIELDS * rows, LANES),
            shaped(RAW * rows, LANES),
            shaped(views * KEPT * rows, LANES),
            shaped(passes * SCENE, entries),
            jax.ShapeDtypeStruct((owners, LANES), jnp.int32),
            jax.ShapeDtypeStruct((2 * passes, entries), jnp.int32),
        ],
        [*near, *[pltpu.with_memory_space_constraint(x, pltpu.HBM) for x in small]],
        in_specs=[whole] * 1 + [far] * len(small),
        scratch=[pltpu.VMEM((TERMS * views, LANES), F32)]
        + [pltpu.VMEM(x.shape, x.dtype) for x in small]
        + [pltpu.SemaphoreType.DMA((len(small),))],
    )
    codes = jax.ShapeDtypeStruct((views * rows, LANES), jnp.int32)
    packets, inverse, turns = call(
        functools.partial(pick_kernel, passes, cams, tiles, rows, cap, aligned),
        [shaped(owners * SENT, LANES), codes, codes],
        [arrived, records],
    )
    fetched = exchange(packets)
    slot_grads = call(
        functools.partial(render_kernel, passes, owners, cap, entries, pixels),
        shaped(owners * SENT, LANES),
        [fetched, lists, scene, source],
        scratch=[pltpu.VMEM((pixels, entries), kind) for kind in (F32, F32, F32, BF16, BF16) for _ in range(passes)],
    )
    coming = exchange(slot_grads)
    g_pos, g_scales, g_rots, g_opac, g_cols = call(
        functools.partial(pull_kernel, passes, cams, tiles, rows, cap, aligned),
        [shaped(3, columns), shaped(3, columns), shaped(4, columns), shaped(rows, LANES), shaped(*colors.shape)],
        [coming, inverse, turns, raw, kept],
        out_specs=[far] * 5,
        scratch=[pltpu.VMEM((RAW * rows, LANES), F32)]
        + [pltpu.VMEM(shape, F32) for shape in ((3, columns), (3, columns), (4, columns), (rows, LANES), colors.shape)]
        + [pltpu.SemaphoreType.DMA((7,))],
    )
    return (g_pos, g_scales, g_rots, g_opac.reshape(columns), g_cols)


def solution(mesh):
    return jax.shard_map(
        functools.partial(body, mesh.shape["cam"], mesh.shape["tile"]),
        mesh=mesh,
        in_specs=(
            P(None, ("cam", "tile")),
            P(None, ("cam", "tile")),
            P(None, ("cam", "tile")),
            P(("cam", "tile")),
            P(None, ("cam", "tile")),
            P(),
            P(None, "cam", "tile", None, None),
            P(None, "cam", "tile"),
            P(None, "cam", "tile"),
            P(None, "cam", "tile", None),
            P(None, "cam", "tile", None, None, None),
        ),
        out_specs=(
            P(None, ("cam", "tile")),
            P(None, ("cam", "tile")),
            P(None, ("cam", "tile")),
            P(("cam", "tile")),
            P(None, ("cam", "tile")),
        ),
        check_vma=False,
    )
```

```python
import functools

import jax
import jax.numpy as jnp
from jax import lax
from jax.experimental import pallas as pl
from jax.experimental.pallas import tpu as pltpu
from jax.sharding import PartitionSpec as P

FOCAL = 4096.0
CENTER_X = 2048.0
CENTER_Y = 1024.0
SH_ZERO = 0.28209479177387814
SH_ONE = 0.4886025119029199
SH_TWO = [
    1.0925484305920792,
    -1.0925484305920792,
    0.31539156525252005,
    -1.0925484305920792,
    0.5462742152960396,
]
SH_THREE = [
    -0.5900435899266435,
    2.890611442640554,
    -0.4570457994644658,
    0.3731763325901154,
    -0.4570457994644658,
    1.445305721320277,
    -0.5900435899266435,
]
LANES = 128
HALF = LANES // 2
FIELDS = 9
SENT = 5
GROUP = 8
RAW = 59
KEPT = 42
SHADE = 18
SCENE = 6
TERMS = 15
F32 = jnp.float32
BF16 = jnp.bfloat16


def dot(left, right, contract):
    return lax.dot_general(left, right, ((contract[0], contract[1]), ((), ())), preferred_element_type=F32)


def split(x):
    high = x.astype(BF16)
    return high, (x - high.astype(F32)).astype(BF16)


def parted(x):
    return x & (LANES - 1), lax.shift_right_arithmetic(x, LANES.bit_length() - 1)


def lane_pick(source, index):
    return jnp.take_along_axis(source, index, axis=1, mode="promise_in_bounds")


def row_pick(source, index):
    return jnp.take_along_axis(source, index, axis=0, mode="promise_in_bounds")


def spin_of(quat):
    norm = jnp.sqrt(quat[0] * quat[0] + quat[1] * quat[1] + quat[2] * quat[2] + quat[3] * quat[3])
    back = 1.0 / norm
    w, x, y, z = [q * back for q in quat]
    spin = [
        [1.0 - 2.0 * (y * y + z * z), 2.0 * (x * y - w * z), 2.0 * (x * z + w * y)],
        [2.0 * (x * y + w * z), 1.0 - 2.0 * (x * x + z * z), 2.0 * (y * z - w * x)],
        [2.0 * (x * z - w * y), 2.0 * (y * z + w * x), 1.0 - 2.0 * (x * x + y * y)],
    ]
    return spin, (w, x, y, z), back


def world_cov(spin, squares):
    scaled = [[spin[i][k] * squares[k] for k in range(3)] for i in range(3)]
    cov = [[None] * 3 for _ in range(3)]
    for i in range(3):
        for j in range(i, 3):
            cov[i][j] = scaled[i][0] * spin[j][0] + scaled[i][1] * spin[j][1] + scaled[i][2] * spin[j][2]
            cov[j][i] = cov[i][j]
    return cov


def dot3(a, b):
    return a[0] * b[0] + a[1] * b[1] + a[2] * b[2]


def screen_of(point, cov, rotate, offset):
    m = [dot3(rotate[i], point) + offset[i] for i in range(3)]
    inverse = 1.0 / m[2]
    main = FOCAL * inverse
    at_x, at_y = m[0] * inverse, m[1] * inverse
    side_x, side_y = -main * at_x, -main * at_y
    t_x = [main * rotate[0][i] + side_x * rotate[2][i] for i in range(3)]
    t_y = [main * rotate[1][i] + side_y * rotate[2][i] for i in range(3)]
    w_x = [dot3(cov[i], t_x) for i in range(3)]
    w_y = [dot3(cov[i], t_y) for i in range(3)]
    s_xx = dot3(t_x, w_x) + 0.3
    s_xy = dot3(t_y, w_x)
    s_yy = dot3(t_y, w_y) + 0.3
    back = 1.0 / (s_xx * s_yy - s_xy * s_xy)
    conic = (s_yy * back, -s_xy * back, s_xx * back)
    return m, inverse, main, at_x, at_y, t_x, t_y, w_x, w_y, conic


def direction_of(point, center):
    toward = [point[j] - center[j] for j in range(3)]
    back = lax.rsqrt(dot3(toward, toward))
    return [t * back for t in toward], back


def basis_of(x, y, z):
    xx, yy, zz = x * x, y * y, z * z
    xy, yz, xz = x * y, y * z, x * z
    less = xx - yy
    four = 4.0 * zz - xx - yy
    return [
        None,
        -SH_ONE * y,
        SH_ONE * z,
        -SH_ONE * x,
        SH_TWO[0] * xy,
        SH_TWO[1] * yz,
        SH_TWO[2] * (2.0 * zz - xx - yy),
        SH_TWO[3] * xz,
        SH_TWO[4] * less,
        SH_THREE[0] * y * (3.0 * xx - yy),
        SH_THREE[1] * xy * z,
        SH_THREE[2] * y * four,
        SH_THREE[3] * z * (2.0 * zz - 3.0 * xx - 3.0 * yy),
        SH_THREE[4] * x * four,
        SH_THREE[5] * z * less,
        SH_THREE[6] * x * (xx - 3.0 * yy),
    ]


def slope_terms(c):
    d = [None] * 4 + [SH_TWO[i] * c[4 + i] for i in range(5)] + [SH_THREE[i] * c[9 + i] for i in range(7)]
    first = [-SH_ONE * c[3], -SH_ONE * c[1], SH_ONE * c[2]]
    in_x = (2.0 * (d[8] - d[6]), 6.0 * d[9] - 2.0 * d[11], 2.0 * d[14] - 6.0 * d[12], 3.0 * d[15])
    in_y = (-2.0 * (d[8] + d[6]), 3.0 * d[9], -2.0 * d[14] - 6.0 * d[12], -2.0 * d[13] - 6.0 * d[15])
    in_z = (4.0 * d[6], 8.0 * d[11], 8.0 * d[13])
    return d, first, in_x, in_y, in_z


def slope_of(x, y, z, terms):
    d, first, in_x, in_y, in_z = terms
    xx, yy, zz = x * x, y * y, z * z
    xy, yz, xz = x * y, y * z, x * z
    less, both = xx - yy, xx + yy
    four = 4.0 * zz - both
    g_x = (
        first[0] + d[4] * y + in_x[0] * x + d[7] * z + in_x[1] * xy + d[10] * yz + in_x[2] * xz
        + d[13] * (four - 2.0 * xx) + in_x[3] * less
    )
    g_y = (
        first[1] + d[4] * x + d[5] * z + in_y[0] * y + in_y[1] * less + d[10] * xz + d[11] * (four - 2.0 * yy)
        + in_y[2] * yz + in_y[3] * xy
    )
    g_z = (
        first[2] + d[5] * y + in_z[0] * z + d[7] * x + d[10] * xy + in_z[1] * yz + d[12] * (6.0 * zz - 3.0 * both)
        + in_z[2] * xz + d[14] * less
    )
    return [g_x, g_y, g_z]


def camera_rows(cam_ref, table, passes, cams):
    views = passes * cams
    for p in range(passes):
        cam = cam_ref[p]
        cos, sin = jnp.cos(cam), jnp.sin(cam)
        ca, cb, cg = [cos[:, k : k + 1] for k in range(3)]
        sa, sb, sg = [sin[:, k : k + 1] for k in range(3)]
        rotate = [
            [cg * cb, cg * sb * sa - sg * ca, cg * sb * ca + sg * sa],
            [sg * cb, sg * sb * sa + cg * ca, sg * sb * ca - cg * sa],
            [-sb, cb * sa, cb * ca],
        ]
        offset = [cam[:, 3:4], cam[:, 4:5], 6.0 + cam[:, 5:6]]
        center = [-(rotate[0][j] * offset[0] + rotate[1][j] * offset[1] + rotate[2][j] * offset[2]) for j in range(3)]
        for k, term in enumerate(rotate[0] + rotate[1] + rotate[2] + offset + center):
            table[k * views + p * cams : k * views + (p + 1) * cams, :] = jnp.broadcast_to(term, (cams, LANES))


def camera_of(table, view, views, shape):
    terms = [jnp.broadcast_to(table[k * views + view : k * views + view + 1, :], shape) for k in range(TERMS)]
    return [terms[0:3], terms[3:6], terms[6:9]], terms[9:12], terms[12:15]


def project_kernel(
    passes, cams, rows, owners, cap, folded, cols, far_pos, far_scales, far_rots, far_opac, far_cam, far_lists, far_wanted,
    far_counts, far_places, rec, raw, kept, scene, source, chosen,
    table, pos, scales, rots, opac, cam, lists, wanted, counts, places, done,
):
    views = passes * cams
    shape = (rows, LANES)
    fars = (far_cam, far_pos, far_scales, far_rots, far_opac, far_lists, far_wanted, far_counts, far_places)
    nears = (cam, pos, scales, rots, opac, lists, wanted, counts, places)
    copies = [pltpu.make_async_copy(away, near, done.at[k]) for k, (away, near) in enumerate(zip(fars, nears))]
    for copy in copies:
        copy.start()
    for i in range(rows):
        raw[pl.ds(11 * rows + i, cols.shape[0], stride=rows), :] = cols[:, i * LANES : (i + 1) * LANES]
    for copy in copies[:5]:
        copy.wait()
    camera_rows(cam, table, passes, cams)
    base = 0
    for ref in (pos, scales, rots):
        count = ref.shape[0]
        for i in range(rows):
            raw[pl.ds(base * rows + i, count, stride=rows), :] = ref[:, i * LANES : (i + 1) * LANES]
        base += count
    raw[base * rows : (base + 1) * rows, :] = opac[...]

    def at(k):
        return raw[k * rows : (k + 1) * rows, :]

    def put(ref, k, value):
        ref[k * rows : (k + 1) * rows, :] = value

    point = [at(k) for k in range(3)]
    squares = [jnp.exp(2.0 * at(3 + k)) for k in range(3)]
    spin, _, _ = spin_of([at(6 + k) for k in range(4)])
    cov = world_cov(spin, squares)
    opacity = 1.0 / (1.0 + jnp.exp(-at(10)))
    sight = []
    for view in range(views):
        rotate, offset, center = camera_of(table, view, views, shape)
        _, inv, main, at_x, at_y, t_x, t_y, w_x, w_y, conic = screen_of(point, cov, rotate, offset)
        direction, back = direction_of(point, center)
        basis = basis_of(*direction)
        fields = [FOCAL * at_x + CENTER_X, FOCAL * at_y + CENTER_Y, conic[0], conic[1], conic[2], opacity]
        for f, value in enumerate(fields):
            put(rec, view * FIELDS + f, value)
        r_x, r_y = [[dot3(rotate[i], w) for i in range(3)] for w in (w_x, w_y)]
        moves = []
        for g_main, g_sx, g_sy in (
            (2.0 * r_x[0], 2.0 * r_x[2], 0.0),
            (r_y[0] + r_x[1], r_y[2], r_x[2]),
            (2.0 * r_y[1], 0.0, 2.0 * r_y[2]),
        ):
            g_m = [g_sx, g_sy, g_main - 2.0 * (at_x * g_sx + at_y * g_sy)]
            size = -main * inv
            moves += [size * (rotate[0][j] * g_m[0] + rotate[1][j] * g_m[1] + rotate[2][j] * g_m[2]) for j in range(3)]
        sight.append((direction, back))
        for k, value in enumerate([*t_x, *t_y, *conic, *moves]):
            put(kept, view * KEPT + k, value)
        for k in range(1, 16):
            put(kept, view * KEPT + KEPT - 16 + k, basis[k])

    for copy in copies[5:]:
        copy.wait()
    entries, pixels = lists.shape[-1], wanted.shape[-1]
    entry_row = lax.broadcasted_iota(jnp.int32, (1, entries), 1)
    slot_owner, slot_lane = [], []
    for p in range(passes):
        for k in range(3):
            scene[p * SCENE + k : p * SCENE + k + 1, :] = wanted[p, k]
        count = jnp.broadcast_to(counts[:, p : p + 1], (1, entries))
        scene[p * SCENE + 3 : p * SCENE + 4, :] = jnp.where(entry_row < count, 1.0, 0.0)
        place = jnp.broadcast_to(places[:, p : p + 1], (1, entries))
        for k, value in enumerate((place % 256 * 16 + 8, place // 256 * 16 + 8)):
            scene[p * SCENE + 4 + k : p * SCENE + 5 + k, :] = value.astype(F32)
        owner, place = lax.div(lists[p, 0], cap), lax.rem(lists[p, 0], cap)
        if folded:
            groups = LANES // cap
            slot_owner.append(lax.div(owner, groups))
            slot_lane.append(lax.rem(owner + p, groups) * cap + place)
        else:
            slot_owner.append(owner)
            slot_lane.append(place + p * cap)
        chosen[p : p + 1, :] = slot_owner[p]
        chosen[passes + p : passes + p + 1, :] = slot_lane[p]
    pair = (LANES, LANES)
    turned = lax.broadcasted_iota(jnp.int32, pair, 0) & (LANES - 1 if folded else HALF - 1)
    entry = (lax.broadcasted_iota(jnp.int32, pair, 1) + 1).astype(F32)
    lines = GROUP if folded else owners
    line_at = lax.broadcasted_iota(jnp.int32, (lines, LANES), 0)
    halves = entries // LANES
    found = jnp.full((lines, LANES), -LANES, jnp.int32)
    for p in range(passes):
        for h in range(halves):
            part = slice(h * LANES, (h + 1) * LANES)
            mine = jnp.where(jnp.broadcast_to(slot_owner[p][:, part], (lines, LANES)) == line_at, 1.0, 0.0).astype(BF16)
            here = jnp.where(jnp.broadcast_to(slot_lane[p][:, part], pair) == turned, entry, 0.0).astype(BF16)
            hit = dot(mine, here, ((1,), (1,)))
            found = jnp.where(hit > 0.5, hit.astype(jnp.int32) + ((p * halves + h) * LANES - 1), found)
        if folded:
            source[p * GROUP : (p + 1) * GROUP, :] = found
            source[(passes + p) * GROUP : (passes + p + 1) * GROUP, :] = pltpu.roll(found, HALF, 1)
            found = jnp.full((lines, LANES), -LANES, jnp.int32)
    if not folded:
        source[...] = found

    for channel in range(3):
        totals = [0.5 + SH_ZERO * at(11 + channel)] * views
        for k in range(1, 16):
            color = at(11 + 3 * k + channel)
            for view in range(views):
                start = (view * KEPT + KEPT - 16 + k) * rows
                totals[view] = totals[view] + kept[start : start + rows, :] * color
        for view in range(views):
            put(rec, view * FIELDS + 6 + channel, totals[view])
    for channel in range(3):
        terms = slope_terms([at(11 + 3 * k + channel) for k in range(16)])
        for view in range(views):
            direction, back = sight[view]
            slope = slope_of(*direction, terms)
            along = dot3(direction, slope)
            for j in range(3):
                put(kept, view * KEPT + SHADE + 3 * channel + j, (slope[j] - direction[j] * along) * back)


def lane_pass(shape, cap):
    lane = lax.broadcasted_iota(jnp.int32, shape, 1) & (HALF - 1)
    return lax.div(lane, cap)


def ids_kernel(passes, cams, rows, cap, folded, ids, *refs):
    count = (len(refs) - 6) // 2
    sources, out, results = refs[:count], refs[count], refs[count + 1 : 2 * count + 1]
    landed, lines, ids_done, out_done, done = refs[2 * count + 1 :]
    first = pltpu.make_async_copy(ids, landed, ids_done)
    first.start()
    copies = [pltpu.make_async_copy(source, result, done.at[k]) for k, (source, result) in enumerate(zip(sources, results))]
    for copy in copies:
        copy.start()
    first.wait()
    for c in range(cams):
        parts = [landed[p, 0, 0, c] for p in range(passes)]
        tiles = parts[0].shape[0]
        if passes * cap < HALF:
            parts.append(jnp.zeros((tiles, HALF - passes * cap), jnp.int32))
        line = jnp.concatenate(parts + parts, axis=1)
        if folded:
            at_row, at_lane = [lax.broadcasted_iota(jnp.int32, line.shape, k) for k in range(2)]
            plain = line
            for m in range(1, passes):
                line = jnp.where(lax.rem(at_row, passes) == m, pltpu.roll(plain, m * cap, 1), line)
            line = line + ((lax.div(at_lane, cap) - at_row) & (LANES // cap - 1)) * (rows * LANES)
        lines[c * tiles : (c + 1) * tiles, :] = line
    last = pltpu.make_async_copy(lines, out, out_done)
    last.start()
    for copy in copies:
        copy.wait()
    last.wait()


def pick_kernel(passes, cams, tiles, rows, cap, aligned, folded, ids, rec, out, inverse, turns):
    shape = (GROUP, LANES)
    lane = lax.broadcasted_iota(jnp.int32, shape, 1)
    sub = lax.broadcasted_iota(jnp.int32, shape, 0)
    if not aligned:
        turns[...] = jnp.zeros(turns.shape, jnp.int32)

    def packets(first, c):
        low, high = parted(ids[pl.ds(first, GROUP), :])
        if folded:
            tag, high = lax.div(high, rows), lax.rem(high, rows)
            lane_p, first_half = lax.rem(tag, passes), tag < passes
            blocks = [
                jnp.broadcast_to(jnp.max(jnp.where(lane_p == p, high, 0), axis=1, keepdims=True), shape)
                for p in range(passes)
            ]
        else:
            lane_p, first_half = lane_pass(shape, cap), lane < HALF
            blocks = [jnp.broadcast_to(high[:, p * cap : p * cap + 1], shape) for p in range(passes)]
        if aligned:
            for p in range(passes):
                turn = jnp.zeros(shape, jnp.int32)
                for t in range(1, tiles):
                    turn = jnp.where(jnp.broadcast_to(blocks[p][t : t + 1, :], shape) == sub, t, turn)
                turns[(p * cams + c) * rows : (p * cams + c + 1) * rows, :] = turn

        def pick(f):
            found = jnp.zeros(shape, F32)
            for p in range(passes):
                start = ((p * cams + c) * FIELDS + f) * rows
                if aligned:
                    own = lane_pick(row_pick(rec[start : start + rows, :], blocks[p]), low)
                else:
                    own = jnp.zeros(shape, F32)
                    for b in range(rows):
                        line = jnp.broadcast_to(rec[start + b : start + b + 1, :], shape)
                        own = jnp.where(high == b, lane_pick(line, low), own)
                found = own if p == 0 else jnp.where(lane_p == p, own, found)
            return found

        for r in range(SENT):
            value = pick(2 * r)
            if 2 * r + 1 < FIELDS:
                value = jnp.where(first_half, value, pick(2 * r + 1))
            out[pl.ds(first * SENT + r, GROUP, stride=SENT), :] = value

    for c in range(cams):
        if tiles == GROUP:
            packets(c * tiles, c)
        else:

            def step(k, carry, c=c):
                packets(pl.multiple_of(c * tiles + k * GROUP, GROUP), c)
                return carry

            lax.fori_loop(0, tiles // GROUP, step, 0)

    square = (LANES, LANES)
    column = lax.broadcasted_iota(jnp.int32, square, 0)
    turn = lax.broadcasted_iota(jnp.int32, square, 1)
    place = ((turn & (HALF - 1)) + 1 + jnp.where(turn < HALF, 0, LANES)).astype(F32)
    if folded:
        tag = lax.div(parted(jnp.broadcast_to(ids[0:1, :], square))[1], rows)
        place = (jnp.where(tag < passes, turn, ((turn + HALF) & (LANES - 1)) + LANES) + 1).astype(F32)
    wide = (passes * rows, LANES)
    wide_lane = lax.broadcasted_iota(jnp.int32, wide, 1)
    key = lax.broadcasted_iota(jnp.int32, wide, 0)
    lane_key = jnp.where((wide_lane & (HALF - 1)) < passes * cap, lane_pass(wide, cap) * rows, -(1 << 20))
    line_lane = lax.broadcasted_iota(jnp.int32, (1, LANES), 1)

    def two(c, t, found):
        these, next_ones = ids[pl.ds(c * tiles + t, 1), :], ids[pl.ds(c * tiles + t + 1, 1), :]
        if folded:
            low, high = parted(jnp.where(these < passes * rows * LANES, these, next_ones))
            high = lax.rem(high, rows * passes)
        else:
            low, high = parted(jnp.where(line_lane < HALF, these, next_ones))
        low = jnp.broadcast_to(low, square)
        high = jnp.broadcast_to(high, wide)
        match = jnp.where(low == column, place, 0.0).astype(BF16)
        owner = jnp.where((high if folded else high + lane_key) == key, 1.0, 0.0).astype(BF16)
        hit = dot(owner, match, ((1,), (1,)))
        return jnp.where(hit > 0.5, hit.astype(jnp.int32) + t * LANES, found)

    for c in range(cams):
        found = jnp.zeros(wide, jnp.int32)
        if tiles <= 8:
            for t in range(0, tiles, 2):
                found = two(c, t, found)
        else:
            found = lax.fori_loop(0, tiles // 2, lambda t, f, c=c: two(c, 2 * t, f), found)
        for p in range(passes):
            start = (p * cams + c) * rows
            inverse[start : start + rows, :] = found[p * rows : (p + 1) * rows, :]


def render_kernel(passes, owners, cap, folded, entries, pixels, got, lists, scene, source, out, *scratch):
    alphas, ratios, sums, high, low = [scratch[k * passes : (k + 1) * passes] for k in range(5)]
    halves = entries // LANES
    shape = (GROUP, LANES)
    wide = 16
    lane = lax.broadcasted_iota(jnp.int32, shape, 1)
    sub = lax.broadcasted_iota(jnp.int32, shape, 0)

    slot_owner, slot_lane = [], []
    for p in range(passes):
        for h in range(halves):
            part = slice(h * LANES, (h + 1) * LANES)
            slot_owner.append(jnp.broadcast_to(lists[p : p + 1, part], shape))
            slot_lane.append(jnp.broadcast_to(lists[passes + p : passes + p + 1, part], shape))
    total = passes * halves

    groups = LANES // cap
    lane_group = lax.div(lane, cap)

    def merged(choices, back):
        value = choices[-back % groups]
        for g in range(1, groups):
            value = jnp.where(lane_group == g, choices[(g - back) % groups], value)
        return value

    def gather(g, found):
        mine = [slot_owner[i] == g * GROUP + sub for i in range(total)]
        new = []
        for f in range(FIELDS):
            lines = got[pl.ds(g * (GROUP * SENT) + f // 2, GROUP, stride=SENT), :]
            for i in range(total):
                new.append(jnp.where(mine[i], lane_pick(lines, slot_lane[i] + f % 2 * HALF), found[f * total + i]))
        return tuple(new)

    fields = tuple(jnp.zeros(shape, F32) for _ in range(FIELDS * total))
    if folded:
        mine = [slot_owner[i] == sub for i in range(total)]
        places = [slot_lane, [(x + HALF) & (LANES - 1) for x in slot_lane]]
        fields = []
        for f in range(FIELDS):
            packets = [got[pl.ds(m * SENT + f // 2, GROUP, stride=groups * SENT), :] for m in range(groups)]
            for p in range(passes):
                tile = merged(packets, f % 2 * passes + p)
                for i in range(p * halves, (p + 1) * halves):
                    fields.append(jnp.where(mine[i], lane_pick(tile, places[f % 2][i]), 0.0))
    elif owners <= 32:
        for g in range(owners // GROUP):
            fields = gather(g, fields)
    else:
        fields = lax.fori_loop(0, owners // GROUP, gather, fields)
    fields = [jnp.sum(x, axis=0, keepdims=True) for x in fields]

    row_at, column_at = [lax.broadcasted_iota(jnp.int32, (entries, entries), k) for k in range(2)]
    before = jnp.where(row_at < column_at, 1.0, 0.0).astype(BF16)
    after = jnp.where(row_at > column_at, 1.0, 0.0).astype(BF16)
    column_x = lax.broadcasted_iota(jnp.int32, (wide, entries), 0).astype(F32) - 7.5
    steps = [slice(y * wide, (y + 1) * wide) for y in range(pixels // wide)]

    lines, spans = [], []
    for p in range(passes):
        line = [
            jnp.concatenate([fields[f * total + p * halves + h] for h in range(halves)], axis=1) for f in range(FIELDS)
        ]
        line[0] = line[0] - scene[p * SCENE + 4 : p * SCENE + 5, :]
        line[1] = line[1] - scene[p * SCENE + 5 : p * SCENE + 6, :]
        lines.append(line)
        spans.append(column_x - line[0])

    def offset_y(p, y):
        return (y - 7.5) - lines[p][1]

    for p in range(passes):
        _, _, c_a, c_b, c_c, base = lines[p][:6]
        live = base * scene[p * SCENE + 3 : p * SCENE + 4, :]
        d_x = spans[p]
        q_xx = (-0.5 * c_a) * d_x * d_x
        q_x = -c_b * d_x
        for y, at in enumerate(steps):
            d_y = offset_y(p, y)
            alpha = live * jnp.exp(q_xx + (q_x * d_y - 0.5 * c_c * d_y * d_y))
            clear = jnp.log(1.0 - alpha)
            alphas[p][at, :] = alpha
            ratios[p][at, :] = alpha * jnp.exp(-clear)
            high[p][at, :], low[p][at, :] = split(clear)
    for p in range(passes):
        sums[p][...] = dot(high[p][...], before, ((1,), (0,))) + dot(low[p][...], before, ((1,), (0,)))
    for p in range(passes):
        for at in steps:
            weight = alphas[p][at, :] * jnp.exp(sums[p][at, :])
            alphas[p][at, :] = weight
            high[p][at, :], low[p][at, :] = split(weight)
    residuals, pair_rows = [], []
    for p in range(passes):
        c_high, c_low = split(jnp.concatenate(lines[p][6:9], axis=0))
        both = dot(jnp.concatenate([c_high, c_low], axis=0), high[p][...], ((1,), (1,)))
        shown = both[0:3, :] + both[3:6, :] + dot(c_high, low[p][...], ((1,), (1,)))
        residuals.append(split(shown - scene[p * SCENE : p * SCENE + 3, :]))
        pair_rows.append(jnp.concatenate([c_high, c_low, c_high], axis=0))
    color_grads = []
    for p in range(passes):
        r_high, r_low = residuals[p]
        sums[p][...] = dot(jnp.concatenate([r_high, r_high, r_low], axis=0), pair_rows[p], ((0,), (0,)))
        both = dot(jnp.concatenate([r_high, r_low], axis=0), high[p][...], ((1,), (0,)))
        color_grads.append(both[0:3, :] + both[3:6, :] + dot(r_high, low[p][...], ((1,), (0,))))
    for p in range(passes):
        for at in steps:
            pulled = alphas[p][at, :] * sums[p][at, :]
            alphas[p][at, :] = pulled
            high[p][at, :], low[p][at, :] = split(pulled)
    for p in range(passes):
        sums[p][...] = dot(high[p][...], after, ((1,), (0,))) + dot(low[p][...], after, ((1,), (0,)))
    grads = []
    for p in range(passes):
        m_1 = m_y = m_yy = jnp.zeros((wide, entries), F32)
        for y, at in enumerate(steps):
            grad = alphas[p][at, :] - ratios[p][at, :] * sums[p][at, :]
            d_y = offset_y(p, y)
            grad_y = grad * d_y
            m_1, m_y, m_yy = m_1 + grad, m_y + grad_y, m_yy + grad_y * d_y
        d_x = spans[p]
        m_x = m_1 * d_x
        s_1, s_x, s_y, s_xx, s_xy, s_yy = [
            jnp.sum(m, axis=0, keepdims=True) for m in (m_1, m_x, m_y, m_x * d_x, m_y * d_x, m_yy)
        ]
        _, _, c_a, c_b, c_c, base = lines[p][:6]
        grads.append(
            [
                c_a * s_x + c_b * s_y,
                c_b * s_x + c_c * s_y,
                -0.5 * s_xx,
                -s_xy,
                -0.5 * s_yy,
                s_1 / base,
                color_grads[p][0:1, :],
                color_grads[p][1:2, :],
                color_grads[p][2:3, :],
            ]
        )

    def pick(f, which, index, tiles):
        found = jnp.zeros(shape, F32)
        for p, h in tiles:
            line = jnp.broadcast_to(grads[p][f][:, h * LANES : (h + 1) * LANES], shape)
            found = jnp.where(which == p * halves + h, lane_pick(line, index), found)
        return found

    if folded:
        codes = [parted(source[n * GROUP : (n + 1) * GROUP, :]) for n in range(2 * passes)]
        for r in range(SENT):
            parts = []
            for n, (index, which) in enumerate(codes):
                p, f = n % passes, min(2 * r + n // passes, FIELDS - 1)
                parts.append(pick(f, which, index, [(p, h) for h in range(halves)]) if 2 * r + n // passes < FIELDS else parts[p])
            for m in range(groups):
                out[pl.ds(m * SENT + r, GROUP, stride=groups * SENT), :] = merged(parts, m)
        return

    every = [(p, h) for p in range(passes) for h in range(halves)]
    for g in range(owners // GROUP):
        index, which = parted(source[g * GROUP : (g + 1) * GROUP, :])
        for r in range(SENT):
            value = pick(2 * r, which, index, every)
            if 2 * r + 1 < FIELDS:
                value = jnp.where(lane < HALF, value, pick(2 * r + 1, which, index, every))
            out[pl.ds(g * GROUP * SENT + r, GROUP, stride=SENT), :] = value


def pull_kernel(
    passes, cams, tiles, rows, cap, aligned, got, inverse, turns, raw, kept,
    far_pos, far_scales, far_rots, far_opac, far_cols, total, pos, scales, rots, opac, cols, done,
):
    views = passes * cams
    shape = (rows, LANES)

    def at(k):
        return raw[k * rows : (k + 1) * rows, :]

    def fetcher(view):
        p, c = view // cams, view % cams
        slot = inverse[view * rows : (view + 1) * rows, :] - 1
        valid = slot >= 0
        slot_lane, slot_t = parted(jnp.maximum(slot, 0))
        row_t = turns[view * rows : (view + 1) * rows, :]
        turned = {}

        def fetch(f):
            row, shift = f // 2, f % 2 * HALF
            if aligned:
                if row not in turned:
                    turned[row] = row_pick(got[pl.ds(c * tiles * SENT + row, tiles, stride=SENT), :], row_t)
                return jnp.where(valid, lane_pick(turned[row], (slot_lane + shift) & (LANES - 1)), 0.0)

            def one(t, found):
                line = jnp.broadcast_to(got[pl.ds((c * tiles + t) * SENT + row, 1), :], shape)
                return jnp.where(valid & (slot_t == t), lane_pick(line, (slot_lane + shift) & (LANES - 1)), found)

            return lax.fori_loop(0, tiles, one, jnp.zeros(shape, F32))

        return fetch

    def held(view, k):
        start = (view * KEPT + k) * rows
        return kept[start : start + rows, :]

    fetchers = [fetcher(view) for view in range(views)]
    shades = [[fetchers[view](6 + channel) for view in range(views)] for channel in range(3)]
    copies = []

    def send(near, away):
        copies.append(pltpu.make_async_copy(near, away, done.at[len(copies)]))
        copies[-1].start()

    sent = 0
    for k in range(16):
        basis = [held(view, KEPT - 16 + k) for view in range(views)] if k else None
        for channel in range(3):
            terms = shades[channel] if k == 0 else [basis[view] * shades[channel][view] for view in range(views)]
            while len(terms) > 1:
                terms = [sum(terms[n : n + 2][1:], terms[n]) for n in range(0, len(terms), 2)]
            start = (11 + 3 * k + channel) * rows
            total[start : start + rows, :] = terms[0] if k else SH_ZERO * terms[0]
        ready = (3 * k + 3) // 16 * 16
        if ready > sent:
            for i in range(rows):
                cols[sent:ready, i * LANES : (i + 1) * LANES] = total[pl.ds((11 + sent) * rows + i, ready - sent, stride=rows), :]
            send(cols.at[pl.ds(sent, ready - sent), :], far_cols.at[pl.ds(sent, ready - sent), :])
            sent = ready

    squares = [jnp.exp(2.0 * at(3 + k)) for k in range(3)]
    spin, quat, quat_back = spin_of([at(6 + k) for k in range(4)])

    g_point = [jnp.zeros(shape, F32) for _ in range(3)]
    g_cov = [[jnp.zeros(shape, F32) for _ in range(3)] for _ in range(3)]
    g_opacity = jnp.zeros(shape, F32)
    for view in range(views):
        g = [fetchers[view](f) for f in range(6)] + [shades[channel][view] for channel in range(3)]
        t_x, t_y, conic, m_xx, m_xy, m_yy, s_r, s_g, s_b = [[held(view, 3 * n + k) for k in range(3)] for n in range(9)]
        c_a, c_b, c_c = conic
        half = 0.5 * g[3]
        p00, p01 = g[2] * c_a + half * c_b, g[2] * c_b + half * c_c
        p10, p11 = half * c_a + g[4] * c_b, half * c_b + g[4] * c_c
        g_xx = -(c_a * p00 + c_b * p10)
        g_xy = -(c_a * p01 + c_b * p11)
        g_yy = -(c_b * p01 + c_c * p11)
        left = [g_xx * t_x[i] + g_xy * t_y[i] for i in range(3)]
        right = [g_yy * t_y[i] + g_xy * t_x[i] for i in range(3)]
        for i in range(3):
            for j in range(i, 3):
                g_cov[i][j] = g_cov[i][j] + (t_x[i] * left[j] + t_y[i] * right[j])
        pulls = ((t_x, g[0]), (t_y, g[1]), (m_xx, g_xx), (m_xy, 2.0 * g_xy), (m_yy, g_yy), (s_r, g[6]), (s_g, g[7]), (s_b, g[8]))
        for j in range(3):
            for slope, value in pulls:
                g_point[j] = g_point[j] + slope[j] * value
        g_opacity = g_opacity + g[5]
    for i in range(3):
        for j in range(i):
            g_cov[i][j] = g_cov[j][i]

    g_scales = []
    g_spin = [[None] * 3 for _ in range(3)]
    for k in range(3):
        column = [spin[j][k] for j in range(3)]
        turned = [dot3(g_cov[i], column) for i in range(3)]
        g_scales.append(2.0 * squares[k] * dot3(column, turned))
        for i in range(3):
            g_spin[i][k] = 2.0 * squares[k] * turned[i]
    w, x, y, z = quat
    d = g_spin
    g_quat = [
        2.0 * (z * (d[1][0] - d[0][1]) + y * (d[0][2] - d[2][0]) + x * (d[2][1] - d[1][2])),
        2.0 * (y * (d[0][1] + d[1][0]) + z * (d[0][2] + d[2][0]) + w * (d[2][1] - d[1][2]) - 2.0 * x * (d[1][1] + d[2][2])),
        2.0 * (x * (d[0][1] + d[1][0]) + z * (d[1][2] + d[2][1]) + w * (d[0][2] - d[2][0]) - 2.0 * y * (d[0][0] + d[2][2])),
        2.0 * (x * (d[0][2] + d[2][0]) + y * (d[1][2] + d[2][1]) + w * (d[1][0] - d[0][1]) - 2.0 * z * (d[0][0] + d[1][1])),
    ]
    along = w * g_quat[0] + x * g_quat[1] + y * g_quat[2] + z * g_quat[3]
    g_rots = [(g_quat[k] - quat[k] * along) * quat_back for k in range(4)]
    opacity = 1.0 / (1.0 + jnp.exp(-at(10)))
    opac[...] = g_opacity * opacity * (1.0 - opacity)
    for k, value in enumerate(g_point + g_scales + g_rots):
        total[k * rows : (k + 1) * rows, :] = value
    base = 0
    for ref in (pos, scales, rots):
        count = ref.shape[0]
        for i in range(rows):
            ref[:, i * LANES : (i + 1) * LANES] = total[pl.ds(base * rows + i, count, stride=rows), :]
        base += count
    for near, away in ((pos, far_pos), (scales, far_scales), (rots, far_rots), (opac, far_opac)):
        send(near, away)
    for copy in copies:
        copy.wait()


def vmem(count):
    return [pl.BlockSpec(memory_space=pltpu.VMEM)] * count


def call(kernel, outs, operands, in_specs=None, scratch=(), flops=1_000_000, out_specs=None):
    return pl.pallas_call(
        kernel,
        out_shape=outs,
        in_specs=in_specs or vmem(len(operands)),
        out_specs=out_specs or jax.tree.map(lambda _: pl.BlockSpec(memory_space=pltpu.VMEM), outs),
        scratch_shapes=list(scratch),
        compiler_params=pltpu.CompilerParams(vmem_limit_bytes=32 << 20),
        cost_estimate=pl.CostEstimate(flops=flops, bytes_accessed=1 << 20, transcendentals=0),
    )(*operands)


def body(
    cams,
    tiles,
    positions,
    log_scales,
    rotations,
    opacities,
    colors,
    cameras,
    targets,
    tile_ids,
    tile_counts,
    tile_lists,
    fetch_ids,
):
    axes = ("cam", "tile")
    passes, cap = fetch_ids.shape[0], fetch_ids.shape[-1]
    entries, pixels = tile_lists.shape[-1], targets.shape[-1]
    columns = positions.shape[-1]
    rows = columns // LANES
    owners = cams * tiles
    views = passes * cams
    aligned = tiles == rows == GROUP
    folded = 2 * passes * cap == LANES and owners * cap == GROUP * LANES and tiles % (LANES // cap) == 0

    def shaped(*shape):
        return jax.ShapeDtypeStruct(shape, F32)

    def exchange(x):
        lines = x.reshape(owners, 1, -1)
        return lax.all_to_all(lines, axes, split_axis=0, concat_axis=0, tiled=True).reshape(x.shape)

    whole, smem, far = [pl.BlockSpec(memory_space=space) for space in (pltpu.VMEM, pltpu.SMEM, pltpu.HBM)]
    near = [colors]
    wanted_ids, *near = call(
        functools.partial(ids_kernel, passes, cams, rows, cap, folded),
        [jax.ShapeDtypeStruct((owners, LANES), jnp.int32)]
        + [pltpu.VMEM(x.shape, x.dtype) for x in near],
        [pltpu.with_memory_space_constraint(x, pltpu.HBM) for x in (fetch_ids, *near)],
        in_specs=[far] * (1 + len(near)),
        out_specs=[far] + [whole] * len(near),
        scratch=[
            pltpu.VMEM(fetch_ids.shape, jnp.int32),
            pltpu.VMEM((owners, LANES), jnp.int32),
            pltpu.SemaphoreType.DMA,
            pltpu.SemaphoreType.DMA,
            pltpu.SemaphoreType.DMA((len(near),)),
        ],
    )
    arrived = exchange(wanted_ids)
    small = [
        positions,
        log_scales,
        rotations,
        opacities.reshape(rows, LANES),
        cameras,
        tile_lists,
        targets.reshape(passes, 3, 1, pixels),
        tile_counts.reshape(1, passes),
        tile_ids.reshape(1, passes),
    ]
    records, raw, kept, scene, source, lists = call(
        functools.partial(project_kernel, passes, cams, rows, owners, cap, folded),
        [
            shaped(views * FIELDS * rows, LANES),
            shaped(RAW * rows, LANES),
            shaped(views * KEPT * rows, LANES),
            shaped(passes * SCENE, entries),
            jax.ShapeDtypeStruct((2 * passes * GROUP if folded else owners, LANES), jnp.int32),
            jax.ShapeDtypeStruct((2 * passes, entries), jnp.int32),
        ],
        [*near, *[pltpu.with_memory_space_constraint(x, pltpu.HBM) for x in small]],
        in_specs=[whole] * 1 + [far] * len(small),
        scratch=[pltpu.VMEM((TERMS * views, LANES), F32)]
        + [pltpu.VMEM(x.shape, x.dtype) for x in small]
        + [pltpu.SemaphoreType.DMA((len(small),))],
    )
    codes = jax.ShapeDtypeStruct((views * rows, LANES), jnp.int32)
    packets, inverse, turns = call(
        functools.partial(pick_kernel, passes, cams, tiles, rows, cap, aligned, folded),
        [shaped(owners * SENT, LANES), codes, codes],
        [arrived, records],
    )
    fetched = exchange(packets)
    slot_grads = call(
        functools.partial(render_kernel, passes, owners, cap, folded, entries, pixels),
        shaped(owners * SENT, LANES),
        [fetched, lists, scene, source],
        scratch=[pltpu.VMEM((pixels, entries), kind) for kind in (F32, F32, F32, BF16, BF16) for _ in range(passes)],
    )
    coming = exchange(slot_grads)
    g_pos, g_scales, g_rots, g_opac, g_cols = call(
        functools.partial(pull_kernel, passes, cams, tiles, rows, cap, aligned),
        [shaped(3, columns), shaped(3, columns), shaped(4, columns), shaped(rows, LANES), shaped(*colors.shape)],
        [coming, inverse, turns, raw, kept],
        out_specs=[far] * 5,
        scratch=[pltpu.VMEM((RAW * rows, LANES), F32)]
        + [pltpu.VMEM(shape, F32) for shape in ((3, columns), (3, columns), (4, columns), (rows, LANES), colors.shape)]
        + [pltpu.SemaphoreType.DMA((7,))],
    )
    return (g_pos, g_scales, g_rots, g_opac.reshape(columns), g_cols)


def solution(mesh):
    return jax.shard_map(
        functools.partial(body, mesh.shape["cam"], mesh.shape["tile"]),
        mesh=mesh,
        in_specs=(
            P(None, ("cam", "tile")),
            P(None, ("cam", "tile")),
            P(None, ("cam", "tile")),
            P(("cam", "tile")),
            P(None, ("cam", "tile")),
            P(),
            P(None, "cam", "tile", None, None),
            P(None, "cam", "tile"),
            P(None, "cam", "tile"),
            P(None, "cam", "tile", None),
            P(None, "cam", "tile", None, None, None),
        ),
        out_specs=(
            P(None, ("cam", "tile")),
            P(None, ("cam", "tile")),
            P(None, ("cam", "tile")),
            P(("cam", "tile")),
            P(None, ("cam", "tile")),
        ),
        check_vma=False,
    )
```

```python
import functools

import jax
import jax.numpy as jnp
from jax import lax
from jax.experimental import pallas as pl
from jax.experimental.pallas import tpu as pltpu
from jax.sharding import PartitionSpec as P

FOCAL = 4096.0
CENTER_X = 2048.0
CENTER_Y = 1024.0
SH_ZERO = 0.28209479177387814
SH_ONE = 0.4886025119029199
SH_TWO = [
    1.0925484305920792,
    -1.0925484305920792,
    0.31539156525252005,
    -1.0925484305920792,
    0.5462742152960396,
]
SH_THREE = [
    -0.5900435899266435,
    2.890611442640554,
    -0.4570457994644658,
    0.3731763325901154,
    -0.4570457994644658,
    1.445305721320277,
    -0.5900435899266435,
]
LANES = 128
HALF = LANES // 2
FIELDS = 9
SENT = 5
GROUP = 8
RAW = 59
KEPT = 42
SHADE = 18
SCENE = 6
TERMS = 15
F32 = jnp.float32
BF16 = jnp.bfloat16


def dot(left, right, contract):
    return lax.dot_general(left, right, ((contract[0], contract[1]), ((), ())), preferred_element_type=F32)


def split(x):
    high = x.astype(BF16)
    return high, (x - high.astype(F32)).astype(BF16)


def parted(x):
    return x & (LANES - 1), lax.shift_right_arithmetic(x, LANES.bit_length() - 1)


def lane_pick(source, index):
    return jnp.take_along_axis(source, index, axis=1, mode="promise_in_bounds")


def row_pick(source, index):
    return jnp.take_along_axis(source, index, axis=0, mode="promise_in_bounds")


def spin_of(quat):
    norm = jnp.sqrt(quat[0] * quat[0] + quat[1] * quat[1] + quat[2] * quat[2] + quat[3] * quat[3])
    back = 1.0 / norm
    w, x, y, z = [q * back for q in quat]
    spin = [
        [1.0 - 2.0 * (y * y + z * z), 2.0 * (x * y - w * z), 2.0 * (x * z + w * y)],
        [2.0 * (x * y + w * z), 1.0 - 2.0 * (x * x + z * z), 2.0 * (y * z - w * x)],
        [2.0 * (x * z - w * y), 2.0 * (y * z + w * x), 1.0 - 2.0 * (x * x + y * y)],
    ]
    return spin, (w, x, y, z), back


def world_cov(spin, squares):
    scaled = [[spin[i][k] * squares[k] for k in range(3)] for i in range(3)]
    cov = [[None] * 3 for _ in range(3)]
    for i in range(3):
        for j in range(i, 3):
            cov[i][j] = scaled[i][0] * spin[j][0] + scaled[i][1] * spin[j][1] + scaled[i][2] * spin[j][2]
            cov[j][i] = cov[i][j]
    return cov


def dot3(a, b):
    return a[0] * b[0] + a[1] * b[1] + a[2] * b[2]


def screen_of(point, cov, rotate, offset):
    m = [dot3(rotate[i], point) + offset[i] for i in range(3)]
    inverse = 1.0 / m[2]
    main = FOCAL * inverse
    at_x, at_y = m[0] * inverse, m[1] * inverse
    side_x, side_y = -main * at_x, -main * at_y
    t_x = [main * rotate[0][i] + side_x * rotate[2][i] for i in range(3)]
    t_y = [main * rotate[1][i] + side_y * rotate[2][i] for i in range(3)]
    w_x = [dot3(cov[i], t_x) for i in range(3)]
    w_y = [dot3(cov[i], t_y) for i in range(3)]
    s_xx = dot3(t_x, w_x) + 0.3
    s_xy = dot3(t_y, w_x)
    s_yy = dot3(t_y, w_y) + 0.3
    back = 1.0 / (s_xx * s_yy - s_xy * s_xy)
    conic = (s_yy * back, -s_xy * back, s_xx * back)
    return m, inverse, main, at_x, at_y, t_x, t_y, w_x, w_y, conic


def direction_of(point, center):
    toward = [point[j] - center[j] for j in range(3)]
    back = lax.rsqrt(dot3(toward, toward))
    return [t * back for t in toward], back


def basis_of(x, y, z):
    xx, yy, zz = x * x, y * y, z * z
    xy, yz, xz = x * y, y * z, x * z
    less = xx - yy
    four = 4.0 * zz - xx - yy
    return [
        None,
        -SH_ONE * y,
        SH_ONE * z,
        -SH_ONE * x,
        SH_TWO[0] * xy,
        SH_TWO[1] * yz,
        SH_TWO[2] * (2.0 * zz - xx - yy),
        SH_TWO[3] * xz,
        SH_TWO[4] * less,
        SH_THREE[0] * y * (3.0 * xx - yy),
        SH_THREE[1] * xy * z,
        SH_THREE[2] * y * four,
        SH_THREE[3] * z * (2.0 * zz - 3.0 * xx - 3.0 * yy),
        SH_THREE[4] * x * four,
        SH_THREE[5] * z * less,
        SH_THREE[6] * x * (xx - 3.0 * yy),
    ]


def slope_terms(c):
    d = [None] * 4 + [SH_TWO[i] * c[4 + i] for i in range(5)] + [SH_THREE[i] * c[9 + i] for i in range(7)]
    first = [-SH_ONE * c[3], -SH_ONE * c[1], SH_ONE * c[2]]
    in_x = (2.0 * (d[8] - d[6]), 6.0 * d[9] - 2.0 * d[11], 2.0 * d[14] - 6.0 * d[12], 3.0 * d[15])
    in_y = (-2.0 * (d[8] + d[6]), 3.0 * d[9], -2.0 * d[14] - 6.0 * d[12], -2.0 * d[13] - 6.0 * d[15])
    in_z = (4.0 * d[6], 8.0 * d[11], 8.0 * d[13])
    return d, first, in_x, in_y, in_z


def slope_of(x, y, z, terms):
    d, first, in_x, in_y, in_z = terms
    xx, yy, zz = x * x, y * y, z * z
    xy, yz, xz = x * y, y * z, x * z
    less, both = xx - yy, xx + yy
    four = 4.0 * zz - both
    g_x = (
        first[0] + d[4] * y + in_x[0] * x + d[7] * z + in_x[1] * xy + d[10] * yz + in_x[2] * xz
        + d[13] * (four - 2.0 * xx) + in_x[3] * less
    )
    g_y = (
        first[1] + d[4] * x + d[5] * z + in_y[0] * y + in_y[1] * less + d[10] * xz + d[11] * (four - 2.0 * yy)
        + in_y[2] * yz + in_y[3] * xy
    )
    g_z = (
        first[2] + d[5] * y + in_z[0] * z + d[7] * x + d[10] * xy + in_z[1] * yz + d[12] * (6.0 * zz - 3.0 * both)
        + in_z[2] * xz + d[14] * less
    )
    return [g_x, g_y, g_z]


def camera_rows(cam_ref, table, passes, cams):
    views = passes * cams
    for p in range(passes):
        cam = cam_ref[p]
        cos, sin = jnp.cos(cam), jnp.sin(cam)
        ca, cb, cg = [cos[:, k : k + 1] for k in range(3)]
        sa, sb, sg = [sin[:, k : k + 1] for k in range(3)]
        rotate = [
            [cg * cb, cg * sb * sa - sg * ca, cg * sb * ca + sg * sa],
            [sg * cb, sg * sb * sa + cg * ca, sg * sb * ca - cg * sa],
            [-sb, cb * sa, cb * ca],
        ]
        offset = [cam[:, 3:4], cam[:, 4:5], 6.0 + cam[:, 5:6]]
        center = [-(rotate[0][j] * offset[0] + rotate[1][j] * offset[1] + rotate[2][j] * offset[2]) for j in range(3)]
        for k, term in enumerate(rotate[0] + rotate[1] + rotate[2] + offset + center):
            table[k * views + p * cams : k * views + (p + 1) * cams, :] = jnp.broadcast_to(term, (cams, LANES))


def camera_of(table, view, views, shape):
    terms = [jnp.broadcast_to(table[k * views + view : k * views + view + 1, :], shape) for k in range(TERMS)]
    return [terms[0:3], terms[3:6], terms[6:9]], terms[9:12], terms[12:15]


def project_kernel(
    passes, cams, rows, owners, cap, folded, cols, far_pos, far_scales, far_rots, far_opac, far_cam, far_lists, far_wanted,
    far_counts, far_places, rec, raw, kept, scene, source, chosen,
    table, pos, scales, rots, opac, cam, lists, wanted, counts, places, done,
):
    views = passes * cams
    shape = (rows, LANES)
    fars = (far_cam, far_pos, far_scales, far_rots, far_opac, far_lists, far_wanted, far_counts, far_places)
    nears = (cam, pos, scales, rots, opac, lists, wanted, counts, places)
    copies = [pltpu.make_async_copy(away, near, done.at[k]) for k, (away, near) in enumerate(zip(fars, nears))]
    for copy in copies:
        copy.start()
    for i in range(rows):
        raw[pl.ds(11 * rows + i, cols.shape[0], stride=rows), :] = cols[:, i * LANES : (i + 1) * LANES]
    for copy in copies[:5]:
        copy.wait()
    camera_rows(cam, table, passes, cams)
    base = 0
    for ref in (pos, scales, rots):
        count = ref.shape[0]
        for i in range(rows):
            raw[pl.ds(base * rows + i, count, stride=rows), :] = ref[:, i * LANES : (i + 1) * LANES]
        base += count
    raw[base * rows : (base + 1) * rows, :] = opac[...]

    def at(k):
        return raw[k * rows : (k + 1) * rows, :]

    def put(ref, k, value):
        ref[k * rows : (k + 1) * rows, :] = value

    point = [at(k) for k in range(3)]
    squares = [jnp.exp(2.0 * at(3 + k)) for k in range(3)]
    spin, _, _ = spin_of([at(6 + k) for k in range(4)])
    cov = world_cov(spin, squares)
    opacity = 1.0 / (1.0 + jnp.exp(-at(10)))
    sight = []
    for view in range(views):
        rotate, offset, center = camera_of(table, view, views, shape)
        _, inv, main, at_x, at_y, t_x, t_y, w_x, w_y, conic = screen_of(point, cov, rotate, offset)
        direction, back = direction_of(point, center)
        basis = basis_of(*direction)
        fields = [FOCAL * at_x + CENTER_X, FOCAL * at_y + CENTER_Y, conic[0], conic[1], conic[2], opacity]
        for f, value in enumerate(fields):
            put(rec, view * FIELDS + f, value)
        r_x, r_y = [[dot3(rotate[i], w) for i in range(3)] for w in (w_x, w_y)]
        moves = []
        for g_main, g_sx, g_sy in (
            (2.0 * r_x[0], 2.0 * r_x[2], 0.0),
            (r_y[0] + r_x[1], r_y[2], r_x[2]),
            (2.0 * r_y[1], 0.0, 2.0 * r_y[2]),
        ):
            g_m = [g_sx, g_sy, g_main - 2.0 * (at_x * g_sx + at_y * g_sy)]
            size = -main * inv
            moves += [size * (rotate[0][j] * g_m[0] + rotate[1][j] * g_m[1] + rotate[2][j] * g_m[2]) for j in range(3)]
        sight.append((direction, back))
        for k, value in enumerate([*t_x, *t_y, *conic, *moves]):
            put(kept, view * KEPT + k, value)
        for k in range(1, 16):
            put(kept, view * KEPT + KEPT - 16 + k, basis[k])

    for copy in copies[5:]:
        copy.wait()
    entries, pixels = lists.shape[-1], wanted.shape[-1]
    entry_row = lax.broadcasted_iota(jnp.int32, (1, entries), 1)
    slot_owner, slot_lane = [], []
    for p in range(passes):
        for k in range(3):
            scene[p * SCENE + k : p * SCENE + k + 1, :] = wanted[p, k]
        count = jnp.broadcast_to(counts[:, p : p + 1], (1, entries))
        scene[p * SCENE + 3 : p * SCENE + 4, :] = jnp.where(entry_row < count, 1.0, 0.0)
        place = jnp.broadcast_to(places[:, p : p + 1], (1, entries))
        for k, value in enumerate((place % 256 * 16 + 8, place // 256 * 16 + 8)):
            scene[p * SCENE + 4 + k : p * SCENE + 5 + k, :] = value.astype(F32)
        owner, place = lax.div(lists[p, 0], cap), lax.rem(lists[p, 0], cap)
        if folded:
            groups = LANES // cap
            slot_owner.append(lax.div(owner, groups))
            slot_lane.append(lax.rem(owner + p, groups) * cap + place)
        else:
            slot_owner.append(owner)
            slot_lane.append(place + p * cap)
        chosen[p : p + 1, :] = slot_owner[p]
        chosen[passes + p : passes + p + 1, :] = slot_lane[p]
    pair = (LANES, LANES)
    turned = lax.broadcasted_iota(jnp.int32, pair, 0) & (LANES - 1 if folded else HALF - 1)
    entry = (lax.broadcasted_iota(jnp.int32, pair, 1) + 1).astype(F32)
    lines = GROUP if folded else owners
    line_at = lax.broadcasted_iota(jnp.int32, (lines, LANES), 0)
    halves = entries // LANES
    found = jnp.full((lines, LANES), -LANES, jnp.int32)
    for p in range(passes):
        for h in range(halves):
            part = slice(h * LANES, (h + 1) * LANES)
            mine = jnp.where(jnp.broadcast_to(slot_owner[p][:, part], (lines, LANES)) == line_at, 1.0, 0.0).astype(BF16)
            here = jnp.where(jnp.broadcast_to(slot_lane[p][:, part], pair) == turned, entry, 0.0).astype(BF16)
            hit = dot(mine, here, ((1,), (1,)))
            found = jnp.where(hit > 0.5, hit.astype(jnp.int32) + ((p * halves + h) * LANES - 1), found)
        if folded:
            source[p * GROUP : (p + 1) * GROUP, :] = found
            source[(passes + p) * GROUP : (passes + p + 1) * GROUP, :] = pltpu.roll(found, HALF, 1)
            found = jnp.full((lines, LANES), -LANES, jnp.int32)
    if not folded:
        source[...] = found

    for channel in range(3):
        totals = [0.5 + SH_ZERO * at(11 + channel)] * views
        for k in range(1, 16):
            color = at(11 + 3 * k + channel)
            for view in range(views):
                start = (view * KEPT + KEPT - 16 + k) * rows
                totals[view] = totals[view] + kept[start : start + rows, :] * color
        for view in range(views):
            put(rec, view * FIELDS + 6 + channel, totals[view])
    for channel in range(3):
        terms = slope_terms([at(11 + 3 * k + channel) for k in range(16)])
        for view in range(views):
            direction, back = sight[view]
            slope = slope_of(*direction, terms)
            along = dot3(direction, slope)
            for j in range(3):
                put(kept, view * KEPT + SHADE + 3 * channel + j, (slope[j] - direction[j] * along) * back)


def lane_pass(shape, cap):
    lane = lax.broadcasted_iota(jnp.int32, shape, 1) & (HALF - 1)
    return lax.div(lane, cap)


def ids_kernel(passes, cams, rows, cap, folded, ids, *refs):
    count = (len(refs) - 6) // 2
    sources, out, results = refs[:count], refs[count], refs[count + 1 : 2 * count + 1]
    landed, lines, ids_done, out_done, done = refs[2 * count + 1 :]
    first = pltpu.make_async_copy(ids, landed, ids_done)
    first.start()
    copies = [pltpu.make_async_copy(source, result, done.at[k]) for k, (source, result) in enumerate(zip(sources, results))]
    for copy in copies:
        copy.start()
    first.wait()
    for c in range(cams):
        parts = [landed[p, 0, 0, c] for p in range(passes)]
        tiles = parts[0].shape[0]
        if passes * cap < HALF:
            parts.append(jnp.zeros((tiles, HALF - passes * cap), jnp.int32))
        line = jnp.concatenate(parts + parts, axis=1)
        if folded:
            at_row, at_lane = [lax.broadcasted_iota(jnp.int32, line.shape, k) for k in range(2)]
            for m in range(1, passes):
                turned = parts[-m:] + parts[:-m]
                line = jnp.where(lax.rem(at_row, passes) == m, jnp.concatenate(turned + turned, axis=1), line)
            line = line + ((lax.div(at_lane, cap) - at_row) & (LANES // cap - 1)) * (rows * LANES)
        lines[c * tiles : (c + 1) * tiles, :] = line
    last = pltpu.make_async_copy(lines, out, out_done)
    last.start()
    for copy in copies:
        copy.wait()
    last.wait()


def pick_kernel(passes, cams, tiles, rows, cap, aligned, folded, ids, rec, out, inverse, turns):
    shape = (GROUP, LANES)
    lane = lax.broadcasted_iota(jnp.int32, shape, 1)
    sub = lax.broadcasted_iota(jnp.int32, shape, 0)
    if not aligned:
        turns[...] = jnp.zeros(turns.shape, jnp.int32)

    def packets(first, c):
        low, high = parted(ids[pl.ds(first, GROUP), :])
        if folded:
            tag, high = lax.div(high, rows), lax.rem(high, rows)
            lane_p, first_half = lax.rem(tag, passes), tag < passes
            blocks = [
                jnp.broadcast_to(jnp.max(jnp.where(lane_p == p, high, 0), axis=1, keepdims=True), shape)
                for p in range(passes)
            ]
        else:
            lane_p, first_half = lane_pass(shape, cap), lane < HALF
            blocks = [jnp.broadcast_to(high[:, p * cap : p * cap + 1], shape) for p in range(passes)]
        if aligned:
            for p in range(passes):
                turn = jnp.zeros(shape, jnp.int32)
                for t in range(1, tiles):
                    turn = jnp.where(jnp.broadcast_to(blocks[p][t : t + 1, :], shape) == sub, t, turn)
                turns[(p * cams + c) * rows : (p * cams + c + 1) * rows, :] = turn

        def pick(f):
            found = jnp.zeros(shape, F32)
            for p in range(passes):
                start = ((p * cams + c) * FIELDS + f) * rows
                if aligned:
                    own = lane_pick(row_pick(rec[start : start + rows, :], blocks[p]), low)
                else:
                    own = jnp.zeros(shape, F32)
                    for b in range(rows):
                        line = jnp.broadcast_to(rec[start + b : start + b + 1, :], shape)
                        own = jnp.where(high == b, lane_pick(line, low), own)
                found = own if p == 0 else jnp.where(lane_p == p, own, found)
            return found

        for r in range(SENT):
            value = pick(2 * r)
            if 2 * r + 1 < FIELDS:
                value = jnp.where(first_half, value, pick(2 * r + 1))
            out[pl.ds(first * SENT + r, GROUP, stride=SENT), :] = value

    for c in range(cams):
        if tiles == GROUP:
            packets(c * tiles, c)
        else:

            def step(k, carry, c=c):
                packets(pl.multiple_of(c * tiles + k * GROUP, GROUP), c)
                return carry

            lax.fori_loop(0, tiles // GROUP, step, 0)

    square = (LANES, LANES)
    column = lax.broadcasted_iota(jnp.int32, square, 0)
    turn = lax.broadcasted_iota(jnp.int32, square, 1)
    place = ((turn & (HALF - 1)) + 1 + jnp.where(turn < HALF, 0, LANES)).astype(F32)
    if folded:
        tag = lax.div(parted(jnp.broadcast_to(ids[0:1, :], square))[1], rows)
        place = (jnp.where(tag < passes, turn, ((turn + HALF) & (LANES - 1)) + LANES) + 1).astype(F32)
    wide = (passes * rows, LANES)
    wide_lane = lax.broadcasted_iota(jnp.int32, wide, 1)
    key = lax.broadcasted_iota(jnp.int32, wide, 0)
    lane_key = jnp.where((wide_lane & (HALF - 1)) < passes * cap, lane_pass(wide, cap) * rows, -(1 << 20))
    line_lane = lax.broadcasted_iota(jnp.int32, (1, LANES), 1)

    def two(c, t, found):
        these, next_ones = ids[pl.ds(c * tiles + t, 1), :], ids[pl.ds(c * tiles + t + 1, 1), :]
        if folded:
            low, high = parted(jnp.where(these < passes * rows * LANES, these, next_ones))
            high = lax.rem(high, rows * passes)
        else:
            low, high = parted(jnp.where(line_lane < HALF, these, next_ones))
        low = jnp.broadcast_to(low, square)
        high = jnp.broadcast_to(high, wide)
        match = jnp.where(low == column, place, 0.0).astype(BF16)
        owner = jnp.where((high if folded else high + lane_key) == key, 1.0, 0.0).astype(BF16)
        hit = dot(owner, match, ((1,), (1,)))
        return jnp.where(hit > 0.5, hit.astype(jnp.int32) + t * LANES, found)

    for c in range(cams):
        found = jnp.zeros(wide, jnp.int32)
        if tiles <= 8:
            for t in range(0, tiles, 2):
                found = two(c, t, found)
        else:
            found = lax.fori_loop(0, tiles // 2, lambda t, f, c=c: two(c, 2 * t, f), found)
        for p in range(passes):
            start = (p * cams + c) * rows
            inverse[start : start + rows, :] = found[p * rows : (p + 1) * rows, :]


def render_kernel(passes, owners, cap, folded, entries, pixels, got, lists, scene, source, out, *scratch):
    alphas, ratios, sums, high, low = [scratch[k * passes : (k + 1) * passes] for k in range(5)]
    halves = entries // LANES
    shape = (GROUP, LANES)
    wide = 16
    lane = lax.broadcasted_iota(jnp.int32, shape, 1)
    sub = lax.broadcasted_iota(jnp.int32, shape, 0)

    slot_owner, slot_lane = [], []
    for p in range(passes):
        for h in range(halves):
            part = slice(h * LANES, (h + 1) * LANES)
            slot_owner.append(jnp.broadcast_to(lists[p : p + 1, part], shape))
            slot_lane.append(jnp.broadcast_to(lists[passes + p : passes + p + 1, part], shape))
    total = passes * halves

    groups = LANES // cap
    lane_group = lax.div(lane, cap)

    def merged(choices, back):
        value = choices[-back % groups]
        for g in range(1, groups):
            value = jnp.where(lane_group == g, choices[(g - back) % groups], value)
        return value

    def gather(g, found):
        mine = [slot_owner[i] == g * GROUP + sub for i in range(total)]
        new = []
        for f in range(FIELDS):
            lines = got[pl.ds(g * (GROUP * SENT) + f // 2, GROUP, stride=SENT), :]
            for i in range(total):
                new.append(jnp.where(mine[i], lane_pick(lines, slot_lane[i] + f % 2 * HALF), found[f * total + i]))
        return tuple(new)

    fields = tuple(jnp.zeros(shape, F32) for _ in range(FIELDS * total))
    if folded:
        mine = [slot_owner[i] == sub for i in range(total)]
        places = [slot_lane, [(x + HALF) & (LANES - 1) for x in slot_lane]]
        fields = []
        for f in range(FIELDS):
            packets = [got[pl.ds(m * SENT + f // 2, GROUP, stride=groups * SENT), :] for m in range(groups)]
            for p in range(passes):
                tile = merged(packets, f % 2 * passes + p)
                for i in range(p * halves, (p + 1) * halves):
                    fields.append(jnp.where(mine[i], lane_pick(tile, places[f % 2][i]), 0.0))
    elif owners <= 32:
        for g in range(owners // GROUP):
            fields = gather(g, fields)
    else:
        fields = lax.fori_loop(0, owners // GROUP, gather, fields)
    fields = [jnp.sum(x, axis=0, keepdims=True) for x in fields]

    row_at, column_at = [lax.broadcasted_iota(jnp.int32, (entries, entries), k) for k in range(2)]
    before = jnp.where(row_at < column_at, 1.0, 0.0).astype(BF16)
    after = jnp.where(row_at > column_at, 1.0, 0.0).astype(BF16)
    column_x = lax.broadcasted_iota(jnp.int32, (wide, entries), 0).astype(F32) - 7.5
    steps = [slice(y * wide, (y + 1) * wide) for y in range(pixels // wide)]

    lines, spans = [], []
    for p in range(passes):
        line = [
            jnp.concatenate([fields[f * total + p * halves + h] for h in range(halves)], axis=1) for f in range(FIELDS)
        ]
        line[0] = line[0] - scene[p * SCENE + 4 : p * SCENE + 5, :]
        line[1] = line[1] - scene[p * SCENE + 5 : p * SCENE + 6, :]
        lines.append(line)
        spans.append(column_x - line[0])

    def offset_y(p, y):
        return (y - 7.5) - lines[p][1]

    for p in range(passes):
        _, _, c_a, c_b, c_c, base = lines[p][:6]
        live = base * scene[p * SCENE + 3 : p * SCENE + 4, :]
        d_x = spans[p]
        q_xx = (-0.5 * c_a) * d_x * d_x
        q_x = -c_b * d_x
        for y, at in enumerate(steps):
            d_y = offset_y(p, y)
            alpha = live * jnp.exp(q_xx + (q_x * d_y - 0.5 * c_c * d_y * d_y))
            clear = jnp.log(1.0 - alpha)
            alphas[p][at, :] = alpha
            ratios[p][at, :] = alpha * jnp.exp(-clear)
            high[p][at, :], low[p][at, :] = split(clear)
    for p in range(passes):
        sums[p][...] = dot(high[p][...], before, ((1,), (0,))) + dot(low[p][...], before, ((1,), (0,)))
    for p in range(passes):
        for at in steps:
            weight = alphas[p][at, :] * jnp.exp(sums[p][at, :])
            alphas[p][at, :] = weight
            high[p][at, :], low[p][at, :] = split(weight)
    residuals, pair_rows = [], []
    for p in range(passes):
        c_high, c_low = split(jnp.concatenate(lines[p][6:9], axis=0))
        both = dot(jnp.concatenate([c_high, c_low], axis=0), high[p][...], ((1,), (1,)))
        shown = both[0:3, :] + both[3:6, :] + dot(c_high, low[p][...], ((1,), (1,)))
        residuals.append(split(shown - scene[p * SCENE : p * SCENE + 3, :]))
        pair_rows.append(jnp.concatenate([c_high, c_low, c_high], axis=0))
    color_grads = []
    for p in range(passes):
        r_high, r_low = residuals[p]
        sums[p][...] = dot(jnp.concatenate([r_high, r_high, r_low], axis=0), pair_rows[p], ((0,), (0,)))
        both = dot(jnp.concatenate([r_high, r_low], axis=0), high[p][...], ((1,), (0,)))
        color_grads.append(both[0:3, :] + both[3:6, :] + dot(r_high, low[p][...], ((1,), (0,))))
    for p in range(passes):
        for at in steps:
            pulled = alphas[p][at, :] * sums[p][at, :]
            alphas[p][at, :] = pulled
            high[p][at, :], low[p][at, :] = split(pulled)
    for p in range(passes):
        sums[p][...] = dot(high[p][...], after, ((1,), (0,))) + dot(low[p][...], after, ((1,), (0,)))
    grads = []
    for p in range(passes):
        m_1 = m_y = m_yy = jnp.zeros((wide, entries), F32)
        for y, at in enumerate(steps):
            grad = alphas[p][at, :] - ratios[p][at, :] * sums[p][at, :]
            d_y = offset_y(p, y)
            grad_y = grad * d_y
            m_1, m_y, m_yy = m_1 + grad, m_y + grad_y, m_yy + grad_y * d_y
        d_x = spans[p]
        m_x = m_1 * d_x
        s_1, s_x, s_y, s_xx, s_xy, s_yy = [
            jnp.sum(m, axis=0, keepdims=True) for m in (m_1, m_x, m_y, m_x * d_x, m_y * d_x, m_yy)
        ]
        _, _, c_a, c_b, c_c, base = lines[p][:6]
        grads.append(
            [
                c_a * s_x + c_b * s_y,
                c_b * s_x + c_c * s_y,
                -0.5 * s_xx,
                -s_xy,
                -0.5 * s_yy,
                s_1 / base,
                color_grads[p][0:1, :],
                color_grads[p][1:2, :],
                color_grads[p][2:3, :],
            ]
        )

    def pick(f, which, index, tiles):
        found = jnp.zeros(shape, F32)
        for p, h in tiles:
            line = jnp.broadcast_to(grads[p][f][:, h * LANES : (h + 1) * LANES], shape)
            found = jnp.where(which == p * halves + h, lane_pick(line, index), found)
        return found

    if folded:
        codes = [parted(source[n * GROUP : (n + 1) * GROUP, :]) for n in range(2 * passes)]
        for r in range(SENT):
            parts = []
            for n, (index, which) in enumerate(codes):
                p, f = n % passes, min(2 * r + n // passes, FIELDS - 1)
                parts.append(pick(f, which, index, [(p, h) for h in range(halves)]) if 2 * r + n // passes < FIELDS else parts[p])
            for m in range(groups):
                out[pl.ds(m * SENT + r, GROUP, stride=groups * SENT), :] = merged(parts, m)
        return

    every = [(p, h) for p in range(passes) for h in range(halves)]
    for g in range(owners // GROUP):
        index, which = parted(source[g * GROUP : (g + 1) * GROUP, :])
        for r in range(SENT):
            value = pick(2 * r, which, index, every)
            if 2 * r + 1 < FIELDS:
                value = jnp.where(lane < HALF, value, pick(2 * r + 1, which, index, every))
            out[pl.ds(g * GROUP * SENT + r, GROUP, stride=SENT), :] = value


def pull_kernel(
    passes, cams, tiles, rows, cap, aligned, got, inverse, turns, raw, kept,
    far_pos, far_scales, far_rots, far_opac, far_cols, total, pos, scales, rots, opac, cols, done,
):
    views = passes * cams
    shape = (rows, LANES)

    def at(k):
        return raw[k * rows : (k + 1) * rows, :]

    def fetcher(view):
        p, c = view // cams, view % cams
        slot = inverse[view * rows : (view + 1) * rows, :] - 1
        valid = slot >= 0
        slot_lane, slot_t = parted(jnp.maximum(slot, 0))
        row_t = turns[view * rows : (view + 1) * rows, :]
        turned = {}

        def fetch(f):
            row, shift = f // 2, f % 2 * HALF
            if aligned:
                if row not in turned:
                    turned[row] = row_pick(got[pl.ds(c * tiles * SENT + row, tiles, stride=SENT), :], row_t)
                return jnp.where(valid, lane_pick(turned[row], (slot_lane + shift) & (LANES - 1)), 0.0)

            def one(t, found):
                line = jnp.broadcast_to(got[pl.ds((c * tiles + t) * SENT + row, 1), :], shape)
                return jnp.where(valid & (slot_t == t), lane_pick(line, (slot_lane + shift) & (LANES - 1)), found)

            return lax.fori_loop(0, tiles, one, jnp.zeros(shape, F32))

        return fetch

    def held(view, k):
        start = (view * KEPT + k) * rows
        return kept[start : start + rows, :]

    fetchers = [fetcher(view) for view in range(views)]
    shades = [[fetchers[view](6 + channel) for view in range(views)] for channel in range(3)]
    copies = []

    def send(near, away):
        copies.append(pltpu.make_async_copy(near, away, done.at[len(copies)]))
        copies[-1].start()

    sent = 0
    for k in range(16):
        basis = [held(view, KEPT - 16 + k) for view in range(views)] if k else None
        for channel in range(3):
            terms = shades[channel] if k == 0 else [basis[view] * shades[channel][view] for view in range(views)]
            while len(terms) > 1:
                terms = [sum(terms[n : n + 2][1:], terms[n]) for n in range(0, len(terms), 2)]
            start = (11 + 3 * k + channel) * rows
            total[start : start + rows, :] = terms[0] if k else SH_ZERO * terms[0]
        ready = (3 * k + 3) // 16 * 16
        if ready > sent:
            for i in range(rows):
                cols[sent:ready, i * LANES : (i + 1) * LANES] = total[pl.ds((11 + sent) * rows + i, ready - sent, stride=rows), :]
            send(cols.at[pl.ds(sent, ready - sent), :], far_cols.at[pl.ds(sent, ready - sent), :])
            sent = ready

    squares = [jnp.exp(2.0 * at(3 + k)) for k in range(3)]
    spin, quat, quat_back = spin_of([at(6 + k) for k in range(4)])

    g_point = [jnp.zeros(shape, F32) for _ in range(3)]
    g_cov = [[jnp.zeros(shape, F32) for _ in range(3)] for _ in range(3)]
    g_opacity = jnp.zeros(shape, F32)
    for view in range(views):
        g = [fetchers[view](f) for f in range(6)] + [shades[channel][view] for channel in range(3)]
        t_x, t_y, conic, m_xx, m_xy, m_yy, s_r, s_g, s_b = [[held(view, 3 * n + k) for k in range(3)] for n in range(9)]
        c_a, c_b, c_c = conic
        half = 0.5 * g[3]
        p00, p01 = g[2] * c_a + half * c_b, g[2] * c_b + half * c_c
        p10, p11 = half * c_a + g[4] * c_b, half * c_b + g[4] * c_c
        g_xx = -(c_a * p00 + c_b * p10)
        g_xy = -(c_a * p01 + c_b * p11)
        g_yy = -(c_b * p01 + c_c * p11)
        left = [g_xx * t_x[i] + g_xy * t_y[i] for i in range(3)]
        right = [g_yy * t_y[i] + g_xy * t_x[i] for i in range(3)]
        for i in range(3):
            for j in range(i, 3):
                g_cov[i][j] = g_cov[i][j] + (t_x[i] * left[j] + t_y[i] * right[j])
        pulls = ((t_x, g[0]), (t_y, g[1]), (m_xx, g_xx), (m_xy, 2.0 * g_xy), (m_yy, g_yy), (s_r, g[6]), (s_g, g[7]), (s_b, g[8]))
        for j in range(3):
            for slope, value in pulls:
                g_point[j] = g_point[j] + slope[j] * value
        g_opacity = g_opacity + g[5]
    for i in range(3):
        for j in range(i):
            g_cov[i][j] = g_cov[j][i]

    g_scales = []
    g_spin = [[None] * 3 for _ in range(3)]
    for k in range(3):
        column = [spin[j][k] for j in range(3)]
        turned = [dot3(g_cov[i], column) for i in range(3)]
        g_scales.append(2.0 * squares[k] * dot3(column, turned))
        for i in range(3):
            g_spin[i][k] = 2.0 * squares[k] * turned[i]
    w, x, y, z = quat
    d = g_spin
    g_quat = [
        2.0 * (z * (d[1][0] - d[0][1]) + y * (d[0][2] - d[2][0]) + x * (d[2][1] - d[1][2])),
        2.0 * (y * (d[0][1] + d[1][0]) + z * (d[0][2] + d[2][0]) + w * (d[2][1] - d[1][2]) - 2.0 * x * (d[1][1] + d[2][2])),
        2.0 * (x * (d[0][1] + d[1][0]) + z * (d[1][2] + d[2][1]) + w * (d[0][2] - d[2][0]) - 2.0 * y * (d[0][0] + d[2][2])),
        2.0 * (x * (d[0][2] + d[2][0]) + y * (d[1][2] + d[2][1]) + w * (d[1][0] - d[0][1]) - 2.0 * z * (d[0][0] + d[1][1])),
    ]
    along = w * g_quat[0] + x * g_quat[1] + y * g_quat[2] + z * g_quat[3]
    g_rots = [(g_quat[k] - quat[k] * along) * quat_back for k in range(4)]
    opacity = 1.0 / (1.0 + jnp.exp(-at(10)))
    opac[...] = g_opacity * opacity * (1.0 - opacity)
    for k, value in enumerate(g_point + g_scales + g_rots):
        total[k * rows : (k + 1) * rows, :] = value
    base = 0
    for ref in (pos, scales, rots):
        count = ref.shape[0]
        for i in range(rows):
            ref[:, i * LANES : (i + 1) * LANES] = total[pl.ds(base * rows + i, count, stride=rows), :]
        base += count
    for near, away in ((pos, far_pos), (scales, far_scales), (rots, far_rots), (opac, far_opac)):
        send(near, away)
    for copy in copies:
        copy.wait()


def vmem(count):
    return [pl.BlockSpec(memory_space=pltpu.VMEM)] * count


def call(kernel, outs, operands, in_specs=None, scratch=(), flops=1_000_000, out_specs=None):
    return pl.pallas_call(
        kernel,
        out_shape=outs,
        in_specs=in_specs or vmem(len(operands)),
        out_specs=out_specs or jax.tree.map(lambda _: pl.BlockSpec(memory_space=pltpu.VMEM), outs),
        scratch_shapes=list(scratch),
        compiler_params=pltpu.CompilerParams(vmem_limit_bytes=32 << 20),
        cost_estimate=pl.CostEstimate(flops=flops, bytes_accessed=1 << 20, transcendentals=0),
    )(*operands)


def body(
    cams,
    tiles,
    positions,
    log_scales,
    rotations,
    opacities,
    colors,
    cameras,
    targets,
    tile_ids,
    tile_counts,
    tile_lists,
    fetch_ids,
):
    axes = ("cam", "tile")
    passes, cap = fetch_ids.shape[0], fetch_ids.shape[-1]
    entries, pixels = tile_lists.shape[-1], targets.shape[-1]
    columns = positions.shape[-1]
    rows = columns // LANES
    owners = cams * tiles
    views = passes * cams
    aligned = tiles == rows == GROUP
    folded = 2 * passes * cap == LANES and owners * cap == GROUP * LANES and tiles % (LANES // cap) == 0

    def shaped(*shape):
        return jax.ShapeDtypeStruct(shape, F32)

    def exchange(x):
        lines = x.reshape(owners, 1, -1)
        return lax.all_to_all(lines, axes, split_axis=0, concat_axis=0, tiled=True).reshape(x.shape)

    whole, smem, far = [pl.BlockSpec(memory_space=space) for space in (pltpu.VMEM, pltpu.SMEM, pltpu.HBM)]
    near = [colors]
    wanted_ids, *near = call(
        functools.partial(ids_kernel, passes, cams, rows, cap, folded),
        [jax.ShapeDtypeStruct((owners, LANES), jnp.int32)]
        + [pltpu.VMEM(x.shape, x.dtype) for x in near],
        [pltpu.with_memory_space_constraint(x, pltpu.HBM) for x in (fetch_ids, *near)],
        in_specs=[far] * (1 + len(near)),
        out_specs=[far] + [whole] * len(near),
        scratch=[
            pltpu.VMEM(fetch_ids.shape, jnp.int32),
            pltpu.VMEM((owners, LANES), jnp.int32),
            pltpu.SemaphoreType.DMA,
            pltpu.SemaphoreType.DMA,
            pltpu.SemaphoreType.DMA((len(near),)),
        ],
    )
    arrived = exchange(wanted_ids)
    small = [
        positions,
        log_scales,
        rotations,
        opacities.reshape(rows, LANES),
        cameras,
        tile_lists,
        targets.reshape(passes, 3, 1, pixels),
        tile_counts.reshape(1, passes),
        tile_ids.reshape(1, passes),
    ]
    records, raw, kept, scene, source, lists = call(
        functools.partial(project_kernel, passes, cams, rows, owners, cap, folded),
        [
            shaped(views * FIELDS * rows, LANES),
            shaped(RAW * rows, LANES),
            shaped(views * KEPT * rows, LANES),
            shaped(passes * SCENE, entries),
            jax.ShapeDtypeStruct((2 * passes * GROUP if folded else owners, LANES), jnp.int32),
            jax.ShapeDtypeStruct((2 * passes, entries), jnp.int32),
        ],
        [*near, *[pltpu.with_memory_space_constraint(x, pltpu.HBM) for x in small]],
        in_specs=[whole] * 1 + [far] * len(small),
        scratch=[pltpu.VMEM((TERMS * views, LANES), F32)]
        + [pltpu.VMEM(x.shape, x.dtype) for x in small]
        + [pltpu.SemaphoreType.DMA((len(small),))],
    )
    codes = jax.ShapeDtypeStruct((views * rows, LANES), jnp.int32)
    packets, inverse, turns = call(
        functools.partial(pick_kernel, passes, cams, tiles, rows, cap, aligned, folded),
        [shaped(owners * SENT, LANES), codes, codes],
        [arrived, records],
    )
    fetched = exchange(packets)
    slot_grads = call(
        functools.partial(render_kernel, passes, owners, cap, folded, entries, pixels),
        shaped(owners * SENT, LANES),
        [fetched, lists, scene, source],
        scratch=[pltpu.VMEM((pixels, entries), kind) for kind in (F32, F32, F32, BF16, BF16) for _ in range(passes)],
    )
    coming = exchange(slot_grads)
    g_pos, g_scales, g_rots, g_opac, g_cols = call(
        functools.partial(pull_kernel, passes, cams, tiles, rows, cap, aligned),
        [shaped(3, columns), shaped(3, columns), shaped(4, columns), shaped(rows, LANES), shaped(*colors.shape)],
        [coming, inverse, turns, raw, kept],
        out_specs=[far] * 5,
        scratch=[pltpu.VMEM((RAW * rows, LANES), F32)]
        + [pltpu.VMEM(shape, F32) for shape in ((3, columns), (3, columns), (4, columns), (rows, LANES), colors.shape)]
        + [pltpu.SemaphoreType.DMA((7,))],
    )
    return (g_pos, g_scales, g_rots, g_opac.reshape(columns), g_cols)


def solution(mesh):
    return jax.shard_map(
        functools.partial(body, mesh.shape["cam"], mesh.shape["tile"]),
        mesh=mesh,
        in_specs=(
            P(None, ("cam", "tile")),
            P(None, ("cam", "tile")),
            P(None, ("cam", "tile")),
            P(("cam", "tile")),
            P(None, ("cam", "tile")),
            P(),
            P(None, "cam", "tile", None, None),
            P(None, "cam", "tile"),
            P(None, "cam", "tile"),
            P(None, "cam", "tile", None),
            P(None, "cam", "tile", None, None, None),
        ),
        out_specs=(
            P(None, ("cam", "tile")),
            P(None, ("cam", "tile")),
            P(None, ("cam", "tile")),
            P(("cam", "tile")),
            P(None, ("cam", "tile")),
        ),
        check_vma=False,
    )
```

```python
import functools

import jax
import jax.numpy as jnp
from jax import lax
from jax.experimental import pallas as pl
from jax.experimental.pallas import tpu as pltpu
from jax.sharding import PartitionSpec as P

FOCAL = 4096.0
CENTER_X = 2048.0
CENTER_Y = 1024.0
SH_ZERO = 0.28209479177387814
SH_ONE = 0.4886025119029199
SH_TWO = [
    1.0925484305920792,
    -1.0925484305920792,
    0.31539156525252005,
    -1.0925484305920792,
    0.5462742152960396,
]
SH_THREE = [
    -0.5900435899266435,
    2.890611442640554,
    -0.4570457994644658,
    0.3731763325901154,
    -0.4570457994644658,
    1.445305721320277,
    -0.5900435899266435,
]
LANES = 128
HALF = LANES // 2
FIELDS = 9
SENT = 5
GROUP = 8
RAW = 59
KEPT = 42
SHADE = 18
SCENE = 6
TERMS = 15
F32 = jnp.float32
BF16 = jnp.bfloat16


def dot(left, right, contract):
    return lax.dot_general(left, right, ((contract[0], contract[1]), ((), ())), preferred_element_type=F32)


def split(x):
    high = x.astype(BF16)
    return high, (x - high.astype(F32)).astype(BF16)


def parted(x):
    return x & (LANES - 1), lax.shift_right_arithmetic(x, LANES.bit_length() - 1)


def lane_pick(source, index):
    return jnp.take_along_axis(source, index, axis=1, mode="promise_in_bounds")


def row_pick(source, index):
    return jnp.take_along_axis(source, index, axis=0, mode="promise_in_bounds")


def spin_of(quat):
    norm = jnp.sqrt(quat[0] * quat[0] + quat[1] * quat[1] + quat[2] * quat[2] + quat[3] * quat[3])
    back = 1.0 / norm
    w, x, y, z = [q * back for q in quat]
    spin = [
        [1.0 - 2.0 * (y * y + z * z), 2.0 * (x * y - w * z), 2.0 * (x * z + w * y)],
        [2.0 * (x * y + w * z), 1.0 - 2.0 * (x * x + z * z), 2.0 * (y * z - w * x)],
        [2.0 * (x * z - w * y), 2.0 * (y * z + w * x), 1.0 - 2.0 * (x * x + y * y)],
    ]
    return spin, (w, x, y, z), back


def world_cov(spin, squares):
    scaled = [[spin[i][k] * squares[k] for k in range(3)] for i in range(3)]
    cov = [[None] * 3 for _ in range(3)]
    for i in range(3):
        for j in range(i, 3):
            cov[i][j] = scaled[i][0] * spin[j][0] + scaled[i][1] * spin[j][1] + scaled[i][2] * spin[j][2]
            cov[j][i] = cov[i][j]
    return cov


def dot3(a, b):
    return a[0] * b[0] + a[1] * b[1] + a[2] * b[2]


def screen_of(point, cov, rotate, offset):
    m = [dot3(rotate[i], point) + offset[i] for i in range(3)]
    inverse = 1.0 / m[2]
    main = FOCAL * inverse
    at_x, at_y = m[0] * inverse, m[1] * inverse
    side_x, side_y = -main * at_x, -main * at_y
    t_x = [main * rotate[0][i] + side_x * rotate[2][i] for i in range(3)]
    t_y = [main * rotate[1][i] + side_y * rotate[2][i] for i in range(3)]
    w_x = [dot3(cov[i], t_x) for i in range(3)]
    w_y = [dot3(cov[i], t_y) for i in range(3)]
    s_xx = dot3(t_x, w_x) + 0.3
    s_xy = dot3(t_y, w_x)
    s_yy = dot3(t_y, w_y) + 0.3
    back = 1.0 / (s_xx * s_yy - s_xy * s_xy)
    conic = (s_yy * back, -s_xy * back, s_xx * back)
    return m, inverse, main, at_x, at_y, t_x, t_y, w_x, w_y, conic


def direction_of(point, center):
    toward = [point[j] - center[j] for j in range(3)]
    back = lax.rsqrt(dot3(toward, toward))
    return [t * back for t in toward], back


def basis_of(x, y, z):
    xx, yy, zz = x * x, y * y, z * z
    xy, yz, xz = x * y, y * z, x * z
    less = xx - yy
    four = 4.0 * zz - xx - yy
    return [
        None,
        -SH_ONE * y,
        SH_ONE * z,
        -SH_ONE * x,
        SH_TWO[0] * xy,
        SH_TWO[1] * yz,
        SH_TWO[2] * (2.0 * zz - xx - yy),
        SH_TWO[3] * xz,
        SH_TWO[4] * less,
        SH_THREE[0] * y * (3.0 * xx - yy),
        SH_THREE[1] * xy * z,
        SH_THREE[2] * y * four,
        SH_THREE[3] * z * (2.0 * zz - 3.0 * xx - 3.0 * yy),
        SH_THREE[4] * x * four,
        SH_THREE[5] * z * less,
        SH_THREE[6] * x * (xx - 3.0 * yy),
    ]


def slope_terms(c):
    d = [None] * 4 + [SH_TWO[i] * c[4 + i] for i in range(5)] + [SH_THREE[i] * c[9 + i] for i in range(7)]
    first = [-SH_ONE * c[3], -SH_ONE * c[1], SH_ONE * c[2]]
    in_x = (2.0 * (d[8] - d[6]), 6.0 * d[9] - 2.0 * d[11], 2.0 * d[14] - 6.0 * d[12], 3.0 * d[15])
    in_y = (-2.0 * (d[8] + d[6]), 3.0 * d[9], -2.0 * d[14] - 6.0 * d[12], -2.0 * d[13] - 6.0 * d[15])
    in_z = (4.0 * d[6], 8.0 * d[11], 8.0 * d[13])
    return d, first, in_x, in_y, in_z


def slope_of(x, y, z, terms):
    d, first, in_x, in_y, in_z = terms
    xx, yy, zz = x * x, y * y, z * z
    xy, yz, xz = x * y, y * z, x * z
    less, both = xx - yy, xx + yy
    four = 4.0 * zz - both
    g_x = (
        first[0] + d[4] * y + in_x[0] * x + d[7] * z + in_x[1] * xy + d[10] * yz + in_x[2] * xz
        + d[13] * (four - 2.0 * xx) + in_x[3] * less
    )
    g_y = (
        first[1] + d[4] * x + d[5] * z + in_y[0] * y + in_y[1] * less + d[10] * xz + d[11] * (four - 2.0 * yy)
        + in_y[2] * yz + in_y[3] * xy
    )
    g_z = (
        first[2] + d[5] * y + in_z[0] * z + d[7] * x + d[10] * xy + in_z[1] * yz + d[12] * (6.0 * zz - 3.0 * both)
        + in_z[2] * xz + d[14] * less
    )
    return [g_x, g_y, g_z]


def camera_rows(cam_ref, table, passes, cams):
    views = passes * cams
    for p in range(passes):
        cam = cam_ref[p]
        cos, sin = jnp.cos(cam), jnp.sin(cam)
        ca, cb, cg = [cos[:, k : k + 1] for k in range(3)]
        sa, sb, sg = [sin[:, k : k + 1] for k in range(3)]
        rotate = [
            [cg * cb, cg * sb * sa - sg * ca, cg * sb * ca + sg * sa],
            [sg * cb, sg * sb * sa + cg * ca, sg * sb * ca - cg * sa],
            [-sb, cb * sa, cb * ca],
        ]
        offset = [cam[:, 3:4], cam[:, 4:5], 6.0 + cam[:, 5:6]]
        center = [-(rotate[0][j] * offset[0] + rotate[1][j] * offset[1] + rotate[2][j] * offset[2]) for j in range(3)]
        for k, term in enumerate(rotate[0] + rotate[1] + rotate[2] + offset + center):
            table[k * views + p * cams : k * views + (p + 1) * cams, :] = jnp.broadcast_to(term, (cams, LANES))


def camera_of(table, view, views, shape):
    terms = [jnp.broadcast_to(table[k * views + view : k * views + view + 1, :], shape) for k in range(TERMS)]
    return [terms[0:3], terms[3:6], terms[6:9]], terms[9:12], terms[12:15]


def project_kernel(
    passes, cams, rows, owners, cap, folded, cols, far_pos, far_scales, far_rots, far_opac, far_cam, far_lists, far_wanted,
    far_counts, far_places, rec, raw, kept, scene, source, chosen,
    table, pos, scales, rots, opac, cam, lists, wanted, counts, places, done,
):
    views = passes * cams
    shape = (rows, LANES)
    fars = (far_cam, far_pos, far_scales, far_rots, far_opac, far_lists, far_wanted, far_counts, far_places)
    nears = (cam, pos, scales, rots, opac, lists, wanted, counts, places)
    copies = [pltpu.make_async_copy(away, near, done.at[k]) for k, (away, near) in enumerate(zip(fars, nears))]
    for copy in copies:
        copy.start()
    for i in range(rows):
        raw[pl.ds(11 * rows + i, cols.shape[0], stride=rows), :] = cols[:, i * LANES : (i + 1) * LANES]
    for copy in copies[:5]:
        copy.wait()
    camera_rows(cam, table, passes, cams)
    base = 0
    for ref in (pos, scales, rots):
        count = ref.shape[0]
        for i in range(rows):
            raw[pl.ds(base * rows + i, count, stride=rows), :] = ref[:, i * LANES : (i + 1) * LANES]
        base += count
    raw[base * rows : (base + 1) * rows, :] = opac[...]

    def at(k):
        return raw[k * rows : (k + 1) * rows, :]

    def put(ref, k, value):
        ref[k * rows : (k + 1) * rows, :] = value

    point = [at(k) for k in range(3)]
    squares = [jnp.exp(2.0 * at(3 + k)) for k in range(3)]
    spin, _, _ = spin_of([at(6 + k) for k in range(4)])
    cov = world_cov(spin, squares)
    opacity = 1.0 / (1.0 + jnp.exp(-at(10)))
    sight = []
    for view in range(views):
        rotate, offset, center = camera_of(table, view, views, shape)
        _, inv, main, at_x, at_y, t_x, t_y, w_x, w_y, conic = screen_of(point, cov, rotate, offset)
        direction, back = direction_of(point, center)
        basis = basis_of(*direction)
        fields = [FOCAL * at_x + CENTER_X, FOCAL * at_y + CENTER_Y, conic[0], conic[1], conic[2], opacity]
        for f, value in enumerate(fields):
            put(rec, view * FIELDS + f, value)
        r_x, r_y = [[dot3(rotate[i], w) for i in range(3)] for w in (w_x, w_y)]
        moves = []
        for g_main, g_sx, g_sy in (
            (2.0 * r_x[0], 2.0 * r_x[2], 0.0),
            (r_y[0] + r_x[1], r_y[2], r_x[2]),
            (2.0 * r_y[1], 0.0, 2.0 * r_y[2]),
        ):
            g_m = [g_sx, g_sy, g_main - 2.0 * (at_x * g_sx + at_y * g_sy)]
            size = -main * inv
            moves += [size * (rotate[0][j] * g_m[0] + rotate[1][j] * g_m[1] + rotate[2][j] * g_m[2]) for j in range(3)]
        sight.append((direction, back))
        for k, value in enumerate([*t_x, *t_y, *conic, *moves]):
            put(kept, view * KEPT + k, value)
        for k in range(1, 16):
            put(kept, view * KEPT + KEPT - 16 + k, basis[k])

    for copy in copies[5:]:
        copy.wait()
    entries, pixels = lists.shape[-1], wanted.shape[-1]
    entry_row = lax.broadcasted_iota(jnp.int32, (1, entries), 1)
    slot_owner, slot_lane = [], []
    for p in range(passes):
        for k in range(3):
            scene[p * SCENE + k : p * SCENE + k + 1, :] = wanted[p, k]
        count = jnp.broadcast_to(counts[:, p : p + 1], (1, entries))
        scene[p * SCENE + 3 : p * SCENE + 4, :] = jnp.where(entry_row < count, 1.0, 0.0)
        place = jnp.broadcast_to(places[:, p : p + 1], (1, entries))
        for k, value in enumerate((place % 256 * 16 + 8, place // 256 * 16 + 8)):
            scene[p * SCENE + 4 + k : p * SCENE + 5 + k, :] = value.astype(F32)
        owner, place = lax.div(lists[p, 0], cap), lax.rem(lists[p, 0], cap)
        if folded:
            groups = LANES // cap
            slot_owner.append(lax.div(owner, groups))
            slot_lane.append(lax.rem(owner + p, groups) * cap + place)
        else:
            slot_owner.append(owner)
            slot_lane.append(place + p * cap)
        chosen[p : p + 1, :] = slot_owner[p]
        chosen[passes + p : passes + p + 1, :] = slot_lane[p]
    pair = (LANES, LANES)
    turned = lax.broadcasted_iota(jnp.int32, pair, 0) & (LANES - 1 if folded else HALF - 1)
    entry = (lax.broadcasted_iota(jnp.int32, pair, 1) + 1).astype(F32)
    lines = GROUP if folded else owners
    line_at = lax.broadcasted_iota(jnp.int32, (lines, LANES), 0)
    halves = entries // LANES
    found = jnp.full((lines, LANES), -LANES, jnp.int32)
    for p in range(passes):
        for h in range(halves):
            part = slice(h * LANES, (h + 1) * LANES)
            mine = jnp.where(jnp.broadcast_to(slot_owner[p][:, part], (lines, LANES)) == line_at, 1.0, 0.0).astype(BF16)
            here = jnp.where(jnp.broadcast_to(slot_lane[p][:, part], pair) == turned, entry, 0.0).astype(BF16)
            hit = dot(mine, here, ((1,), (1,)))
            found = jnp.where(hit > 0.5, hit.astype(jnp.int32) + ((p * halves + h) * LANES - 1), found)
        if folded:
            source[p * GROUP : (p + 1) * GROUP, :] = found
            source[(passes + p) * GROUP : (passes + p + 1) * GROUP, :] = pltpu.roll(found, HALF, 1)
            found = jnp.full((lines, LANES), -LANES, jnp.int32)
    if not folded:
        source[...] = found

    for channel in range(3):
        totals = [0.5 + SH_ZERO * at(11 + channel)] * views
        for k in range(1, 16):
            color = at(11 + 3 * k + channel)
            for view in range(views):
                start = (view * KEPT + KEPT - 16 + k) * rows
                totals[view] = totals[view] + kept[start : start + rows, :] * color
        for view in range(views):
            put(rec, view * FIELDS + 6 + channel, totals[view])
    for channel in range(3):
        terms = slope_terms([at(11 + 3 * k + channel) for k in range(16)])
        for view in range(views):
            direction, back = sight[view]
            slope = slope_of(*direction, terms)
            along = dot3(direction, slope)
            for j in range(3):
                put(kept, view * KEPT + SHADE + 3 * channel + j, (slope[j] - direction[j] * along) * back)


def lane_pass(shape, cap):
    lane = lax.broadcasted_iota(jnp.int32, shape, 1) & (HALF - 1)
    return lax.div(lane, cap)


def ids_kernel(passes, cams, rows, cap, folded, ids, *refs):
    count = (len(refs) - 6) // 2
    sources, out, results = refs[:count], refs[count], refs[count + 1 : 2 * count + 1]
    landed, lines, ids_done, out_done, done = refs[2 * count + 1 :]
    first = pltpu.make_async_copy(ids, landed, ids_done)
    first.start()
    copies = [pltpu.make_async_copy(source, result, done.at[k]) for k, (source, result) in enumerate(zip(sources, results))]
    for copy in copies:
        copy.start()
    first.wait()
    for c in range(cams):
        parts = [landed[p, 0, 0, c] for p in range(passes)]
        tiles = parts[0].shape[0]
        if passes * cap < HALF:
            parts.append(jnp.zeros((tiles, HALF - passes * cap), jnp.int32))
        line = jnp.concatenate(parts + parts, axis=1)
        if folded:
            at_row, at_lane = [lax.broadcasted_iota(jnp.int32, line.shape, k) for k in range(2)]
            for m in range(1, passes):
                turned = parts[-m:] + parts[:-m]
                line = jnp.where(lax.rem(at_row, passes) == m, jnp.concatenate(turned + turned, axis=1), line)
            line = line + ((lax.div(at_lane, cap) - at_row) & (LANES // cap - 1)) * (rows * LANES)
        lines[c * tiles : (c + 1) * tiles, :] = line
    last = pltpu.make_async_copy(lines, out, out_done)
    last.start()
    for copy in copies:
        copy.wait()
    last.wait()


def pick_kernel(passes, cams, tiles, rows, cap, aligned, folded, ids, rec, out, inverse, turns):
    shape = (GROUP, LANES)
    lane = lax.broadcasted_iota(jnp.int32, shape, 1)
    sub = lax.broadcasted_iota(jnp.int32, shape, 0)
    if not aligned:
        turns[...] = jnp.zeros(turns.shape, jnp.int32)

    def packets(first, c):
        low, high = parted(ids[pl.ds(first, GROUP), :])
        if folded:
            tag, high = lax.div(high, rows), lax.rem(high, rows)
            lane_p, first_half = lax.rem(tag, passes), tag < passes
            blocks = [
                jnp.broadcast_to(jnp.max(jnp.where(lane_p == p, high, 0), axis=1, keepdims=True), shape)
                for p in range(passes)
            ]
        else:
            lane_p, first_half = lane_pass(shape, cap), lane < HALF
            blocks = [jnp.broadcast_to(high[:, p * cap : p * cap + 1], shape) for p in range(passes)]
        if aligned:
            for p in range(passes):
                turn = jnp.zeros(shape, jnp.int32)
                for t in range(1, tiles):
                    turn = jnp.where(jnp.broadcast_to(blocks[p][t : t + 1, :], shape) == sub, t, turn)
                turns[(p * cams + c) * rows : (p * cams + c + 1) * rows, :] = turn

        def pick(f):
            found = jnp.zeros(shape, F32)
            for p in range(passes):
                start = ((p * cams + c) * FIELDS + f) * rows
                if aligned:
                    own = lane_pick(row_pick(rec[start : start + rows, :], blocks[p]), low)
                else:
                    own = jnp.zeros(shape, F32)
                    for b in range(rows):
                        line = jnp.broadcast_to(rec[start + b : start + b + 1, :], shape)
                        own = jnp.where(high == b, lane_pick(line, low), own)
                found = own if p == 0 else jnp.where(lane_p == p, own, found)
            return found

        for r in range(SENT):
            value = pick(2 * r)
            if 2 * r + 1 < FIELDS:
                value = jnp.where(first_half, value, pick(2 * r + 1))
            out[pl.ds(first * SENT + r, GROUP, stride=SENT), :] = value

    for c in range(cams):
        if tiles == GROUP:
            packets(c * tiles, c)
        else:

            def step(k, carry, c=c):
                packets(pl.multiple_of(c * tiles + k * GROUP, GROUP), c)
                return carry

            lax.fori_loop(0, tiles // GROUP, step, 0)

    square = (LANES, LANES)
    column = lax.broadcasted_iota(jnp.int32, square, 0)
    turn = lax.broadcasted_iota(jnp.int32, square, 1)
    place = ((turn & (HALF - 1)) + 1 + jnp.where(turn < HALF, 0, LANES)).astype(F32)
    if folded:
        tag = lax.div(parted(jnp.broadcast_to(ids[0:1, :], square))[1], rows)
        place = (jnp.where(tag < passes, turn, ((turn + HALF) & (LANES - 1)) + LANES) + 1).astype(F32)
    wide = (passes * rows, LANES)
    wide_lane = lax.broadcasted_iota(jnp.int32, wide, 1)
    key = lax.broadcasted_iota(jnp.int32, wide, 0)
    lane_key = jnp.where((wide_lane & (HALF - 1)) < passes * cap, lane_pass(wide, cap) * rows, -(1 << 20))
    line_lane = lax.broadcasted_iota(jnp.int32, (1, LANES), 1)

    def two(c, t, found):
        these, next_ones = ids[pl.ds(c * tiles + t, 1), :], ids[pl.ds(c * tiles + t + 1, 1), :]
        if folded:
            low, high = parted(jnp.where(these < passes * rows * LANES, these, next_ones))
            high = lax.rem(high, rows * passes)
        else:
            low, high = parted(jnp.where(line_lane < HALF, these, next_ones))
        low = jnp.broadcast_to(low, square)
        high = jnp.broadcast_to(high, wide)
        match = jnp.where(low == column, place, 0.0).astype(BF16)
        owner = jnp.where((high if folded else high + lane_key) == key, 1.0, 0.0).astype(BF16)
        hit = dot(owner, match, ((1,), (1,)))
        return jnp.where(hit > 0.5, hit.astype(jnp.int32) + t * LANES, found)

    for c in range(cams):
        found = jnp.zeros(wide, jnp.int32)
        if tiles <= 8:
            for t in range(0, tiles, 2):
                found = two(c, t, found)
        else:
            found = lax.fori_loop(0, tiles // 2, lambda t, f, c=c: two(c, 2 * t, f), found)
        for p in range(passes):
            start = (p * cams + c) * rows
            inverse[start : start + rows, :] = found[p * rows : (p + 1) * rows, :]


def render_kernel(passes, owners, cap, folded, entries, pixels, got, lists, scene, source, out, *scratch):
    alphas, ratios, weights, pulls, before_sums, slopes, after_sums = [scratch[k * passes : (k + 1) * passes] for k in range(7)]
    clears, shares, pulled_parts = [
        [scratch[(7 + 2 * k) * passes + p :: passes][:2] for p in range(passes)] for k in range(3)
    ]
    halves = entries // LANES
    shape = (GROUP, LANES)
    wide = 16
    lane = lax.broadcasted_iota(jnp.int32, shape, 1)
    sub = lax.broadcasted_iota(jnp.int32, shape, 0)

    slot_owner, slot_lane = [], []
    for p in range(passes):
        for h in range(halves):
            part = slice(h * LANES, (h + 1) * LANES)
            slot_owner.append(jnp.broadcast_to(lists[p : p + 1, part], shape))
            slot_lane.append(jnp.broadcast_to(lists[passes + p : passes + p + 1, part], shape))
    total = passes * halves

    groups = LANES // cap
    lane_group = lax.div(lane, cap)

    def merged(choices, back):
        value = choices[-back % groups]
        for g in range(1, groups):
            value = jnp.where(lane_group == g, choices[(g - back) % groups], value)
        return value

    def gather(g, found):
        mine = [slot_owner[i] == g * GROUP + sub for i in range(total)]
        new = []
        for f in range(FIELDS):
            lines = got[pl.ds(g * (GROUP * SENT) + f // 2, GROUP, stride=SENT), :]
            for i in range(total):
                new.append(jnp.where(mine[i], lane_pick(lines, slot_lane[i] + f % 2 * HALF), found[f * total + i]))
        return tuple(new)

    fields = tuple(jnp.zeros(shape, F32) for _ in range(FIELDS * total))
    if folded:
        mine = [slot_owner[i] == sub for i in range(total)]
        places = [slot_lane, [(x + HALF) & (LANES - 1) for x in slot_lane]]
        fields = []
        for f in range(FIELDS):
            packets = [got[pl.ds(m * SENT + f // 2, GROUP, stride=groups * SENT), :] for m in range(groups)]
            for p in range(passes):
                tile = merged(packets, f % 2 * passes + p)
                for i in range(p * halves, (p + 1) * halves):
                    fields.append(jnp.where(mine[i], lane_pick(tile, places[f % 2][i]), 0.0))
    elif owners <= 32:
        for g in range(owners // GROUP):
            fields = gather(g, fields)
    else:
        fields = lax.fori_loop(0, owners // GROUP, gather, fields)
    fields = [jnp.sum(x, axis=0, keepdims=True) for x in fields]

    row_at, column_at = [lax.broadcasted_iota(jnp.int32, (entries, entries), k) for k in range(2)]
    before = jnp.where(row_at < column_at, 1.0, 0.0).astype(BF16)
    after = jnp.where(row_at > column_at, 1.0, 0.0).astype(BF16)
    column_x = lax.broadcasted_iota(jnp.int32, (wide, entries), 0).astype(F32) - 7.5
    steps = [slice(y * wide, (y + 1) * wide) for y in range(pixels // wide)]

    lines, spans = [], []
    for p in range(passes):
        line = [
            jnp.concatenate([fields[f * total + p * halves + h] for h in range(halves)], axis=1) for f in range(FIELDS)
        ]
        line[0] = line[0] - scene[p * SCENE + 4 : p * SCENE + 5, :]
        line[1] = line[1] - scene[p * SCENE + 5 : p * SCENE + 6, :]
        lines.append(line)
        spans.append(column_x - line[0])

    def offset_y(p, y):
        return (y - 7.5) - lines[p][1]

    def through(parts, at, matrix):
        return dot(parts[0][at, :], matrix, ((1,), (0,))) + dot(parts[1][at, :], matrix, ((1,), (0,)))

    consts = []
    for p in range(passes):
        _, _, c_a, c_b, c_c, base = lines[p][:6]
        live = base * scene[p * SCENE + 3 : p * SCENE + 4, :]
        consts.append((live, (-0.5 * c_a) * spans[p] * spans[p], -c_b * spans[p], 0.5 * c_c))

    def blend(p, y, at):
        live, q_xx, q_x, c_c = consts[p]
        d_y = offset_y(p, y)
        alpha = live * jnp.exp(q_xx + (q_x * d_y - c_c * d_y * d_y))
        clear = jnp.log(1.0 - alpha)
        alphas[p][at, :] = alpha
        ratios[p][at, :] = alpha * jnp.exp(-clear)
        clears[p][0][at, :], clears[p][1][at, :] = split(clear)

    def weigh(p, y, at):
        weight = alphas[p][at, :] * jnp.exp(before_sums[p][at, :])
        weights[p][at, :] = weight
        shares[p][0][at, :], shares[p][1][at, :] = split(weight)

    def pull(p, y, at):
        pulled = weights[p][at, :] * slopes[p][at, :]
        pulls[p][at, :] = pulled
        pulled_parts[p][0][at, :], pulled_parts[p][1][at, :] = split(pulled)

    totals = [[jnp.zeros((wide, entries), F32)] * 3 for _ in range(passes)]

    def add(p, y, at):
        m_1, m_y, m_yy = totals[p]
        grad = pulls[p][at, :] - ratios[p][at, :] * after_sums[p][at, :]
        d_y = offset_y(p, y)
        grad_y = grad * d_y
        totals[p] = [m_1 + grad, m_y + grad_y, m_yy + grad_y * d_y]

    blocks = [slice(n, n + 128) for n in range(0, pixels, 128)]
    both = range(passes)

    def each(work, p, block):
        for y, at in enumerate(steps):
            if block.start <= at.start < block.stop:
                work(p, y, at)

    def sum_before(p, block):
        before_sums[p][block, :] = through(clears[p], block, before)

    def sum_after(p, block):
        after_sums[p][block, :] = through(pulled_parts[p], block, after)

    def slope(p, block):
        r_high, r_low = [r[:, block] for r in residuals[p]]
        slopes[p][block, :] = dot(jnp.concatenate([r_high, r_high, r_low], axis=0), pair_rows[p], ((0,), (0,)))

    def emit(first, second, third):
        jobs = [(block, p) for block in blocks for p in both]
        depth = 2
        for n in range(len(jobs) + 2 * depth):
            if n < len(jobs) and first:
                each(first, jobs[n][1], jobs[n][0])
            if 0 <= n - depth < len(jobs):
                second(jobs[n - depth][1], jobs[n - depth][0])
            if 0 <= n - 2 * depth < len(jobs):
                each(third, jobs[n - 2 * depth][1], jobs[n - 2 * depth][0])

    emit(blend, sum_before, weigh)
    residuals, pair_rows = [], []
    for p in both:
        c_high, c_low = split(jnp.concatenate(lines[p][6:9], axis=0))
        pair = dot(jnp.concatenate([c_high, c_low], axis=0), shares[p][0][...], ((1,), (1,)))
        shown = pair[0:3, :] + pair[3:6, :] + dot(c_high, shares[p][1][...], ((1,), (1,)))
        residuals.append(split(shown - scene[p * SCENE : p * SCENE + 3, :]))
        pair_rows.append(jnp.concatenate([c_high, c_low, c_high], axis=0))
    for block in blocks:
        for p in both:
            slope(p, block)
    emit(pull, sum_after, add)
    color_grads = []
    for p in both:
        r_high, r_low = residuals[p]
        pair = dot(jnp.concatenate([r_high, r_low], axis=0), shares[p][0][...], ((1,), (0,)))
        color_grads.append(pair[0:3, :] + pair[3:6, :] + dot(r_high, shares[p][1][...], ((1,), (0,))))
    grads = []
    for p in both:
        m_1, m_y, m_yy = totals[p]
        d_x = spans[p]
        m_x = m_1 * d_x
        s_1, s_x, s_y, s_xx, s_xy, s_yy = [
            jnp.sum(m, axis=0, keepdims=True) for m in (m_1, m_x, m_y, m_x * d_x, m_y * d_x, m_yy)
        ]
        _, _, c_a, c_b, c_c, base = lines[p][:6]
        grads.append(
            [
                c_a * s_x + c_b * s_y,
                c_b * s_x + c_c * s_y,
                -0.5 * s_xx,
                -s_xy,
                -0.5 * s_yy,
                s_1 / base,
                color_grads[p][0:1, :],
                color_grads[p][1:2, :],
                color_grads[p][2:3, :],
            ]
        )

    def pick(f, which, index, tiles):
        found = jnp.zeros(shape, F32)
        for p, h in tiles:
            line = jnp.broadcast_to(grads[p][f][:, h * LANES : (h + 1) * LANES], shape)
            found = jnp.where(which == p * halves + h, lane_pick(line, index), found)
        return found

    if folded:
        codes = [parted(source[n * GROUP : (n + 1) * GROUP, :]) for n in range(2 * passes)]
        for r in range(SENT):
            parts = []
            for n, (index, which) in enumerate(codes):
                p, f = n % passes, min(2 * r + n // passes, FIELDS - 1)
                parts.append(pick(f, which, index, [(p, h) for h in range(halves)]) if 2 * r + n // passes < FIELDS else parts[p])
            for m in range(groups):
                out[pl.ds(m * SENT + r, GROUP, stride=groups * SENT), :] = merged(parts, m)
        return

    every = [(p, h) for p in range(passes) for h in range(halves)]
    for g in range(owners // GROUP):
        index, which = parted(source[g * GROUP : (g + 1) * GROUP, :])
        for r in range(SENT):
            value = pick(2 * r, which, index, every)
            if 2 * r + 1 < FIELDS:
                value = jnp.where(lane < HALF, value, pick(2 * r + 1, which, index, every))
            out[pl.ds(g * GROUP * SENT + r, GROUP, stride=SENT), :] = value


def pull_kernel(
    passes, cams, tiles, rows, cap, aligned, got, inverse, turns, raw, kept,
    far_pos, far_scales, far_rots, far_opac, far_cols, total, pos, scales, rots, opac, cols, done,
):
    views = passes * cams
    shape = (rows, LANES)

    def at(k):
        return raw[k * rows : (k + 1) * rows, :]

    def fetcher(view):
        p, c = view // cams, view % cams
        slot = inverse[view * rows : (view + 1) * rows, :] - 1
        valid = slot >= 0
        slot_lane, slot_t = parted(jnp.maximum(slot, 0))
        row_t = turns[view * rows : (view + 1) * rows, :]
        turned = {}

        def fetch(f):
            row, shift = f // 2, f % 2 * HALF
            if aligned:
                if row not in turned:
                    turned[row] = row_pick(got[pl.ds(c * tiles * SENT + row, tiles, stride=SENT), :], row_t)
                return jnp.where(valid, lane_pick(turned[row], (slot_lane + shift) & (LANES - 1)), 0.0)

            def one(t, found):
                line = jnp.broadcast_to(got[pl.ds((c * tiles + t) * SENT + row, 1), :], shape)
                return jnp.where(valid & (slot_t == t), lane_pick(line, (slot_lane + shift) & (LANES - 1)), found)

            return lax.fori_loop(0, tiles, one, jnp.zeros(shape, F32))

        return fetch

    def held(view, k):
        start = (view * KEPT + k) * rows
        return kept[start : start + rows, :]

    fetchers = [fetcher(view) for view in range(views)]
    shades = [[fetchers[view](6 + channel) for view in range(views)] for channel in range(3)]
    copies = []

    def send(near, away):
        copies.append(pltpu.make_async_copy(near, away, done.at[len(copies)]))
        copies[-1].start()

    sent = 0
    for k in range(16):
        basis = [held(view, KEPT - 16 + k) for view in range(views)] if k else None
        for channel in range(3):
            terms = shades[channel] if k == 0 else [basis[view] * shades[channel][view] for view in range(views)]
            while len(terms) > 1:
                terms = [sum(terms[n : n + 2][1:], terms[n]) for n in range(0, len(terms), 2)]
            start = (11 + 3 * k + channel) * rows
            total[start : start + rows, :] = terms[0] if k else SH_ZERO * terms[0]
        ready = (3 * k + 3) // 16 * 16
        if ready > sent:
            for i in range(rows):
                cols[sent:ready, i * LANES : (i + 1) * LANES] = total[pl.ds((11 + sent) * rows + i, ready - sent, stride=rows), :]
            send(cols.at[pl.ds(sent, ready - sent), :], far_cols.at[pl.ds(sent, ready - sent), :])
            sent = ready

    squares = [jnp.exp(2.0 * at(3 + k)) for k in range(3)]
    spin, quat, quat_back = spin_of([at(6 + k) for k in range(4)])

    g_point = [jnp.zeros(shape, F32) for _ in range(3)]
    g_cov = [[jnp.zeros(shape, F32) for _ in range(3)] for _ in range(3)]
    g_opacity = jnp.zeros(shape, F32)
    for view in range(views):
        g = [fetchers[view](f) for f in range(6)] + [shades[channel][view] for channel in range(3)]
        t_x, t_y, conic, m_xx, m_xy, m_yy, s_r, s_g, s_b = [[held(view, 3 * n + k) for k in range(3)] for n in range(9)]
        c_a, c_b, c_c = conic
        half = 0.5 * g[3]
        p00, p01 = g[2] * c_a + half * c_b, g[2] * c_b + half * c_c
        p10, p11 = half * c_a + g[4] * c_b, half * c_b + g[4] * c_c
        g_xx = -(c_a * p00 + c_b * p10)
        g_xy = -(c_a * p01 + c_b * p11)
        g_yy = -(c_b * p01 + c_c * p11)
        left = [g_xx * t_x[i] + g_xy * t_y[i] for i in range(3)]
        right = [g_yy * t_y[i] + g_xy * t_x[i] for i in range(3)]
        for i in range(3):
            for j in range(i, 3):
                g_cov[i][j] = g_cov[i][j] + (t_x[i] * left[j] + t_y[i] * right[j])
        pulls = ((t_x, g[0]), (t_y, g[1]), (m_xx, g_xx), (m_xy, 2.0 * g_xy), (m_yy, g_yy), (s_r, g[6]), (s_g, g[7]), (s_b, g[8]))
        for j in range(3):
            for slope, value in pulls:
                g_point[j] = g_point[j] + slope[j] * value
        g_opacity = g_opacity + g[5]
    for i in range(3):
        for j in range(i):
            g_cov[i][j] = g_cov[j][i]

    g_scales = []
    g_spin = [[None] * 3 for _ in range(3)]
    for k in range(3):
        column = [spin[j][k] for j in range(3)]
        turned = [dot3(g_cov[i], column) for i in range(3)]
        g_scales.append(2.0 * squares[k] * dot3(column, turned))
        for i in range(3):
            g_spin[i][k] = 2.0 * squares[k] * turned[i]
    w, x, y, z = quat
    d = g_spin
    g_quat = [
        2.0 * (z * (d[1][0] - d[0][1]) + y * (d[0][2] - d[2][0]) + x * (d[2][1] - d[1][2])),
        2.0 * (y * (d[0][1] + d[1][0]) + z * (d[0][2] + d[2][0]) + w * (d[2][1] - d[1][2]) - 2.0 * x * (d[1][1] + d[2][2])),
        2.0 * (x * (d[0][1] + d[1][0]) + z * (d[1][2] + d[2][1]) + w * (d[0][2] - d[2][0]) - 2.0 * y * (d[0][0] + d[2][2])),
        2.0 * (x * (d[0][2] + d[2][0]) + y * (d[1][2] + d[2][1]) + w * (d[1][0] - d[0][1]) - 2.0 * z * (d[0][0] + d[1][1])),
    ]
    along = w * g_quat[0] + x * g_quat[1] + y * g_quat[2] + z * g_quat[3]
    g_rots = [(g_quat[k] - quat[k] * along) * quat_back for k in range(4)]
    opacity = 1.0 / (1.0 + jnp.exp(-at(10)))
    opac[...] = g_opacity * opacity * (1.0 - opacity)
    for k, value in enumerate(g_point + g_scales + g_rots):
        total[k * rows : (k + 1) * rows, :] = value
    base = 0
    for ref in (pos, scales, rots):
        count = ref.shape[0]
        for i in range(rows):
            ref[:, i * LANES : (i + 1) * LANES] = total[pl.ds(base * rows + i, count, stride=rows), :]
        base += count
    for near, away in ((pos, far_pos), (scales, far_scales), (rots, far_rots), (opac, far_opac)):
        send(near, away)
    for copy in copies:
        copy.wait()


def render_scratch(passes, pixels, entries):
    return [pltpu.VMEM((pixels, entries), F32)] * (7 * passes) + [pltpu.VMEM((pixels, entries), BF16)] * (6 * passes)


def vmem(count):
    return [pl.BlockSpec(memory_space=pltpu.VMEM)] * count


def call(kernel, outs, operands, in_specs=None, scratch=(), flops=1_000_000, out_specs=None):
    return pl.pallas_call(
        kernel,
        out_shape=outs,
        in_specs=in_specs or vmem(len(operands)),
        out_specs=out_specs or jax.tree.map(lambda _: pl.BlockSpec(memory_space=pltpu.VMEM), outs),
        scratch_shapes=list(scratch),
        compiler_params=pltpu.CompilerParams(vmem_limit_bytes=32 << 20),
        cost_estimate=pl.CostEstimate(flops=flops, bytes_accessed=1 << 20, transcendentals=0),
    )(*operands)


def body(
    cams,
    tiles,
    positions,
    log_scales,
    rotations,
    opacities,
    colors,
    cameras,
    targets,
    tile_ids,
    tile_counts,
    tile_lists,
    fetch_ids,
):
    axes = ("cam", "tile")
    passes, cap = fetch_ids.shape[0], fetch_ids.shape[-1]
    entries, pixels = tile_lists.shape[-1], targets.shape[-1]
    columns = positions.shape[-1]
    rows = columns // LANES
    owners = cams * tiles
    views = passes * cams
    aligned = tiles == rows == GROUP
    folded = 2 * passes * cap == LANES and owners * cap == GROUP * LANES and tiles % (LANES // cap) == 0

    def shaped(*shape):
        return jax.ShapeDtypeStruct(shape, F32)

    def exchange(x):
        lines = x.reshape(owners, 1, -1)
        return lax.all_to_all(lines, axes, split_axis=0, concat_axis=0, tiled=True).reshape(x.shape)

    whole, smem, far = [pl.BlockSpec(memory_space=space) for space in (pltpu.VMEM, pltpu.SMEM, pltpu.HBM)]
    near = [colors]
    wanted_ids, *near = call(
        functools.partial(ids_kernel, passes, cams, rows, cap, folded),
        [jax.ShapeDtypeStruct((owners, LANES), jnp.int32)]
        + [pltpu.VMEM(x.shape, x.dtype) for x in near],
        [pltpu.with_memory_space_constraint(x, pltpu.HBM) for x in (fetch_ids, *near)],
        in_specs=[far] * (1 + len(near)),
        out_specs=[far] + [whole] * len(near),
        scratch=[
            pltpu.VMEM(fetch_ids.shape, jnp.int32),
            pltpu.VMEM((owners, LANES), jnp.int32),
            pltpu.SemaphoreType.DMA,
            pltpu.SemaphoreType.DMA,
            pltpu.SemaphoreType.DMA((len(near),)),
        ],
    )
    arrived = exchange(wanted_ids)
    small = [
        positions,
        log_scales,
        rotations,
        opacities.reshape(rows, LANES),
        cameras,
        tile_lists,
        targets.reshape(passes, 3, 1, pixels),
        tile_counts.reshape(1, passes),
        tile_ids.reshape(1, passes),
    ]
    records, raw, kept, scene, source, lists = call(
        functools.partial(project_kernel, passes, cams, rows, owners, cap, folded),
        [
            shaped(views * FIELDS * rows, LANES),
            shaped(RAW * rows, LANES),
            shaped(views * KEPT * rows, LANES),
            shaped(passes * SCENE, entries),
            jax.ShapeDtypeStruct((2 * passes * GROUP if folded else owners, LANES), jnp.int32),
            jax.ShapeDtypeStruct((2 * passes, entries), jnp.int32),
        ],
        [*near, *[pltpu.with_memory_space_constraint(x, pltpu.HBM) for x in small]],
        in_specs=[whole] * 1 + [far] * len(small),
        scratch=[pltpu.VMEM((TERMS * views, LANES), F32)]
        + [pltpu.VMEM(x.shape, x.dtype) for x in small]
        + [pltpu.SemaphoreType.DMA((len(small),))],
    )
    codes = jax.ShapeDtypeStruct((views * rows, LANES), jnp.int32)
    packets, inverse, turns = call(
        functools.partial(pick_kernel, passes, cams, tiles, rows, cap, aligned, folded),
        [shaped(owners * SENT, LANES), codes, codes],
        [arrived, records],
    )
    fetched = exchange(packets)
    slot_grads = call(
        functools.partial(render_kernel, passes, owners, cap, folded, entries, pixels),
        shaped(owners * SENT, LANES),
        [fetched, lists, scene, source],
        scratch=render_scratch(passes, pixels, entries),
    )
    coming = exchange(slot_grads)
    g_pos, g_scales, g_rots, g_opac, g_cols = call(
        functools.partial(pull_kernel, passes, cams, tiles, rows, cap, aligned),
        [shaped(3, columns), shaped(3, columns), shaped(4, columns), shaped(rows, LANES), shaped(*colors.shape)],
        [coming, inverse, turns, raw, kept],
        out_specs=[far] * 5,
        scratch=[pltpu.VMEM((RAW * rows, LANES), F32)]
        + [pltpu.VMEM(shape, F32) for shape in ((3, columns), (3, columns), (4, columns), (rows, LANES), colors.shape)]
        + [pltpu.SemaphoreType.DMA((7,))],
    )
    return (g_pos, g_scales, g_rots, g_opac.reshape(columns), g_cols)


def solution(mesh):
    return jax.shard_map(
        functools.partial(body, mesh.shape["cam"], mesh.shape["tile"]),
        mesh=mesh,
        in_specs=(
            P(None, ("cam", "tile")),
            P(None, ("cam", "tile")),
            P(None, ("cam", "tile")),
            P(("cam", "tile")),
            P(None, ("cam", "tile")),
            P(),
            P(None, "cam", "tile", None, None),
            P(None, "cam", "tile"),
            P(None, "cam", "tile"),
            P(None, "cam", "tile", None),
            P(None, "cam", "tile", None, None, None),
        ),
        out_specs=(
            P(None, ("cam", "tile")),
            P(None, ("cam", "tile")),
            P(None, ("cam", "tile")),
            P(("cam", "tile")),
            P(None, ("cam", "tile")),
        ),
        check_vma=False,
    )
```

```python
import functools

import jax
import jax.numpy as jnp
from jax import lax
from jax.experimental import pallas as pl
from jax.experimental.pallas import tpu as pltpu
from jax.sharding import PartitionSpec as P

FOCAL = 4096.0
CENTER_X = 2048.0
CENTER_Y = 1024.0
SH_ZERO = 0.28209479177387814
SH_ONE = 0.4886025119029199
SH_TWO = [
    1.0925484305920792,
    -1.0925484305920792,
    0.31539156525252005,
    -1.0925484305920792,
    0.5462742152960396,
]
SH_THREE = [
    -0.5900435899266435,
    2.890611442640554,
    -0.4570457994644658,
    0.3731763325901154,
    -0.4570457994644658,
    1.445305721320277,
    -0.5900435899266435,
]
LANES = 128
HALF = LANES // 2
FIELDS = 9
SENT = 5
GROUP = 8
RAW = 59
KEPT = 42
SHADE = 18
SCENE = 6
TERMS = 15
F32 = jnp.float32
BF16 = jnp.bfloat16


def dot(left, right, contract):
    return lax.dot_general(left, right, ((contract[0], contract[1]), ((), ())), preferred_element_type=F32)


def split(x):
    high = x.astype(BF16)
    return high, (x - high.astype(F32)).astype(BF16)


def parted(x):
    return x & (LANES - 1), lax.shift_right_arithmetic(x, LANES.bit_length() - 1)


def lane_pick(source, index):
    return jnp.take_along_axis(source, index, axis=1, mode="promise_in_bounds")


def row_pick(source, index):
    return jnp.take_along_axis(source, index, axis=0, mode="promise_in_bounds")


def spin_of(quat):
    norm = jnp.sqrt(quat[0] * quat[0] + quat[1] * quat[1] + quat[2] * quat[2] + quat[3] * quat[3])
    back = 1.0 / norm
    w, x, y, z = [q * back for q in quat]
    spin = [
        [1.0 - 2.0 * (y * y + z * z), 2.0 * (x * y - w * z), 2.0 * (x * z + w * y)],
        [2.0 * (x * y + w * z), 1.0 - 2.0 * (x * x + z * z), 2.0 * (y * z - w * x)],
        [2.0 * (x * z - w * y), 2.0 * (y * z + w * x), 1.0 - 2.0 * (x * x + y * y)],
    ]
    return spin, (w, x, y, z), back


def world_cov(spin, squares):
    scaled = [[spin[i][k] * squares[k] for k in range(3)] for i in range(3)]
    cov = [[None] * 3 for _ in range(3)]
    for i in range(3):
        for j in range(i, 3):
            cov[i][j] = scaled[i][0] * spin[j][0] + scaled[i][1] * spin[j][1] + scaled[i][2] * spin[j][2]
            cov[j][i] = cov[i][j]
    return cov


def dot3(a, b):
    return a[0] * b[0] + a[1] * b[1] + a[2] * b[2]


def screen_of(point, cov, rotate, offset):
    m = [dot3(rotate[i], point) + offset[i] for i in range(3)]
    inverse = 1.0 / m[2]
    main = FOCAL * inverse
    at_x, at_y = m[0] * inverse, m[1] * inverse
    side_x, side_y = -main * at_x, -main * at_y
    t_x = [main * rotate[0][i] + side_x * rotate[2][i] for i in range(3)]
    t_y = [main * rotate[1][i] + side_y * rotate[2][i] for i in range(3)]
    w_x = [dot3(cov[i], t_x) for i in range(3)]
    w_y = [dot3(cov[i], t_y) for i in range(3)]
    s_xx = dot3(t_x, w_x) + 0.3
    s_xy = dot3(t_y, w_x)
    s_yy = dot3(t_y, w_y) + 0.3
    back = 1.0 / (s_xx * s_yy - s_xy * s_xy)
    conic = (s_yy * back, -s_xy * back, s_xx * back)
    return m, inverse, main, at_x, at_y, t_x, t_y, w_x, w_y, conic


def direction_of(point, center):
    toward = [point[j] - center[j] for j in range(3)]
    back = lax.rsqrt(dot3(toward, toward))
    return [t * back for t in toward], back


def basis_of(x, y, z):
    xx, yy, zz = x * x, y * y, z * z
    xy, yz, xz = x * y, y * z, x * z
    less = xx - yy
    four = 4.0 * zz - xx - yy
    return [
        None,
        -SH_ONE * y,
        SH_ONE * z,
        -SH_ONE * x,
        SH_TWO[0] * xy,
        SH_TWO[1] * yz,
        SH_TWO[2] * (2.0 * zz - xx - yy),
        SH_TWO[3] * xz,
        SH_TWO[4] * less,
        SH_THREE[0] * y * (3.0 * xx - yy),
        SH_THREE[1] * xy * z,
        SH_THREE[2] * y * four,
        SH_THREE[3] * z * (2.0 * zz - 3.0 * xx - 3.0 * yy),
        SH_THREE[4] * x * four,
        SH_THREE[5] * z * less,
        SH_THREE[6] * x * (xx - 3.0 * yy),
    ]


def slope_terms(c):
    d = [None] * 4 + [SH_TWO[i] * c[4 + i] for i in range(5)] + [SH_THREE[i] * c[9 + i] for i in range(7)]
    first = [-SH_ONE * c[3], -SH_ONE * c[1], SH_ONE * c[2]]
    in_x = (2.0 * (d[8] - d[6]), 6.0 * d[9] - 2.0 * d[11], 2.0 * d[14] - 6.0 * d[12], 3.0 * d[15])
    in_y = (-2.0 * (d[8] + d[6]), 3.0 * d[9], -2.0 * d[14] - 6.0 * d[12], -2.0 * d[13] - 6.0 * d[15])
    in_z = (4.0 * d[6], 8.0 * d[11], 8.0 * d[13])
    return d, first, in_x, in_y, in_z


def slope_of(x, y, z, terms):
    d, first, in_x, in_y, in_z = terms
    xx, yy, zz = x * x, y * y, z * z
    xy, yz, xz = x * y, y * z, x * z
    less, both = xx - yy, xx + yy
    four = 4.0 * zz - both
    g_x = (
        first[0] + d[4] * y + in_x[0] * x + d[7] * z + in_x[1] * xy + d[10] * yz + in_x[2] * xz
        + d[13] * (four - 2.0 * xx) + in_x[3] * less
    )
    g_y = (
        first[1] + d[4] * x + d[5] * z + in_y[0] * y + in_y[1] * less + d[10] * xz + d[11] * (four - 2.0 * yy)
        + in_y[2] * yz + in_y[3] * xy
    )
    g_z = (
        first[2] + d[5] * y + in_z[0] * z + d[7] * x + d[10] * xy + in_z[1] * yz + d[12] * (6.0 * zz - 3.0 * both)
        + in_z[2] * xz + d[14] * less
    )
    return [g_x, g_y, g_z]


def camera_rows(cam_ref, table, passes, cams):
    views = passes * cams
    for p in range(passes):
        cam = cam_ref[p]
        cos, sin = jnp.cos(cam), jnp.sin(cam)
        ca, cb, cg = [cos[:, k : k + 1] for k in range(3)]
        sa, sb, sg = [sin[:, k : k + 1] for k in range(3)]
        rotate = [
            [cg * cb, cg * sb * sa - sg * ca, cg * sb * ca + sg * sa],
            [sg * cb, sg * sb * sa + cg * ca, sg * sb * ca - cg * sa],
            [-sb, cb * sa, cb * ca],
        ]
        offset = [cam[:, 3:4], cam[:, 4:5], 6.0 + cam[:, 5:6]]
        center = [-(rotate[0][j] * offset[0] + rotate[1][j] * offset[1] + rotate[2][j] * offset[2]) for j in range(3)]
        for k, term in enumerate(rotate[0] + rotate[1] + rotate[2] + offset + center):
            table[k * views + p * cams : k * views + (p + 1) * cams, :] = jnp.broadcast_to(term, (cams, LANES))


def camera_of(table, view, views, shape):
    terms = [jnp.broadcast_to(table[k * views + view : k * views + view + 1, :], shape) for k in range(TERMS)]
    return [terms[0:3], terms[3:6], terms[6:9]], terms[9:12], terms[12:15]


def project_kernel(
    passes, cams, rows, owners, cap, folded, cols, far_pos, far_scales, far_rots, far_opac, far_cam, far_lists, far_wanted,
    far_counts, far_places, rec, raw, kept, scene, source, chosen,
    table, pos, scales, rots, opac, cam, lists, wanted, counts, places, done,
):
    views = passes * cams
    shape = (rows, LANES)
    fars = (far_cam, far_pos, far_scales, far_rots, far_opac, far_lists, far_wanted, far_counts, far_places)
    nears = (cam, pos, scales, rots, opac, lists, wanted, counts, places)
    copies = [pltpu.make_async_copy(away, near, done.at[k]) for k, (away, near) in enumerate(zip(fars, nears))]
    for copy in copies:
        copy.start()
    for i in range(rows):
        raw[pl.ds(11 * rows + i, cols.shape[0], stride=rows), :] = cols[:, i * LANES : (i + 1) * LANES]
    for copy in copies[:5]:
        copy.wait()
    camera_rows(cam, table, passes, cams)
    base = 0
    for ref in (pos, scales, rots):
        count = ref.shape[0]
        for i in range(rows):
            raw[pl.ds(base * rows + i, count, stride=rows), :] = ref[:, i * LANES : (i + 1) * LANES]
        base += count
    raw[base * rows : (base + 1) * rows, :] = opac[...]

    def at(k):
        return raw[k * rows : (k + 1) * rows, :]

    def put(ref, k, value):
        ref[k * rows : (k + 1) * rows, :] = value

    point = [at(k) for k in range(3)]
    squares = [jnp.exp(2.0 * at(3 + k)) for k in range(3)]
    spin, _, _ = spin_of([at(6 + k) for k in range(4)])
    cov = world_cov(spin, squares)
    opacity = 1.0 / (1.0 + jnp.exp(-at(10)))
    sight = []
    for view in range(views):
        rotate, offset, center = camera_of(table, view, views, shape)
        _, inv, main, at_x, at_y, t_x, t_y, w_x, w_y, conic = screen_of(point, cov, rotate, offset)
        direction, back = direction_of(point, center)
        basis = basis_of(*direction)
        fields = [FOCAL * at_x + CENTER_X, FOCAL * at_y + CENTER_Y, conic[0], conic[1], conic[2], opacity]
        for f, value in enumerate(fields):
            put(rec, view * FIELDS + f, value)
        r_x, r_y = [[dot3(rotate[i], w) for i in range(3)] for w in (w_x, w_y)]
        moves = []
        for g_main, g_sx, g_sy in (
            (2.0 * r_x[0], 2.0 * r_x[2], 0.0),
            (r_y[0] + r_x[1], r_y[2], r_x[2]),
            (2.0 * r_y[1], 0.0, 2.0 * r_y[2]),
        ):
            g_m = [g_sx, g_sy, g_main - 2.0 * (at_x * g_sx + at_y * g_sy)]
            size = -main * inv
            moves += [size * (rotate[0][j] * g_m[0] + rotate[1][j] * g_m[1] + rotate[2][j] * g_m[2]) for j in range(3)]
        sight.append((direction, back))
        for k, value in enumerate([*t_x, *t_y, *conic, *moves]):
            put(kept, view * KEPT + k, value)
        for k in range(1, 16):
            put(kept, view * KEPT + KEPT - 16 + k, basis[k])

    for copy in copies[5:]:
        copy.wait()
    entries, pixels = lists.shape[-1], wanted.shape[-1]
    entry_row = lax.broadcasted_iota(jnp.int32, (1, entries), 1)
    slot_owner, slot_lane = [], []
    for p in range(passes):
        for k in range(3):
            scene[p * SCENE + k : p * SCENE + k + 1, :] = wanted[p, k]
        count = jnp.broadcast_to(counts[:, p : p + 1], (1, entries))
        scene[p * SCENE + 3 : p * SCENE + 4, :] = jnp.where(entry_row < count, 1.0, 0.0)
        place = jnp.broadcast_to(places[:, p : p + 1], (1, entries))
        for k, value in enumerate((place % 256 * 16 + 8, place // 256 * 16 + 8)):
            scene[p * SCENE + 4 + k : p * SCENE + 5 + k, :] = value.astype(F32)
        owner, place = lax.div(lists[p, 0], cap), lax.rem(lists[p, 0], cap)
        if folded:
            groups = LANES // cap
            slot_owner.append(lax.div(owner, groups))
            slot_lane.append(lax.rem(owner + p, groups) * cap + place)
        else:
            slot_owner.append(owner)
            slot_lane.append(place + p * cap)
        chosen[p : p + 1, :] = slot_owner[p]
        chosen[passes + p : passes + p + 1, :] = slot_lane[p]
    pair = (LANES, LANES)
    turned = lax.broadcasted_iota(jnp.int32, pair, 0) & (LANES - 1 if folded else HALF - 1)
    entry = (lax.broadcasted_iota(jnp.int32, pair, 1) + 1).astype(F32)
    lines = GROUP if folded else owners
    line_at = lax.broadcasted_iota(jnp.int32, (lines, LANES), 0)
    halves = entries // LANES
    found = jnp.full((lines, LANES), -LANES, jnp.int32)
    for p in range(passes):
        for h in range(halves):
            part = slice(h * LANES, (h + 1) * LANES)
            mine = jnp.where(jnp.broadcast_to(slot_owner[p][:, part], (lines, LANES)) == line_at, 1.0, 0.0).astype(BF16)
            here = jnp.where(jnp.broadcast_to(slot_lane[p][:, part], pair) == turned, entry, 0.0).astype(BF16)
            hit = dot(mine, here, ((1,), (1,)))
            found = jnp.where(hit > 0.5, hit.astype(jnp.int32) + ((p * halves + h) * LANES - 1), found)
        if folded:
            source[p * GROUP : (p + 1) * GROUP, :] = found
            source[(passes + p) * GROUP : (passes + p + 1) * GROUP, :] = pltpu.roll(found, HALF, 1)
            found = jnp.full((lines, LANES), -LANES, jnp.int32)
    if not folded:
        source[...] = found

    for channel in range(3):
        totals = [0.5 + SH_ZERO * at(11 + channel)] * views
        for k in range(1, 16):
            color = at(11 + 3 * k + channel)
            for view in range(views):
                start = (view * KEPT + KEPT - 16 + k) * rows
                totals[view] = totals[view] + kept[start : start + rows, :] * color
        for view in range(views):
            put(rec, view * FIELDS + 6 + channel, totals[view])
    for channel in range(3):
        terms = slope_terms([at(11 + 3 * k + channel) for k in range(16)])
        for view in range(views):
            direction, back = sight[view]
            slope = slope_of(*direction, terms)
            along = dot3(direction, slope)
            for j in range(3):
                put(kept, view * KEPT + SHADE + 3 * channel + j, (slope[j] - direction[j] * along) * back)


def lane_pass(shape, cap):
    lane = lax.broadcasted_iota(jnp.int32, shape, 1) & (HALF - 1)
    return lax.div(lane, cap)


def ids_kernel(passes, cams, rows, cap, folded, ids, *refs):
    count = (len(refs) - 6) // 2
    sources, out, results = refs[:count], refs[count], refs[count + 1 : 2 * count + 1]
    landed, lines, ids_done, out_done, done = refs[2 * count + 1 :]
    firsts = [pltpu.make_async_copy(ids.at[p], landed.at[p], ids_done.at[p]) for p in range(passes)]
    for first in firsts:
        first.start()
    copies = [pltpu.make_async_copy(source, result, done.at[k]) for k, (source, result) in enumerate(zip(sources, results))]
    for copy in copies:
        copy.start()
    for first in firsts:
        first.wait()
    for c in range(cams):
        parts = [landed[p, 0, 0, c] for p in range(passes)]
        tiles = parts[0].shape[0]
        if passes * cap < HALF:
            parts.append(jnp.zeros((tiles, HALF - passes * cap), jnp.int32))
        line = jnp.concatenate(parts + parts, axis=1)
        if folded:
            at_row, at_lane = [lax.broadcasted_iota(jnp.int32, line.shape, k) for k in range(2)]
            for m in range(1, passes):
                turned = parts[-m:] + parts[:-m]
                line = jnp.where(lax.rem(at_row, passes) == m, jnp.concatenate(turned + turned, axis=1), line)
            line = line + ((lax.div(at_lane, cap) - at_row) & (LANES // cap - 1)) * (rows * LANES)
        lines[c * tiles : (c + 1) * tiles, :] = line
    last = pltpu.make_async_copy(lines, out, out_done)
    last.start()
    for copy in copies:
        copy.wait()
    last.wait()


def pick_kernel(passes, cams, tiles, rows, cap, aligned, folded, ids, rec, out, inverse, turns):
    shape = (GROUP, LANES)
    lane = lax.broadcasted_iota(jnp.int32, shape, 1)
    sub = lax.broadcasted_iota(jnp.int32, shape, 0)
    if not aligned:
        turns[...] = jnp.zeros(turns.shape, jnp.int32)

    def packets(first, c):
        low, high = parted(ids[pl.ds(first, GROUP), :])
        if folded:
            tag, high = lax.div(high, rows), lax.rem(high, rows)
            lane_p, first_half = lax.rem(tag, passes), tag < passes
            blocks = [
                jnp.broadcast_to(jnp.max(jnp.where(lane_p == p, high, 0), axis=1, keepdims=True), shape)
                for p in range(passes)
            ]
        else:
            lane_p, first_half = lane_pass(shape, cap), lane < HALF
            blocks = [jnp.broadcast_to(high[:, p * cap : p * cap + 1], shape) for p in range(passes)]
        if aligned:
            for p in range(passes):
                turn = jnp.zeros(shape, jnp.int32)
                for t in range(1, tiles):
                    turn = jnp.where(jnp.broadcast_to(blocks[p][t : t + 1, :], shape) == sub, t, turn)
                turns[(p * cams + c) * rows : (p * cams + c + 1) * rows, :] = turn

        def pick(f):
            found = jnp.zeros(shape, F32)
            for p in range(passes):
                start = ((p * cams + c) * FIELDS + f) * rows
                if aligned:
                    own = lane_pick(row_pick(rec[start : start + rows, :], blocks[p]), low)
                else:
                    own = jnp.zeros(shape, F32)
                    for b in range(rows):
                        line = jnp.broadcast_to(rec[start + b : start + b + 1, :], shape)
                        own = jnp.where(high == b, lane_pick(line, low), own)
                found = own if p == 0 else jnp.where(lane_p == p, own, found)
            return found

        for r in range(SENT):
            value = pick(2 * r)
            if 2 * r + 1 < FIELDS:
                value = jnp.where(first_half, value, pick(2 * r + 1))
            out[pl.ds(first * SENT + r, GROUP, stride=SENT), :] = value

    for c in range(cams):
        if tiles == GROUP:
            packets(c * tiles, c)
        else:

            def step(k, carry, c=c):
                packets(pl.multiple_of(c * tiles + k * GROUP, GROUP), c)
                return carry

            lax.fori_loop(0, tiles // GROUP, step, 0)

    square = (LANES, LANES)
    column = lax.broadcasted_iota(jnp.int32, square, 0)
    turn = lax.broadcasted_iota(jnp.int32, square, 1)
    place = ((turn & (HALF - 1)) + 1 + jnp.where(turn < HALF, 0, LANES)).astype(F32)
    if folded:
        tag = lax.div(parted(jnp.broadcast_to(ids[0:1, :], square))[1], rows)
        place = (jnp.where(tag < passes, turn, ((turn + HALF) & (LANES - 1)) + LANES) + 1).astype(F32)
    wide = (passes * rows, LANES)
    wide_lane = lax.broadcasted_iota(jnp.int32, wide, 1)
    key = lax.broadcasted_iota(jnp.int32, wide, 0)
    lane_key = jnp.where((wide_lane & (HALF - 1)) < passes * cap, lane_pass(wide, cap) * rows, -(1 << 20))
    line_lane = lax.broadcasted_iota(jnp.int32, (1, LANES), 1)

    def two(c, t, found):
        these, next_ones = ids[pl.ds(c * tiles + t, 1), :], ids[pl.ds(c * tiles + t + 1, 1), :]
        if folded:
            low, high = parted(jnp.where(these < passes * rows * LANES, these, next_ones))
            high = lax.rem(high, rows * passes)
        else:
            low, high = parted(jnp.where(line_lane < HALF, these, next_ones))
        low = jnp.broadcast_to(low, square)
        high = jnp.broadcast_to(high, wide)
        match = jnp.where(low == column, place, 0.0).astype(BF16)
        owner = jnp.where((high if folded else high + lane_key) == key, 1.0, 0.0).astype(BF16)
        hit = dot(owner, match, ((1,), (1,)))
        return jnp.where(hit > 0.5, hit.astype(jnp.int32) + t * LANES, found)

    for c in range(cams):
        found = jnp.zeros(wide, jnp.int32)
        if tiles <= 8:
            for t in range(0, tiles, 2):
                found = two(c, t, found)
        else:
            found = lax.fori_loop(0, tiles // 2, lambda t, f, c=c: two(c, 2 * t, f), found)
        for p in range(passes):
            start = (p * cams + c) * rows
            inverse[start : start + rows, :] = found[p * rows : (p + 1) * rows, :]


def render_kernel(passes, owners, cap, folded, entries, pixels, got, lists, scene, source, out, *scratch):
    alphas, ratios, weights, pulls, before_sums, slopes, after_sums = [scratch[k * passes : (k + 1) * passes] for k in range(7)]
    clears, shares, pulled_parts = [
        [scratch[(7 + 2 * k) * passes + p :: passes][:2] for p in range(passes)] for k in range(3)
    ]
    halves = entries // LANES
    shape = (GROUP, LANES)
    wide = 16
    lane = lax.broadcasted_iota(jnp.int32, shape, 1)
    sub = lax.broadcasted_iota(jnp.int32, shape, 0)

    slot_owner, slot_lane = [], []
    for p in range(passes):
        for h in range(halves):
            part = slice(h * LANES, (h + 1) * LANES)
            slot_owner.append(jnp.broadcast_to(lists[p : p + 1, part], shape))
            slot_lane.append(jnp.broadcast_to(lists[passes + p : passes + p + 1, part], shape))
    total = passes * halves

    groups = LANES // cap
    lane_group = lax.div(lane, cap)

    def merged(choices, back):
        value = choices[-back % groups]
        for g in range(1, groups):
            value = jnp.where(lane_group == g, choices[(g - back) % groups], value)
        return value

    def gather(g, found):
        mine = [slot_owner[i] == g * GROUP + sub for i in range(total)]
        new = []
        for f in range(FIELDS):
            lines = got[pl.ds(g * (GROUP * SENT) + f // 2, GROUP, stride=SENT), :]
            for i in range(total):
                new.append(jnp.where(mine[i], lane_pick(lines, slot_lane[i] + f % 2 * HALF), found[f * total + i]))
        return tuple(new)

    fields = tuple(jnp.zeros(shape, F32) for _ in range(FIELDS * total))
    if folded:
        mine = [slot_owner[i] == sub for i in range(total)]
        places = [slot_lane, [(x + HALF) & (LANES - 1) for x in slot_lane]]
        fields = []
        for f in range(FIELDS):
            packets = [got[pl.ds(m * SENT + f // 2, GROUP, stride=groups * SENT), :] for m in range(groups)]
            for p in range(passes):
                tile = merged(packets, f % 2 * passes + p)
                for i in range(p * halves, (p + 1) * halves):
                    fields.append(jnp.where(mine[i], lane_pick(tile, places[f % 2][i]), 0.0))
    elif owners <= 32:
        for g in range(owners // GROUP):
            fields = gather(g, fields)
    else:
        fields = lax.fori_loop(0, owners // GROUP, gather, fields)
    fields = [jnp.sum(x, axis=0, keepdims=True) for x in fields]

    row_at, column_at = [lax.broadcasted_iota(jnp.int32, (entries, entries), k) for k in range(2)]
    before = jnp.where(row_at < column_at, 1.0, 0.0).astype(BF16)
    after = jnp.where(row_at > column_at, 1.0, 0.0).astype(BF16)
    column_x = lax.broadcasted_iota(jnp.int32, (wide, entries), 0).astype(F32) - 7.5
    steps = [slice(y * wide, (y + 1) * wide) for y in range(pixels // wide)]

    lines, spans = [], []
    for p in range(passes):
        line = [
            jnp.concatenate([fields[f * total + p * halves + h] for h in range(halves)], axis=1) for f in range(FIELDS)
        ]
        line[0] = line[0] - scene[p * SCENE + 4 : p * SCENE + 5, :]
        line[1] = line[1] - scene[p * SCENE + 5 : p * SCENE + 6, :]
        lines.append(line)
        spans.append(column_x - line[0])

    def offset_y(p, y):
        return (y - 7.5) - lines[p][1]

    def through(parts, at, matrix):
        return dot(parts[0][at, :], matrix, ((1,), (0,))) + dot(parts[1][at, :], matrix, ((1,), (0,)))

    consts = []
    for p in range(passes):
        _, _, c_a, c_b, c_c, base = lines[p][:6]
        live = base * scene[p * SCENE + 3 : p * SCENE + 4, :]
        consts.append((live, (-0.5 * c_a) * spans[p] * spans[p], -c_b * spans[p], 0.5 * c_c))

    def blend(p, y, at):
        live, q_xx, q_x, c_c = consts[p]
        d_y = offset_y(p, y)
        alpha = live * jnp.exp(q_xx + (q_x * d_y - c_c * d_y * d_y))
        clear = jnp.log(1.0 - alpha)
        alphas[p][at, :] = alpha
        ratios[p][at, :] = alpha * jnp.exp(-clear)
        clears[p][0][at, :], clears[p][1][at, :] = split(clear)

    def weigh(p, y, at):
        weight = alphas[p][at, :] * jnp.exp(before_sums[p][at, :])
        weights[p][at, :] = weight
        shares[p][0][at, :], shares[p][1][at, :] = split(weight)

    def pull(p, y, at):
        pulled = weights[p][at, :] * slopes[p][at, :]
        pulls[p][at, :] = pulled
        pulled_parts[p][0][at, :], pulled_parts[p][1][at, :] = split(pulled)

    totals = [[jnp.zeros((wide, entries), F32)] * 3 for _ in range(passes)]

    def add(p, y, at):
        m_1, m_y, m_yy = totals[p]
        grad = pulls[p][at, :] - ratios[p][at, :] * after_sums[p][at, :]
        d_y = offset_y(p, y)
        grad_y = grad * d_y
        totals[p] = [m_1 + grad, m_y + grad_y, m_yy + grad_y * d_y]

    blocks = [slice(n, n + 128) for n in range(0, pixels, 128)]
    both = range(passes)

    def each(work, p, block):
        for y, at in enumerate(steps):
            if block.start <= at.start < block.stop:
                work(p, y, at)

    def sum_before(p, block):
        before_sums[p][block, :] = through(clears[p], block, before)

    def sum_after(p, block):
        after_sums[p][block, :] = through(pulled_parts[p], block, after)

    def slope(p, block):
        r_high, r_low = [r[:, block] for r in residuals[p]]
        slopes[p][block, :] = dot(jnp.concatenate([r_high, r_high, r_low], axis=0), pair_rows[p], ((0,), (0,)))

    def emit(first, second, third):
        jobs = [(block, p) for block in blocks for p in both]
        depth = 2
        for n in range(len(jobs) + 2 * depth):
            if n < len(jobs) and first:
                each(first, jobs[n][1], jobs[n][0])
            if 0 <= n - depth < len(jobs):
                second(jobs[n - depth][1], jobs[n - depth][0])
            if 0 <= n - 2 * depth < len(jobs):
                each(third, jobs[n - 2 * depth][1], jobs[n - 2 * depth][0])

    emit(blend, sum_before, weigh)
    residuals, pair_rows = [], []
    for p in both:
        c_high, c_low = split(jnp.concatenate(lines[p][6:9], axis=0))
        pair = dot(jnp.concatenate([c_high, c_low], axis=0), shares[p][0][...], ((1,), (1,)))
        shown = pair[0:3, :] + pair[3:6, :] + dot(c_high, shares[p][1][...], ((1,), (1,)))
        residuals.append(split(shown - scene[p * SCENE : p * SCENE + 3, :]))
        pair_rows.append(jnp.concatenate([c_high, c_low, c_high], axis=0))
    for block in blocks:
        for p in both:
            slope(p, block)
    emit(pull, sum_after, add)
    color_grads = []
    for p in both:
        r_high, r_low = residuals[p]
        pair = dot(jnp.concatenate([r_high, r_low], axis=0), shares[p][0][...], ((1,), (0,)))
        color_grads.append(pair[0:3, :] + pair[3:6, :] + dot(r_high, shares[p][1][...], ((1,), (0,))))
    grads = []
    for p in both:
        m_1, m_y, m_yy = totals[p]
        d_x = spans[p]
        m_x = m_1 * d_x
        s_1, s_x, s_y, s_xx, s_xy, s_yy = [
            jnp.sum(m, axis=0, keepdims=True) for m in (m_1, m_x, m_y, m_x * d_x, m_y * d_x, m_yy)
        ]
        _, _, c_a, c_b, c_c, base = lines[p][:6]
        grads.append(
            [
                c_a * s_x + c_b * s_y,
                c_b * s_x + c_c * s_y,
                -0.5 * s_xx,
                -s_xy,
                -0.5 * s_yy,
                s_1 / base,
                color_grads[p][0:1, :],
                color_grads[p][1:2, :],
                color_grads[p][2:3, :],
            ]
        )

    def pick(f, which, index, tiles):
        found = jnp.zeros(shape, F32)
        for p, h in tiles:
            line = jnp.broadcast_to(grads[p][f][:, h * LANES : (h + 1) * LANES], shape)
            found = jnp.where(which == p * halves + h, lane_pick(line, index), found)
        return found

    if folded:
        codes = [parted(source[n * GROUP : (n + 1) * GROUP, :]) for n in range(2 * passes)]
        for r in range(SENT):
            parts = []
            for n, (index, which) in enumerate(codes):
                p, f = n % passes, min(2 * r + n // passes, FIELDS - 1)
                parts.append(pick(f, which, index, [(p, h) for h in range(halves)]) if 2 * r + n // passes < FIELDS else parts[p])
            for m in range(groups):
                out[pl.ds(m * SENT + r, GROUP, stride=groups * SENT), :] = merged(parts, m)
        return

    every = [(p, h) for p in range(passes) for h in range(halves)]
    for g in range(owners // GROUP):
        index, which = parted(source[g * GROUP : (g + 1) * GROUP, :])
        for r in range(SENT):
            value = pick(2 * r, which, index, every)
            if 2 * r + 1 < FIELDS:
                value = jnp.where(lane < HALF, value, pick(2 * r + 1, which, index, every))
            out[pl.ds(g * GROUP * SENT + r, GROUP, stride=SENT), :] = value


def pull_kernel(
    passes, cams, tiles, rows, cap, aligned, got, inverse, turns, raw, kept,
    far_pos, far_scales, far_rots, far_opac, far_cols, total, pos, scales, rots, opac, cols, done,
):
    views = passes * cams
    shape = (rows, LANES)

    def at(k):
        return raw[k * rows : (k + 1) * rows, :]

    def fetcher(view):
        p, c = view // cams, view % cams
        slot = inverse[view * rows : (view + 1) * rows, :] - 1
        valid = slot >= 0
        slot_lane, slot_t = parted(jnp.maximum(slot, 0))
        row_t = turns[view * rows : (view + 1) * rows, :]
        turned = {}

        def fetch(f):
            row, shift = f // 2, f % 2 * HALF
            if aligned:
                if row not in turned:
                    turned[row] = row_pick(got[pl.ds(c * tiles * SENT + row, tiles, stride=SENT), :], row_t)
                return jnp.where(valid, lane_pick(turned[row], (slot_lane + shift) & (LANES - 1)), 0.0)

            def one(t, found):
                line = jnp.broadcast_to(got[pl.ds((c * tiles + t) * SENT + row, 1), :], shape)
                return jnp.where(valid & (slot_t == t), lane_pick(line, (slot_lane + shift) & (LANES - 1)), found)

            return lax.fori_loop(0, tiles, one, jnp.zeros(shape, F32))

        return fetch

    def held(view, k):
        start = (view * KEPT + k) * rows
        return kept[start : start + rows, :]

    fetchers = [fetcher(view) for view in range(views)]
    shades = [[fetchers[view](6 + channel) for view in range(views)] for channel in range(3)]
    copies = []

    def send(near, away):
        copies.append(pltpu.make_async_copy(near, away, done.at[len(copies)]))
        copies[-1].start()

    sent = 0
    for k in range(16):
        basis = [held(view, KEPT - 16 + k) for view in range(views)] if k else None
        for channel in range(3):
            terms = shades[channel] if k == 0 else [basis[view] * shades[channel][view] for view in range(views)]
            while len(terms) > 1:
                terms = [sum(terms[n : n + 2][1:], terms[n]) for n in range(0, len(terms), 2)]
            start = (11 + 3 * k + channel) * rows
            total[start : start + rows, :] = terms[0] if k else SH_ZERO * terms[0]
        ready = (3 * k + 3) // 16 * 16
        if ready > sent:
            for i in range(rows):
                cols[sent:ready, i * LANES : (i + 1) * LANES] = total[pl.ds((11 + sent) * rows + i, ready - sent, stride=rows), :]
            send(cols.at[pl.ds(sent, ready - sent), :], far_cols.at[pl.ds(sent, ready - sent), :])
            sent = ready

    squares = [jnp.exp(2.0 * at(3 + k)) for k in range(3)]
    spin, quat, quat_back = spin_of([at(6 + k) for k in range(4)])

    g_point = [jnp.zeros(shape, F32) for _ in range(3)]
    g_cov = [[jnp.zeros(shape, F32) for _ in range(3)] for _ in range(3)]
    g_opacity = jnp.zeros(shape, F32)
    for view in range(views):
        g = [fetchers[view](f) for f in range(6)] + [shades[channel][view] for channel in range(3)]
        t_x, t_y, conic, m_xx, m_xy, m_yy, s_r, s_g, s_b = [[held(view, 3 * n + k) for k in range(3)] for n in range(9)]
        c_a, c_b, c_c = conic
        half = 0.5 * g[3]
        p00, p01 = g[2] * c_a + half * c_b, g[2] * c_b + half * c_c
        p10, p11 = half * c_a + g[4] * c_b, half * c_b + g[4] * c_c
        g_xx = -(c_a * p00 + c_b * p10)
        g_xy = -(c_a * p01 + c_b * p11)
        g_yy = -(c_b * p01 + c_c * p11)
        left = [g_xx * t_x[i] + g_xy * t_y[i] for i in range(3)]
        right = [g_yy * t_y[i] + g_xy * t_x[i] for i in range(3)]
        for i in range(3):
            for j in range(i, 3):
                g_cov[i][j] = g_cov[i][j] + (t_x[i] * left[j] + t_y[i] * right[j])
        pulls = ((t_x, g[0]), (t_y, g[1]), (m_xx, g_xx), (m_xy, 2.0 * g_xy), (m_yy, g_yy), (s_r, g[6]), (s_g, g[7]), (s_b, g[8]))
        for j in range(3):
            for slope, value in pulls:
                g_point[j] = g_point[j] + slope[j] * value
        g_opacity = g_opacity + g[5]
    for i in range(3):
        for j in range(i):
            g_cov[i][j] = g_cov[j][i]

    g_scales = []
    g_spin = [[None] * 3 for _ in range(3)]
    for k in range(3):
        column = [spin[j][k] for j in range(3)]
        turned = [dot3(g_cov[i], column) for i in range(3)]
        g_scales.append(2.0 * squares[k] * dot3(column, turned))
        for i in range(3):
            g_spin[i][k] = 2.0 * squares[k] * turned[i]
    w, x, y, z = quat
    d = g_spin
    g_quat = [
        2.0 * (z * (d[1][0] - d[0][1]) + y * (d[0][2] - d[2][0]) + x * (d[2][1] - d[1][2])),
        2.0 * (y * (d[0][1] + d[1][0]) + z * (d[0][2] + d[2][0]) + w * (d[2][1] - d[1][2]) - 2.0 * x * (d[1][1] + d[2][2])),
        2.0 * (x * (d[0][1] + d[1][0]) + z * (d[1][2] + d[2][1]) + w * (d[0][2] - d[2][0]) - 2.0 * y * (d[0][0] + d[2][2])),
        2.0 * (x * (d[0][2] + d[2][0]) + y * (d[1][2] + d[2][1]) + w * (d[1][0] - d[0][1]) - 2.0 * z * (d[0][0] + d[1][1])),
    ]
    along = w * g_quat[0] + x * g_quat[1] + y * g_quat[2] + z * g_quat[3]
    g_rots = [(g_quat[k] - quat[k] * along) * quat_back for k in range(4)]
    opacity = 1.0 / (1.0 + jnp.exp(-at(10)))
    opac[...] = g_opacity * opacity * (1.0 - opacity)
    for k, value in enumerate(g_point + g_scales + g_rots):
        total[k * rows : (k + 1) * rows, :] = value
    base = 0
    for ref in (pos, scales, rots):
        count = ref.shape[0]
        for i in range(rows):
            ref[:, i * LANES : (i + 1) * LANES] = total[pl.ds(base * rows + i, count, stride=rows), :]
        base += count
    for near, away in ((pos, far_pos), (scales, far_scales), (rots, far_rots), (opac, far_opac)):
        send(near, away)
    for copy in copies:
        copy.wait()


def render_scratch(passes, pixels, entries):
    return [pltpu.VMEM((pixels, entries), F32)] * (7 * passes) + [pltpu.VMEM((pixels, entries), BF16)] * (6 * passes)


def vmem(count):
    return [pl.BlockSpec(memory_space=pltpu.VMEM)] * count


def call(kernel, outs, operands, in_specs=None, scratch=(), flops=1_000_000, out_specs=None):
    return pl.pallas_call(
        kernel,
        out_shape=outs,
        in_specs=in_specs or vmem(len(operands)),
        out_specs=out_specs or jax.tree.map(lambda _: pl.BlockSpec(memory_space=pltpu.VMEM), outs),
        scratch_shapes=list(scratch),
        compiler_params=pltpu.CompilerParams(vmem_limit_bytes=32 << 20),
        cost_estimate=pl.CostEstimate(flops=flops, bytes_accessed=1 << 20, transcendentals=0),
    )(*operands)


def body(
    cams,
    tiles,
    positions,
    log_scales,
    rotations,
    opacities,
    colors,
    cameras,
    targets,
    tile_ids,
    tile_counts,
    tile_lists,
    fetch_ids,
):
    axes = ("cam", "tile")
    passes, cap = fetch_ids.shape[0], fetch_ids.shape[-1]
    entries, pixels = tile_lists.shape[-1], targets.shape[-1]
    columns = positions.shape[-1]
    rows = columns // LANES
    owners = cams * tiles
    views = passes * cams
    aligned = tiles == rows == GROUP
    folded = 2 * passes * cap == LANES and owners * cap == GROUP * LANES and tiles % (LANES // cap) == 0

    def shaped(*shape):
        return jax.ShapeDtypeStruct(shape, F32)

    def exchange(x):
        lines = x.reshape(owners, 1, -1)
        return lax.all_to_all(lines, axes, split_axis=0, concat_axis=0, tiled=True).reshape(x.shape)

    whole, smem, far = [pl.BlockSpec(memory_space=space) for space in (pltpu.VMEM, pltpu.SMEM, pltpu.HBM)]
    near = [colors]
    wanted_ids, *near = call(
        functools.partial(ids_kernel, passes, cams, rows, cap, folded),
        [jax.ShapeDtypeStruct((owners, LANES), jnp.int32)]
        + [pltpu.VMEM(x.shape, x.dtype) for x in near],
        [pltpu.with_memory_space_constraint(x, pltpu.HBM) for x in (fetch_ids, *near)],
        in_specs=[far] * (1 + len(near)),
        out_specs=[far] + [whole] * len(near),
        scratch=[
            pltpu.VMEM(fetch_ids.shape, jnp.int32),
            pltpu.VMEM((owners, LANES), jnp.int32),
            pltpu.SemaphoreType.DMA((passes,)),
            pltpu.SemaphoreType.DMA,
            pltpu.SemaphoreType.DMA((len(near),)),
        ],
    )
    arrived = exchange(wanted_ids)
    small = [
        positions,
        log_scales,
        rotations,
        opacities.reshape(rows, LANES),
        cameras,
        tile_lists,
        targets.reshape(passes, 3, 1, pixels),
        tile_counts.reshape(1, passes),
        tile_ids.reshape(1, passes),
    ]
    records, raw, kept, scene, source, lists = call(
        functools.partial(project_kernel, passes, cams, rows, owners, cap, folded),
        [
            shaped(views * FIELDS * rows, LANES),
            shaped(RAW * rows, LANES),
            shaped(views * KEPT * rows, LANES),
            shaped(passes * SCENE, entries),
            jax.ShapeDtypeStruct((2 * passes * GROUP if folded else owners, LANES), jnp.int32),
            jax.ShapeDtypeStruct((2 * passes, entries), jnp.int32),
        ],
        [*near, *[pltpu.with_memory_space_constraint(x, pltpu.HBM) for x in small]],
        in_specs=[whole] * 1 + [far] * len(small),
        scratch=[pltpu.VMEM((TERMS * views, LANES), F32)]
        + [pltpu.VMEM(x.shape, x.dtype) for x in small]
        + [pltpu.SemaphoreType.DMA((len(small),))],
    )
    codes = jax.ShapeDtypeStruct((views * rows, LANES), jnp.int32)
    packets, inverse, turns = call(
        functools.partial(pick_kernel, passes, cams, tiles, rows, cap, aligned, folded),
        [shaped(owners * SENT, LANES), codes, codes],
        [arrived, records],
    )
    fetched = exchange(packets)
    slot_grads = call(
        functools.partial(render_kernel, passes, owners, cap, folded, entries, pixels),
        shaped(owners * SENT, LANES),
        [fetched, lists, scene, source],
        scratch=render_scratch(passes, pixels, entries),
    )
    coming = exchange(slot_grads)
    g_pos, g_scales, g_rots, g_opac, g_cols = call(
        functools.partial(pull_kernel, passes, cams, tiles, rows, cap, aligned),
        [shaped(3, columns), shaped(3, columns), shaped(4, columns), shaped(rows, LANES), shaped(*colors.shape)],
        [coming, inverse, turns, raw, kept],
        out_specs=[far] * 5,
        scratch=[pltpu.VMEM((RAW * rows, LANES), F32)]
        + [pltpu.VMEM(shape, F32) for shape in ((3, columns), (3, columns), (4, columns), (rows, LANES), colors.shape)]
        + [pltpu.SemaphoreType.DMA((7,))],
    )
    return (g_pos, g_scales, g_rots, g_opac.reshape(columns), g_cols)


def solution(mesh):
    return jax.shard_map(
        functools.partial(body, mesh.shape["cam"], mesh.shape["tile"]),
        mesh=mesh,
        in_specs=(
            P(None, ("cam", "tile")),
            P(None, ("cam", "tile")),
            P(None, ("cam", "tile")),
            P(("cam", "tile")),
            P(None, ("cam", "tile")),
            P(),
            P(None, "cam", "tile", None, None),
            P(None, "cam", "tile"),
            P(None, "cam", "tile"),
            P(None, "cam", "tile", None),
            P(None, "cam", "tile", None, None, None),
        ),
        out_specs=(
            P(None, ("cam", "tile")),
            P(None, ("cam", "tile")),
            P(None, ("cam", "tile")),
            P(("cam", "tile")),
            P(None, ("cam", "tile")),
        ),
        check_vma=False,
    )
```

```python
import functools

import jax
import jax.numpy as jnp
from jax import lax
from jax.experimental import pallas as pl
from jax.experimental.pallas import tpu as pltpu
from jax.sharding import PartitionSpec as P

FOCAL = 4096.0
CENTER_X = 2048.0
CENTER_Y = 1024.0
SH_ZERO = 0.28209479177387814
SH_ONE = 0.4886025119029199
SH_TWO = [
    1.0925484305920792,
    -1.0925484305920792,
    0.31539156525252005,
    -1.0925484305920792,
    0.5462742152960396,
]
SH_THREE = [
    -0.5900435899266435,
    2.890611442640554,
    -0.4570457994644658,
    0.3731763325901154,
    -0.4570457994644658,
    1.445305721320277,
    -0.5900435899266435,
]
LANES = 128
HALF = LANES // 2
FIELDS = 9
SENT = 5
GROUP = 8
RAW = 59
KEPT = 42
SHADE = 18
SCENE = 6
TERMS = 15
F32 = jnp.float32
BF16 = jnp.bfloat16


def dot(left, right, contract):
    return lax.dot_general(left, right, ((contract[0], contract[1]), ((), ())), preferred_element_type=F32)


def split(x):
    high = x.astype(BF16)
    return high, (x - high.astype(F32)).astype(BF16)


def parted(x):
    return x & (LANES - 1), lax.shift_right_arithmetic(x, LANES.bit_length() - 1)


def lane_pick(source, index):
    return jnp.take_along_axis(source, index, axis=1, mode="promise_in_bounds")


def row_pick(source, index):
    return jnp.take_along_axis(source, index, axis=0, mode="promise_in_bounds")


def spin_of(quat):
    norm = jnp.sqrt(quat[0] * quat[0] + quat[1] * quat[1] + quat[2] * quat[2] + quat[3] * quat[3])
    back = 1.0 / norm
    w, x, y, z = [q * back for q in quat]
    spin = [
        [1.0 - 2.0 * (y * y + z * z), 2.0 * (x * y - w * z), 2.0 * (x * z + w * y)],
        [2.0 * (x * y + w * z), 1.0 - 2.0 * (x * x + z * z), 2.0 * (y * z - w * x)],
        [2.0 * (x * z - w * y), 2.0 * (y * z + w * x), 1.0 - 2.0 * (x * x + y * y)],
    ]
    return spin, (w, x, y, z), back


def world_cov(spin, squares):
    scaled = [[spin[i][k] * squares[k] for k in range(3)] for i in range(3)]
    cov = [[None] * 3 for _ in range(3)]
    for i in range(3):
        for j in range(i, 3):
            cov[i][j] = scaled[i][0] * spin[j][0] + scaled[i][1] * spin[j][1] + scaled[i][2] * spin[j][2]
            cov[j][i] = cov[i][j]
    return cov


def dot3(a, b):
    return a[0] * b[0] + a[1] * b[1] + a[2] * b[2]


def screen_of(point, cov, rotate, offset):
    m = [dot3(rotate[i], point) + offset[i] for i in range(3)]
    inverse = 1.0 / m[2]
    main = FOCAL * inverse
    at_x, at_y = m[0] * inverse, m[1] * inverse
    side_x, side_y = -main * at_x, -main * at_y
    t_x = [main * rotate[0][i] + side_x * rotate[2][i] for i in range(3)]
    t_y = [main * rotate[1][i] + side_y * rotate[2][i] for i in range(3)]
    w_x = [dot3(cov[i], t_x) for i in range(3)]
    w_y = [dot3(cov[i], t_y) for i in range(3)]
    s_xx = dot3(t_x, w_x) + 0.3
    s_xy = dot3(t_y, w_x)
    s_yy = dot3(t_y, w_y) + 0.3
    back = 1.0 / (s_xx * s_yy - s_xy * s_xy)
    conic = (s_yy * back, -s_xy * back, s_xx * back)
    return m, inverse, main, at_x, at_y, t_x, t_y, w_x, w_y, conic


def direction_of(point, center):
    toward = [point[j] - center[j] for j in range(3)]
    back = lax.rsqrt(dot3(toward, toward))
    return [t * back for t in toward], back


def basis_of(x, y, z):
    xx, yy, zz = x * x, y * y, z * z
    xy, yz, xz = x * y, y * z, x * z
    less = xx - yy
    four = 4.0 * zz - xx - yy
    return [
        None,
        -SH_ONE * y,
        SH_ONE * z,
        -SH_ONE * x,
        SH_TWO[0] * xy,
        SH_TWO[1] * yz,
        SH_TWO[2] * (2.0 * zz - xx - yy),
        SH_TWO[3] * xz,
        SH_TWO[4] * less,
        SH_THREE[0] * y * (3.0 * xx - yy),
        SH_THREE[1] * xy * z,
        SH_THREE[2] * y * four,
        SH_THREE[3] * z * (2.0 * zz - 3.0 * xx - 3.0 * yy),
        SH_THREE[4] * x * four,
        SH_THREE[5] * z * less,
        SH_THREE[6] * x * (xx - 3.0 * yy),
    ]


def slope_terms(c):
    d = [None] * 4 + [SH_TWO[i] * c[4 + i] for i in range(5)] + [SH_THREE[i] * c[9 + i] for i in range(7)]
    first = [-SH_ONE * c[3], -SH_ONE * c[1], SH_ONE * c[2]]
    in_x = (2.0 * (d[8] - d[6]), 6.0 * d[9] - 2.0 * d[11], 2.0 * d[14] - 6.0 * d[12], 3.0 * d[15])
    in_y = (-2.0 * (d[8] + d[6]), 3.0 * d[9], -2.0 * d[14] - 6.0 * d[12], -2.0 * d[13] - 6.0 * d[15])
    in_z = (4.0 * d[6], 8.0 * d[11], 8.0 * d[13])
    return d, first, in_x, in_y, in_z


def slope_of(x, y, z, terms):
    d, first, in_x, in_y, in_z = terms
    xx, yy, zz = x * x, y * y, z * z
    xy, yz, xz = x * y, y * z, x * z
    less, both = xx - yy, xx + yy
    four = 4.0 * zz - both
    g_x = (
        first[0] + d[4] * y + in_x[0] * x + d[7] * z + in_x[1] * xy + d[10] * yz + in_x[2] * xz
        + d[13] * (four - 2.0 * xx) + in_x[3] * less
    )
    g_y = (
        first[1] + d[4] * x + d[5] * z + in_y[0] * y + in_y[1] * less + d[10] * xz + d[11] * (four - 2.0 * yy)
        + in_y[2] * yz + in_y[3] * xy
    )
    g_z = (
        first[2] + d[5] * y + in_z[0] * z + d[7] * x + d[10] * xy + in_z[1] * yz + d[12] * (6.0 * zz - 3.0 * both)
        + in_z[2] * xz + d[14] * less
    )
    return [g_x, g_y, g_z]


def camera_rows(cam_ref, table, passes, cams):
    views = passes * cams
    for p in range(passes):
        cam = cam_ref[p]
        cos, sin = jnp.cos(cam), jnp.sin(cam)
        ca, cb, cg = [cos[:, k : k + 1] for k in range(3)]
        sa, sb, sg = [sin[:, k : k + 1] for k in range(3)]
        rotate = [
            [cg * cb, cg * sb * sa - sg * ca, cg * sb * ca + sg * sa],
            [sg * cb, sg * sb * sa + cg * ca, sg * sb * ca - cg * sa],
            [-sb, cb * sa, cb * ca],
        ]
        offset = [cam[:, 3:4], cam[:, 4:5], 6.0 + cam[:, 5:6]]
        center = [-(rotate[0][j] * offset[0] + rotate[1][j] * offset[1] + rotate[2][j] * offset[2]) for j in range(3)]
        for k, term in enumerate(rotate[0] + rotate[1] + rotate[2] + offset + center):
            table[k * views + p * cams : k * views + (p + 1) * cams, :] = jnp.broadcast_to(term, (cams, LANES))


def camera_of(table, view, views, shape):
    terms = [jnp.broadcast_to(table[k * views + view : k * views + view + 1, :], shape) for k in range(TERMS)]
    return [terms[0:3], terms[3:6], terms[6:9]], terms[9:12], terms[12:15]


def project_kernel(
    passes, cams, rows, owners, cap, folded, cols, far_pos, far_scales, far_rots, far_opac, far_cam, far_lists, far_wanted,
    far_counts, far_places, rec, raw, kept, scene, source, chosen,
    table, pos, scales, rots, opac, cam, lists, wanted, counts, places, done,
):
    views = passes * cams
    shape = (rows, LANES)
    fars = (far_cam, far_pos, far_scales, far_rots, far_opac, far_lists, far_wanted, far_counts, far_places)
    nears = (cam, pos, scales, rots, opac, lists, wanted, counts, places)
    copies = [pltpu.make_async_copy(away, near, done.at[k]) for k, (away, near) in enumerate(zip(fars, nears))]
    for copy in copies:
        copy.start()
    for i in range(rows):
        raw[pl.ds(11 * rows + i, cols.shape[0], stride=rows), :] = cols[:, i * LANES : (i + 1) * LANES]
    for copy in copies[:5]:
        copy.wait()
    camera_rows(cam, table, passes, cams)
    base = 0
    for ref in (pos, scales, rots):
        count = ref.shape[0]
        for i in range(rows):
            raw[pl.ds(base * rows + i, count, stride=rows), :] = ref[:, i * LANES : (i + 1) * LANES]
        base += count
    raw[base * rows : (base + 1) * rows, :] = opac[...]

    def at(k):
        return raw[k * rows : (k + 1) * rows, :]

    def put(ref, k, value):
        ref[k * rows : (k + 1) * rows, :] = value

    point = [at(k) for k in range(3)]
    squares = [jnp.exp(2.0 * at(3 + k)) for k in range(3)]
    spin, _, _ = spin_of([at(6 + k) for k in range(4)])
    cov = world_cov(spin, squares)
    opacity = 1.0 / (1.0 + jnp.exp(-at(10)))
    sight = []
    for view in range(views):
        rotate, offset, center = camera_of(table, view, views, shape)
        _, inv, main, at_x, at_y, t_x, t_y, w_x, w_y, conic = screen_of(point, cov, rotate, offset)
        direction, back = direction_of(point, center)
        basis = basis_of(*direction)
        fields = [FOCAL * at_x + CENTER_X, FOCAL * at_y + CENTER_Y, conic[0], conic[1], conic[2], opacity]
        for f, value in enumerate(fields):
            put(rec, view * FIELDS + f, value)
        r_x, r_y = [[dot3(rotate[i], w) for i in range(3)] for w in (w_x, w_y)]
        moves = []
        for g_main, g_sx, g_sy in (
            (2.0 * r_x[0], 2.0 * r_x[2], 0.0),
            (r_y[0] + r_x[1], r_y[2], r_x[2]),
            (2.0 * r_y[1], 0.0, 2.0 * r_y[2]),
        ):
            g_m = [g_sx, g_sy, g_main - 2.0 * (at_x * g_sx + at_y * g_sy)]
            size = -main * inv
            moves += [size * (rotate[0][j] * g_m[0] + rotate[1][j] * g_m[1] + rotate[2][j] * g_m[2]) for j in range(3)]
        sight.append((direction, back))
        for k, value in enumerate([*t_x, *t_y, *conic, *moves]):
            put(kept, view * KEPT + k, value)
        for k in range(1, 16):
            put(kept, view * KEPT + KEPT - 16 + k, basis[k])

    for copy in copies[5:]:
        copy.wait()
    entries, pixels = lists.shape[-1], wanted.shape[-1]
    entry_row = lax.broadcasted_iota(jnp.int32, (1, entries), 1)
    slot_owner, slot_lane = [], []
    for p in range(passes):
        for k in range(3):
            scene[p * SCENE + k : p * SCENE + k + 1, :] = wanted[p, k]
        count = jnp.broadcast_to(counts[:, p : p + 1], (1, entries))
        scene[p * SCENE + 3 : p * SCENE + 4, :] = jnp.where(entry_row < count, 1.0, 0.0)
        place = jnp.broadcast_to(places[:, p : p + 1], (1, entries))
        for k, value in enumerate((place % 256 * 16 + 8, place // 256 * 16 + 8)):
            scene[p * SCENE + 4 + k : p * SCENE + 5 + k, :] = value.astype(F32)
        owner, place = lax.div(lists[p, 0], cap), lax.rem(lists[p, 0], cap)
        if folded:
            groups = LANES // cap
            slot_owner.append(lax.div(owner, groups))
            slot_lane.append(lax.rem(owner + p, groups) * cap + place)
        else:
            slot_owner.append(owner)
            slot_lane.append(place + p * cap)
        chosen[p : p + 1, :] = slot_owner[p]
        chosen[passes + p : passes + p + 1, :] = slot_lane[p]
    pair = (LANES, LANES)
    turned = lax.broadcasted_iota(jnp.int32, pair, 0) & (LANES - 1 if folded else HALF - 1)
    entry = (lax.broadcasted_iota(jnp.int32, pair, 1) + 1).astype(F32)
    lines = GROUP if folded else owners
    line_at = lax.broadcasted_iota(jnp.int32, (lines, LANES), 0)
    halves = entries // LANES
    found = jnp.full((lines, LANES), -LANES, jnp.int32)
    for p in range(passes):
        for h in range(halves):
            part = slice(h * LANES, (h + 1) * LANES)
            mine = jnp.where(jnp.broadcast_to(slot_owner[p][:, part], (lines, LANES)) == line_at, 1.0, 0.0).astype(BF16)
            here = jnp.where(jnp.broadcast_to(slot_lane[p][:, part], pair) == turned, entry, 0.0).astype(BF16)
            hit = dot(mine, here, ((1,), (1,)))
            found = jnp.where(hit > 0.5, hit.astype(jnp.int32) + ((p * halves + h) * LANES - 1), found)
        if folded:
            source[p * GROUP : (p + 1) * GROUP, :] = found
            source[(passes + p) * GROUP : (passes + p + 1) * GROUP, :] = pltpu.roll(found, HALF, 1)
            found = jnp.full((lines, LANES), -LANES, jnp.int32)
    if not folded:
        source[...] = found

    for channel in range(3):
        totals = [0.5 + SH_ZERO * at(11 + channel)] * views
        for k in range(1, 16):
            color = at(11 + 3 * k + channel)
            for view in range(views):
                start = (view * KEPT + KEPT - 16 + k) * rows
                totals[view] = totals[view] + kept[start : start + rows, :] * color
        for view in range(views):
            put(rec, view * FIELDS + 6 + channel, totals[view])
    for channel in range(3):
        terms = slope_terms([at(11 + 3 * k + channel) for k in range(16)])
        for view in range(views):
            direction, back = sight[view]
            slope = slope_of(*direction, terms)
            along = dot3(direction, slope)
            for j in range(3):
                put(kept, view * KEPT + SHADE + 3 * channel + j, (slope[j] - direction[j] * along) * back)


def lane_pass(shape, cap):
    lane = lax.broadcasted_iota(jnp.int32, shape, 1) & (HALF - 1)
    return lax.div(lane, cap)


def ids_kernel(passes, cams, rows, cap, folded, ids, *refs):
    count = (len(refs) - 6) // 2
    sources, out, results = refs[:count], refs[count], refs[count + 1 : 2 * count + 1]
    landed, lines, ids_done, out_done, done = refs[2 * count + 1 :]
    first = pltpu.make_async_copy(ids, landed, ids_done)
    first.start()
    copies = [pltpu.make_async_copy(source, result, done.at[k]) for k, (source, result) in enumerate(zip(sources, results))]
    for copy in copies:
        copy.start()
    first.wait()
    for c in range(cams):
        parts = [landed[p, 0, 0, c] for p in range(passes)]
        tiles = parts[0].shape[0]
        if passes * cap < HALF:
            parts.append(jnp.zeros((tiles, HALF - passes * cap), jnp.int32))
        line = jnp.concatenate(parts + parts, axis=1)
        if folded:
            at_row, at_lane = [lax.broadcasted_iota(jnp.int32, line.shape, k) for k in range(2)]
            for m in range(1, passes):
                turned = parts[-m:] + parts[:-m]
                line = jnp.where(lax.rem(at_row, passes) == m, jnp.concatenate(turned + turned, axis=1), line)
            line = line + ((lax.div(at_lane, cap) - at_row) & (LANES // cap - 1)) * (rows * LANES)
        lines[c * tiles : (c + 1) * tiles, :] = line
    last = pltpu.make_async_copy(lines, out, out_done)
    last.start()
    for copy in copies:
        copy.wait()
    last.wait()


def pick_kernel(passes, cams, tiles, rows, cap, aligned, folded, ids, rec, out, inverse, turns):
    shape = (GROUP, LANES)
    lane = lax.broadcasted_iota(jnp.int32, shape, 1)
    sub = lax.broadcasted_iota(jnp.int32, shape, 0)
    if not aligned:
        turns[...] = jnp.zeros(turns.shape, jnp.int32)

    def packets(first, c):
        low, high = parted(ids[pl.ds(first, GROUP), :])
        if folded:
            tag, high = lax.div(high, rows), lax.rem(high, rows)
            lane_p, first_half = lax.rem(tag, passes), tag < passes
            blocks = [
                jnp.broadcast_to(jnp.max(jnp.where(lane_p == p, high, 0), axis=1, keepdims=True), shape)
                for p in range(passes)
            ]
        else:
            lane_p, first_half = lane_pass(shape, cap), lane < HALF
            blocks = [jnp.broadcast_to(high[:, p * cap : p * cap + 1], shape) for p in range(passes)]
        if aligned:
            for p in range(passes):
                turn = jnp.zeros(shape, jnp.int32)
                for t in range(1, tiles):
                    turn = jnp.where(jnp.broadcast_to(blocks[p][t : t + 1, :], shape) == sub, t, turn)
                turns[(p * cams + c) * rows : (p * cams + c + 1) * rows, :] = turn

        def pick(f):
            found = jnp.zeros(shape, F32)
            for p in range(passes):
                start = ((p * cams + c) * FIELDS + f) * rows
                if aligned:
                    own = lane_pick(row_pick(rec[start : start + rows, :], blocks[p]), low)
                else:
                    own = jnp.zeros(shape, F32)
                    for b in range(rows):
                        line = jnp.broadcast_to(rec[start + b : start + b + 1, :], shape)
                        own = jnp.where(high == b, lane_pick(line, low), own)
                found = own if p == 0 else jnp.where(lane_p == p, own, found)
            return found

        for r in range(SENT):
            value = pick(2 * r)
            if 2 * r + 1 < FIELDS:
                value = jnp.where(first_half, value, pick(2 * r + 1))
            out[pl.ds(first * SENT + r, GROUP, stride=SENT), :] = value

    for c in range(cams):
        if tiles == GROUP:
            packets(c * tiles, c)
        else:

            def step(k, carry, c=c):
                packets(pl.multiple_of(c * tiles + k * GROUP, GROUP), c)
                return carry

            lax.fori_loop(0, tiles // GROUP, step, 0)

    square = (LANES, LANES)
    column = lax.broadcasted_iota(jnp.int32, square, 0)
    turn = lax.broadcasted_iota(jnp.int32, square, 1)
    place = ((turn & (HALF - 1)) + 1 + jnp.where(turn < HALF, 0, LANES)).astype(F32)
    if folded:
        tag = lax.div(parted(jnp.broadcast_to(ids[0:1, :], square))[1], rows)
        place = (jnp.where(tag < passes, turn, ((turn + HALF) & (LANES - 1)) + LANES) + 1).astype(F32)
    wide = (passes * rows, LANES)
    wide_lane = lax.broadcasted_iota(jnp.int32, wide, 1)
    key = lax.broadcasted_iota(jnp.int32, wide, 0)
    lane_key = jnp.where((wide_lane & (HALF - 1)) < passes * cap, lane_pass(wide, cap) * rows, -(1 << 20))
    line_lane = lax.broadcasted_iota(jnp.int32, (1, LANES), 1)

    def two(c, t, found):
        these, next_ones = ids[pl.ds(c * tiles + t, 1), :], ids[pl.ds(c * tiles + t + 1, 1), :]
        if folded:
            low, high = parted(jnp.where(these < passes * rows * LANES, these, next_ones))
            high = lax.rem(high, rows * passes)
        else:
            low, high = parted(jnp.where(line_lane < HALF, these, next_ones))
        low = jnp.broadcast_to(low, square)
        high = jnp.broadcast_to(high, wide)
        match = jnp.where(low == column, place, 0.0).astype(BF16)
        owner = jnp.where((high if folded else high + lane_key) == key, 1.0, 0.0).astype(BF16)
        hit = dot(owner, match, ((1,), (1,)))
        return jnp.where(hit > 0.5, hit.astype(jnp.int32) + t * LANES, found)

    for c in range(cams):
        found = jnp.zeros(wide, jnp.int32)
        if tiles <= 8:
            for t in range(0, tiles, 2):
                found = two(c, t, found)
        else:
            found = lax.fori_loop(0, tiles // 2, lambda t, f, c=c: two(c, 2 * t, f), found)
        for p in range(passes):
            start = (p * cams + c) * rows
            inverse[start : start + rows, :] = found[p * rows : (p + 1) * rows, :]


def render_kernel(passes, owners, cap, folded, entries, pixels, got, lists, scene, source, out, *scratch):
    alphas, ratios, weights, pulls, before_sums, slopes, after_sums = [scratch[k * passes : (k + 1) * passes] for k in range(7)]
    clears, shares, pulled_parts = [
        [scratch[(7 + 2 * k) * passes + p :: passes][:2] for p in range(passes)] for k in range(3)
    ]
    halves = entries // LANES
    shape = (GROUP, LANES)
    wide = 16
    lane = lax.broadcasted_iota(jnp.int32, shape, 1)
    sub = lax.broadcasted_iota(jnp.int32, shape, 0)

    slot_owner, slot_lane = [], []
    for p in range(passes):
        for h in range(halves):
            part = slice(h * LANES, (h + 1) * LANES)
            slot_owner.append(jnp.broadcast_to(lists[p : p + 1, part], shape))
            slot_lane.append(jnp.broadcast_to(lists[passes + p : passes + p + 1, part], shape))
    total = passes * halves

    groups = LANES // cap
    lane_group = lax.div(lane, cap)

    def merged(choices, back):
        value = choices[-back % groups]
        for g in range(1, groups):
            value = jnp.where(lane_group == g, choices[(g - back) % groups], value)
        return value

    def gather(g, found):
        mine = [slot_owner[i] == g * GROUP + sub for i in range(total)]
        new = []
        for f in range(FIELDS):
            lines = got[pl.ds(g * (GROUP * SENT) + f // 2, GROUP, stride=SENT), :]
            for i in range(total):
                new.append(jnp.where(mine[i], lane_pick(lines, slot_lane[i] + f % 2 * HALF), found[f * total + i]))
        return tuple(new)

    fields = tuple(jnp.zeros(shape, F32) for _ in range(FIELDS * total))
    if folded:
        mine = [slot_owner[i] == sub for i in range(total)]
        places = [slot_lane, [(x + HALF) & (LANES - 1) for x in slot_lane]]
        fields = []
        for f in range(FIELDS):
            packets = [got[pl.ds(m * SENT + f // 2, GROUP, stride=groups * SENT), :] for m in range(groups)]
            for p in range(passes):
                tile = merged(packets, f % 2 * passes + p)
                for i in range(p * halves, (p + 1) * halves):
                    fields.append(jnp.where(mine[i], lane_pick(tile, places[f % 2][i]), 0.0))
    elif owners <= 32:
        for g in range(owners // GROUP):
            fields = gather(g, fields)
    else:
        fields = lax.fori_loop(0, owners // GROUP, gather, fields)
    fields = [jnp.sum(x, axis=0, keepdims=True) for x in fields]

    row_at, column_at = [lax.broadcasted_iota(jnp.int32, (entries, entries), k) for k in range(2)]
    before = jnp.where(row_at < column_at, 1.0, 0.0).astype(BF16)
    after = jnp.where(row_at > column_at, 1.0, 0.0).astype(BF16)
    column_x = lax.broadcasted_iota(jnp.int32, (wide, entries), 0).astype(F32) - 7.5
    steps = [slice(y * wide, (y + 1) * wide) for y in range(pixels // wide)]

    lines, spans = [], []
    for p in range(passes):
        line = [
            jnp.concatenate([fields[f * total + p * halves + h] for h in range(halves)], axis=1) for f in range(FIELDS)
        ]
        line[0] = line[0] - scene[p * SCENE + 4 : p * SCENE + 5, :]
        line[1] = line[1] - scene[p * SCENE + 5 : p * SCENE + 6, :]
        lines.append(line)
        spans.append(column_x - line[0])

    def offset_y(p, y):
        return (y - 7.5) - lines[p][1]

    def through(parts, at, matrix):
        return dot(parts[0][at, :], matrix, ((1,), (0,))) + dot(parts[1][at, :], matrix, ((1,), (0,)))

    consts = []
    for p in range(passes):
        _, _, c_a, c_b, c_c, base = lines[p][:6]
        live = base * scene[p * SCENE + 3 : p * SCENE + 4, :]
        consts.append((live, (-0.5 * c_a) * spans[p] * spans[p], -c_b * spans[p], 0.5 * c_c))

    def blend(p, y, at):
        live, q_xx, q_x, c_c = consts[p]
        d_y = offset_y(p, y)
        alpha = live * jnp.exp(q_xx + (q_x * d_y - c_c * d_y * d_y))
        clear = jnp.log(1.0 - alpha)
        alphas[p][at, :] = alpha
        ratios[p][at, :] = alpha * jnp.exp(-clear)
        clears[p][0][at, :], clears[p][1][at, :] = split(clear)

    def weigh(p, y, at):
        weight = alphas[p][at, :] * jnp.exp(before_sums[p][at, :])
        weights[p][at, :] = weight
        shares[p][0][at, :], shares[p][1][at, :] = split(weight)

    def pull(p, y, at):
        pulled = weights[p][at, :] * slopes[p][at, :]
        pulls[p][at, :] = pulled
        pulled_parts[p][0][at, :], pulled_parts[p][1][at, :] = split(pulled)

    totals = [[jnp.zeros((wide, entries), F32)] * 3 for _ in range(passes)]

    def add(p, y, at):
        m_1, m_y, m_yy = totals[p]
        grad = pulls[p][at, :] - ratios[p][at, :] * after_sums[p][at, :]
        d_y = offset_y(p, y)
        grad_y = grad * d_y
        totals[p] = [m_1 + grad, m_y + grad_y, m_yy + grad_y * d_y]

    blocks = [slice(n, n + 128) for n in range(0, pixels, 128)]
    both = range(passes)

    def each(work, p, block):
        for y, at in enumerate(steps):
            if block.start <= at.start < block.stop:
                work(p, y, at)

    def sum_before(p, block):
        before_sums[p][block, :] = through(clears[p], block, before)

    def sum_after(p, block):
        after_sums[p][block, :] = through(pulled_parts[p], block, after)

    def slope(p, block):
        r_high, r_low = [r[:, block] for r in residuals[p]]
        slopes[p][block, :] = dot(jnp.concatenate([r_high, r_high, r_low], axis=0), pair_rows[p], ((0,), (0,)))

    def emit(first, second, third):
        jobs = [(block, p) for block in blocks for p in both]
        depth = 2
        for n in range(len(jobs) + 2 * depth):
            if n < len(jobs) and first:
                each(first, jobs[n][1], jobs[n][0])
            if 0 <= n - depth < len(jobs):
                second(jobs[n - depth][1], jobs[n - depth][0])
            if 0 <= n - 2 * depth < len(jobs):
                each(third, jobs[n - 2 * depth][1], jobs[n - 2 * depth][0])

    emit(blend, sum_before, weigh)
    residuals, pair_rows = [], []
    for p in both:
        c_high, c_low = split(jnp.concatenate(lines[p][6:9], axis=0))
        pair = dot(jnp.concatenate([c_high, c_low], axis=0), shares[p][0][...], ((1,), (1,)))
        shown = pair[0:3, :] + pair[3:6, :] + dot(c_high, shares[p][1][...], ((1,), (1,)))
        residuals.append(split(shown - scene[p * SCENE : p * SCENE + 3, :]))
        pair_rows.append(jnp.concatenate([c_high, c_low, c_high], axis=0))
    for block in blocks:
        for p in both:
            slope(p, block)
    emit(pull, sum_after, add)
    color_grads = []
    for p in both:
        r_high, r_low = residuals[p]
        pair = dot(jnp.concatenate([r_high, r_low], axis=0), shares[p][0][...], ((1,), (0,)))
        color_grads.append(pair[0:3, :] + pair[3:6, :] + dot(r_high, shares[p][1][...], ((1,), (0,))))
    grads = []
    for p in both:
        m_1, m_y, m_yy = totals[p]
        d_x = spans[p]
        m_x = m_1 * d_x
        s_1, s_x, s_y, s_xx, s_xy, s_yy = [
            jnp.sum(m, axis=0, keepdims=True) for m in (m_1, m_x, m_y, m_x * d_x, m_y * d_x, m_yy)
        ]
        _, _, c_a, c_b, c_c, base = lines[p][:6]
        grads.append(
            [
                c_a * s_x + c_b * s_y,
                c_b * s_x + c_c * s_y,
                -0.5 * s_xx,
                -s_xy,
                -0.5 * s_yy,
                s_1 / base,
                color_grads[p][0:1, :],
                color_grads[p][1:2, :],
                color_grads[p][2:3, :],
            ]
        )

    def pick(f, which, index, tiles):
        found = jnp.zeros(shape, F32)
        for p, h in tiles:
            line = jnp.broadcast_to(grads[p][f][:, h * LANES : (h + 1) * LANES], shape)
            found = jnp.where(which == p * halves + h, lane_pick(line, index), found)
        return found

    if folded:
        codes = [parted(source[n * GROUP : (n + 1) * GROUP, :]) for n in range(2 * passes)]
        for r in range(SENT):
            parts = []
            for n, (index, which) in enumerate(codes):
                p, f = n % passes, min(2 * r + n // passes, FIELDS - 1)
                parts.append(pick(f, which, index, [(p, h) for h in range(halves)]) if 2 * r + n // passes < FIELDS else parts[p])
            for m in range(groups):
                out[pl.ds(m * SENT + r, GROUP, stride=groups * SENT), :] = merged(parts, m)
        return

    every = [(p, h) for p in range(passes) for h in range(halves)]
    for g in range(owners // GROUP):
        index, which = parted(source[g * GROUP : (g + 1) * GROUP, :])
        for r in range(SENT):
            value = pick(2 * r, which, index, every)
            if 2 * r + 1 < FIELDS:
                value = jnp.where(lane < HALF, value, pick(2 * r + 1, which, index, every))
            out[pl.ds(g * GROUP * SENT + r, GROUP, stride=SENT), :] = value


def pull_kernel(
    passes, cams, tiles, rows, cap, aligned, got, inverse, turns, raw, kept,
    far_pos, far_scales, far_rots, far_opac, far_cols, total, pos, scales, rots, opac, cols, done,
):
    views = passes * cams
    shape = (rows, LANES)

    def at(k):
        return raw[k * rows : (k + 1) * rows, :]

    squares = [jnp.exp(2.0 * at(3 + k)) for k in range(3)]
    spin, quat, quat_back = spin_of([at(6 + k) for k in range(4)])
    opacity = 1.0 / (1.0 + jnp.exp(-at(10)))

    def fetcher(view):
        p, c = view // cams, view % cams
        slot = inverse[view * rows : (view + 1) * rows, :] - 1
        valid = slot >= 0
        slot_lane, slot_t = parted(jnp.maximum(slot, 0))
        row_t = turns[view * rows : (view + 1) * rows, :]
        turned = {}

        def fetch(f):
            row, shift = f // 2, f % 2 * HALF
            if aligned:
                if row not in turned:
                    turned[row] = row_pick(got[pl.ds(c * tiles * SENT + row, tiles, stride=SENT), :], row_t)
                return jnp.where(valid, lane_pick(turned[row], (slot_lane + shift) & (LANES - 1)), 0.0)

            def one(t, found):
                line = jnp.broadcast_to(got[pl.ds((c * tiles + t) * SENT + row, 1), :], shape)
                return jnp.where(valid & (slot_t == t), lane_pick(line, (slot_lane + shift) & (LANES - 1)), found)

            return lax.fori_loop(0, tiles, one, jnp.zeros(shape, F32))

        return fetch

    def held(view, k):
        start = (view * KEPT + k) * rows
        return kept[start : start + rows, :]

    fetchers = [fetcher(view) for view in range(views)]
    shades = [[fetchers[view](6 + channel) for view in range(views)] for channel in range(3)]
    copies = []

    def send(near, away):
        copies.append(pltpu.make_async_copy(near, away, done.at[len(copies)]))
        copies[-1].start()

    sent = 0
    for k in range(16):
        basis = [held(view, KEPT - 16 + k) for view in range(views)] if k else None
        for channel in range(3):
            terms = shades[channel] if k == 0 else [basis[view] * shades[channel][view] for view in range(views)]
            while len(terms) > 1:
                terms = [sum(terms[n : n + 2][1:], terms[n]) for n in range(0, len(terms), 2)]
            start = (11 + 3 * k + channel) * rows
            total[start : start + rows, :] = terms[0] if k else SH_ZERO * terms[0]
        ready = (3 * k + 3) // 16 * 16
        if ready > sent:
            for i in range(rows):
                cols[sent:ready, i * LANES : (i + 1) * LANES] = total[pl.ds((11 + sent) * rows + i, ready - sent, stride=rows), :]
            send(cols.at[pl.ds(sent, ready - sent), :], far_cols.at[pl.ds(sent, ready - sent), :])
            sent = ready


    g_point = [jnp.zeros(shape, F32) for _ in range(3)]
    g_cov = [[jnp.zeros(shape, F32) for _ in range(3)] for _ in range(3)]
    g_opacity = jnp.zeros(shape, F32)
    for view in range(views):
        g = [fetchers[view](f) for f in range(6)] + [shades[channel][view] for channel in range(3)]
        t_x, t_y, conic, m_xx, m_xy, m_yy, s_r, s_g, s_b = [[held(view, 3 * n + k) for k in range(3)] for n in range(9)]
        c_a, c_b, c_c = conic
        half = 0.5 * g[3]
        p00, p01 = g[2] * c_a + half * c_b, g[2] * c_b + half * c_c
        p10, p11 = half * c_a + g[4] * c_b, half * c_b + g[4] * c_c
        g_xx = -(c_a * p00 + c_b * p10)
        g_xy = -(c_a * p01 + c_b * p11)
        g_yy = -(c_b * p01 + c_c * p11)
        left = [g_xx * t_x[i] + g_xy * t_y[i] for i in range(3)]
        right = [g_yy * t_y[i] + g_xy * t_x[i] for i in range(3)]
        for i in range(3):
            for j in range(i, 3):
                g_cov[i][j] = g_cov[i][j] + (t_x[i] * left[j] + t_y[i] * right[j])
        pulls = ((t_x, g[0]), (t_y, g[1]), (m_xx, g_xx), (m_xy, 2.0 * g_xy), (m_yy, g_yy), (s_r, g[6]), (s_g, g[7]), (s_b, g[8]))
        for j in range(3):
            for slope, value in pulls:
                g_point[j] = g_point[j] + slope[j] * value
        g_opacity = g_opacity + g[5]
    for i in range(3):
        for j in range(i):
            g_cov[i][j] = g_cov[j][i]

    g_scales = []
    g_spin = [[None] * 3 for _ in range(3)]
    for k in range(3):
        column = [spin[j][k] for j in range(3)]
        turned = [dot3(g_cov[i], column) for i in range(3)]
        g_scales.append(2.0 * squares[k] * dot3(column, turned))
        for i in range(3):
            g_spin[i][k] = 2.0 * squares[k] * turned[i]
    w, x, y, z = quat
    d = g_spin
    g_quat = [
        2.0 * (z * (d[1][0] - d[0][1]) + y * (d[0][2] - d[2][0]) + x * (d[2][1] - d[1][2])),
        2.0 * (y * (d[0][1] + d[1][0]) + z * (d[0][2] + d[2][0]) + w * (d[2][1] - d[1][2]) - 2.0 * x * (d[1][1] + d[2][2])),
        2.0 * (x * (d[0][1] + d[1][0]) + z * (d[1][2] + d[2][1]) + w * (d[0][2] - d[2][0]) - 2.0 * y * (d[0][0] + d[2][2])),
        2.0 * (x * (d[0][2] + d[2][0]) + y * (d[1][2] + d[2][1]) + w * (d[1][0] - d[0][1]) - 2.0 * z * (d[0][0] + d[1][1])),
    ]
    along = w * g_quat[0] + x * g_quat[1] + y * g_quat[2] + z * g_quat[3]
    g_rots = [(g_quat[k] - quat[k] * along) * quat_back for k in range(4)]
    opac[...] = g_opacity * opacity * (1.0 - opacity)
    for k, value in enumerate(g_point + g_scales + g_rots):
        total[k * rows : (k + 1) * rows, :] = value
    base = 0
    for ref in (pos, scales, rots):
        count = ref.shape[0]
        for i in range(rows):
            ref[:, i * LANES : (i + 1) * LANES] = total[pl.ds(base * rows + i, count, stride=rows), :]
        base += count
    for near, away in ((pos, far_pos), (scales, far_scales), (rots, far_rots), (opac, far_opac)):
        send(near, away)
    for copy in copies:
        copy.wait()


def render_scratch(passes, pixels, entries):
    return [pltpu.VMEM((pixels, entries), F32)] * (7 * passes) + [pltpu.VMEM((pixels, entries), BF16)] * (6 * passes)


def vmem(count):
    return [pl.BlockSpec(memory_space=pltpu.VMEM)] * count


def call(kernel, outs, operands, in_specs=None, scratch=(), flops=1_000_000, out_specs=None):
    return pl.pallas_call(
        kernel,
        out_shape=outs,
        in_specs=in_specs or vmem(len(operands)),
        out_specs=out_specs or jax.tree.map(lambda _: pl.BlockSpec(memory_space=pltpu.VMEM), outs),
        scratch_shapes=list(scratch),
        compiler_params=pltpu.CompilerParams(vmem_limit_bytes=32 << 20),
        cost_estimate=pl.CostEstimate(flops=flops, bytes_accessed=1 << 20, transcendentals=0),
    )(*operands)


def body(
    cams,
    tiles,
    positions,
    log_scales,
    rotations,
    opacities,
    colors,
    cameras,
    targets,
    tile_ids,
    tile_counts,
    tile_lists,
    fetch_ids,
):
    axes = ("cam", "tile")
    passes, cap = fetch_ids.shape[0], fetch_ids.shape[-1]
    entries, pixels = tile_lists.shape[-1], targets.shape[-1]
    columns = positions.shape[-1]
    rows = columns // LANES
    owners = cams * tiles
    views = passes * cams
    aligned = tiles == rows == GROUP
    folded = 2 * passes * cap == LANES and owners * cap == GROUP * LANES and tiles % (LANES // cap) == 0

    def shaped(*shape):
        return jax.ShapeDtypeStruct(shape, F32)

    def exchange(x):
        lines = x.reshape(owners, 1, -1)
        return lax.all_to_all(lines, axes, split_axis=0, concat_axis=0, tiled=True).reshape(x.shape)

    whole, smem, far = [pl.BlockSpec(memory_space=space) for space in (pltpu.VMEM, pltpu.SMEM, pltpu.HBM)]
    near = [colors]
    wanted_ids, *near = call(
        functools.partial(ids_kernel, passes, cams, rows, cap, folded),
        [jax.ShapeDtypeStruct((owners, LANES), jnp.int32)]
        + [pltpu.VMEM(x.shape, x.dtype) for x in near],
        [pltpu.with_memory_space_constraint(x, pltpu.HBM) for x in (fetch_ids, *near)],
        in_specs=[far] * (1 + len(near)),
        out_specs=[far] + [whole] * len(near),
        scratch=[
            pltpu.VMEM(fetch_ids.shape, jnp.int32),
            pltpu.VMEM((owners, LANES), jnp.int32),
            pltpu.SemaphoreType.DMA,
            pltpu.SemaphoreType.DMA,
            pltpu.SemaphoreType.DMA((len(near),)),
        ],
    )
    arrived = exchange(wanted_ids)
    small = [
        positions,
        log_scales,
        rotations,
        opacities.reshape(rows, LANES),
        cameras,
        tile_lists,
        targets.reshape(passes, 3, 1, pixels),
        tile_counts.reshape(1, passes),
        tile_ids.reshape(1, passes),
    ]
    records, raw, kept, scene, source, lists = call(
        functools.partial(project_kernel, passes, cams, rows, owners, cap, folded),
        [
            shaped(views * FIELDS * rows, LANES),
            shaped(RAW * rows, LANES),
            shaped(views * KEPT * rows, LANES),
            shaped(passes * SCENE, entries),
            jax.ShapeDtypeStruct((2 * passes * GROUP if folded else owners, LANES), jnp.int32),
            jax.ShapeDtypeStruct((2 * passes, entries), jnp.int32),
        ],
        [*near, *[pltpu.with_memory_space_constraint(x, pltpu.HBM) for x in small]],
        in_specs=[whole] * 1 + [far] * len(small),
        scratch=[pltpu.VMEM((TERMS * views, LANES), F32)]
        + [pltpu.VMEM(x.shape, x.dtype) for x in small]
        + [pltpu.SemaphoreType.DMA((len(small),))],
    )
    codes = jax.ShapeDtypeStruct((views * rows, LANES), jnp.int32)
    packets, inverse, turns = call(
        functools.partial(pick_kernel, passes, cams, tiles, rows, cap, aligned, folded),
        [shaped(owners * SENT, LANES), codes, codes],
        [arrived, records],
    )
    fetched = exchange(packets)
    slot_grads = call(
        functools.partial(render_kernel, passes, owners, cap, folded, entries, pixels),
        shaped(owners * SENT, LANES),
        [fetched, lists, scene, source],
        scratch=render_scratch(passes, pixels, entries),
    )
    coming = exchange(slot_grads)
    g_pos, g_scales, g_rots, g_opac, g_cols = call(
        functools.partial(pull_kernel, passes, cams, tiles, rows, cap, aligned),
        [shaped(3, columns), shaped(3, columns), shaped(4, columns), shaped(rows, LANES), shaped(*colors.shape)],
        [coming, inverse, turns, raw, kept],
        out_specs=[far] * 5,
        scratch=[pltpu.VMEM((RAW * rows, LANES), F32)]
        + [pltpu.VMEM(shape, F32) for shape in ((3, columns), (3, columns), (4, columns), (rows, LANES), colors.shape)]
        + [pltpu.SemaphoreType.DMA((7,))],
    )
    return (g_pos, g_scales, g_rots, g_opac.reshape(columns), g_cols)


def solution(mesh):
    return jax.shard_map(
        functools.partial(body, mesh.shape["cam"], mesh.shape["tile"]),
        mesh=mesh,
        in_specs=(
            P(None, ("cam", "tile")),
            P(None, ("cam", "tile")),
            P(None, ("cam", "tile")),
            P(("cam", "tile")),
            P(None, ("cam", "tile")),
            P(),
            P(None, "cam", "tile", None, None),
            P(None, "cam", "tile"),
            P(None, "cam", "tile"),
            P(None, "cam", "tile", None),
            P(None, "cam", "tile", None, None, None),
        ),
        out_specs=(
            P(None, ("cam", "tile")),
            P(None, ("cam", "tile")),
            P(None, ("cam", "tile")),
            P(("cam", "tile")),
            P(None, ("cam", "tile")),
        ),
        check_vma=False,
    )
```
